32 devices in a mesh: grp: 2 (over x), tile: 8 (over z, y), lev: 2 (over core).
Axes of the slice: x: 2, y: 2, z: 4, core: 2. Of those that a mesh axis runs over, the one named last changes fastest.
Arguments:
- perturb: bfloat16 [32, 80, 2048], P('lev', 'grp', 'tile'), may hold values from -0.625 to 0.625
- control: float32 [32, 80, 2048], P('lev', 'grp', 'tile'), may hold values from -6 to 6
- level_loc: float32 [32, 32], P('lev'), may hold values from 0 to 1
- static_control: float32 [32, 8192], P('lev', 'tile'), may hold values from -6 to 6
- filter_diag: float32 [8192], P('tile'), may hold values from 0.5 to 2
- filter_off: float32 [8192], P('tile'), may hold values from 0.2 to 0.6
- send_src: int32 [8, 8, 128], P('tile'), may hold values from 0 to 255
- send_wt: float32 [8, 8, 128], P('tile'), may hold values from 0.2 to 1
- counts: int32 [8, 8], P('tile'), may hold values from 1 to 128, as said below
- recv_tgt: int32 [8, 8, 128], P('tile'), may hold values from 0 to 1023
- obs_weight: float32 [32, 8192], P('lev', 'tile'), may hold values from 0.2 to 2
- innovation: float32 [32, 8192], P('lev', 'tile'), may hold values from -6 to 6
Outputs:
- increment: float32 [32, 8192], P('lev', 'tile')
- grad_static: float32 [32, 8192], P('lev', 'tile')
- grad_ens: float32 [32, 80, 2048], P('lev', 'grp', 'tile')
The draws below stay inside these ranges and needn't reach their ends.
Inputs may be any that keep to these rules, and one draw needn't show every extreme that they name: Slot j from band s to tile d is the same intersection in send_src[s, d, j], send_wt[s, d, j] and recv_tgt[d, s, j]; only slots below counts[s, d] are live. One tile receives 128 live slots from every band.
All inputs are finite; a program needn't handle non-finite values.
Results may differ from the reference program's by a relative error of at most 0.0003.
Values may be sent and summed in bfloat16 or wider, within the bound.
No kernel may reach another device: no remote copies, remote signals or barrier semaphores. Data moves between devices by JAX's collectives and lax.ppermute only.
A program may use at most 64 MiB of HBM per device.

```python
import math
import jax
import jax.numpy as jnp
from jax import lax

LEV = 32
NE = 80
BCOLS = 256
TCOLS = 1024
CAP = 128
NB = 2048
NA = 8192
N_TILE = 8


def draw_level_loc(key, part):
    key = jax.random.fold_in(key, 7)
    levels = jnp.arange(LEV, dtype=jnp.float32)
    spacing = (levels[:, None] - levels[None, :]) / (LEV / 4.0)
    jitter = jax.random.uniform(key, (LEV, LEV), jnp.float32)
    return jnp.exp(-spacing * spacing) * (0.5 + jitter) / jnp.sqrt(LEV / 4.0)


def draw_counts(key, part):
    key = jax.random.fold_in(key, 11)
    first_key, second_key = jax.random.split(key)
    common = jax.random.randint(first_key, (N_TILE, N_TILE), 1, CAP // 2 + 1)
    busiest = jax.random.randint(second_key, (), 0, N_TILE)
    column = jnp.arange(N_TILE, dtype=jnp.int32)[None, :]
    return jnp.where(column == busiest, CAP, common).astype(jnp.int32)


def set_ends(drawn, rng, least, high):
    dims = drawn.shape
    spot = [jax.random.randint(jax.random.fold_in(rng, axis), (), 0, dims[axis]) for axis in range(len(dims))]
    drawn = drawn.at[tuple(spot)].set(least)
    longest = dims.index(max(dims))
    spot[longest] = (spot[longest] + 1) % dims[longest]
    return drawn.at[tuple(spot)].set(high)


def block_levels(own_key, extent, pieces, least, high):
    def one(position, shards_of):
        draws = jax.random.uniform(jax.random.fold_in(jax.random.fold_in(own_key, 6), position), (shards_of,), jnp.float32, least / len(pieces), high / len(pieces))
        return jnp.repeat(jnp.exp(draws), extent[position] // shards_of).reshape((-1,) + (1,) * (len(extent) - position - 1))

    gain = one(*pieces[0])
    for cut in pieces[1:]:
        gain = gain * one(*cut)
    return gain


def noise(own_key, extent, spread, limit, pieces=(), kind=jnp.bfloat16):
    level = block_levels(own_key, extent, pieces, -0.22, 0.18) if pieces else 1.0
    array = jax.random.normal(own_key, extent, jnp.float32) * spread * level
    return jnp.minimum(jnp.maximum(array, -limit), limit).astype(kind)


def setup_inputs(seed: int = 0) -> dict:
    splits = jax.random.split(jax.random.key(seed), 13)
    perturb = noise(splits[0], (LEV, NE, NB), NE ** -0.5, 0.625, ((0, 2), (1, 2), (2, 8)))
    control = noise(splits[1], (LEV, NE, NB), 1.0, 6.0, ((0, 2), (1, 2), (2, 8)), jnp.float32)
    level_loc = draw_level_loc(jax.random.fold_in(splits[12], 71), 0)
    static_control = noise(splits[3], (LEV, NA), 1.0, 6.0, ((0, 2), (1, 8)), jnp.float32)
    filter_diag = jnp.clip(jnp.exp(math.log(2.0) - 1.3862944 * jax.random.uniform(splits[4], (NA,), jnp.float32) ** block_levels(splits[4], (NA,), ((0, 8),), -0.2, 0.2)), 0.5, 2.0)
    filter_off = jnp.clip(jnp.exp(math.log(0.6) - 1.0986123 * jax.random.uniform(splits[5], (NA,), jnp.float32) ** block_levels(splits[5], (NA,), ((0, 8),), -0.2, 0.2)), 0.2, 0.6)
    send_src = set_ends(jax.random.randint(splits[6], (N_TILE, N_TILE, CAP), 0, BCOLS), jax.random.fold_in(splits[6], 1), 0, BCOLS - 1).astype(jnp.int32)
    send_wt = jnp.clip(jnp.exp(math.log(1.0) - 1.609438 * jax.random.uniform(splits[7], (N_TILE, N_TILE, CAP), jnp.float32) ** block_levels(splits[7], (N_TILE, N_TILE, CAP), ((0, 8),), -0.2, 0.2)), 0.2, 1.0)
    counts = draw_counts(jax.random.fold_in(splits[12], 71), 0)
    recv_tgt = set_ends(jax.random.randint(splits[9], (N_TILE, N_TILE, CAP), 0, TCOLS), jax.random.fold_in(splits[9], 1), 0, TCOLS - 1).astype(jnp.int32)
    obs_weight = jnp.clip(jnp.exp(math.log(2.0) - 2.3025851 * jax.random.uniform(splits[10], (LEV, NA), jnp.float32) ** block_levels(splits[10], (LEV, NA), ((0, 2), (1, 8)), -0.2, 0.2)), 0.2, 2.0)
    innovation = noise(splits[11], (LEV, NA), 1.0, 6.0, ((0, 2), (1, 8)), jnp.float32)
    return dict(perturb=perturb, control=control, level_loc=level_loc, static_control=static_control, filter_diag=filter_diag, filter_off=filter_off, send_src=send_src, send_wt=send_wt, counts=counts, recv_tgt=recv_tgt, obs_weight=obs_weight, innovation=innovation)


def neighbours(values):
    zero_col = jnp.zeros_like(values[:, :1])
    left_side = jnp.concatenate([zero_col, values[:, :-1]], axis=1)
    right_side = jnp.concatenate([values[:, 1:], zero_col], axis=1)
    return left_side, right_side


def reference(perturb, control, level_loc, static_control, filter_diag, filter_off, send_src, send_wt, counts, recv_tgt, obs_weight, innovation):
    highest = lax.Precision.HIGHEST
    localized = jnp.einsum("kl,lmc->kmc", level_loc, control, precision=highest)
    band_sum = jnp.sum(perturb.astype(jnp.float32) * localized, axis=1)
    band_index = jnp.arange(N_TILE, dtype=jnp.int32)
    source = (band_index[:, None, None] * BCOLS + send_src).reshape(-1)
    target = (band_index[None, :, None] * TCOLS + jnp.transpose(recv_tgt, (1, 0, 2))).reshape(-1)
    slot_index = jnp.arange(CAP, dtype=jnp.int32)
    factor = jnp.where(slot_index[None, None, :] < counts[:, :, None], send_wt, jnp.zeros_like(send_wt)).reshape(-1)

    def remap_row(one_row):
        return jnp.zeros((NA,), jnp.float32).at[target].add(one_row[source] * factor)

    remapped = lax.map(remap_row, band_sum)
    left_side, right_side = neighbours(static_control)
    increment = remapped + filter_diag * static_control + filter_off * (left_side + right_side)
    misfit = obs_weight * (increment - innovation)
    left_side, right_side = neighbours(filter_off * misfit)
    grad_static = static_control + filter_diag * misfit + left_side + right_side

    def adjoint_row(one_row):
        return jnp.zeros((NB,), jnp.float32).at[source].add(one_row[target] * factor)

    band_grad = lax.map(adjoint_row, misfit)
    weighted = perturb.astype(jnp.float32) * band_grad[:, None, :]
    grad_ens = control + jnp.einsum("kl,kmc->lmc", level_loc, weighted, precision=highest)
    return increment, grad_static, grad_ens
```

```python
import functools

import jax
import jax.numpy as jnp
from jax import lax
from jax.experimental import pallas as pl
from jax.experimental.pallas import tpu as pltpu
from jax.sharding import PartitionSpec as P

F32 = jnp.float32
BF16 = jnp.bfloat16
SUB = 8
EXTRA = 8
VMEM = pl.BlockSpec(memory_space=pltpu.VMEM)
SMEM = pl.BlockSpec(memory_space=pltpu.SMEM)
PARAMS = pltpu.CompilerParams(vmem_limit_bytes=40 * 1024 * 1024)


def halves(values):
    high = values.astype(BF16)
    low = (values - high.astype(F32)).astype(BF16)
    return high, low


def product(a, b, dims=((1,), (0,))):
    return lax.dot_general(a, b, (dims, ((), ())), preferred_element_type=F32)


def select(values, chosen, dims=((1,), (0,))):
    rows = values.shape[0]
    both = product(jnp.concatenate(halves(values), axis=0), chosen, dims)
    return both[:rows] + both[rows:]


def spread(matrix, first, second):
    rows, cols = matrix.shape
    row = lax.broadcasted_iota(jnp.int32, (rows * SUB, rows), 0) // SUB
    left = (row == lax.broadcasted_iota(jnp.int32, (rows * SUB, rows), 1) ).astype(F32)
    col = lax.broadcasted_iota(jnp.int32, (cols, cols * SUB), 1) // SUB
    turned = (col + second) % cols
    right = (turned == lax.broadcasted_iota(jnp.int32, (cols, cols * SUB), 0)).astype(BF16)
    out = []
    same = (
        lax.broadcasted_iota(jnp.int32, (rows * SUB, cols * SUB), 0) % SUB
        == lax.broadcasted_iota(jnp.int32, (rows * SUB, cols * SUB), 1) % SUB
    )
    for part in halves(matrix):
        wide = product(part, right)
        tall = product(left.astype(BF16), wide.astype(BF16))
        out.append(jnp.where(same, tall, 0.0).astype(BF16))
    return out


def mix(weights, values):
    high, low = halves(values)
    return product(weights[0], high) + (product(weights[0], low) + product(weights[1], high))


def one_hot(index, size):
    rows = lax.broadcasted_iota(jnp.int32, (size, index.shape[1]), 0)
    return jnp.where(rows == index, 1.0, 0.0).astype(BF16)


def column_as_row(column, lane, offset):
    n = column.shape[0]
    place = lax.broadcasted_iota(jnp.int32, (n, 128), 1) == lax.broadcasted_iota(jnp.int32, (n, 128), 0) + offset
    return jnp.sum(jnp.where(place, column, 0.0), axis=0, keepdims=True)


def row_as_column(row, n, offset):
    place = lax.broadcasted_iota(jnp.int32, (n, 128), 1) == lax.broadcasted_iota(jnp.int32, (n, 128), 0) + offset
    return jnp.sum(jnp.where(place, row, 0.0), axis=1, keepdims=True)


def edge_rows(values):
    n = values.shape[0]
    row = column_as_row(values[:, -1:], None, 0) + column_as_row(values[:, :1], None, n)
    return jnp.broadcast_to(row, (EXTRA, 128))


def factor_of(counts_ref, weight_ref, d):
    slot = lax.broadcasted_iota(jnp.int32, (1, weight_ref.shape[2]), 1)
    return jnp.where(slot < counts_ref[0, d], weight_ref[0, pl.ds(d, 1), :], 0.0)


def loop(n, step, init):
    return lax.fori_loop(0, n, step, init, unroll=n if n <= 8 else 1)


def band_kernel(lev_ref, counts_ref, perturb_ref, own_ref, other_ref, loc_ref, static_ref, src_ref, weight_ref, out_ref, acc_ref):
    levels, members, cols = perturb_ref.shape
    weights = spread(loc_ref[...], 0, lev_ref[0] * levels)
    total = jnp.zeros((levels, SUB, cols), F32)
    perturb = perturb_ref[...].astype(F32)
    for m in range(0, members, SUB):
        tile = jnp.concatenate([own_ref[:, m : m + SUB, :], other_ref[:, m : m + SUB, :]], axis=0)
        localized = mix(weights, tile.reshape(2 * levels * SUB, cols)).reshape(levels, SUB, cols)
        total = total + perturb[:, m : m + SUB, :] * localized
    band_sum = jnp.sum(total, axis=1)
    acc_ref[...] = jnp.concatenate(halves(band_sum), axis=0)
    n = src_ref.shape[1]
    edges = edge_rows(static_ref[...])

    def step(d, carry):
        chosen = one_hot(src_ref[0, pl.ds(d, 1), :], cols)
        both = product(acc_ref[...], chosen)
        payload = (both[:levels] + both[levels:]) * factor_of(counts_ref, weight_ref, d)
        for g in range(out_ref.shape[0]):
            out_ref[g, d, :levels, :] = payload
            out_ref[g, d, levels:, :] = edges
        return carry

    loop(n, step, 0)


def tile_kernel(pos_ref, arrived_ref, tgt_ref, static_ref, diag_ref, off_ref, obs_ref, innov_ref,
                increment_ref, partial_ref, out_ref):
    levels, cols = static_ref.shape
    groups, n = arrived_ref.shape[:2]
    me = pos_ref[0]

    def step(s, total):
        values = sum(arrived_ref[g, s, :levels, :] for g in range(groups))
        chosen = one_hot(tgt_ref[0, pl.ds(s, 1), :], cols)
        return total + select(values, chosen, ((1,), (1,)))

    remapped = loop(n, step, jnp.zeros((levels, cols), F32))
    before = arrived_ref[0, jnp.maximum(me - 1, 0), levels : levels + 1, :]
    after = arrived_ref[0, jnp.minimum(me + 1, n - 1), levels : levels + 1, :]
    before = jnp.where(me > 0, row_as_column(before, levels, 0), 0.0)
    after = jnp.where(me < n - 1, row_as_column(after, levels, levels), 0.0)
    static = static_ref[...]
    lane = lax.broadcasted_iota(jnp.int32, (levels, cols), 1)
    left = jnp.where(lane == 0, before, pltpu.roll(static, 1, 1))
    right = jnp.where(lane == cols - 1, after, pltpu.roll(static, cols - 1, 1))
    increment = remapped + diag_ref[...] * static + off_ref[...] * (left + right)
    increment_ref[...] = increment
    misfit = obs_ref[...] * (increment - innov_ref[...])
    coupled = off_ref[...] * misfit
    left = jnp.where(lane == 0, 0.0, pltpu.roll(coupled, 1, 1))
    right = jnp.where(lane == cols - 1, 0.0, pltpu.roll(coupled, cols - 1, 1))
    partial_ref[...] = static + diag_ref[...] * misfit + left + right
    edges = edge_rows(coupled)
    both = jnp.concatenate(halves(misfit), axis=0)

    def give(s, carry):
        chosen = one_hot(tgt_ref[0, pl.ds(s, 1), :], cols)
        picked = product(both, chosen)
        out_ref[s, :levels, :] = picked[:levels] + picked[levels:]
        out_ref[s, levels:, :] = edges
        return carry

    loop(n, give, 0)


def adjoint_kernel(pos_ref, counts_ref, returned_ref, src_ref, weight_ref, partial_ref, loc_ref, grad_ref, out_ref):
    levels, cols = partial_ref.shape
    n = returned_ref.shape[0]
    band = out_ref.shape[1] - 128
    me = pos_ref[0]

    def step(d, total):
        values = returned_ref[d, :levels, :] * factor_of(counts_ref, weight_ref, d)
        return total + select(values, one_hot(src_ref[0, pl.ds(d, 1), :], band), ((1,), (1,)))

    out_ref[:, :band] = loop(n, step, jnp.zeros((levels, band), F32))
    out_ref[:, band:] = jnp.concatenate([loc_ref[...], jnp.zeros((levels, 128 - loc_ref.shape[1]), F32)], axis=1)
    before = returned_ref[jnp.maximum(me - 1, 0), levels : levels + 1, :]
    after = returned_ref[jnp.minimum(me + 1, n - 1), levels : levels + 1, :]
    before = jnp.where(me > 0, row_as_column(before, levels, 0), 0.0)
    after = jnp.where(me < n - 1, row_as_column(after, levels, levels), 0.0)
    lane = lax.broadcasted_iota(jnp.int32, (levels, cols), 1)
    grad_ref[...] = partial_ref[...] + (jnp.where(lane == 0, before, 0.0) + jnp.where(lane == cols - 1, after, 0.0))


def ens_kernel(lev_ref, perturb_ref, other_ref, control_ref, mine_ref, theirs_ref, out_ref):
    levels, members, cols = perturb_ref.shape
    mine, theirs = mine_ref[...], theirs_ref[...]
    loc = jnp.concatenate([mine[:, cols : cols + 2 * levels], theirs[:, cols : cols + 2 * levels]], axis=0)
    full = loc.shape[0]
    l_row = lax.broadcasted_iota(jnp.int32, (levels * SUB, full), 0) // SUB + lev_ref[0] * levels
    pick_l = (l_row == lax.broadcasted_iota(jnp.int32, (levels * SUB, full), 1)).astype(BF16)
    k_col = lax.broadcasted_iota(jnp.int32, (full, full * SUB), 1) // SUB
    pick_k = (k_col == lax.broadcasted_iota(jnp.int32, (full, full * SUB), 0)).astype(BF16)
    same = (
        lax.broadcasted_iota(jnp.int32, (levels * SUB, full * SUB), 0) % SUB
        == lax.broadcasted_iota(jnp.int32, (levels * SUB, full * SUB), 1) % SUB
    )
    weights = []
    for part in halves(loc):
        tall = product(pick_l, part, ((1,), (1,)))
        wide = product(tall.astype(BF16), pick_k)
        weights.append(jnp.where(same, wide, 0.0).astype(BF16))
    perturb = perturb_ref[...].astype(F32)
    other = other_ref[...].astype(F32)
    grad = jnp.concatenate([mine[:, :cols], theirs[:, :cols]], axis=0)[:, None, :]
    for m in range(0, members, SUB):
        tile = jnp.concatenate([perturb[:, m : m + SUB, :], other[:, m : m + SUB, :]], axis=0) * grad
        mixed = mix(weights, tile.reshape(full * SUB, cols)).reshape(levels, SUB, cols)
        out_ref[:, m : m + SUB, :] = control_ref[:, m : m + SUB, :] + mixed


def call(kernel, out_shape, spaces, scratch=()):
    return pl.pallas_call(
        kernel,
        out_shape=out_shape,
        in_specs=spaces,
        out_specs=jax.tree.map(lambda _: VMEM, out_shape),
        scratch_shapes=scratch,
        compiler_params=PARAMS,
    )


def body(
    perturb,
    control,
    level_loc,
    static_control,
    filter_diag,
    filter_off,
    send_src,
    send_wt,
    counts,
    recv_tgt,
    obs_weight,
    innovation,
):
    levels, members, band_cols = control.shape
    tile_cols = static_control.shape[1]
    n = lax.axis_size("tile")
    groups = lax.axis_size("grp")
    cap = send_src.shape[2]
    shape = jax.ShapeDtypeStruct
    swap = [(0, 1), (1, 0)]
    lev = lax.axis_index("lev").astype(jnp.int32).reshape(1)
    pos = lax.axis_index("tile").astype(jnp.int32).reshape(1)
    other_control = lax.ppermute(control, "lev", swap)
    other_perturb = lax.ppermute(perturb, "lev", swap)
    payload = call(
        band_kernel,
        shape((groups, n, levels + EXTRA, cap), F32),
        [SMEM, SMEM] + [VMEM] * 7,
        [pltpu.VMEM((2 * levels, band_cols), BF16)],
    )(lev, counts, perturb, control, other_control, level_loc, static_control, send_src, send_wt)
    arrived = lax.all_to_all(
        payload.reshape(groups * n, levels + EXTRA, cap), ("grp", "tile"), split_axis=0, concat_axis=0, tiled=True
    ).reshape(groups, n, levels + EXTRA, cap)
    flat = shape((levels, tile_cols), F32)
    increment, partial, giving = call(
        tile_kernel, (flat, flat, shape((n, levels + EXTRA, cap), F32)), [SMEM] + [VMEM] * 7
    )(pos, arrived, recv_tgt, static_control, filter_diag.reshape(1, -1), filter_off.reshape(1, -1), obs_weight, innovation)
    returned = lax.all_to_all(giving, "tile", split_axis=0, concat_axis=0, tiled=True)
    grad_static, mine = call(
        adjoint_kernel, (flat, shape((levels, band_cols + 128), F32)), [SMEM, SMEM] + [VMEM] * 5
    )(pos, counts, returned, send_src, send_wt, partial, level_loc)
    theirs = lax.ppermute(mine, "lev", swap)
    grad_ens = call(ens_kernel, shape(control.shape, F32), [SMEM] + [VMEM] * 5)(
        lev, perturb, other_perturb, control, mine, theirs
    )
    return (increment, grad_static, grad_ens)


def solution(mesh):
    return jax.shard_map(
        body,
        mesh=mesh,
        in_specs=(
            P("lev", "grp", "tile"),
            P("lev", "grp", "tile"),
            P("lev", None),
            P("lev", "tile"),
            P("tile"),
            P("tile"),
            P("tile", None, None),
            P("tile", None, None),
            P("tile", None),
            P("tile", None, None),
            P("lev", "tile"),
            P("lev", "tile"),
        ),
        out_specs=(P("lev", "tile"), P("lev", "tile"), P("lev", "grp", "tile")),
        check_vma=False,
    )
```

```python
import functools

import jax
import jax.numpy as jnp
from jax import lax
from jax.experimental import pallas as pl
from jax.experimental.pallas import tpu as pltpu
from jax.sharding import PartitionSpec as P

F32 = jnp.float32
BF16 = jnp.bfloat16
SUB = 8
EXTRA = 8
VMEM = pl.BlockSpec(memory_space=pltpu.VMEM)
HBM = pl.BlockSpec(memory_space=pltpu.HBM)
SMEM = pl.BlockSpec(memory_space=pltpu.SMEM)
MIB = 1024 * 1024


def halves(values):
    high = values.astype(BF16)
    low = (values - high.astype(F32)).astype(BF16)
    return high, low


def product(a, b, dims=((1,), (0,))):
    return lax.dot_general(a, b, (dims, ((), ())), preferred_element_type=F32)


def select(values, chosen, dims=((1,), (0,))):
    rows = values.shape[0]
    both = product(jnp.concatenate(halves(values), axis=0), chosen, dims)
    return both[:rows] + both[rows:]


def spread(matrix, start, count):
    rows, cols = matrix.shape

    def iota(shape, axis):
        return lax.broadcasted_iota(jnp.int32, shape, axis)

    shape = (rows * SUB, count * SUB)
    tall = (iota((rows * SUB, rows), 0) // SUB == iota((rows * SUB, rows), 1)).astype(BF16)
    wide = (iota((cols, count * SUB), 1) // SUB + start == iota((cols, count * SUB), 0)).astype(BF16)
    same = iota(shape, 0) % SUB == iota(shape, 1) % SUB
    out = []
    for part in halves(matrix):
        filled = product(tall, product(part, wide).astype(BF16))
        out.append(jnp.where(same, filled, 0.0).astype(BF16))
    return out


def mix(weights, values):
    high, low = halves(values)
    return product(weights[0], high) + (product(weights[0], low) + product(weights[1], high))


def one_hot(index, size):
    rows = lax.broadcasted_iota(jnp.int32, (size, index.shape[1]), 0)
    return jnp.where(rows == index, 1.0, 0.0).astype(BF16)


def column_as_row(column, lane, offset):
    n = column.shape[0]
    place = lax.broadcasted_iota(jnp.int32, (n, 128), 1) == lax.broadcasted_iota(jnp.int32, (n, 128), 0) + offset
    return jnp.sum(jnp.where(place, column, 0.0), axis=0, keepdims=True)


def row_as_column(row, n, offset):
    place = lax.broadcasted_iota(jnp.int32, (n, 128), 1) == lax.broadcasted_iota(jnp.int32, (n, 128), 0) + offset
    return jnp.sum(jnp.where(place, row, 0.0), axis=1, keepdims=True)


def edge_rows(values):
    n = values.shape[0]
    row = column_as_row(values[:, -1:], None, 0) + column_as_row(values[:, :1], None, n)
    return jnp.broadcast_to(row, (EXTRA, 128))


def factor_of(counts_ref, weight_ref, d):
    slot = lax.broadcasted_iota(jnp.int32, (1, weight_ref.shape[2]), 1)
    return jnp.where(slot < counts_ref[0, d], weight_ref[0, pl.ds(d, 1), :], 0.0)


def loop(n, step, init):
    return lax.fori_loop(0, n, step, init, unroll=n if n <= 8 else 1)


def own_kernel(lev_ref, perturb_hbm, control_hbm, loc_hbm, part_ref, perturb_ref, control_ref, loc_ref, sems):
    staged = [(loc_hbm, loc_ref), (control_hbm, control_ref), (perturb_hbm, perturb_ref)]
    copies = [pltpu.make_async_copy(source, target, sems.at[i]) for i, (source, target) in enumerate(staged)]
    for copy in copies:
        copy.start()
    levels = perturb_ref.shape[0]
    copies[0].wait()
    weights = spread(loc_ref[...], lev_ref[0] * levels, levels)
    copies[1].wait()
    copies[2].wait()
    part_ref[...] = mixed_sum(weights, perturb_ref, control_ref)


def mixed_sum(weights, perturb_ref, control_ref):
    levels, members, cols = perturb_ref.shape
    perturb = perturb_ref[...].astype(F32)
    total = jnp.zeros((levels, SUB, cols), F32)
    for m in range(0, members, SUB):
        tile = control_ref[:, m : m + SUB, :].reshape(levels * SUB, cols)
        total = total + perturb[:, m : m + SUB, :] * mix(weights, tile).reshape(levels, SUB, cols)
    return jnp.sum(total, axis=1)


def band_kernel(lev_ref, counts_ref, perturb_ref, other_ref, part_ref, loc_ref, static_ref, src_ref, weight_ref,
                out_ref, acc_ref):
    levels, members, cols = perturb_ref.shape
    weights = spread(loc_ref[...], (1 - lev_ref[0]) * levels, levels)
    band_sum = part_ref[...] + mixed_sum(weights, perturb_ref, other_ref)
    acc_ref[...] = jnp.concatenate(halves(band_sum), axis=0)
    n = src_ref.shape[1]
    edges = edge_rows(static_ref[...])

    def step(d, carry):
        chosen = one_hot(src_ref[0, pl.ds(d, 1), :], cols)
        both = product(acc_ref[...], chosen)
        payload = (both[:levels] + both[levels:]) * factor_of(counts_ref, weight_ref, d)
        for g in range(out_ref.shape[0]):
            out_ref[g, d, :levels, :] = payload
            out_ref[g, d, levels:, :] = edges
        return carry

    loop(n, step, 0)


def tile_kernel(pos_ref, arrived_ref, tgt_ref, static_ref, diag_ref, off_ref, obs_ref, innov_ref,
                increment_ref, partial_ref, out_ref):
    levels, cols = static_ref.shape
    groups, n = arrived_ref.shape[:2]
    me = pos_ref[0]

    def step(s, total):
        values = sum(arrived_ref[g, s, :levels, :] for g in range(groups))
        chosen = one_hot(tgt_ref[0, pl.ds(s, 1), :], cols)
        return total + select(values, chosen, ((1,), (1,)))

    remapped = loop(n, step, jnp.zeros((levels, cols), F32))
    before = arrived_ref[0, jnp.maximum(me - 1, 0), levels : levels + 1, :]
    after = arrived_ref[0, jnp.minimum(me + 1, n - 1), levels : levels + 1, :]
    before = jnp.where(me > 0, row_as_column(before, levels, 0), 0.0)
    after = jnp.where(me < n - 1, row_as_column(after, levels, levels), 0.0)
    static = static_ref[...]
    lane = lax.broadcasted_iota(jnp.int32, (levels, cols), 1)
    left = jnp.where(lane == 0, before, pltpu.roll(static, 1, 1))
    right = jnp.where(lane == cols - 1, after, pltpu.roll(static, cols - 1, 1))
    increment = remapped + diag_ref[...] * static + off_ref[...] * (left + right)
    increment_ref[...] = increment
    misfit = obs_ref[...] * (increment - innov_ref[...])
    coupled = off_ref[...] * misfit
    left = jnp.where(lane == 0, 0.0, pltpu.roll(coupled, 1, 1))
    right = jnp.where(lane == cols - 1, 0.0, pltpu.roll(coupled, cols - 1, 1))
    partial_ref[...] = static + diag_ref[...] * misfit + left + right
    edges = edge_rows(coupled)
    both = jnp.concatenate(halves(misfit), axis=0)

    def give(s, carry):
        chosen = one_hot(tgt_ref[0, pl.ds(s, 1), :], cols)
        picked = product(both, chosen)
        out_ref[s, :levels, :] = picked[:levels] + picked[levels:]
        out_ref[s, levels:, :] = edges
        return carry

    loop(n, give, 0)


def adjoint_kernel(pos_ref, counts_ref, returned_ref, src_ref, weight_ref, partial_ref, loc_ref, grad_ref, out_ref):
    levels, cols = partial_ref.shape
    n = returned_ref.shape[0]
    band = out_ref.shape[1] - 128
    me = pos_ref[0]

    def step(d, total):
        values = returned_ref[d, :levels, :] * factor_of(counts_ref, weight_ref, d)
        return total + select(values, one_hot(src_ref[0, pl.ds(d, 1), :], band), ((1,), (1,)))

    out_ref[:, :band] = loop(n, step, jnp.zeros((levels, band), F32))
    out_ref[:, band:] = jnp.concatenate([loc_ref[...], jnp.zeros((levels, 128 - loc_ref.shape[1]), F32)], axis=1)
    before = returned_ref[jnp.maximum(me - 1, 0), levels : levels + 1, :]
    after = returned_ref[jnp.minimum(me + 1, n - 1), levels : levels + 1, :]
    before = jnp.where(me > 0, row_as_column(before, levels, 0), 0.0)
    after = jnp.where(me < n - 1, row_as_column(after, levels, levels), 0.0)
    lane = lax.broadcasted_iota(jnp.int32, (levels, cols), 1)
    grad_ref[...] = partial_ref[...] + (jnp.where(lane == 0, before, 0.0) + jnp.where(lane == cols - 1, after, 0.0))


def ens_kernel(lev_ref, perturb_ref, other_ref, control_ref, mine_ref, theirs_ref, out_ref):
    levels, members, cols = perturb_ref.shape
    mine, theirs = mine_ref[...], theirs_ref[...]
    loc = jnp.concatenate([mine[:, cols : cols + 2 * levels], theirs[:, cols : cols + 2 * levels]], axis=0)
    full = loc.shape[0]
    l_row = lax.broadcasted_iota(jnp.int32, (levels * SUB, full), 0) // SUB + lev_ref[0] * levels
    pick_l = (l_row == lax.broadcasted_iota(jnp.int32, (levels * SUB, full), 1)).astype(BF16)
    k_col = lax.broadcasted_iota(jnp.int32, (full, full * SUB), 1) // SUB
    pick_k = (k_col == lax.broadcasted_iota(jnp.int32, (full, full * SUB), 0)).astype(BF16)
    same = (
        lax.broadcasted_iota(jnp.int32, (levels * SUB, full * SUB), 0) % SUB
        == lax.broadcasted_iota(jnp.int32, (levels * SUB, full * SUB), 1) % SUB
    )
    weights = []
    for part in halves(loc):
        tall = product(pick_l, part, ((1,), (1,)))
        wide = product(tall.astype(BF16), pick_k)
        weights.append(jnp.where(same, wide, 0.0).astype(BF16))
    perturb = perturb_ref[...].astype(F32)
    other = other_ref[...].astype(F32)
    grad = jnp.concatenate([mine[:, :cols], theirs[:, :cols]], axis=0)[:, None, :]
    for m in range(0, members, SUB):
        tile = jnp.concatenate([perturb[:, m : m + SUB, :], other[:, m : m + SUB, :]], axis=0) * grad
        mixed = mix(weights, tile.reshape(full * SUB, cols)).reshape(levels, SUB, cols)
        out_ref[:, m : m + SUB, :] = control_ref[:, m : m + SUB, :] + mixed


def call(kernel, out_shape, spaces, scratch=(), limit=40 * MIB):
    return pl.pallas_call(
        kernel,
        out_shape=out_shape,
        in_specs=spaces,
        out_specs=jax.tree.map(lambda _: VMEM, out_shape),
        scratch_shapes=scratch,
        compiler_params=pltpu.CompilerParams(vmem_limit_bytes=limit),
    )


def body(
    perturb,
    control,
    level_loc,
    static_control,
    filter_diag,
    filter_off,
    send_src,
    send_wt,
    counts,
    recv_tgt,
    obs_weight,
    innovation,
):
    levels, members, band_cols = control.shape
    tile_cols = static_control.shape[1]
    n = lax.axis_size("tile")
    groups = lax.axis_size("grp")
    cap = send_src.shape[2]
    shape = jax.ShapeDtypeStruct
    swap = [(0, 1), (1, 0)]
    lev = lax.axis_index("lev").astype(jnp.int32).reshape(1)
    pos = lax.axis_index("tile").astype(jnp.int32).reshape(1)
    other_control = lax.ppermute(control, "lev", swap)
    other_perturb = lax.ppermute(perturb, "lev", swap)
    part = call(
        own_kernel,
        shape((levels, band_cols), F32),
        [SMEM] + [HBM] * 3,
        [pltpu.VMEM(a.shape, a.dtype) for a in (perturb, control, level_loc)] + [pltpu.SemaphoreType.DMA((3,))],
        limit=58 * MIB,
    )(lev, perturb, control, level_loc)
    payload = call(
        band_kernel,
        shape((groups, n, levels + EXTRA, cap), F32),
        [SMEM] * 2 + [VMEM] * 7,
        [pltpu.VMEM((2 * levels, band_cols), BF16)],
    )(lev, counts, perturb, other_control, part, level_loc, static_control, send_src, send_wt)
    arrived = lax.all_to_all(
        payload.reshape(groups * n, levels + EXTRA, cap), ("grp", "tile"), split_axis=0, concat_axis=0, tiled=True
    ).reshape(groups, n, levels + EXTRA, cap)
    flat = shape((levels, tile_cols), F32)
    increment, partial, giving = call(
        tile_kernel, (flat, flat, shape((n, levels + EXTRA, cap), F32)), [SMEM] + [VMEM] * 7
    )(pos, arrived, recv_tgt, static_control, filter_diag.reshape(1, -1), filter_off.reshape(1, -1), obs_weight, innovation)
    returned = lax.all_to_all(giving, "tile", split_axis=0, concat_axis=0, tiled=True)
    grad_static, mine = call(
        adjoint_kernel, (flat, shape((levels, band_cols + 128), F32)), [SMEM, SMEM] + [VMEM] * 5
    )(pos, counts, returned, send_src, send_wt, partial, level_loc)
    theirs = lax.ppermute(mine, "lev", swap)
    grad_ens = call(ens_kernel, shape(control.shape, F32), [SMEM] + [VMEM] * 5)(
        lev, perturb, other_perturb, control, mine, theirs
    )
    return (increment, grad_static, grad_ens)


def solution(mesh):
    return jax.shard_map(
        body,
        mesh=mesh,
        in_specs=(
            P("lev", "grp", "tile"),
            P("lev", "grp", "tile"),
            P("lev", None),
            P("lev", "tile"),
            P("tile"),
            P("tile"),
            P("tile", None, None),
            P("tile", None, None),
            P("tile", None),
            P("tile", None, None),
            P("lev", "tile"),
            P("lev", "tile"),
        ),
        out_specs=(P("lev", "tile"), P("lev", "tile"), P("lev", "grp", "tile")),
        check_vma=False,
    )
```

```python
import functools

import jax
import jax.numpy as jnp
from jax import lax
from jax.experimental import pallas as pl
from jax.experimental.pallas import tpu as pltpu
from jax.sharding import PartitionSpec as P

F32 = jnp.float32
BF16 = jnp.bfloat16
SUB = 8
EXTRA = 8
VMEM = pl.BlockSpec(memory_space=pltpu.VMEM)
HBM = pl.BlockSpec(memory_space=pltpu.HBM)
SMEM = pl.BlockSpec(memory_space=pltpu.SMEM)
MIB = 1024 * 1024


def halves(values):
    high = values.astype(BF16)
    low = (values - high.astype(F32)).astype(BF16)
    return high, low


def product(a, b, dims=((1,), (0,))):
    return lax.dot_general(a, b, (dims, ((), ())), preferred_element_type=F32)


def select(values, chosen, dims=((1,), (0,))):
    rows = values.shape[0]
    both = product(jnp.concatenate(halves(values), axis=0), chosen, dims)
    return both[:rows] + both[rows:]


def spread(matrix, start, count):
    rows, cols = matrix.shape

    def iota(shape, axis):
        return lax.broadcasted_iota(jnp.int32, shape, axis)

    shape = (rows * SUB, count * SUB)
    tall = (iota((rows * SUB, rows), 0) // SUB == iota((rows * SUB, rows), 1)).astype(BF16)
    wide = (iota((cols, count * SUB), 1) // SUB + start == iota((cols, count * SUB), 0)).astype(BF16)
    same = iota(shape, 0) % SUB == iota(shape, 1) % SUB
    out = []
    for part in halves(matrix):
        filled = product(tall, product(part, wide).astype(BF16))
        out.append(jnp.where(same, filled, 0.0).astype(BF16))
    return out


def mix(weights, values):
    high, low = halves(values)
    return product(weights[0], high) + (product(weights[0], low) + product(weights[1], high))


def one_hot(index, size):
    rows = lax.broadcasted_iota(jnp.int32, (size, index.shape[1]), 0)
    return jnp.where(rows == index, 1.0, 0.0).astype(BF16)


def column_as_row(column, lane, offset):
    n = column.shape[0]
    place = lax.broadcasted_iota(jnp.int32, (n, 128), 1) == lax.broadcasted_iota(jnp.int32, (n, 128), 0) + offset
    return jnp.sum(jnp.where(place, column, 0.0), axis=0, keepdims=True)


def row_as_column(row, n, offset):
    place = lax.broadcasted_iota(jnp.int32, (n, 128), 1) == lax.broadcasted_iota(jnp.int32, (n, 128), 0) + offset
    return jnp.sum(jnp.where(place, row, 0.0), axis=1, keepdims=True)


def edge_rows(values):
    n = values.shape[0]
    row = column_as_row(values[:, -1:], None, 0) + column_as_row(values[:, :1], None, n)
    return jnp.broadcast_to(row, (EXTRA, 128))


def factor_of(counts_ref, weight_ref, d):
    slot = lax.broadcasted_iota(jnp.int32, (1, weight_ref.shape[2]), 1)
    return jnp.where(slot < counts_ref[0, d], weight_ref[0, pl.ds(d, 1), :], 0.0)


def loop(n, step, init):
    return lax.fori_loop(0, n, step, init, unroll=n if n <= 8 else 1)


def own_kernel(lev_ref, perturb_hbm, control_hbm, loc_hbm, part_ref, perturb_ref, control_ref, loc_ref, sems):
    staged = [(loc_hbm, loc_ref), (control_hbm, control_ref), (perturb_hbm, perturb_ref)]
    copies = [pltpu.make_async_copy(source, target, sems.at[i]) for i, (source, target) in enumerate(staged)]
    for copy in copies:
        copy.start()
    levels = perturb_ref.shape[0]
    copies[0].wait()
    weights = spread(loc_ref[...], lev_ref[0] * levels, levels)
    copies[1].wait()
    copies[2].wait()
    part_ref[...] = mixed_sum(weights, perturb_ref, control_ref)


def mixed_sum(weights, perturb_ref, control_ref):
    levels, members, cols = perturb_ref.shape
    perturb = perturb_ref[...].astype(F32)
    total = jnp.zeros((levels, SUB, cols), F32)
    for m in range(0, members, SUB):
        tile = control_ref[:, m : m + SUB, :].reshape(levels * SUB, cols)
        total = total + perturb[:, m : m + SUB, :] * mix(weights, tile).reshape(levels, SUB, cols)
    return jnp.sum(total, axis=1)


def band_kernel(lev_ref, counts_ref, perturb_ref, other_ref, part_ref, loc_ref, static_ref, src_ref, weight_ref,
                out_ref, acc_ref):
    levels, members, cols = perturb_ref.shape
    weights = spread(loc_ref[...], (1 - lev_ref[0]) * levels, levels)
    band_sum = part_ref[...] + mixed_sum(weights, perturb_ref, other_ref)
    acc_ref[...] = jnp.concatenate(halves(band_sum), axis=0)
    n = src_ref.shape[1]
    edges = edge_rows(static_ref[...])

    def step(d, carry):
        chosen = one_hot(src_ref[0, pl.ds(d, 1), :], cols)
        both = product(acc_ref[...], chosen)
        payload = (both[:levels] + both[levels:]) * factor_of(counts_ref, weight_ref, d)
        for g in range(out_ref.shape[0]):
            out_ref[g, d, :levels, :] = payload
            out_ref[g, d, levels:, :] = edges
        return carry

    loop(n, step, 0)


def tile_kernel(pos_ref, arrived_ref, tgt_ref, static_ref, diag_ref, off_ref, obs_ref, innov_ref,
                increment_ref, partial_ref, out_ref):
    levels, cols = static_ref.shape
    groups, n = arrived_ref.shape[:2]
    me = pos_ref[0]

    def step(s, total):
        values = sum(arrived_ref[g, s, :levels, :] for g in range(groups))
        chosen = one_hot(tgt_ref[0, pl.ds(s, 1), :], cols)
        return total + select(values, chosen, ((1,), (1,)))

    remapped = loop(n, step, jnp.zeros((levels, cols), F32))
    before = arrived_ref[0, jnp.maximum(me - 1, 0), levels : levels + 1, :]
    after = arrived_ref[0, jnp.minimum(me + 1, n - 1), levels : levels + 1, :]
    before = jnp.where(me > 0, row_as_column(before, levels, 0), 0.0)
    after = jnp.where(me < n - 1, row_as_column(after, levels, levels), 0.0)
    static = static_ref[...]
    lane = lax.broadcasted_iota(jnp.int32, (levels, cols), 1)
    left = jnp.where(lane == 0, before, pltpu.roll(static, 1, 1))
    right = jnp.where(lane == cols - 1, after, pltpu.roll(static, cols - 1, 1))
    increment = remapped + diag_ref[...] * static + off_ref[...] * (left + right)
    increment_ref[...] = increment
    misfit = obs_ref[...] * (increment - innov_ref[...])
    coupled = off_ref[...] * misfit
    left = jnp.where(lane == 0, 0.0, pltpu.roll(coupled, 1, 1))
    right = jnp.where(lane == cols - 1, 0.0, pltpu.roll(coupled, cols - 1, 1))
    partial_ref[...] = static + diag_ref[...] * misfit + left + right
    edges = edge_rows(coupled)
    both = jnp.concatenate(halves(misfit), axis=0)

    def give(s, carry):
        chosen = one_hot(tgt_ref[0, pl.ds(s, 1), :], cols)
        picked = product(both, chosen)
        out_ref[s, :levels, :] = picked[:levels] + picked[levels:]
        out_ref[s, levels:, :] = edges
        return carry

    loop(n, give, 0)


def adjoint_kernel(pos_ref, counts_ref, returned_ref, src_ref, weight_ref, partial_ref, loc_ref, grad_ref, out_ref):
    levels, cols = partial_ref.shape
    n = returned_ref.shape[0]
    band = out_ref.shape[1] - 128
    me = pos_ref[0]

    def step(d, total):
        values = returned_ref[d, :levels, :] * factor_of(counts_ref, weight_ref, d)
        return total + select(values, one_hot(src_ref[0, pl.ds(d, 1), :], band), ((1,), (1,)))

    out_ref[:, :band] = loop(n, step, jnp.zeros((levels, band), F32))
    out_ref[:, band:] = jnp.concatenate([loc_ref[...], jnp.zeros((levels, 128 - loc_ref.shape[1]), F32)], axis=1)
    before = returned_ref[jnp.maximum(me - 1, 0), levels : levels + 1, :]
    after = returned_ref[jnp.minimum(me + 1, n - 1), levels : levels + 1, :]
    before = jnp.where(me > 0, row_as_column(before, levels, 0), 0.0)
    after = jnp.where(me < n - 1, row_as_column(after, levels, levels), 0.0)
    lane = lax.broadcasted_iota(jnp.int32, (levels, cols), 1)
    grad_ref[...] = partial_ref[...] + (jnp.where(lane == 0, before, 0.0) + jnp.where(lane == cols - 1, after, 0.0))


def ens_kernel(lev_ref, perturb_ref, other_ref, control_ref, mine_ref, theirs_ref, out_ref):
    levels, members, cols = perturb_ref.shape
    mine, theirs = mine_ref[...], theirs_ref[...]
    loc = jnp.concatenate([mine[:, cols : cols + 2 * levels], theirs[:, cols : cols + 2 * levels]], axis=0)
    full = loc.shape[0]
    l_row = lax.broadcasted_iota(jnp.int32, (levels * SUB, full), 0) // SUB + lev_ref[0] * levels
    pick_l = (l_row == lax.broadcasted_iota(jnp.int32, (levels * SUB, full), 1)).astype(BF16)
    k_col = lax.broadcasted_iota(jnp.int32, (full, full * SUB), 1) // SUB
    pick_k = (k_col == lax.broadcasted_iota(jnp.int32, (full, full * SUB), 0)).astype(BF16)
    same = (
        lax.broadcasted_iota(jnp.int32, (levels * SUB, full * SUB), 0) % SUB
        == lax.broadcasted_iota(jnp.int32, (levels * SUB, full * SUB), 1) % SUB
    )
    weights = []
    for part in halves(loc):
        tall = product(pick_l, part, ((1,), (1,)))
        wide = product(tall.astype(BF16), pick_k)
        weights.append(jnp.where(same, wide, 0.0).astype(BF16))
    perturb = perturb_ref[...].astype(F32)
    other = other_ref[...].astype(F32)
    grad = jnp.concatenate([mine[:, :cols], theirs[:, :cols]], axis=0)[:, None, :]
    for m in range(0, members, SUB):
        tile = jnp.concatenate([perturb[:, m : m + SUB, :], other[:, m : m + SUB, :]], axis=0) * grad
        mixed = mix(weights, tile.reshape(full * SUB, cols)).reshape(levels, SUB, cols)
        out_ref[:, m : m + SUB, :] = control_ref[:, m : m + SUB, :] + mixed


class Rows:
    def __init__(self, levels, band, n, cap):
        self.sums = [slice(i * levels, (i + 1) * levels) for i in range(band // cap)]
        at = band // cap * levels
        self.first = at
        self.weight = slice(at, at + levels)
        self.base = slice(at + levels, at + 2 * levels)
        at += 2 * levels
        self.src, self.factor, self.tgt, self.edge = at, at + n, at + 2 * n, at + 3 * n
        self.total = at + 3 * n + EXTRA


def static_kernel(counts_ref, static_ref, diag_ref, off_ref, obs_ref, innov_ref, src_ref, weight_ref, tgt_ref, out_ref):
    levels, cols = static_ref.shape
    n, _, cap = out_ref.shape
    rows = Rows(levels, 0, n, cap)
    static, off, obs = static_ref[...], off_ref[...], obs_ref[...]
    lane = lax.broadcasted_iota(jnp.int32, (levels, cols), 1)
    left = jnp.where(lane == 0, 0.0, pltpu.roll(static, 1, 1))
    right = jnp.where(lane == cols - 1, 0.0, pltpu.roll(static, cols - 1, 1))
    base = diag_ref[...] * static + off * (left + right) - innov_ref[...]
    coupled = off * obs
    ends = [v[:, i] for v in (static, coupled, base) for i in (slice(cols - 1, cols), slice(0, 1))]
    edge = sum(column_as_row(end, None, i * levels) for i, end in enumerate(ends))
    place = lax.broadcasted_iota(jnp.int32, (1, cap), 1)
    edge = edge + jnp.where(place == 6 * levels, off[:, cols - 1 :], 0.0)
    edge = edge + jnp.where(place == 6 * levels + 1, off[:, :1], 0.0)
    edge = jnp.broadcast_to(edge, (EXTRA, cap))
    both = jnp.concatenate(halves(jnp.concatenate([obs, base], axis=0)), axis=0)
    src = src_ref[0].astype(F32)
    tgt = tgt_ref[0].astype(F32)
    factor = jnp.concatenate([factor_of(counts_ref, weight_ref, d) for d in range(n)], axis=0)
    for q in range(n):
        picked = product(both, one_hot(tgt_ref[0, q : q + 1, :], cols))
        out_ref[q, : 2 * levels, :] = picked[: 2 * levels] + picked[2 * levels :]
        out_ref[q, rows.src : rows.src + n, :] = src
        out_ref[q, rows.factor : rows.factor + n, :] = factor
        out_ref[q, rows.tgt : rows.tgt + n, :] = tgt
        out_ref[q, rows.edge :, :] = edge


def sum_kernel(lev_ref, perturb_ref, other_ref, part_ref, loc_ref, out_ref):
    levels = perturb_ref.shape[0]
    weights = spread(loc_ref[...], (1 - lev_ref[0]) * levels, levels)
    out_ref[...] = part_ref[...] + mixed_sum(weights, perturb_ref, other_ref)


def payload_kernel(*refs):
    *sums, rest_ref, out_ref = refs
    total = sum(ref[...] for ref in sums)
    levels, band = total.shape
    n, _, cap = out_ref.shape
    rows = Rows(levels, band, n, cap)
    for q in range(n):
        for i, place in enumerate(rows.sums):
            out_ref[q, place, :] = total[:, i * cap : (i + 1) * cap]
        out_ref[q, rows.first :, :] = rest_ref[q]


def shared_kernel(cols, pos_ref, arrived_ref, loc_ref, out_ref, slots_ref):
    levels = loc_ref.shape[0]
    n, _, cap = arrived_ref.shape
    band = out_ref.shape[1] - 128
    rows = Rows(levels, band, n, cap)
    me = pos_ref[0]
    column = lax.broadcasted_iota(jnp.int32, (band, cap), 0).astype(F32)

    def chosen(s, d):
        return jnp.where(column == arrived_ref[s, rows.src + d : rows.src + d + 1, :], 1.0, 0.0).astype(BF16)

    for s in range(n):
        sums = jnp.concatenate([arrived_ref[s, place, :] for place in rows.sums], axis=1)
        both = jnp.concatenate(halves(sums), axis=0)
        for d in range(n):
            picked = product(both, chosen(s, d))
            values = (picked[:levels] + picked[levels:]) * arrived_ref[s, rows.factor + d : rows.factor + d + 1, :]
            slots_ref[d, :, s * cap : (s + 1) * cap] = jnp.concatenate(halves(values), axis=0)
    own = jnp.concatenate([arrived_ref[d, pl.ds(rows.tgt + me, 1), :] for d in range(n)], axis=0)
    turned = own.T
    last = cols - 1.0
    total = jnp.zeros((levels, band), F32)
    for d in range(n):
        same = [
            jnp.where(turned[:, d : d + 1] == arrived_ref[d, rows.tgt + s : rows.tgt + s + 1, :], 1.0, 0.0).astype(BF16)
            for s in range(n)
        ]
        met = product(slots_ref[d], jnp.concatenate(same, axis=1), ((1,), (1,)))
        value = met[:levels] + met[levels:] + arrived_ref[d, rows.base, :]
        edge = arrived_ref[d, rows.edge : rows.edge + 1, :]
        if d > 0:
            before = row_as_column(arrived_ref[d - 1, rows.edge : rows.edge + 1, :], levels, 0)
            near = jnp.where(own[d : d + 1] == 0.0, edge[:, 6 * levels + 1 : 6 * levels + 2], 0.0)
            value = value + before * near
        if d < n - 1:
            after = row_as_column(arrived_ref[d + 1, rows.edge : rows.edge + 1, :], levels, levels)
            near = jnp.where(own[d : d + 1] == last, edge[:, 6 * levels : 6 * levels + 1], 0.0)
            value = value + after * near
        misfit = arrived_ref[d, rows.weight, :] * value
        given = misfit * arrived_ref[me, rows.factor + d : rows.factor + d + 1, :]
        total = total + select(given, chosen(me, d), ((1,), (1,)))
    out_ref[:, :band] = total
    out_ref[:, band:] = jnp.concatenate([loc_ref[...], jnp.zeros((levels, 128 - loc_ref.shape[1]), F32)], axis=1)


def outputs_kernel(pos_ref, arrived_ref, slots_ref, tgt_ref, static_ref, diag_ref, off_ref, obs_ref, innov_ref,
                   increment_ref, grad_ref):
    levels, cols = static_ref.shape
    n, _, cap = arrived_ref.shape
    edge_at = arrived_ref.shape[1] - EXTRA
    tgt_at = edge_at - n
    me = pos_ref[0]
    remapped = jnp.zeros((2 * levels, cols), F32)
    for s in range(n):
        remapped = remapped + product(
            slots_ref[me, :, s * cap : (s + 1) * cap], one_hot(tgt_ref[0, s : s + 1, :], cols), ((1,), (1,))
        )
    remapped = remapped[:levels] + remapped[levels:]
    static, off = static_ref[...], off_ref[...]
    lane = lax.broadcasted_iota(jnp.int32, (levels, cols), 1)

    def beside(there, exists, column, own_end, side):
        edge = arrived_ref[there, edge_at : edge_at + 1, :]
        static_end, coupling, base = (row_as_column(edge, levels, (2 * i + side) * levels) for i in range(3))
        values = slots_ref[there, :levels, :].astype(F32) + slots_ref[there, levels:, :].astype(F32)
        landed = [
            jnp.where(arrived_ref[there, tgt_at + s : tgt_at + s + 1, :] == column, values[:, s * cap : (s + 1) * cap], 0.0)
            for s in range(n)
        ]
        remap_end = jnp.sum(sum(landed), axis=1, keepdims=True)
        off_end = edge[:, 6 * levels + side : 6 * levels + side + 1]
        coupled = coupling * (remap_end + base + off_end * own_end)
        return jnp.where(exists, static_end, 0.0), jnp.where(exists, coupled, 0.0)

    before, coupled_before = beside(jnp.maximum(me - 1, 0), me > 0, cols - 1.0, static[:, :1], 0)
    after, coupled_after = beside(jnp.minimum(me + 1, n - 1), me < n - 1, 0.0, static[:, cols - 1 :], 1)
    left = jnp.where(lane == 0, before, pltpu.roll(static, 1, 1))
    right = jnp.where(lane == cols - 1, after, pltpu.roll(static, cols - 1, 1))
    increment = remapped + diag_ref[...] * static + off * (left + right)
    increment_ref[...] = increment
    misfit = obs_ref[...] * (increment - innov_ref[...])
    coupled = off * misfit
    left = jnp.where(lane == 0, coupled_before, pltpu.roll(coupled, 1, 1))
    right = jnp.where(lane == cols - 1, coupled_after, pltpu.roll(coupled, cols - 1, 1))
    grad_ref[...] = static + diag_ref[...] * misfit + left + right


def call(kernel, out_shape, spaces, scratch=(), limit=40 * MIB):
    return pl.pallas_call(
        kernel,
        out_shape=out_shape,
        in_specs=spaces,
        out_specs=jax.tree.map(lambda _: VMEM, out_shape),
        scratch_shapes=scratch,
        compiler_params=pltpu.CompilerParams(vmem_limit_bytes=limit),
    )


def body(
    perturb,
    control,
    level_loc,
    static_control,
    filter_diag,
    filter_off,
    send_src,
    send_wt,
    counts,
    recv_tgt,
    obs_weight,
    innovation,
):
    levels, members, band_cols = control.shape
    tile_cols = static_control.shape[1]
    n = lax.axis_size("tile")
    groups = lax.axis_size("grp")
    cap = send_src.shape[2]
    shape = jax.ShapeDtypeStruct
    swap = [(0, 1), (1, 0)]
    lev = lax.axis_index("lev").astype(jnp.int32).reshape(1)
    pos = lax.axis_index("tile").astype(jnp.int32).reshape(1)
    other_control = lax.ppermute(control, "lev", swap)
    other_perturb = lax.ppermute(perturb, "lev", swap)
    part = call(
        own_kernel,
        shape((levels, band_cols), F32),
        [SMEM] + [HBM] * 3,
        [pltpu.VMEM(a.shape, a.dtype) for a in (perturb, control, level_loc)] + [pltpu.SemaphoreType.DMA((3,))],
        limit=58 * MIB,
    )(lev, perturb, control, level_loc)
    flat = shape((levels, tile_cols), F32)
    mine_shape = shape((levels, band_cols + 128), F32)
    diag, off = filter_diag.reshape(1, -1), filter_off.reshape(1, -1)
    if n * cap <= tile_cols:
        rows = Rows(levels, band_cols, n, cap)
        rest = call(static_kernel, shape((n, rows.total - rows.first, cap), F32), [SMEM] + [VMEM] * 8)(
            counts, static_control, diag, off, obs_weight, innovation, send_src, send_wt, recv_tgt
        )
        sums = [
            call(sum_kernel, shape((levels, band_cols), F32), [SMEM] + [VMEM] * 4)(
                lev, perturb, other_control, part, level_loc
            )
        ]
        for k in range(1, groups):
            sums.append(lax.ppermute(sums[0], "grp", [(g, (g + k) % groups) for g in range(groups)]))
        payload = call(payload_kernel, shape((n, rows.total, cap), F32), [VMEM] * (groups + 1))(*sums, rest)
        arrived = lax.all_to_all(payload, "tile", split_axis=0, concat_axis=0, tiled=True)
        mine, slots = call(
            functools.partial(shared_kernel, tile_cols), (mine_shape, shape((n, 2 * levels, n * cap), BF16)), [SMEM] + [VMEM] * 2
        )(pos, arrived, level_loc)
        increment, grad_static = call(outputs_kernel, (flat, flat), [SMEM] + [VMEM] * 8)(
            pos, arrived, slots, recv_tgt, static_control, diag, off, obs_weight, innovation
        )
    else:
        payload = call(
            band_kernel,
            shape((groups, n, levels + EXTRA, cap), F32),
            [SMEM] * 2 + [VMEM] * 7,
            [pltpu.VMEM((2 * levels, band_cols), BF16)],
        )(lev, counts, perturb, other_control, part, level_loc, static_control, send_src, send_wt)
        arrived = lax.all_to_all(
            payload.reshape(groups * n, levels + EXTRA, cap), ("grp", "tile"), split_axis=0, concat_axis=0, tiled=True
        ).reshape(groups, n, levels + EXTRA, cap)
        increment, partial, giving = call(
            tile_kernel, (flat, flat, shape((n, levels + EXTRA, cap), F32)), [SMEM] + [VMEM] * 7
        )(pos, arrived, recv_tgt, static_control, diag, off, obs_weight, innovation)
        returned = lax.all_to_all(giving, "tile", split_axis=0, concat_axis=0, tiled=True)
        grad_static, mine = call(adjoint_kernel, (flat, mine_shape), [SMEM, SMEM] + [VMEM] * 5)(
            pos, counts, returned, send_src, send_wt, partial, level_loc
        )
    theirs = lax.ppermute(mine, "lev", swap)
    grad_ens = call(ens_kernel, shape(control.shape, F32), [SMEM] + [VMEM] * 5)(
        lev, perturb, other_perturb, control, mine, theirs
    )
    return (increment, grad_static, grad_ens)


def solution(mesh):
    return jax.shard_map(
        body,
        mesh=mesh,
        in_specs=(
            P("lev", "grp", "tile"),
            P("lev", "grp", "tile"),
            P("lev", None),
            P("lev", "tile"),
            P("tile"),
            P("tile"),
            P("tile", None, None),
            P("tile", None, None),
            P("tile", None),
            P("tile", None, None),
            P("lev", "tile"),
            P("lev", "tile"),
        ),
        out_specs=(P("lev", "tile"), P("lev", "tile"), P("lev", "grp", "tile")),
        check_vma=False,
    )
```

```python
import functools

import jax
import jax.numpy as jnp
from jax import lax
from jax.experimental import pallas as pl
from jax.experimental.pallas import tpu as pltpu
from jax.sharding import PartitionSpec as P

F32 = jnp.float32
BF16 = jnp.bfloat16
SUB = 8
EXTRA = 8
VMEM = pl.BlockSpec(memory_space=pltpu.VMEM)
HBM = pl.BlockSpec(memory_space=pltpu.HBM)
SMEM = pl.BlockSpec(memory_space=pltpu.SMEM)
MIB = 1024 * 1024


def halves(values):
    high = values.astype(BF16)
    low = (values - high.astype(F32)).astype(BF16)
    return high, low


def product(a, b, dims=((1,), (0,))):
    return lax.dot_general(a, b, (dims, ((), ())), preferred_element_type=F32)


def select(values, chosen, dims=((1,), (0,))):
    rows = values.shape[0]
    both = product(jnp.concatenate(halves(values), axis=0), chosen, dims)
    return both[:rows] + both[rows:]


def spread(matrix, start, count):
    rows, cols = matrix.shape

    def iota(shape, axis):
        return lax.broadcasted_iota(jnp.int32, shape, axis)

    shape = (rows * SUB, count * SUB)
    tall = (iota((rows * SUB, rows), 0) // SUB == iota((rows * SUB, rows), 1)).astype(BF16)
    wide = (iota((cols, count * SUB), 1) // SUB + start == iota((cols, count * SUB), 0)).astype(BF16)
    same = iota(shape, 0) % SUB == iota(shape, 1) % SUB
    out = []
    for part in halves(matrix):
        filled = product(tall, product(part, wide).astype(BF16))
        out.append(jnp.where(same, filled, 0.0).astype(BF16))
    return out


def mix(weights, values):
    high, low = halves(values)
    return product(weights[0], high) + (product(weights[0], low) + product(weights[1], high))


def one_hot(index, size):
    rows = lax.broadcasted_iota(jnp.int32, (size, index.shape[1]), 0)
    return jnp.where(rows == index, 1.0, 0.0).astype(BF16)


def column_as_row(column, lane, offset):
    n = column.shape[0]
    place = lax.broadcasted_iota(jnp.int32, (n, 128), 1) == lax.broadcasted_iota(jnp.int32, (n, 128), 0) + offset
    return jnp.sum(jnp.where(place, column, 0.0), axis=0, keepdims=True)


def row_as_column(row, n, offset):
    place = lax.broadcasted_iota(jnp.int32, (n, 128), 1) == lax.broadcasted_iota(jnp.int32, (n, 128), 0) + offset
    return jnp.sum(jnp.where(place, row, 0.0), axis=1, keepdims=True)


def edge_rows(values):
    n = values.shape[0]
    row = column_as_row(values[:, -1:], None, 0) + column_as_row(values[:, :1], None, n)
    return jnp.broadcast_to(row, (EXTRA, 128))


def factor_of(counts_ref, weight_ref, d):
    slot = lax.broadcasted_iota(jnp.int32, (1, weight_ref.shape[2]), 1)
    return jnp.where(slot < counts_ref[0, d], weight_ref[0, pl.ds(d, 1), :], 0.0)


def loop(n, step, init):
    return lax.fori_loop(0, n, step, init, unroll=n if n <= 8 else 1)


def own_kernel(lev_ref, perturb_hbm, control_hbm, loc_hbm, part_ref, perturb_ref, control_ref, loc_ref, sems):
    staged = [(loc_hbm, loc_ref), (control_hbm, control_ref), (perturb_hbm, perturb_ref)]
    copies = [pltpu.make_async_copy(source, target, sems.at[i]) for i, (source, target) in enumerate(staged)]
    for copy in copies:
        copy.start()
    levels = perturb_ref.shape[0]
    copies[0].wait()
    weights = spread(loc_ref[...], lev_ref[0] * levels, levels)
    copies[1].wait()
    copies[2].wait()
    part_ref[...] = mixed_sum(weights, perturb_ref, control_ref)


def mixed_sum(weights, perturb_ref, control_ref):
    levels, members, cols = perturb_ref.shape
    perturb = perturb_ref[...].astype(F32)
    total = jnp.zeros((levels, SUB, cols), F32)
    for m in range(0, members, SUB):
        tile = control_ref[:, m : m + SUB, :].reshape(levels * SUB, cols)
        total = total + perturb[:, m : m + SUB, :] * mix(weights, tile).reshape(levels, SUB, cols)
    return jnp.sum(total, axis=1)


def band_kernel(lev_ref, counts_ref, perturb_ref, other_ref, part_ref, loc_ref, static_ref, src_ref, weight_ref,
                out_ref, acc_ref):
    levels, members, cols = perturb_ref.shape
    weights = spread(loc_ref[...], (1 - lev_ref[0]) * levels, levels)
    band_sum = part_ref[...] + mixed_sum(weights, perturb_ref, other_ref)
    acc_ref[...] = jnp.concatenate(halves(band_sum), axis=0)
    n = src_ref.shape[1]
    edges = edge_rows(static_ref[...])

    def step(d, carry):
        chosen = one_hot(src_ref[0, pl.ds(d, 1), :], cols)
        both = product(acc_ref[...], chosen)
        payload = (both[:levels] + both[levels:]) * factor_of(counts_ref, weight_ref, d)
        for g in range(out_ref.shape[0]):
            out_ref[g, d, :levels, :] = payload
            out_ref[g, d, levels:, :] = edges
        return carry

    loop(n, step, 0)


def tile_kernel(pos_ref, arrived_ref, tgt_ref, static_ref, diag_ref, off_ref, obs_ref, innov_ref,
                increment_ref, partial_ref, out_ref):
    levels, cols = static_ref.shape
    groups, n = arrived_ref.shape[:2]
    me = pos_ref[0]

    def step(s, total):
        values = sum(arrived_ref[g, s, :levels, :] for g in range(groups))
        chosen = one_hot(tgt_ref[0, pl.ds(s, 1), :], cols)
        return total + select(values, chosen, ((1,), (1,)))

    remapped = loop(n, step, jnp.zeros((levels, cols), F32))
    before = arrived_ref[0, jnp.maximum(me - 1, 0), levels : levels + 1, :]
    after = arrived_ref[0, jnp.minimum(me + 1, n - 1), levels : levels + 1, :]
    before = jnp.where(me > 0, row_as_column(before, levels, 0), 0.0)
    after = jnp.where(me < n - 1, row_as_column(after, levels, levels), 0.0)
    static = static_ref[...]
    lane = lax.broadcasted_iota(jnp.int32, (levels, cols), 1)
    left = jnp.where(lane == 0, before, pltpu.roll(static, 1, 1))
    right = jnp.where(lane == cols - 1, after, pltpu.roll(static, cols - 1, 1))
    increment = remapped + diag_ref[...] * static + off_ref[...] * (left + right)
    increment_ref[...] = increment
    misfit = obs_ref[...] * (increment - innov_ref[...])
    coupled = off_ref[...] * misfit
    left = jnp.where(lane == 0, 0.0, pltpu.roll(coupled, 1, 1))
    right = jnp.where(lane == cols - 1, 0.0, pltpu.roll(coupled, cols - 1, 1))
    partial_ref[...] = static + diag_ref[...] * misfit + left + right
    edges = edge_rows(coupled)
    both = jnp.concatenate(halves(misfit), axis=0)

    def give(s, carry):
        chosen = one_hot(tgt_ref[0, pl.ds(s, 1), :], cols)
        picked = product(both, chosen)
        out_ref[s, :levels, :] = picked[:levels] + picked[levels:]
        out_ref[s, levels:, :] = edges
        return carry

    loop(n, give, 0)


def adjoint_kernel(pos_ref, counts_ref, returned_ref, src_ref, weight_ref, partial_ref, loc_ref, grad_ref, out_ref):
    levels, cols = partial_ref.shape
    n = returned_ref.shape[0]
    band = out_ref.shape[1] - 128
    me = pos_ref[0]

    def step(d, total):
        values = returned_ref[d, :levels, :] * factor_of(counts_ref, weight_ref, d)
        return total + select(values, one_hot(src_ref[0, pl.ds(d, 1), :], band), ((1,), (1,)))

    out_ref[:, :band] = loop(n, step, jnp.zeros((levels, band), F32))
    out_ref[:, band:] = jnp.concatenate([loc_ref[...], jnp.zeros((levels, 128 - loc_ref.shape[1]), F32)], axis=1)
    before = returned_ref[jnp.maximum(me - 1, 0), levels : levels + 1, :]
    after = returned_ref[jnp.minimum(me + 1, n - 1), levels : levels + 1, :]
    before = jnp.where(me > 0, row_as_column(before, levels, 0), 0.0)
    after = jnp.where(me < n - 1, row_as_column(after, levels, levels), 0.0)
    lane = lax.broadcasted_iota(jnp.int32, (levels, cols), 1)
    grad_ref[...] = partial_ref[...] + (jnp.where(lane == 0, before, 0.0) + jnp.where(lane == cols - 1, after, 0.0))


def ens_kernel(lev_ref, perturb_ref, other_ref, control_ref, mine_ref, theirs_ref, out_ref):
    levels, members, cols = perturb_ref.shape
    mine, theirs = mine_ref[...], theirs_ref[...]
    loc = jnp.concatenate([mine[:, cols : cols + 2 * levels], theirs[:, cols : cols + 2 * levels]], axis=0)
    full = loc.shape[0]
    l_row = lax.broadcasted_iota(jnp.int32, (levels * SUB, full), 0) // SUB + lev_ref[0] * levels
    pick_l = (l_row == lax.broadcasted_iota(jnp.int32, (levels * SUB, full), 1)).astype(BF16)
    k_col = lax.broadcasted_iota(jnp.int32, (full, full * SUB), 1) // SUB
    pick_k = (k_col == lax.broadcasted_iota(jnp.int32, (full, full * SUB), 0)).astype(BF16)
    same = (
        lax.broadcasted_iota(jnp.int32, (levels * SUB, full * SUB), 0) % SUB
        == lax.broadcasted_iota(jnp.int32, (levels * SUB, full * SUB), 1) % SUB
    )
    weights = []
    for part in halves(loc):
        tall = product(pick_l, part, ((1,), (1,)))
        wide = product(tall.astype(BF16), pick_k)
        weights.append(jnp.where(same, wide, 0.0).astype(BF16))
    perturb = perturb_ref[...].astype(F32)
    other = other_ref[...].astype(F32)
    grad = jnp.concatenate([mine[:, :cols], theirs[:, :cols]], axis=0)[:, None, :]
    for m in range(0, members, SUB):
        tile = jnp.concatenate([perturb[:, m : m + SUB, :], other[:, m : m + SUB, :]], axis=0) * grad
        mixed = mix(weights, tile.reshape(full * SUB, cols)).reshape(levels, SUB, cols)
        out_ref[:, m : m + SUB, :] = control_ref[:, m : m + SUB, :] + mixed


class Rows:
    def __init__(self, levels, n):
        self.weight = slice(0, levels)
        self.base = slice(levels, 2 * levels)
        at = 2 * levels
        self.src, self.factor, self.tgt, self.edge = at, at + n, at + 2 * n, at + 3 * n
        self.total = at + 3 * n + EXTRA


def static_kernel(pos_ref, counts_ref, static_ref, diag_ref, off_ref, obs_ref, innov_ref, src_ref, weight_ref, tgt_ref,
                  *out_refs):
    levels, cols = static_ref.shape
    n = len(out_refs)
    cap = src_ref.shape[2]
    rows = Rows(levels, n)
    me = pos_ref[0]
    static, off, obs = static_ref[...], off_ref[...], obs_ref[...]
    lane = lax.broadcasted_iota(jnp.int32, (levels, cols), 1)
    left = jnp.where(lane == 0, 0.0, pltpu.roll(static, 1, 1))
    right = jnp.where(lane == cols - 1, 0.0, pltpu.roll(static, cols - 1, 1))
    base = diag_ref[...] * static + off * (left + right) - innov_ref[...]
    coupled = off * obs
    ends = [v[:, i] for v in (static, coupled, base) for i in (slice(cols - 1, cols), slice(0, 1))]
    edge = sum(column_as_row(end, None, i * levels) for i, end in enumerate(ends))
    place = lax.broadcasted_iota(jnp.int32, (1, cap), 1)
    edge = edge + jnp.where(place == 6 * levels, off[:, cols - 1 :], 0.0)
    edge = edge + jnp.where(place == 6 * levels + 1, off[:, :1], 0.0)
    edge = jnp.broadcast_to(edge, (EXTRA, cap))
    both = jnp.concatenate(halves(jnp.concatenate([obs, base], axis=0)), axis=0)
    tgts = [tgt_ref[0, pl.ds(me ^ r, 1), :] for r in range(n)]
    src = jnp.concatenate([src_ref[0, pl.ds(me ^ r, 1), :] for r in range(n)], axis=0).astype(F32)
    tgt = jnp.concatenate(tgts, axis=0).astype(F32)
    factor = jnp.concatenate([factor_of(counts_ref, weight_ref, me ^ r) for r in range(n)], axis=0)
    for r, out_ref in enumerate(out_refs):
        picked = product(both, one_hot(tgts[r], cols))
        out_ref[: 2 * levels, :] = picked[: 2 * levels] + picked[2 * levels :]
        out_ref[rows.src : rows.src + n, :] = src
        out_ref[rows.factor : rows.factor + n, :] = factor
        out_ref[rows.tgt : rows.tgt + n, :] = tgt
        out_ref[rows.edge :, :] = edge


def sum_kernel(lev_ref, perturb_ref, other_ref, part_ref, loc_ref, out_ref):
    levels = perturb_ref.shape[0]
    weights = spread(loc_ref[...], (1 - lev_ref[0]) * levels, levels)
    out_ref[...] = part_ref[...] + mixed_sum(weights, perturb_ref, other_ref)


def blocks_kernel(groups, *refs):
    sums = refs[:groups]
    count = (len(refs) - groups - 1) // 2
    rests = refs[groups : groups + count]
    total_ref = refs[groups + count]
    out_refs = refs[groups + count + 1 :]
    total = sum(ref[...] for ref in sums)
    cap = total_ref.shape[1]
    total = jnp.concatenate([total[:, at : at + cap] for at in range(0, total.shape[1], cap)], axis=0)
    total_ref[...] = total
    for rest_ref, out_ref in zip(rests, out_refs):
        out_ref[: total.shape[0], :] = total
        out_ref[total.shape[0] :, :] = rest_ref[...]


def shared_kernel(n, levels, cols, pos_ref, loc_ref, *refs):
    sums_refs, rest_refs = refs[:n], refs[n : 2 * n]
    out_ref, slots_ref, tables_ref = refs[2 * n :]
    cap = slots_ref.shape[2] // n
    band = out_ref.shape[1] - 128
    rows = Rows(levels, n)
    parts = band // cap
    me = pos_ref[0]
    heads = [ref.shape[0] - rows.total for ref in rest_refs]

    def rest(r, at, size):
        return rest_refs[r][heads[r] + at : heads[r] + at + size, :]

    def row(r, at):
        return rest(r, at, 1)

    column = lax.broadcasted_iota(jnp.int32, (band, cap), 0).astype(F32)

    def chosen(s, d):
        return jnp.where(column == row(s, rows.src + (s ^ d)), 1.0, 0.0).astype(BF16)

    for r in range(n):
        tables_ref[me ^ r] = rest(r, rows.tgt, n + EXTRA)
    for s in range(n):
        sums = jnp.concatenate([sums_refs[s][i * levels : (i + 1) * levels, :] for i in range(parts)], axis=1)
        both = jnp.concatenate(halves(sums), axis=0)
        for d in range(n):
            picked = product(both, chosen(s, d))
            values = (picked[:levels] + picked[levels:]) * row(s, rows.factor + (s ^ d))
            slots_ref[d, :, s * cap : (s + 1) * cap] = jnp.concatenate(halves(values), axis=0)
    own = jnp.concatenate([row(d, rows.tgt + d) for d in range(n)], axis=0)
    turned = own.T
    last = cols - 1.0
    total = jnp.zeros((levels, band), F32)
    for d in range(n):
        same = [
            jnp.where(turned[:, d : d + 1] == row(d, rows.tgt + (s ^ d)), 1.0, 0.0).astype(BF16) for s in range(n)
        ]
        met = product(slots_ref[d], jnp.concatenate(same, axis=1), ((1,), (1,)))
        value = met[:levels] + met[levels:] + rest(d, levels, levels)
        edge = row(d, rows.edge)
        there = me ^ d
        before = tables_ref[jnp.maximum(there - 1, 0), n : n + 1, :]
        near = jnp.where((own[d : d + 1] == 0.0) & (there > 0), edge[:, 6 * levels + 1 : 6 * levels + 2], 0.0)
        value = value + row_as_column(before, levels, 0) * near
        after = tables_ref[jnp.minimum(there + 1, n - 1), n : n + 1, :]
        near = jnp.where((own[d : d + 1] == last) & (there < n - 1), edge[:, 6 * levels : 6 * levels + 1], 0.0)
        value = value + row_as_column(after, levels, levels) * near
        misfit = rest(d, 0, levels) * value
        given = misfit * row(0, rows.factor + d)
        total = total + select(given, chosen(0, d), ((1,), (1,)))
    out_ref[:, :band] = total
    out_ref[:, band:] = jnp.concatenate([loc_ref[...], jnp.zeros((levels, 128 - loc_ref.shape[1]), F32)], axis=1)


def outputs_kernel(pos_ref, slots_ref, tables_ref, static_ref, diag_ref, off_ref, obs_ref, innov_ref,
                   increment_ref, grad_ref):
    levels, cols = static_ref.shape
    n = tables_ref.shape[0]
    cap = tables_ref.shape[2]
    me = pos_ref[0]
    row = lax.broadcasted_iota(jnp.int32, (cols, cap), 0).astype(F32)
    remapped = jnp.zeros((2 * levels, cols), F32)
    for s in range(n):
        landing = jnp.where(row == tables_ref[me, s : s + 1, :], 1.0, 0.0).astype(BF16)
        remapped = remapped + product(slots_ref[0, :, s * cap : (s + 1) * cap], landing, ((1,), (1,)))
    remapped = remapped[:levels] + remapped[levels:]
    static, off = static_ref[...], off_ref[...]
    lane = lax.broadcasted_iota(jnp.int32, (levels, cols), 1)

    def beside(there, exists, column, own_end, side):
        edge = tables_ref[there, n : n + 1, :]
        static_end, coupling, base = (row_as_column(edge, levels, (2 * i + side) * levels) for i in range(3))
        far = me ^ there
        values = slots_ref[far, :levels, :].astype(F32) + slots_ref[far, levels:, :].astype(F32)
        landed = [
            jnp.where(tables_ref[there, pl.ds(s ^ far, 1), :] == column, values[:, s * cap : (s + 1) * cap], 0.0)
            for s in range(n)
        ]
        remap_end = jnp.sum(sum(landed), axis=1, keepdims=True)
        off_end = edge[:, 6 * levels + side : 6 * levels + side + 1]
        coupled = coupling * (remap_end + base + off_end * own_end)
        return jnp.where(exists, static_end, 0.0), jnp.where(exists, coupled, 0.0)

    before, coupled_before = beside(jnp.maximum(me - 1, 0), me > 0, cols - 1.0, static[:, :1], 0)
    after, coupled_after = beside(jnp.minimum(me + 1, n - 1), me < n - 1, 0.0, static[:, cols - 1 :], 1)
    left = jnp.where(lane == 0, before, pltpu.roll(static, 1, 1))
    right = jnp.where(lane == cols - 1, after, pltpu.roll(static, cols - 1, 1))
    increment = remapped + diag_ref[...] * static + off * (left + right)
    increment_ref[...] = increment
    misfit = obs_ref[...] * (increment - innov_ref[...])
    coupled = off * misfit
    left = jnp.where(lane == 0, coupled_before, pltpu.roll(coupled, 1, 1))
    right = jnp.where(lane == cols - 1, coupled_after, pltpu.roll(coupled, cols - 1, 1))
    grad_ref[...] = static + diag_ref[...] * misfit + left + right


def call(kernel, out_shape, spaces, scratch=(), limit=40 * MIB):
    return pl.pallas_call(
        kernel,
        out_shape=out_shape,
        in_specs=spaces,
        out_specs=jax.tree.map(lambda _: VMEM, out_shape),
        scratch_shapes=scratch,
        compiler_params=pltpu.CompilerParams(vmem_limit_bytes=limit),
    )


def body(
    perturb,
    control,
    level_loc,
    static_control,
    filter_diag,
    filter_off,
    send_src,
    send_wt,
    counts,
    recv_tgt,
    obs_weight,
    innovation,
):
    levels, members, band_cols = control.shape
    tile_cols = static_control.shape[1]
    n = lax.axis_size("tile")
    groups = lax.axis_size("grp")
    cap = send_src.shape[2]
    shape = jax.ShapeDtypeStruct
    swap = [(0, 1), (1, 0)]
    lev = lax.axis_index("lev").astype(jnp.int32).reshape(1)
    pos = lax.axis_index("tile").astype(jnp.int32).reshape(1)
    other_control = lax.ppermute(control, "lev", swap)
    other_perturb = lax.ppermute(perturb, "lev", swap)
    part = call(
        own_kernel,
        shape((levels, band_cols), F32),
        [SMEM] + [HBM] * 3,
        [pltpu.VMEM(a.shape, a.dtype) for a in (perturb, control, level_loc)] + [pltpu.SemaphoreType.DMA((3,))],
        limit=58 * MIB,
    )(lev, perturb, control, level_loc)
    flat = shape((levels, tile_cols), F32)
    mine_shape = shape((levels, band_cols + 128), F32)
    diag, off = filter_diag.reshape(1, -1), filter_off.reshape(1, -1)
    if n * cap <= tile_cols and n & (n - 1) == 0:
        rows = Rows(levels, n)
        stacked = band_cols // cap * levels
        rests = call(static_kernel, [shape((rows.total, cap), F32)] * n, [SMEM] * 2 + [VMEM] * 8)(
            pos, counts, static_control, diag, off, obs_weight, innovation, send_src, send_wt, recv_tgt
        )
        sums = [
            call(sum_kernel, shape((levels, band_cols), F32), [SMEM] + [VMEM] * 4)(
                lev, perturb, other_control, part, level_loc
            )
        ]
        for k in range(1, groups):
            sums.append(lax.ppermute(sums[0], "grp", [(g, (g + k) % groups) for g in range(groups)]))
        total, *blocks = call(
            functools.partial(blocks_kernel, groups),
            [shape((stacked, cap), F32)] + [shape((stacked + rows.total, cap), F32)] * (n - 1),
            [VMEM] * (groups + n - 1),
        )(*sums, *rests[1:])
        arrived = {}
        for r in reversed(range(1, n)):
            arrived[r] = lax.ppermute(blocks[r - 1], "tile", [(i, i ^ r) for i in range(n)])
        arrived = [arrived[r] for r in range(1, n)]
        mine, slots, tables = call(
            functools.partial(shared_kernel, n, levels, tile_cols),
            (mine_shape, shape((n, 2 * levels, n * cap), BF16), shape((n, n + EXTRA, cap), F32)),
            [SMEM] + [VMEM] * (2 * n + 1),
        )(pos, level_loc, total, *arrived, rests[0], *arrived)
        increment, grad_static = call(outputs_kernel, (flat, flat), [SMEM] + [VMEM] * 7)(
            pos, slots, tables, static_control, diag, off, obs_weight, innovation
        )
    else:
        payload = call(
            band_kernel,
            shape((groups, n, levels + EXTRA, cap), F32),
            [SMEM] * 2 + [VMEM] * 7,
            [pltpu.VMEM((2 * levels, band_cols), BF16)],
        )(lev, counts, perturb, other_control, part, level_loc, static_control, send_src, send_wt)
        arrived = lax.all_to_all(
            payload.reshape(groups * n, levels + EXTRA, cap), ("grp", "tile"), split_axis=0, concat_axis=0, tiled=True
        ).reshape(groups, n, levels + EXTRA, cap)
        increment, partial, giving = call(
            tile_kernel, (flat, flat, shape((n, levels + EXTRA, cap), F32)), [SMEM] + [VMEM] * 7
        )(pos, arrived, recv_tgt, static_control, diag, off, obs_weight, innovation)
        returned = lax.all_to_all(giving, "tile", split_axis=0, concat_axis=0, tiled=True)
        grad_static, mine = call(adjoint_kernel, (flat, mine_shape), [SMEM, SMEM] + [VMEM] * 5)(
            pos, counts, returned, send_src, send_wt, partial, level_loc
        )
    theirs = lax.ppermute(mine, "lev", swap)
    grad_ens = call(ens_kernel, shape(control.shape, F32), [SMEM] + [VMEM] * 5)(
        lev, perturb, other_perturb, control, mine, theirs
    )
    return (increment, grad_static, grad_ens)


def solution(mesh):
    return jax.shard_map(
        body,
        mesh=mesh,
        in_specs=(
            P("lev", "grp", "tile"),
            P("lev", "grp", "tile"),
            P("lev", None),
            P("lev", "tile"),
            P("tile"),
            P("tile"),
            P("tile", None, None),
            P("tile", None, None),
            P("tile", None),
            P("tile", None, None),
            P("lev", "tile"),
            P("lev", "tile"),
        ),
        out_specs=(P("lev", "tile"), P("lev", "tile"), P("lev", "grp", "tile")),
        check_vma=False,
    )
```

```python
import functools

import jax
import jax.numpy as jnp
from jax import lax
from jax.experimental import pallas as pl
from jax.experimental.pallas import tpu as pltpu
from jax.sharding import PartitionSpec as P

F32 = jnp.float32
BF16 = jnp.bfloat16
SUB = 8
EXTRA = 8
VMEM = pl.BlockSpec(memory_space=pltpu.VMEM)
HBM = pl.BlockSpec(memory_space=pltpu.HBM)
SMEM = pl.BlockSpec(memory_space=pltpu.SMEM)
MIB = 1024 * 1024


def halves(values):
    high = values.astype(BF16)
    low = (values - high.astype(F32)).astype(BF16)
    return high, low


def product(a, b, dims=((1,), (0,))):
    return lax.dot_general(a, b, (dims, ((), ())), preferred_element_type=F32)


def select(values, chosen, dims=((1,), (0,))):
    rows = values.shape[0]
    both = product(jnp.concatenate(halves(values), axis=0), chosen, dims)
    return both[:rows] + both[rows:]


def spread(matrix, start, count):
    rows, cols = matrix.shape

    def iota(shape, axis):
        return lax.broadcasted_iota(jnp.int32, shape, axis)

    shape = (rows * SUB, count * SUB)
    tall = (iota((rows * SUB, rows), 0) // SUB == iota((rows * SUB, rows), 1)).astype(BF16)
    wide = (iota((cols, count * SUB), 1) // SUB + start == iota((cols, count * SUB), 0)).astype(BF16)
    same = iota(shape, 0) % SUB == iota(shape, 1) % SUB
    out = []
    for part in halves(matrix):
        filled = product(tall, product(part, wide).astype(BF16))
        out.append(jnp.where(same, filled, 0.0).astype(BF16))
    return out


def mix(weights, values):
    high, low = halves(values)
    return product(weights[0], high) + (product(weights[0], low) + product(weights[1], high))


def one_hot(index, size):
    rows = lax.broadcasted_iota(jnp.int32, (size, index.shape[1]), 0)
    return jnp.where(rows == index, 1.0, 0.0).astype(BF16)


def column_as_row(column, lane, offset):
    n = column.shape[0]
    place = lax.broadcasted_iota(jnp.int32, (n, 128), 1) == lax.broadcasted_iota(jnp.int32, (n, 128), 0) + offset
    return jnp.sum(jnp.where(place, column, 0.0), axis=0, keepdims=True)


def row_as_column(row, n, offset):
    place = lax.broadcasted_iota(jnp.int32, (n, 128), 1) == lax.broadcasted_iota(jnp.int32, (n, 128), 0) + offset
    return jnp.sum(jnp.where(place, row, 0.0), axis=1, keepdims=True)


def edge_rows(values):
    n = values.shape[0]
    row = column_as_row(values[:, -1:], None, 0) + column_as_row(values[:, :1], None, n)
    return jnp.broadcast_to(row, (EXTRA, 128))


def factor_of(counts_ref, weight_ref, d):
    slot = lax.broadcasted_iota(jnp.int32, (1, weight_ref.shape[2]), 1)
    return jnp.where(slot < counts_ref[0, d], weight_ref[0, pl.ds(d, 1), :], 0.0)


def loop(n, step, init):
    return lax.fori_loop(0, n, step, init, unroll=n if n <= 8 else 1)


def own_kernel(lev_ref, perturb_hbm, control_hbm, loc_hbm, part_ref, perturb_ref, control_ref, loc_ref, sems):
    staged = [(loc_hbm, loc_ref), (control_hbm, control_ref), (perturb_hbm, perturb_ref)]
    copies = [pltpu.make_async_copy(source, target, sems.at[i]) for i, (source, target) in enumerate(staged)]
    for copy in copies:
        copy.start()
    levels = perturb_ref.shape[0]
    copies[0].wait()
    weights = spread(loc_ref[...], lev_ref[0] * levels, levels)
    copies[1].wait()
    copies[2].wait()
    part_ref[...] = mixed_sum(weights, perturb_ref, control_ref)


def mixed_sum(weights, perturb_ref, control_ref):
    levels, members, cols = perturb_ref.shape
    perturb = perturb_ref[...].astype(F32)
    total = jnp.zeros((levels, SUB, cols), F32)
    for m in range(0, members, SUB):
        tile = control_ref[:, m : m + SUB, :].reshape(levels * SUB, cols)
        total = total + perturb[:, m : m + SUB, :] * mix(weights, tile).reshape(levels, SUB, cols)
    return jnp.sum(total, axis=1)


def band_kernel(lev_ref, counts_ref, perturb_ref, other_ref, part_ref, loc_ref, static_ref, src_ref, weight_ref,
                out_ref, acc_ref):
    levels, members, cols = perturb_ref.shape
    weights = spread(loc_ref[...], (1 - lev_ref[0]) * levels, levels)
    band_sum = part_ref[...] + mixed_sum(weights, perturb_ref, other_ref)
    acc_ref[...] = jnp.concatenate(halves(band_sum), axis=0)
    n = src_ref.shape[1]
    edges = edge_rows(static_ref[...])

    def step(d, carry):
        chosen = one_hot(src_ref[0, pl.ds(d, 1), :], cols)
        both = product(acc_ref[...], chosen)
        payload = (both[:levels] + both[levels:]) * factor_of(counts_ref, weight_ref, d)
        for g in range(out_ref.shape[0]):
            out_ref[g, d, :levels, :] = payload
            out_ref[g, d, levels:, :] = edges
        return carry

    loop(n, step, 0)


def tile_kernel(pos_ref, arrived_ref, tgt_ref, static_ref, diag_ref, off_ref, obs_ref, innov_ref,
                increment_ref, partial_ref, out_ref):
    levels, cols = static_ref.shape
    groups, n = arrived_ref.shape[:2]
    me = pos_ref[0]

    def step(s, total):
        values = sum(arrived_ref[g, s, :levels, :] for g in range(groups))
        chosen = one_hot(tgt_ref[0, pl.ds(s, 1), :], cols)
        return total + select(values, chosen, ((1,), (1,)))

    remapped = loop(n, step, jnp.zeros((levels, cols), F32))
    before = arrived_ref[0, jnp.maximum(me - 1, 0), levels : levels + 1, :]
    after = arrived_ref[0, jnp.minimum(me + 1, n - 1), levels : levels + 1, :]
    before = jnp.where(me > 0, row_as_column(before, levels, 0), 0.0)
    after = jnp.where(me < n - 1, row_as_column(after, levels, levels), 0.0)
    static = static_ref[...]
    lane = lax.broadcasted_iota(jnp.int32, (levels, cols), 1)
    left = jnp.where(lane == 0, before, pltpu.roll(static, 1, 1))
    right = jnp.where(lane == cols - 1, after, pltpu.roll(static, cols - 1, 1))
    increment = remapped + diag_ref[...] * static + off_ref[...] * (left + right)
    increment_ref[...] = increment
    misfit = obs_ref[...] * (increment - innov_ref[...])
    coupled = off_ref[...] * misfit
    left = jnp.where(lane == 0, 0.0, pltpu.roll(coupled, 1, 1))
    right = jnp.where(lane == cols - 1, 0.0, pltpu.roll(coupled, cols - 1, 1))
    partial_ref[...] = static + diag_ref[...] * misfit + left + right
    edges = edge_rows(coupled)
    both = jnp.concatenate(halves(misfit), axis=0)

    def give(s, carry):
        chosen = one_hot(tgt_ref[0, pl.ds(s, 1), :], cols)
        picked = product(both, chosen)
        out_ref[s, :levels, :] = picked[:levels] + picked[levels:]
        out_ref[s, levels:, :] = edges
        return carry

    loop(n, give, 0)


def adjoint_kernel(pos_ref, counts_ref, returned_ref, src_ref, weight_ref, partial_ref, loc_ref, grad_ref, out_ref):
    levels, cols = partial_ref.shape
    n = returned_ref.shape[0]
    band = out_ref.shape[1] - 128
    me = pos_ref[0]

    def step(d, total):
        values = returned_ref[d, :levels, :] * factor_of(counts_ref, weight_ref, d)
        return total + select(values, one_hot(src_ref[0, pl.ds(d, 1), :], band), ((1,), (1,)))

    out_ref[:, :band] = loop(n, step, jnp.zeros((levels, band), F32))
    out_ref[:, band:] = jnp.concatenate([loc_ref[...], jnp.zeros((levels, 128 - loc_ref.shape[1]), F32)], axis=1)
    before = returned_ref[jnp.maximum(me - 1, 0), levels : levels + 1, :]
    after = returned_ref[jnp.minimum(me + 1, n - 1), levels : levels + 1, :]
    before = jnp.where(me > 0, row_as_column(before, levels, 0), 0.0)
    after = jnp.where(me < n - 1, row_as_column(after, levels, levels), 0.0)
    lane = lax.broadcasted_iota(jnp.int32, (levels, cols), 1)
    grad_ref[...] = partial_ref[...] + (jnp.where(lane == 0, before, 0.0) + jnp.where(lane == cols - 1, after, 0.0))


def ens_kernel(lev_ref, perturb_ref, other_ref, control_ref, mine_ref, theirs_ref, out_ref):
    levels, members, cols = perturb_ref.shape
    mine, theirs = mine_ref[...], theirs_ref[...]
    loc = jnp.concatenate([mine[:, cols : cols + 2 * levels], theirs[:, cols : cols + 2 * levels]], axis=0)
    full = loc.shape[0]
    l_row = lax.broadcasted_iota(jnp.int32, (levels * SUB, full), 0) // SUB + lev_ref[0] * levels
    pick_l = (l_row == lax.broadcasted_iota(jnp.int32, (levels * SUB, full), 1)).astype(BF16)
    k_col = lax.broadcasted_iota(jnp.int32, (full, full * SUB), 1) // SUB
    pick_k = (k_col == lax.broadcasted_iota(jnp.int32, (full, full * SUB), 0)).astype(BF16)
    same = (
        lax.broadcasted_iota(jnp.int32, (levels * SUB, full * SUB), 0) % SUB
        == lax.broadcasted_iota(jnp.int32, (levels * SUB, full * SUB), 1) % SUB
    )
    weights = []
    for part in halves(loc):
        tall = product(pick_l, part, ((1,), (1,)))
        wide = product(tall.astype(BF16), pick_k)
        weights.append(jnp.where(same, wide, 0.0).astype(BF16))
    perturb = perturb_ref[...].astype(F32)
    other = other_ref[...].astype(F32)
    grad = jnp.concatenate([mine[:, :cols], theirs[:, :cols]], axis=0)[:, None, :]
    for m in range(0, members, SUB):
        tile = jnp.concatenate([perturb[:, m : m + SUB, :], other[:, m : m + SUB, :]], axis=0) * grad
        mixed = mix(weights, tile.reshape(full * SUB, cols)).reshape(levels, SUB, cols)
        out_ref[:, m : m + SUB, :] = control_ref[:, m : m + SUB, :] + mixed


class Rows:
    def __init__(self, levels, n):
        self.weight = slice(0, levels)
        self.base = slice(levels, 2 * levels)
        at = 2 * levels
        self.factor, self.index, self.edge = at, at + n, at + 2 * n
        self.total = at + 2 * n + EXTRA


def static_kernel(band, pos_ref, counts_ref, static_ref, diag_ref, off_ref, obs_ref, innov_ref, src_ref, weight_ref, tgt_ref,
                  *out_refs):
    levels, cols = static_ref.shape
    n = len(out_refs)
    cap = src_ref.shape[2]
    rows = Rows(levels, n)
    me = pos_ref[0]
    static, off, obs = static_ref[...], off_ref[...], obs_ref[...]
    lane = lax.broadcasted_iota(jnp.int32, (levels, cols), 1)
    left = jnp.where(lane == 0, 0.0, pltpu.roll(static, 1, 1))
    right = jnp.where(lane == cols - 1, 0.0, pltpu.roll(static, cols - 1, 1))
    base = diag_ref[...] * static + off * (left + right) - innov_ref[...]
    coupled = off * obs
    ends = [v[:, i] for v in (static, coupled, base) for i in (slice(cols - 1, cols), slice(0, 1))]
    edge = sum(column_as_row(end, None, i * levels) for i, end in enumerate(ends))
    place = lax.broadcasted_iota(jnp.int32, (1, cap), 1)
    edge = edge + jnp.where(place == 6 * levels, off[:, cols - 1 :], 0.0)
    edge = edge + jnp.where(place == 6 * levels + 1, off[:, :1], 0.0)
    edge = jnp.broadcast_to(edge, (EXTRA, cap))
    both = jnp.concatenate(halves(jnp.concatenate([obs, base], axis=0)), axis=0)
    tgts = [tgt_ref[0, pl.ds(me ^ r, 1), :] for r in range(n)]
    src = jnp.concatenate([src_ref[0, pl.ds(me ^ r, 1), :] for r in range(n)], axis=0).astype(F32)
    index = jnp.concatenate(tgts, axis=0).astype(F32) * float(band) + src
    factor = jnp.concatenate([factor_of(counts_ref, weight_ref, me ^ r) for r in range(n)], axis=0)
    for r, out_ref in enumerate(out_refs):
        picked = product(both, one_hot(tgts[r], cols))
        out_ref[: 2 * levels, :] = picked[: 2 * levels] + picked[2 * levels :]
        out_ref[rows.factor : rows.factor + n, :] = factor
        out_ref[rows.index : rows.index + n, :] = index
        out_ref[rows.edge :, :] = edge


def sum_kernel(lev_ref, perturb_ref, other_ref, part_ref, loc_ref, out_ref):
    levels = perturb_ref.shape[0]
    weights = spread(loc_ref[...], (1 - lev_ref[0]) * levels, levels)
    out_ref[...] = part_ref[...] + mixed_sum(weights, perturb_ref, other_ref)


def blocks_kernel(groups, *refs):
    sums = refs[:groups]
    count = (len(refs) - groups - 1) // 2
    rests = refs[groups : groups + count]
    total_ref = refs[groups + count]
    out_refs = refs[groups + count + 1 :]
    total = sum(ref[...] for ref in sums)
    cap = total_ref.shape[1]
    total = jnp.concatenate([total[:, at : at + cap] for at in range(0, total.shape[1], cap)], axis=0)
    total_ref[...] = total
    for rest_ref, out_ref in zip(rests, out_refs):
        out_ref[: total.shape[0], :] = total
        out_ref[total.shape[0] :, :] = rest_ref[...]


def shared_kernel(order, levels, cols, pos_ref, loc_ref, total_ref, rest_ref, *refs):
    n = len(order) + 1
    blocks = dict(zip(order, refs))
    sums_refs = [total_ref] + [blocks[r] for r in range(1, n)]
    rest_refs = [rest_ref] + [blocks[r] for r in range(1, n)]
    out_ref, slots_ref, tables_ref = refs[n - 1 :]
    cap = slots_ref.shape[2] // n
    band = out_ref.shape[1] - 128
    rows = Rows(levels, n)
    parts = band // cap
    me = pos_ref[0]
    heads = [ref.shape[0] - rows.total for ref in rest_refs]

    def rest(r, at, size):
        return rest_refs[r][heads[r] + at : heads[r] + at + size, :]

    def row(r, at):
        return rest(r, at, 1)

    column = lax.broadcasted_iota(jnp.int32, (band, cap), 0).astype(F32)
    src, tgt = [], []
    for r in range(n):
        words = rest(r, rows.index, n)
        tgt.append(jnp.floor((words + 0.5) * (1.0 / band)))
        src.append(words - tgt[r] * float(band))
        tables_ref[me ^ r, :n, :] = tgt[r]
        tables_ref[me ^ r, n:, :] = rest(r, rows.edge, EXTRA)

    def chosen(s, d):
        return jnp.where(column == src[s][s ^ d : (s ^ d) + 1], 1.0, 0.0).astype(BF16)

    for s in range(n):
        sums = jnp.concatenate([sums_refs[s][i * levels : (i + 1) * levels, :] for i in range(parts)], axis=1)
        both = jnp.concatenate(halves(sums), axis=0)
        for d in range(n):
            picked = product(both, chosen(s, d))
            values = (picked[:levels] + picked[levels:]) * row(s, rows.factor + (s ^ d))
            slots_ref[d, :, s * cap : (s + 1) * cap] = jnp.concatenate(halves(values), axis=0)
    own = jnp.concatenate([tgt[d][d : d + 1] for d in range(n)], axis=0)
    turned = own.T
    last = cols - 1.0
    total = jnp.zeros((levels, band), F32)
    for d in range(n):
        same = [
            jnp.where(turned[:, d : d + 1] == tgt[d][s ^ d : (s ^ d) + 1], 1.0, 0.0).astype(BF16) for s in range(n)
        ]
        met = product(slots_ref[d], jnp.concatenate(same, axis=1), ((1,), (1,)))
        value = met[:levels] + met[levels:] + rest(d, levels, levels)
        edge = row(d, rows.edge)
        there = me ^ d
        before = tables_ref[jnp.maximum(there - 1, 0), n : n + 1, :]
        near = jnp.where((own[d : d + 1] == 0.0) & (there > 0), edge[:, 6 * levels + 1 : 6 * levels + 2], 0.0)
        value = value + row_as_column(before, levels, 0) * near
        after = tables_ref[jnp.minimum(there + 1, n - 1), n : n + 1, :]
        near = jnp.where((own[d : d + 1] == last) & (there < n - 1), edge[:, 6 * levels : 6 * levels + 1], 0.0)
        value = value + row_as_column(after, levels, levels) * near
        misfit = rest(d, 0, levels) * value
        given = misfit * row(0, rows.factor + d)
        total = total + select(given, chosen(0, d), ((1,), (1,)))
    out_ref[:, :band] = total
    out_ref[:, band:] = jnp.concatenate([loc_ref[...], jnp.zeros((levels, 128 - loc_ref.shape[1]), F32)], axis=1)


def outputs_kernel(pos_ref, slots_ref, tables_ref, static_ref, diag_ref, off_ref, obs_ref, innov_ref,
                   increment_ref, grad_ref):
    levels, cols = static_ref.shape
    n = tables_ref.shape[0]
    cap = tables_ref.shape[2]
    me = pos_ref[0]
    row = lax.broadcasted_iota(jnp.int32, (cols, cap), 0).astype(F32)
    remapped = jnp.zeros((2 * levels, cols), F32)
    for s in range(n):
        landing = jnp.where(row == tables_ref[me, s : s + 1, :], 1.0, 0.0).astype(BF16)
        remapped = remapped + product(slots_ref[0, :, s * cap : (s + 1) * cap], landing, ((1,), (1,)))
    remapped = remapped[:levels] + remapped[levels:]
    static, off = static_ref[...], off_ref[...]
    lane = lax.broadcasted_iota(jnp.int32, (levels, cols), 1)

    def beside(there, exists, column, own_end, side):
        edge = tables_ref[there, n : n + 1, :]
        static_end, coupling, base = (row_as_column(edge, levels, (2 * i + side) * levels) for i in range(3))
        far = me ^ there
        values = slots_ref[far, :levels, :].astype(F32) + slots_ref[far, levels:, :].astype(F32)
        landed = [
            jnp.where(tables_ref[there, pl.ds(s ^ far, 1), :] == column, values[:, s * cap : (s + 1) * cap], 0.0)
            for s in range(n)
        ]
        remap_end = jnp.sum(sum(landed), axis=1, keepdims=True)
        off_end = edge[:, 6 * levels + side : 6 * levels + side + 1]
        coupled = coupling * (remap_end + base + off_end * own_end)
        return jnp.where(exists, static_end, 0.0), jnp.where(exists, coupled, 0.0)

    before, coupled_before = beside(jnp.maximum(me - 1, 0), me > 0, cols - 1.0, static[:, :1], 0)
    after, coupled_after = beside(jnp.minimum(me + 1, n - 1), me < n - 1, 0.0, static[:, cols - 1 :], 1)
    left = jnp.where(lane == 0, before, pltpu.roll(static, 1, 1))
    right = jnp.where(lane == cols - 1, after, pltpu.roll(static, cols - 1, 1))
    increment = remapped + diag_ref[...] * static + off * (left + right)
    increment_ref[...] = increment
    misfit = obs_ref[...] * (increment - innov_ref[...])
    coupled = off * misfit
    left = jnp.where(lane == 0, coupled_before, pltpu.roll(coupled, 1, 1))
    right = jnp.where(lane == cols - 1, coupled_after, pltpu.roll(coupled, cols - 1, 1))
    grad_ref[...] = static + diag_ref[...] * misfit + left + right


def call(kernel, out_shape, spaces, scratch=(), limit=40 * MIB):
    return pl.pallas_call(
        kernel,
        out_shape=out_shape,
        in_specs=spaces,
        out_specs=jax.tree.map(lambda _: VMEM, out_shape),
        scratch_shapes=scratch,
        compiler_params=pltpu.CompilerParams(vmem_limit_bytes=limit),
    )


def body(
    perturb,
    control,
    level_loc,
    static_control,
    filter_diag,
    filter_off,
    send_src,
    send_wt,
    counts,
    recv_tgt,
    obs_weight,
    innovation,
):
    levels, members, band_cols = control.shape
    tile_cols = static_control.shape[1]
    n = lax.axis_size("tile")
    groups = lax.axis_size("grp")
    cap = send_src.shape[2]
    shape = jax.ShapeDtypeStruct
    swap = [(0, 1), (1, 0)]
    lev = lax.axis_index("lev").astype(jnp.int32).reshape(1)
    pos = lax.axis_index("tile").astype(jnp.int32).reshape(1)
    other_control = lax.ppermute(control, "lev", swap)
    other_perturb = lax.ppermute(perturb, "lev", swap)
    part = call(
        own_kernel,
        shape((levels, band_cols), F32),
        [SMEM] + [HBM] * 3,
        [pltpu.VMEM(a.shape, a.dtype) for a in (perturb, control, level_loc)] + [pltpu.SemaphoreType.DMA((3,))],
        limit=58 * MIB,
    )(lev, perturb, control, level_loc)
    flat = shape((levels, tile_cols), F32)
    mine_shape = shape((levels, band_cols + 128), F32)
    diag, off = filter_diag.reshape(1, -1), filter_off.reshape(1, -1)
    if n * cap <= tile_cols and n & (n - 1) == 0 and band_cols * tile_cols <= 2**20:
        rows = Rows(levels, n)
        stacked = band_cols // cap * levels
        rests = call(functools.partial(static_kernel, band_cols), [shape((rows.total, cap), F32)] * n, [SMEM] * 2 + [VMEM] * 8)(
            pos, counts, static_control, diag, off, obs_weight, innovation, send_src, send_wt, recv_tgt
        )
        sums = [
            call(sum_kernel, shape((levels, band_cols), F32), [SMEM] + [VMEM] * 4)(
                lev, perturb, other_control, part, level_loc
            )
        ]
        sums[0], other_perturb = lax.optimization_barrier((sums[0], other_perturb))
        for k in range(1, groups):
            sums.append(lax.ppermute(sums[0], "grp", [(g, (g + k) % groups) for g in range(groups)]))
        total, *blocks = call(
            functools.partial(blocks_kernel, groups),
            [shape((stacked, cap), F32)] + [shape((stacked + rows.total, cap), F32)] * (n - 1),
            [VMEM] * (groups + n - 1),
        )(*sums, *rests[1:])
        order = [*range(n // 2, n), *range(1, n // 2)]
        arrived = [lax.ppermute(blocks[r - 1], "tile", [(i, i ^ r) for i in range(n)]) for r in order]
        mine, slots, tables = call(
            functools.partial(shared_kernel, order, levels, tile_cols),
            (mine_shape, shape((n, 2 * levels, n * cap), BF16), shape((n, n + EXTRA, cap), F32)),
            [SMEM] + [VMEM] * (n + 2),
        )(pos, level_loc, total, rests[0], *arrived)
        increment, grad_static = call(outputs_kernel, (flat, flat), [SMEM] + [VMEM] * 7)(
            pos, slots, tables, static_control, diag, off, obs_weight, innovation
        )
    else:
        payload = call(
            band_kernel,
            shape((groups, n, levels + EXTRA, cap), F32),
            [SMEM] * 2 + [VMEM] * 7,
            [pltpu.VMEM((2 * levels, band_cols), BF16)],
        )(lev, counts, perturb, other_control, part, level_loc, static_control, send_src, send_wt)
        arrived = lax.all_to_all(
            payload.reshape(groups * n, levels + EXTRA, cap), ("grp", "tile"), split_axis=0, concat_axis=0, tiled=True
        ).reshape(groups, n, levels + EXTRA, cap)
        increment, partial, giving = call(
            tile_kernel, (flat, flat, shape((n, levels + EXTRA, cap), F32)), [SMEM] + [VMEM] * 7
        )(pos, arrived, recv_tgt, static_control, diag, off, obs_weight, innovation)
        returned = lax.all_to_all(giving, "tile", split_axis=0, concat_axis=0, tiled=True)
        grad_static, mine = call(adjoint_kernel, (flat, mine_shape), [SMEM, SMEM] + [VMEM] * 5)(
            pos, counts, returned, send_src, send_wt, partial, level_loc
        )
    theirs = lax.ppermute(mine, "lev", swap)
    grad_ens = call(ens_kernel, shape(control.shape, F32), [SMEM] + [VMEM] * 5)(
        lev, perturb, other_perturb, control, mine, theirs
    )
    return (increment, grad_static, grad_ens)


def solution(mesh):
    return jax.shard_map(
        body,
        mesh=mesh,
        in_specs=(
            P("lev", "grp", "tile"),
            P("lev", "grp", "tile"),
            P("lev", None),
            P("lev", "tile"),
            P("tile"),
            P("tile"),
            P("tile", None, None),
            P("tile", None, None),
            P("tile", None),
            P("tile", None, None),
            P("lev", "tile"),
            P("lev", "tile"),
        ),
        out_specs=(P("lev", "tile"), P("lev", "tile"), P("lev", "grp", "tile")),
        check_vma=False,
    )
```

```python
import functools

import jax
import jax.numpy as jnp
from jax import lax
from jax.experimental import pallas as pl
from jax.experimental.pallas import tpu as pltpu
from jax.sharding import PartitionSpec as P

F32 = jnp.float32
BF16 = jnp.bfloat16
SUB = 8
EXTRA = 8
VMEM = pl.BlockSpec(memory_space=pltpu.VMEM)
HBM = pl.BlockSpec(memory_space=pltpu.HBM)
SMEM = pl.BlockSpec(memory_space=pltpu.SMEM)
MIB = 1024 * 1024


def halves(values):
    high = values.astype(BF16)
    low = (values - high.astype(F32)).astype(BF16)
    return high, low


def product(a, b, dims=((1,), (0,))):
    return lax.dot_general(a, b, (dims, ((), ())), preferred_element_type=F32)


def select(values, chosen, dims=((1,), (0,))):
    rows = values.shape[0]
    both = product(jnp.concatenate(halves(values), axis=0), chosen, dims)
    return both[:rows] + both[rows:]


def spread(matrix, start, count):
    rows, cols = matrix.shape

    def iota(shape, axis):
        return lax.broadcasted_iota(jnp.int32, shape, axis)

    shape = (rows * SUB, count * SUB)
    tall = (iota((rows * SUB, rows), 0) // SUB == iota((rows * SUB, rows), 1)).astype(BF16)
    wide = (iota((cols, count * SUB), 1) // SUB + start == iota((cols, count * SUB), 0)).astype(BF16)
    same = iota(shape, 0) % SUB == iota(shape, 1) % SUB
    out = []
    for part in halves(matrix):
        filled = product(tall, product(part, wide).astype(BF16))
        out.append(jnp.where(same, filled, 0.0).astype(BF16))
    return out


def mix(weights, values):
    high, low = halves(values)
    return product(weights[0], high) + (product(weights[0], low) + product(weights[1], high))


def one_hot(index, size):
    rows = lax.broadcasted_iota(jnp.int32, (size, index.shape[1]), 0)
    return jnp.where(rows == index, 1.0, 0.0).astype(BF16)


def column_as_row(column, lane, offset):
    n = column.shape[0]
    place = lax.broadcasted_iota(jnp.int32, (n, 128), 1) == lax.broadcasted_iota(jnp.int32, (n, 128), 0) + offset
    return jnp.sum(jnp.where(place, column, 0.0), axis=0, keepdims=True)


def row_as_column(row, n, offset):
    place = lax.broadcasted_iota(jnp.int32, (n, 128), 1) == lax.broadcasted_iota(jnp.int32, (n, 128), 0) + offset
    return jnp.sum(jnp.where(place, row, 0.0), axis=1, keepdims=True)


def edge_rows(values):
    n = values.shape[0]
    row = column_as_row(values[:, -1:], None, 0) + column_as_row(values[:, :1], None, n)
    return jnp.broadcast_to(row, (EXTRA, 128))


def factor_of(counts_ref, weight_ref, d):
    slot = lax.broadcasted_iota(jnp.int32, (1, weight_ref.shape[2]), 1)
    return jnp.where(slot < counts_ref[0, d], weight_ref[0, pl.ds(d, 1), :], 0.0)


def loop(n, step, init):
    return lax.fori_loop(0, n, step, init, unroll=n if n <= 8 else 1)


def own_kernel(lev_ref, perturb_hbm, control_hbm, loc_hbm, part_ref, perturb_ref, control_ref, loc_ref, sems):
    staged = [(loc_hbm, loc_ref), (control_hbm, control_ref), (perturb_hbm, perturb_ref)]
    copies = [pltpu.make_async_copy(source, target, sems.at[i]) for i, (source, target) in enumerate(staged)]
    for copy in copies:
        copy.start()
    levels = perturb_ref.shape[0]
    copies[0].wait()
    weights = spread(loc_ref[...], lev_ref[0] * levels, levels)
    copies[1].wait()
    copies[2].wait()
    part_ref[...] = mixed_sum(weights, perturb_ref, control_ref)


def mixed_sum(weights, perturb_ref, control_ref):
    levels, members, cols = perturb_ref.shape
    perturb = perturb_ref[...].astype(F32)
    total = jnp.zeros((levels, SUB, cols), F32)
    for m in range(0, members, SUB):
        tile = control_ref[:, m : m + SUB, :].reshape(levels * SUB, cols)
        total = total + perturb[:, m : m + SUB, :] * mix(weights, tile).reshape(levels, SUB, cols)
    return jnp.sum(total, axis=1)


def band_kernel(lev_ref, counts_ref, perturb_ref, other_ref, part_ref, loc_ref, static_ref, src_ref, weight_ref,
                out_ref, acc_ref):
    levels, members, cols = perturb_ref.shape
    weights = spread(loc_ref[...], (1 - lev_ref[0]) * levels, levels)
    band_sum = part_ref[...] + mixed_sum(weights, perturb_ref, other_ref)
    acc_ref[...] = jnp.concatenate(halves(band_sum), axis=0)
    n = src_ref.shape[1]
    edges = edge_rows(static_ref[...])

    def step(d, carry):
        chosen = one_hot(src_ref[0, pl.ds(d, 1), :], cols)
        both = product(acc_ref[...], chosen)
        payload = (both[:levels] + both[levels:]) * factor_of(counts_ref, weight_ref, d)
        for g in range(out_ref.shape[0]):
            out_ref[g, d, :levels, :] = payload
            out_ref[g, d, levels:, :] = edges
        return carry

    loop(n, step, 0)


def tile_kernel(pos_ref, arrived_ref, tgt_ref, static_ref, diag_ref, off_ref, obs_ref, innov_ref,
                increment_ref, partial_ref, out_ref):
    levels, cols = static_ref.shape
    groups, n = arrived_ref.shape[:2]
    me = pos_ref[0]

    def step(s, total):
        values = sum(arrived_ref[g, s, :levels, :] for g in range(groups))
        chosen = one_hot(tgt_ref[0, pl.ds(s, 1), :], cols)
        return total + select(values, chosen, ((1,), (1,)))

    remapped = loop(n, step, jnp.zeros((levels, cols), F32))
    before = arrived_ref[0, jnp.maximum(me - 1, 0), levels : levels + 1, :]
    after = arrived_ref[0, jnp.minimum(me + 1, n - 1), levels : levels + 1, :]
    before = jnp.where(me > 0, row_as_column(before, levels, 0), 0.0)
    after = jnp.where(me < n - 1, row_as_column(after, levels, levels), 0.0)
    static = static_ref[...]
    lane = lax.broadcasted_iota(jnp.int32, (levels, cols), 1)
    left = jnp.where(lane == 0, before, pltpu.roll(static, 1, 1))
    right = jnp.where(lane == cols - 1, after, pltpu.roll(static, cols - 1, 1))
    increment = remapped + diag_ref[...] * static + off_ref[...] * (left + right)
    increment_ref[...] = increment
    misfit = obs_ref[...] * (increment - innov_ref[...])
    coupled = off_ref[...] * misfit
    left = jnp.where(lane == 0, 0.0, pltpu.roll(coupled, 1, 1))
    right = jnp.where(lane == cols - 1, 0.0, pltpu.roll(coupled, cols - 1, 1))
    partial_ref[...] = static + diag_ref[...] * misfit + left + right
    edges = edge_rows(coupled)
    both = jnp.concatenate(halves(misfit), axis=0)

    def give(s, carry):
        chosen = one_hot(tgt_ref[0, pl.ds(s, 1), :], cols)
        picked = product(both, chosen)
        out_ref[s, :levels, :] = picked[:levels] + picked[levels:]
        out_ref[s, levels:, :] = edges
        return carry

    loop(n, give, 0)


def adjoint_kernel(pos_ref, counts_ref, returned_ref, src_ref, weight_ref, partial_ref, loc_ref, grad_ref, out_ref):
    levels, cols = partial_ref.shape
    n = returned_ref.shape[0]
    band = out_ref.shape[1] - 128
    me = pos_ref[0]

    def step(d, total):
        values = returned_ref[d, :levels, :] * factor_of(counts_ref, weight_ref, d)
        return total + select(values, one_hot(src_ref[0, pl.ds(d, 1), :], band), ((1,), (1,)))

    out_ref[:, :band] = loop(n, step, jnp.zeros((levels, band), F32))
    out_ref[:, band:] = jnp.concatenate([loc_ref[...], jnp.zeros((levels, 128 - loc_ref.shape[1]), F32)], axis=1)
    before = returned_ref[jnp.maximum(me - 1, 0), levels : levels + 1, :]
    after = returned_ref[jnp.minimum(me + 1, n - 1), levels : levels + 1, :]
    before = jnp.where(me > 0, row_as_column(before, levels, 0), 0.0)
    after = jnp.where(me < n - 1, row_as_column(after, levels, levels), 0.0)
    lane = lax.broadcasted_iota(jnp.int32, (levels, cols), 1)
    grad_ref[...] = partial_ref[...] + (jnp.where(lane == 0, before, 0.0) + jnp.where(lane == cols - 1, after, 0.0))


def ens_kernel(lev_ref, perturb_ref, other_ref, control_ref, mine_ref, theirs_ref, out_ref):
    levels, members, cols = perturb_ref.shape
    mine, theirs = mine_ref[...], theirs_ref[...]
    loc = jnp.concatenate([mine[:, cols : cols + 2 * levels], theirs[:, cols : cols + 2 * levels]], axis=0)
    full = loc.shape[0]
    l_row = lax.broadcasted_iota(jnp.int32, (levels * SUB, full), 0) // SUB + lev_ref[0] * levels
    pick_l = (l_row == lax.broadcasted_iota(jnp.int32, (levels * SUB, full), 1)).astype(BF16)
    k_col = lax.broadcasted_iota(jnp.int32, (full, full * SUB), 1) // SUB
    pick_k = (k_col == lax.broadcasted_iota(jnp.int32, (full, full * SUB), 0)).astype(BF16)
    same = (
        lax.broadcasted_iota(jnp.int32, (levels * SUB, full * SUB), 0) % SUB
        == lax.broadcasted_iota(jnp.int32, (levels * SUB, full * SUB), 1) % SUB
    )
    weights = []
    for part in halves(loc):
        tall = product(pick_l, part, ((1,), (1,)))
        wide = product(tall.astype(BF16), pick_k)
        weights.append(jnp.where(same, wide, 0.0).astype(BF16))
    perturb = perturb_ref[...].astype(F32)
    other = other_ref[...].astype(F32)
    grad = jnp.concatenate([mine[:, :cols], theirs[:, :cols]], axis=0)[:, None, :]
    for m in range(0, members, SUB):
        tile = jnp.concatenate([perturb[:, m : m + SUB, :], other[:, m : m + SUB, :]], axis=0) * grad
        mixed = mix(weights, tile.reshape(full * SUB, cols)).reshape(levels, SUB, cols)
        out_ref[:, m : m + SUB, :] = control_ref[:, m : m + SUB, :] + mixed


class Rows:
    def __init__(self, levels, n):
        self.weight = slice(0, levels)
        self.base = slice(levels, 2 * levels)
        at = 2 * levels
        self.factor, self.index, self.edge = at, at + n, at + 2 * n
        self.total = at + 2 * n + EXTRA


def static_kernel(band, pos_ref, counts_ref, static_ref, diag_ref, off_ref, obs_ref, innov_ref, src_ref, weight_ref, tgt_ref,
                  *out_refs):
    levels, cols = static_ref.shape
    n = len(out_refs)
    cap = src_ref.shape[2]
    rows = Rows(levels, n)
    me = pos_ref[0]
    static, off, obs = static_ref[...], off_ref[...], obs_ref[...]
    lane = lax.broadcasted_iota(jnp.int32, (levels, cols), 1)
    left = jnp.where(lane == 0, 0.0, pltpu.roll(static, 1, 1))
    right = jnp.where(lane == cols - 1, 0.0, pltpu.roll(static, cols - 1, 1))
    base = diag_ref[...] * static + off * (left + right) - innov_ref[...]
    coupled = off * obs
    ends = [v[:, i] for v in (static, coupled, base) for i in (slice(cols - 1, cols), slice(0, 1))]
    edge = sum(column_as_row(end, None, i * levels) for i, end in enumerate(ends))
    place = lax.broadcasted_iota(jnp.int32, (1, cap), 1)
    edge = edge + jnp.where(place == 6 * levels, off[:, cols - 1 :], 0.0)
    edge = edge + jnp.where(place == 6 * levels + 1, off[:, :1], 0.0)
    edge = jnp.broadcast_to(edge, (EXTRA, cap))
    both = jnp.concatenate(halves(jnp.concatenate([obs, base], axis=0)), axis=0)
    tgts = [tgt_ref[0, pl.ds(me ^ r, 1), :] for r in range(n)]
    src = jnp.concatenate([src_ref[0, pl.ds(me ^ r, 1), :] for r in range(n)], axis=0).astype(F32)
    index = jnp.concatenate(tgts, axis=0).astype(F32) * float(band) + src
    factor = jnp.concatenate([factor_of(counts_ref, weight_ref, me ^ r) for r in range(n)], axis=0)
    for r, out_ref in enumerate(out_refs):
        picked = product(both, one_hot(tgts[r], cols))
        out_ref[: 2 * levels, :] = picked[: 2 * levels] + picked[2 * levels :]
        out_ref[rows.factor : rows.factor + n, :] = factor
        out_ref[rows.index : rows.index + n, :] = index
        out_ref[rows.edge :, :] = edge


def sum_kernel(lev_ref, perturb_ref, other_ref, part_ref, loc_ref, out_ref):
    levels = perturb_ref.shape[0]
    weights = spread(loc_ref[...], (1 - lev_ref[0]) * levels, levels)
    out_ref[...] = part_ref[...] + mixed_sum(weights, perturb_ref, other_ref)


def blocks_kernel(groups, *refs):
    sums = refs[:groups]
    count = (len(refs) - groups - 1) // 2
    rests = refs[groups : groups + count]
    total_ref = refs[groups + count]
    out_refs = refs[groups + count + 1 :]
    total = sum(ref[...] for ref in sums)
    cap = total_ref.shape[1]
    total = jnp.concatenate([total[:, at : at + cap] for at in range(0, total.shape[1], cap)], axis=0)
    total_ref[...] = total
    for rest_ref, out_ref in zip(rests, out_refs):
        out_ref[: total.shape[0], :] = total
        out_ref[total.shape[0] :, :] = rest_ref[...]


class Block:
    def __init__(self, refs, n, levels, band):
        cap = refs[0].shape[1]
        self.levels, self.parts, self.cap = levels, band // cap, cap
        self.sums_ref, self.rest_ref = refs[0], refs[-1]
        self.head = 0 if len(refs) == 2 else self.parts * levels
        self.rows = Rows(levels, n)
        words = self.rest(self.rows.index, n)
        self.tgt = jnp.floor((words + 0.5) * (1.0 / band))
        self.src = words - self.tgt * float(band)
        self.factor = self.rest(self.rows.factor, n)

    def rest(self, at, size):
        return self.rest_ref[self.head + at : self.head + at + size, :]

    def sums(self):
        parts = [self.sums_ref[i * self.levels : (i + 1) * self.levels, :] for i in range(self.parts)]
        return jnp.concatenate(halves(jnp.concatenate(parts, axis=1)), axis=0)


def line(table, i):
    return table[i : i + 1]


def pick_source(block, r):
    band = block.parts * block.cap
    column = lax.broadcasted_iota(jnp.int32, (band, block.cap), 0).astype(F32)
    return jnp.where(column == line(block.src, r), 1.0, 0.0).astype(BF16)


def fill_slots(bands, blocks, n, slots_ref):
    for i, s in enumerate(bands):
        block = blocks[s]
        both = block.sums()
        for d in range(n):
            picked = product(both, pick_source(block, s ^ d))
            values = (picked[: block.levels] + picked[block.levels :]) * line(block.factor, s ^ d)
            slots_ref[d, :, i * block.cap : (i + 1) * block.cap] = jnp.concatenate(halves(values), axis=0)


def met_at(d, block, bands, slots_ref):
    own = jnp.broadcast_to(line(block.tgt, d), (block.cap, block.cap)).T
    same = [jnp.where(own == line(block.tgt, s ^ d), 1.0, 0.0).astype(BF16) for s in bands]
    met = product(slots_ref[d], jnp.concatenate(same, axis=1), ((1,), (1,)))
    return met[: block.levels] + met[block.levels :]


def open_blocks(order, counts, refs, n, levels, band):
    blocks = {}
    for r, count in zip(order, counts):
        blocks[r] = Block(refs[:count], n, levels, band)
        refs = refs[count:]
    return blocks, refs


def early_kernel(n, levels, band, first, counts, *refs):
    blocks, (slots_ref, met_ref) = open_blocks(first, counts, refs, n, levels, band)
    fill_slots(first, blocks, n, slots_ref)
    for i, d in enumerate(first):
        met_ref[i] = met_at(d, blocks[d], first, slots_ref)


def shared_kernel(n, cols, first, second, counts, pos_ref, loc_ref, slots_ref, met_ref, *refs):
    levels = loc_ref.shape[0]
    band = refs[-3].shape[1] - 128
    blocks, (out_ref, late_ref, tables_ref) = open_blocks(first + second, counts, refs, n, levels, band)
    me = pos_ref[0]
    for r, block in blocks.items():
        tables_ref[me ^ r, :n, :] = block.tgt
        tables_ref[me ^ r, n:, :] = block.rest(block.rows.edge, EXTRA)
    fill_slots(second, blocks, n, late_ref)
    last = cols - 1.0
    total = jnp.zeros((levels, band), F32)
    for d, block in blocks.items():
        value = met_at(d, block, second, late_ref) + block.rest(levels, levels)
        value = value + (met_ref[first.index(d)] if d in first else met_at(d, block, first, slots_ref))
        edge = block.rest(block.rows.edge, 1)
        own = line(block.tgt, d)
        there = me ^ d
        before = tables_ref[jnp.maximum(there - 1, 0), n : n + 1, :]
        near = jnp.where((own == 0.0) & (there > 0), edge[:, 6 * levels + 1 : 6 * levels + 2], 0.0)
        value = value + row_as_column(before, levels, 0) * near
        after = tables_ref[jnp.minimum(there + 1, n - 1), n : n + 1, :]
        near = jnp.where((own == last) & (there < n - 1), edge[:, 6 * levels : 6 * levels + 1], 0.0)
        value = value + row_as_column(after, levels, levels) * near
        given = block.rest(0, levels) * value * line(blocks[0].factor, d)
        total = total + select(given, pick_source(blocks[0], d), ((1,), (1,)))
    out_ref[:, :band] = total
    out_ref[:, band:] = jnp.concatenate([loc_ref[...], jnp.zeros((levels, 128 - loc_ref.shape[1]), F32)], axis=1)


def outputs_kernel(first, second, pos_ref, early_ref, late_ref, tables_ref, static_ref, diag_ref, off_ref, obs_ref, innov_ref,
                   increment_ref, grad_ref):
    levels, cols = static_ref.shape
    n = tables_ref.shape[0]
    cap = tables_ref.shape[2]
    me = pos_ref[0]
    row = lax.broadcasted_iota(jnp.int32, (cols, cap), 0).astype(F32)
    remapped = jnp.zeros((2 * levels, cols), F32)
    given = [(s, ref, slice(i * cap, (i + 1) * cap)) for bands, ref in ((first, early_ref), (second, late_ref))
             for i, s in enumerate(bands)]
    for s, ref, place in given:
        landing = jnp.where(row == tables_ref[me, s : s + 1, :], 1.0, 0.0).astype(BF16)
        remapped = remapped + product(ref[0, :, place], landing, ((1,), (1,)))
    remapped = remapped[:levels] + remapped[levels:]
    static, off = static_ref[...], off_ref[...]
    lane = lax.broadcasted_iota(jnp.int32, (levels, cols), 1)

    def beside(there, exists, column, own_end, side):
        edge = tables_ref[there, n : n + 1, :]
        static_end, coupling, base = (row_as_column(edge, levels, (2 * i + side) * levels) for i in range(3))
        far = me ^ there
        landed = []
        for s, ref, place in given:
            values = ref[far, :levels, place].astype(F32) + ref[far, levels:, place].astype(F32)
            landed.append(jnp.where(tables_ref[there, pl.ds(s ^ far, 1), :] == column, values, 0.0))
        remap_end = jnp.sum(sum(landed), axis=1, keepdims=True)
        off_end = edge[:, 6 * levels + side : 6 * levels + side + 1]
        coupled = coupling * (remap_end + base + off_end * own_end)
        return jnp.where(exists, static_end, 0.0), jnp.where(exists, coupled, 0.0)

    before, coupled_before = beside(jnp.maximum(me - 1, 0), me > 0, cols - 1.0, static[:, :1], 0)
    after, coupled_after = beside(jnp.minimum(me + 1, n - 1), me < n - 1, 0.0, static[:, cols - 1 :], 1)
    left = jnp.where(lane == 0, before, pltpu.roll(static, 1, 1))
    right = jnp.where(lane == cols - 1, after, pltpu.roll(static, cols - 1, 1))
    increment = remapped + diag_ref[...] * static + off * (left + right)
    increment_ref[...] = increment
    misfit = obs_ref[...] * (increment - innov_ref[...])
    coupled = off * misfit
    left = jnp.where(lane == 0, coupled_before, pltpu.roll(coupled, 1, 1))
    right = jnp.where(lane == cols - 1, coupled_after, pltpu.roll(coupled, cols - 1, 1))
    grad_ref[...] = static + diag_ref[...] * misfit + left + right


def call(kernel, out_shape, spaces, scratch=(), limit=40 * MIB):
    return pl.pallas_call(
        kernel,
        out_shape=out_shape,
        in_specs=spaces,
        out_specs=jax.tree.map(lambda _: VMEM, out_shape),
        scratch_shapes=scratch,
        compiler_params=pltpu.CompilerParams(vmem_limit_bytes=limit),
    )


def body(
    perturb,
    control,
    level_loc,
    static_control,
    filter_diag,
    filter_off,
    send_src,
    send_wt,
    counts,
    recv_tgt,
    obs_weight,
    innovation,
):
    levels, members, band_cols = control.shape
    tile_cols = static_control.shape[1]
    n = lax.axis_size("tile")
    groups = lax.axis_size("grp")
    cap = send_src.shape[2]
    shape = jax.ShapeDtypeStruct
    swap = [(0, 1), (1, 0)]
    lev = lax.axis_index("lev").astype(jnp.int32).reshape(1)
    pos = lax.axis_index("tile").astype(jnp.int32).reshape(1)
    other_control = lax.ppermute(control, "lev", swap)
    other_perturb = lax.ppermute(perturb, "lev", swap)
    part = call(
        own_kernel,
        shape((levels, band_cols), F32),
        [SMEM] + [HBM] * 3,
        [pltpu.VMEM(a.shape, a.dtype) for a in (perturb, control, level_loc)] + [pltpu.SemaphoreType.DMA((3,))],
        limit=58 * MIB,
    )(lev, perturb, control, level_loc)
    flat = shape((levels, tile_cols), F32)
    mine_shape = shape((levels, band_cols + 128), F32)
    diag, off = filter_diag.reshape(1, -1), filter_off.reshape(1, -1)
    if n * cap <= tile_cols and n & (n - 1) == 0 and band_cols * tile_cols <= 2**20:
        rows = Rows(levels, n)
        stacked = band_cols // cap * levels
        rests = call(functools.partial(static_kernel, band_cols), [shape((rows.total, cap), F32)] * n, [SMEM] * 2 + [VMEM] * 8)(
            pos, counts, static_control, diag, off, obs_weight, innovation, send_src, send_wt, recv_tgt
        )
        sums = [
            call(sum_kernel, shape((levels, band_cols), F32), [SMEM] + [VMEM] * 4)(
                lev, perturb, other_control, part, level_loc
            )
        ]
        sums[0], other_perturb = lax.optimization_barrier((sums[0], other_perturb))
        for k in range(1, groups):
            sums.append(lax.ppermute(sums[0], "grp", [(g, (g + k) % groups) for g in range(groups)]))
        far, near = list(range(n // 2, n)), list(range(1, n // 2))
        ahead = far[len(far) // 2 :]
        whole = [r for r in far + near if r not in ahead]

        def to(r, block):
            return lax.ppermute(block, "tile", [(i, i ^ r) for i in range(n)])

        static_parts = {r: to(r, rests[r]) for r in ahead}
        total, *blocks = call(
            functools.partial(blocks_kernel, groups),
            [shape((stacked, cap), F32)] + [shape((stacked + rows.total, cap), F32)] * len(whole),
            [VMEM] * (groups + len(whole)),
        )(*sums, *[rests[r] for r in whole])
        blocks = dict(zip(whole, blocks))
        arrived = {r: (to(r, total), static_parts[r]) if r in ahead else (to(r, blocks[r]),) for r in far + near}
        arrived[0] = (total, rests[0])
        first, second = [0] + far, near

        def taken(order):
            return tuple(len(arrived[r]) for r in order), [ref for r in order for ref in arrived[r]]

        counts_first, refs_first = taken(first)
        slots, met = call(
            functools.partial(early_kernel, n, levels, band_cols, first, counts_first),
            (shape((n, 2 * levels, len(first) * cap), BF16), shape((len(first), levels, cap), F32)),
            [VMEM] * len(refs_first),
        )(*refs_first)
        counts_all, refs_all = taken(first + second)
        mine, late, tables = call(
            functools.partial(shared_kernel, n, tile_cols, first, second, counts_all),
            (mine_shape, shape((n, 2 * levels, len(second) * cap), BF16), shape((n, n + EXTRA, cap), F32)),
            [SMEM] + [VMEM] * (3 + len(refs_all)),
        )(pos, level_loc, slots, met, *refs_all)
        increment, grad_static = call(functools.partial(outputs_kernel, first, second), (flat, flat), [SMEM] + [VMEM] * 8)(
            pos, slots, late, tables, static_control, diag, off, obs_weight, innovation
        )
    else:
        payload = call(
            band_kernel,
            shape((groups, n, levels + EXTRA, cap), F32),
            [SMEM] * 2 + [VMEM] * 7,
            [pltpu.VMEM((2 * levels, band_cols), BF16)],
        )(lev, counts, perturb, other_control, part, level_loc, static_control, send_src, send_wt)
        arrived = lax.all_to_all(
            payload.reshape(groups * n, levels + EXTRA, cap), ("grp", "tile"), split_axis=0, concat_axis=0, tiled=True
        ).reshape(groups, n, levels + EXTRA, cap)
        increment, partial, giving = call(
            tile_kernel, (flat, flat, shape((n, levels + EXTRA, cap), F32)), [SMEM] + [VMEM] * 7
        )(pos, arrived, recv_tgt, static_control, diag, off, obs_weight, innovation)
        returned = lax.all_to_all(giving, "tile", split_axis=0, concat_axis=0, tiled=True)
        grad_static, mine = call(adjoint_kernel, (flat, mine_shape), [SMEM, SMEM] + [VMEM] * 5)(
            pos, counts, returned, send_src, send_wt, partial, level_loc
        )
    theirs = lax.ppermute(mine, "lev", swap)
    grad_ens = call(ens_kernel, shape(control.shape, F32), [SMEM] + [VMEM] * 5)(
        lev, perturb, other_perturb, control, mine, theirs
    )
    return (increment, grad_static, grad_ens)


def solution(mesh):
    return jax.shard_map(
        body,
        mesh=mesh,
        in_specs=(
            P("lev", "grp", "tile"),
            P("lev", "grp", "tile"),
            P("lev", None),
            P("lev", "tile"),
            P("tile"),
            P("tile"),
            P("tile", None, None),
            P("tile", None, None),
            P("tile", None),
            P("tile", None, None),
            P("lev", "tile"),
            P("lev", "tile"),
        ),
        out_specs=(P("lev", "tile"), P("lev", "tile"), P("lev", "grp", "tile")),
        check_vma=False,
    )
```

```python
import functools

import jax
import jax.numpy as jnp
from jax import lax
from jax.experimental import pallas as pl
from jax.experimental.pallas import tpu as pltpu
from jax.sharding import PartitionSpec as P

F32 = jnp.float32
BF16 = jnp.bfloat16
SUB = 8
EXTRA = 8
VMEM = pl.BlockSpec(memory_space=pltpu.VMEM)
HBM = pl.BlockSpec(memory_space=pltpu.HBM)
SMEM = pl.BlockSpec(memory_space=pltpu.SMEM)
MIB = 1024 * 1024


def halves(values):
    high = values.astype(BF16)
    low = (values - high.astype(F32)).astype(BF16)
    return high, low


def product(a, b, dims=((1,), (0,))):
    return lax.dot_general(a, b, (dims, ((), ())), preferred_element_type=F32)


def select(values, chosen, dims=((1,), (0,))):
    rows = values.shape[0]
    both = product(jnp.concatenate(halves(values), axis=0), chosen, dims)
    return both[:rows] + both[rows:]


def spread(matrix, start, count):
    rows, cols = matrix.shape

    def iota(shape, axis):
        return lax.broadcasted_iota(jnp.int32, shape, axis)

    shape = (rows * SUB, count * SUB)
    tall = (iota((rows * SUB, rows), 0) // SUB == iota((rows * SUB, rows), 1)).astype(BF16)
    wide = (iota((cols, count * SUB), 1) // SUB + start == iota((cols, count * SUB), 0)).astype(BF16)
    same = iota(shape, 0) % SUB == iota(shape, 1) % SUB
    out = []
    for part in halves(matrix):
        filled = product(tall, product(part, wide).astype(BF16))
        out.append(jnp.where(same, filled, 0.0).astype(BF16))
    return out


def mix(weights, values):
    high, low = halves(values)
    return product(weights[0], high) + (product(weights[0], low) + product(weights[1], high))


def one_hot(index, size):
    rows = lax.broadcasted_iota(jnp.int32, (size, index.shape[1]), 0)
    return jnp.where(rows == index, 1.0, 0.0).astype(BF16)


def column_as_row(column, lane, offset):
    n = column.shape[0]
    place = lax.broadcasted_iota(jnp.int32, (n, 128), 1) == lax.broadcasted_iota(jnp.int32, (n, 128), 0) + offset
    return jnp.sum(jnp.where(place, column, 0.0), axis=0, keepdims=True)


def row_as_column(row, n, offset):
    place = lax.broadcasted_iota(jnp.int32, (n, 128), 1) == lax.broadcasted_iota(jnp.int32, (n, 128), 0) + offset
    return jnp.sum(jnp.where(place, row, 0.0), axis=1, keepdims=True)


def edge_rows(values):
    n = values.shape[0]
    row = column_as_row(values[:, -1:], None, 0) + column_as_row(values[:, :1], None, n)
    return jnp.broadcast_to(row, (EXTRA, 128))


def factor_of(counts_ref, weight_ref, d):
    slot = lax.broadcasted_iota(jnp.int32, (1, weight_ref.shape[2]), 1)
    return jnp.where(slot < counts_ref[0, d], weight_ref[0, pl.ds(d, 1), :], 0.0)


def loop(n, step, init):
    return lax.fori_loop(0, n, step, init, unroll=n if n <= 8 else 1)


def own_kernel(lev_ref, perturb_hbm, control_hbm, loc_hbm, part_ref, perturb_ref, control_ref, loc_ref, sems):
    staged = [(loc_hbm, loc_ref), (control_hbm, control_ref), (perturb_hbm, perturb_ref)]
    copies = [pltpu.make_async_copy(source, target, sems.at[i]) for i, (source, target) in enumerate(staged)]
    for copy in copies:
        copy.start()
    levels = perturb_ref.shape[0]
    copies[0].wait()
    weights = spread(loc_ref[...], lev_ref[0] * levels, levels)
    copies[1].wait()
    copies[2].wait()
    part_ref[...] = mixed_sum(weights, perturb_ref, control_ref)


def mixed_sum(weights, perturb_ref, control_ref):
    levels, members, cols = perturb_ref.shape
    perturb = perturb_ref[...].astype(F32)
    total = jnp.zeros((levels, SUB, cols), F32)
    for m in range(0, members, SUB):
        tile = control_ref[:, m : m + SUB, :].reshape(levels * SUB, cols)
        total = total + perturb[:, m : m + SUB, :] * mix(weights, tile).reshape(levels, SUB, cols)
    return jnp.sum(total, axis=1)


def band_kernel(lev_ref, counts_ref, perturb_ref, other_ref, part_ref, loc_ref, static_ref, src_ref, weight_ref,
                out_ref, acc_ref):
    levels, members, cols = perturb_ref.shape
    weights = spread(loc_ref[...], (1 - lev_ref[0]) * levels, levels)
    band_sum = part_ref[...] + mixed_sum(weights, perturb_ref, other_ref)
    acc_ref[...] = jnp.concatenate(halves(band_sum), axis=0)
    n = src_ref.shape[1]
    edges = edge_rows(static_ref[...])

    def step(d, carry):
        chosen = one_hot(src_ref[0, pl.ds(d, 1), :], cols)
        both = product(acc_ref[...], chosen)
        payload = (both[:levels] + both[levels:]) * factor_of(counts_ref, weight_ref, d)
        for g in range(out_ref.shape[0]):
            out_ref[g, d, :levels, :] = payload
            out_ref[g, d, levels:, :] = edges
        return carry

    loop(n, step, 0)


def tile_kernel(pos_ref, arrived_ref, tgt_ref, static_ref, diag_ref, off_ref, obs_ref, innov_ref,
                increment_ref, partial_ref, out_ref):
    levels, cols = static_ref.shape
    groups, n = arrived_ref.shape[:2]
    me = pos_ref[0]

    def step(s, total):
        values = sum(arrived_ref[g, s, :levels, :] for g in range(groups))
        chosen = one_hot(tgt_ref[0, pl.ds(s, 1), :], cols)
        return total + select(values, chosen, ((1,), (1,)))

    remapped = loop(n, step, jnp.zeros((levels, cols), F32))
    before = arrived_ref[0, jnp.maximum(me - 1, 0), levels : levels + 1, :]
    after = arrived_ref[0, jnp.minimum(me + 1, n - 1), levels : levels + 1, :]
    before = jnp.where(me > 0, row_as_column(before, levels, 0), 0.0)
    after = jnp.where(me < n - 1, row_as_column(after, levels, levels), 0.0)
    static = static_ref[...]
    lane = lax.broadcasted_iota(jnp.int32, (levels, cols), 1)
    left = jnp.where(lane == 0, before, pltpu.roll(static, 1, 1))
    right = jnp.where(lane == cols - 1, after, pltpu.roll(static, cols - 1, 1))
    increment = remapped + diag_ref[...] * static + off_ref[...] * (left + right)
    increment_ref[...] = increment
    misfit = obs_ref[...] * (increment - innov_ref[...])
    coupled = off_ref[...] * misfit
    left = jnp.where(lane == 0, 0.0, pltpu.roll(coupled, 1, 1))
    right = jnp.where(lane == cols - 1, 0.0, pltpu.roll(coupled, cols - 1, 1))
    partial_ref[...] = static + diag_ref[...] * misfit + left + right
    edges = edge_rows(coupled)
    both = jnp.concatenate(halves(misfit), axis=0)

    def give(s, carry):
        chosen = one_hot(tgt_ref[0, pl.ds(s, 1), :], cols)
        picked = product(both, chosen)
        out_ref[s, :levels, :] = picked[:levels] + picked[levels:]
        out_ref[s, levels:, :] = edges
        return carry

    loop(n, give, 0)


def adjoint_kernel(pos_ref, counts_ref, returned_ref, src_ref, weight_ref, partial_ref, loc_ref, grad_ref, out_ref):
    levels, cols = partial_ref.shape
    n = returned_ref.shape[0]
    band = out_ref.shape[1] - 128
    me = pos_ref[0]

    def step(d, total):
        values = returned_ref[d, :levels, :] * factor_of(counts_ref, weight_ref, d)
        return total + select(values, one_hot(src_ref[0, pl.ds(d, 1), :], band), ((1,), (1,)))

    out_ref[:, :band] = loop(n, step, jnp.zeros((levels, band), F32))
    out_ref[:, band:] = jnp.concatenate([loc_ref[...], jnp.zeros((levels, 128 - loc_ref.shape[1]), F32)], axis=1)
    before = returned_ref[jnp.maximum(me - 1, 0), levels : levels + 1, :]
    after = returned_ref[jnp.minimum(me + 1, n - 1), levels : levels + 1, :]
    before = jnp.where(me > 0, row_as_column(before, levels, 0), 0.0)
    after = jnp.where(me < n - 1, row_as_column(after, levels, levels), 0.0)
    lane = lax.broadcasted_iota(jnp.int32, (levels, cols), 1)
    grad_ref[...] = partial_ref[...] + (jnp.where(lane == 0, before, 0.0) + jnp.where(lane == cols - 1, after, 0.0))


def ens_kernel(lev_ref, perturb_ref, other_ref, control_ref, mine_ref, theirs_ref, out_ref):
    levels, members, cols = perturb_ref.shape
    mine, theirs = mine_ref[...], theirs_ref[...]
    loc = jnp.concatenate([mine[:, cols : cols + 2 * levels], theirs[:, cols : cols + 2 * levels]], axis=0)
    full = loc.shape[0]
    l_row = lax.broadcasted_iota(jnp.int32, (levels * SUB, full), 0) // SUB + lev_ref[0] * levels
    pick_l = (l_row == lax.broadcasted_iota(jnp.int32, (levels * SUB, full), 1)).astype(BF16)
    k_col = lax.broadcasted_iota(jnp.int32, (full, full * SUB), 1) // SUB
    pick_k = (k_col == lax.broadcasted_iota(jnp.int32, (full, full * SUB), 0)).astype(BF16)
    same = (
        lax.broadcasted_iota(jnp.int32, (levels * SUB, full * SUB), 0) % SUB
        == lax.broadcasted_iota(jnp.int32, (levels * SUB, full * SUB), 1) % SUB
    )
    weights = []
    for part in halves(loc):
        tall = product(pick_l, part, ((1,), (1,)))
        wide = product(tall.astype(BF16), pick_k)
        weights.append(jnp.where(same, wide, 0.0).astype(BF16))
    perturb = perturb_ref[...].astype(F32)
    other = other_ref[...].astype(F32)
    grad = jnp.concatenate([mine[:, :cols], theirs[:, :cols]], axis=0)[:, None, :]
    for m in range(0, members, SUB):
        tile = jnp.concatenate([perturb[:, m : m + SUB, :], other[:, m : m + SUB, :]], axis=0) * grad
        mixed = mix(weights, tile.reshape(full * SUB, cols)).reshape(levels, SUB, cols)
        out_ref[:, m : m + SUB, :] = control_ref[:, m : m + SUB, :] + mixed


def relabel(r, n, lev):
    high, low = n // 2, n // 4
    if low == 0:
        return r
    both = high | low
    turned = (r & ~both) | ((r & low) << 1) | ((r & high) >> 1)
    return r + (turned - r) * lev


class Rows:
    def __init__(self, levels, n):
        self.weight = slice(0, levels)
        self.base = slice(levels, 2 * levels)
        at = 2 * levels
        self.factor, self.index, self.edge = at, at + n, at + 2 * n
        self.total = at + 2 * n + EXTRA


def static_kernel(band, pos_ref, lev_ref, counts_ref, static_ref, diag_ref, off_ref, obs_ref, innov_ref, src_ref, weight_ref, tgt_ref,
                  *out_refs):
    levels, cols = static_ref.shape
    n = len(out_refs)
    cap = src_ref.shape[2]
    rows = Rows(levels, n)
    peers = [pos_ref[0] ^ relabel(r, n, lev_ref[0]) for r in range(n)]
    static, off, obs = static_ref[...], off_ref[...], obs_ref[...]
    lane = lax.broadcasted_iota(jnp.int32, (levels, cols), 1)
    left = jnp.where(lane == 0, 0.0, pltpu.roll(static, 1, 1))
    right = jnp.where(lane == cols - 1, 0.0, pltpu.roll(static, cols - 1, 1))
    base = diag_ref[...] * static + off * (left + right) - innov_ref[...]
    coupled = off * obs
    ends = [v[:, i] for v in (static, coupled, base) for i in (slice(cols - 1, cols), slice(0, 1))]
    edge = sum(column_as_row(end, None, i * levels) for i, end in enumerate(ends))
    place = lax.broadcasted_iota(jnp.int32, (1, cap), 1)
    edge = edge + jnp.where(place == 6 * levels, off[:, cols - 1 :], 0.0)
    edge = edge + jnp.where(place == 6 * levels + 1, off[:, :1], 0.0)
    edge = jnp.broadcast_to(edge, (EXTRA, cap))
    both = jnp.concatenate(halves(jnp.concatenate([obs, base], axis=0)), axis=0)
    tgts = [tgt_ref[0, pl.ds(peer, 1), :] for peer in peers]
    src = jnp.concatenate([src_ref[0, pl.ds(peer, 1), :] for peer in peers], axis=0).astype(F32)
    index = jnp.concatenate(tgts, axis=0).astype(F32) * float(band) + src
    factor = jnp.concatenate([factor_of(counts_ref, weight_ref, peer) for peer in peers], axis=0)
    for r, out_ref in enumerate(out_refs):
        picked = product(both, one_hot(tgts[r], cols))
        out_ref[: 2 * levels, :] = picked[: 2 * levels] + picked[2 * levels :]
        out_ref[rows.factor : rows.factor + n, :] = factor
        out_ref[rows.index : rows.index + n, :] = index
        out_ref[rows.edge :, :] = edge


def sum_kernel(lev_ref, perturb_ref, other_ref, part_ref, loc_ref, out_ref):
    levels = perturb_ref.shape[0]
    weights = spread(loc_ref[...], (1 - lev_ref[0]) * levels, levels)
    out_ref[...] = part_ref[...] + mixed_sum(weights, perturb_ref, other_ref)


def blocks_kernel(groups, *refs):
    sums = refs[:groups]
    count = (len(refs) - groups - 1) // 2
    rests = refs[groups : groups + count]
    total_ref = refs[groups + count]
    out_refs = refs[groups + count + 1 :]
    total = sum(ref[...] for ref in sums)
    cap = total_ref.shape[1]
    total = jnp.concatenate([total[:, at : at + cap] for at in range(0, total.shape[1], cap)], axis=0)
    total_ref[...] = total
    for rest_ref, out_ref in zip(rests, out_refs):
        out_ref[: total.shape[0], :] = total
        out_ref[total.shape[0] :, :] = rest_ref[...]


class Block:
    def __init__(self, refs, n, levels, band):
        cap = refs[0].shape[1]
        self.levels, self.parts, self.cap = levels, band // cap, cap
        self.sums_ref, self.rest_ref = refs[0], refs[-1]
        self.head = 0 if len(refs) == 2 else self.parts * levels
        self.rows = Rows(levels, n)
        words = self.rest(self.rows.index, n)
        self.tgt = jnp.floor((words + 0.5) * (1.0 / band))
        self.src = words - self.tgt * float(band)
        self.factor = self.rest(self.rows.factor, n)

    def rest(self, at, size):
        return self.rest_ref[self.head + at : self.head + at + size, :]

    def sums(self):
        parts = [self.sums_ref[i * self.levels : (i + 1) * self.levels, :] for i in range(self.parts)]
        return jnp.concatenate(halves(jnp.concatenate(parts, axis=1)), axis=0)


def line(table, i):
    return table[i : i + 1]


def pick_source(block, r):
    band = block.parts * block.cap
    column = lax.broadcasted_iota(jnp.int32, (band, block.cap), 0).astype(F32)
    return jnp.where(column == line(block.src, r), 1.0, 0.0).astype(BF16)


def fill_slots(bands, blocks, n, slots_ref):
    for i, s in enumerate(bands):
        block = blocks[s]
        both = block.sums()
        for d in range(n):
            picked = product(both, pick_source(block, s ^ d))
            values = (picked[: block.levels] + picked[block.levels :]) * line(block.factor, s ^ d)
            slots_ref[d, :, i * block.cap : (i + 1) * block.cap] = jnp.concatenate(halves(values), axis=0)


def met_at(d, block, bands, slots_ref):
    own = jnp.broadcast_to(line(block.tgt, d), (block.cap, block.cap)).T
    same = [jnp.where(own == line(block.tgt, s ^ d), 1.0, 0.0).astype(BF16) for s in bands]
    met = product(slots_ref[d], jnp.concatenate(same, axis=1), ((1,), (1,)))
    return met[: block.levels] + met[block.levels :]


def open_blocks(order, counts, refs, n, levels, band):
    blocks = {}
    for r, count in zip(order, counts):
        blocks[r] = Block(refs[:count], n, levels, band)
        refs = refs[count:]
    return blocks, refs


def early_kernel(n, levels, band, first, counts, *refs):
    blocks, (slots_ref, met_ref) = open_blocks(first, counts, refs, n, levels, band)
    fill_slots(first, blocks, n, slots_ref)
    for i, d in enumerate(first):
        met_ref[i] = met_at(d, blocks[d], first, slots_ref)


def shared_kernel(n, cols, first, second, counts, pos_ref, lev_ref, loc_ref, slots_ref, met_ref, *refs):
    levels = loc_ref.shape[0]
    band = refs[-3].shape[1] - 128
    blocks, (out_ref, late_ref, tables_ref) = open_blocks(first + second, counts, refs, n, levels, band)
    me = pos_ref[0]
    for r, block in blocks.items():
        there = me ^ relabel(r, n, lev_ref[0])
        tables_ref[there, :n, :] = block.tgt
        tables_ref[there, n:, :] = block.rest(block.rows.edge, EXTRA)
    fill_slots(second, blocks, n, late_ref)
    last = cols - 1.0
    total = jnp.zeros((levels, band), F32)
    for d, block in blocks.items():
        value = met_at(d, block, second, late_ref) + block.rest(levels, levels)
        value = value + (met_ref[first.index(d)] if d in first else met_at(d, block, first, slots_ref))
        edge = block.rest(block.rows.edge, 1)
        own = line(block.tgt, d)
        there = me ^ relabel(d, n, lev_ref[0])
        before = tables_ref[jnp.maximum(there - 1, 0), n : n + 1, :]
        near = jnp.where((own == 0.0) & (there > 0), edge[:, 6 * levels + 1 : 6 * levels + 2], 0.0)
        value = value + row_as_column(before, levels, 0) * near
        after = tables_ref[jnp.minimum(there + 1, n - 1), n : n + 1, :]
        near = jnp.where((own == last) & (there < n - 1), edge[:, 6 * levels : 6 * levels + 1], 0.0)
        value = value + row_as_column(after, levels, levels) * near
        given = block.rest(0, levels) * value * line(blocks[0].factor, d)
        total = total + select(given, pick_source(blocks[0], d), ((1,), (1,)))
    out_ref[:, :band] = total
    out_ref[:, band:] = jnp.concatenate([loc_ref[...], jnp.zeros((levels, 128 - loc_ref.shape[1]), F32)], axis=1)


def outputs_kernel(first, second, pos_ref, lev_ref, early_ref, late_ref, tables_ref, static_ref, diag_ref, off_ref, obs_ref, innov_ref,
                   increment_ref, grad_ref):
    levels, cols = static_ref.shape
    n = tables_ref.shape[0]
    cap = tables_ref.shape[2]
    me = pos_ref[0]
    row = lax.broadcasted_iota(jnp.int32, (cols, cap), 0).astype(F32)
    remapped = jnp.zeros((2 * levels, cols), F32)
    given = [(s, ref, slice(i * cap, (i + 1) * cap)) for bands, ref in ((first, early_ref), (second, late_ref))
             for i, s in enumerate(bands)]
    for s, ref, place in given:
        landing = jnp.where(row == tables_ref[me, s : s + 1, :], 1.0, 0.0).astype(BF16)
        remapped = remapped + product(ref[0, :, place], landing, ((1,), (1,)))
    remapped = remapped[:levels] + remapped[levels:]
    static, off = static_ref[...], off_ref[...]
    lane = lax.broadcasted_iota(jnp.int32, (levels, cols), 1)

    def beside(there, exists, column, own_end, side):
        edge = tables_ref[there, n : n + 1, :]
        static_end, coupling, base = (row_as_column(edge, levels, (2 * i + side) * levels) for i in range(3))
        far = relabel(me ^ there, n, lev_ref[0])
        landed = []
        for s, ref, place in given:
            values = ref[far, :levels, place].astype(F32) + ref[far, levels:, place].astype(F32)
            landed.append(jnp.where(tables_ref[there, pl.ds(s ^ far, 1), :] == column, values, 0.0))
        remap_end = jnp.sum(sum(landed), axis=1, keepdims=True)
        off_end = edge[:, 6 * levels + side : 6 * levels + side + 1]
        coupled = coupling * (remap_end + base + off_end * own_end)
        return jnp.where(exists, static_end, 0.0), jnp.where(exists, coupled, 0.0)

    before, coupled_before = beside(jnp.maximum(me - 1, 0), me > 0, cols - 1.0, static[:, :1], 0)
    after, coupled_after = beside(jnp.minimum(me + 1, n - 1), me < n - 1, 0.0, static[:, cols - 1 :], 1)
    left = jnp.where(lane == 0, before, pltpu.roll(static, 1, 1))
    right = jnp.where(lane == cols - 1, after, pltpu.roll(static, cols - 1, 1))
    increment = remapped + diag_ref[...] * static + off * (left + right)
    increment_ref[...] = increment
    misfit = obs_ref[...] * (increment - innov_ref[...])
    coupled = off * misfit
    left = jnp.where(lane == 0, coupled_before, pltpu.roll(coupled, 1, 1))
    right = jnp.where(lane == cols - 1, coupled_after, pltpu.roll(coupled, cols - 1, 1))
    grad_ref[...] = static + diag_ref[...] * misfit + left + right


def call(kernel, out_shape, spaces, scratch=(), limit=40 * MIB):
    return pl.pallas_call(
        kernel,
        out_shape=out_shape,
        in_specs=spaces,
        out_specs=jax.tree.map(lambda _: VMEM, out_shape),
        scratch_shapes=scratch,
        compiler_params=pltpu.CompilerParams(vmem_limit_bytes=limit),
    )


def body(
    perturb,
    control,
    level_loc,
    static_control,
    filter_diag,
    filter_off,
    send_src,
    send_wt,
    counts,
    recv_tgt,
    obs_weight,
    innovation,
):
    levels, members, band_cols = control.shape
    tile_cols = static_control.shape[1]
    n = lax.axis_size("tile")
    groups = lax.axis_size("grp")
    cap = send_src.shape[2]
    shape = jax.ShapeDtypeStruct
    swap = [(0, 1), (1, 0)]
    lev = lax.axis_index("lev").astype(jnp.int32).reshape(1)
    pos = lax.axis_index("tile").astype(jnp.int32).reshape(1)
    other_control = lax.ppermute(control, "lev", swap)
    other_perturb = lax.ppermute(perturb, "lev", swap)
    part = call(
        own_kernel,
        shape((levels, band_cols), F32),
        [SMEM] + [HBM] * 3,
        [pltpu.VMEM(a.shape, a.dtype) for a in (perturb, control, level_loc)] + [pltpu.SemaphoreType.DMA((3,))],
        limit=58 * MIB,
    )(lev, perturb, control, level_loc)
    flat = shape((levels, tile_cols), F32)
    mine_shape = shape((levels, band_cols + 128), F32)
    diag, off = filter_diag.reshape(1, -1), filter_off.reshape(1, -1)
    if n * cap <= tile_cols and n >= 4 and lax.axis_size("lev") == 2 and n & (n - 1) == 0 and band_cols * tile_cols <= 2**20:
        rows = Rows(levels, n)
        stacked = band_cols // cap * levels
        rests = call(functools.partial(static_kernel, band_cols), [shape((rows.total, cap), F32)] * n, [SMEM] * 3 + [VMEM] * 8)(
            pos, lev, counts, static_control, diag, off, obs_weight, innovation, send_src, send_wt, recv_tgt
        )
        sums = [
            call(sum_kernel, shape((levels, band_cols), F32), [SMEM] + [VMEM] * 4)(
                lev, perturb, other_control, part, level_loc
            )
        ]
        sums[0], other_perturb = lax.optimization_barrier((sums[0], other_perturb))
        for k in range(1, groups):
            sums.append(lax.ppermute(sums[0], "grp", [(g, (g + k) % groups) for g in range(groups)]))
        total, *blocks = call(
            functools.partial(blocks_kernel, groups),
            [shape((stacked, cap), F32)] + [shape((stacked + rows.total, cap), F32)] * (n - 1),
            [VMEM] * (groups + n - 1),
        )(*sums, *rests[1:])
        first = sorted(range(n // 2, n), key=lambda r: (relabel(r, n, 1) != r, r))
        first = first[: n // 4 // 2] + first[n // 4 :] + first[n // 4 // 2 : n // 4]
        second = [*range(2, n // 2), *range(1, min(2, n // 2))]
        levs = lax.axis_size("lev")
        arrived = {0: (total, rests[0])}
        for r in first + second:
            pairs = [(i * levs + v, (i ^ relabel(r, n, v)) * levs + v) for i in range(n) for v in range(levs)]
            arrived[r] = (lax.ppermute(blocks[r - 1], ("tile", "lev"), pairs),)
        first = [0] + first

        def taken(order):
            return tuple(len(arrived[r]) for r in order), [ref for r in order for ref in arrived[r]]

        counts_first, refs_first = taken(first)
        slots, met = call(
            functools.partial(early_kernel, n, levels, band_cols, first, counts_first),
            (shape((n, 2 * levels, len(first) * cap), BF16), shape((len(first), levels, cap), F32)),
            [VMEM] * len(refs_first),
        )(*refs_first)
        counts_all, refs_all = taken(first + second)
        mine, late, tables = call(
            functools.partial(shared_kernel, n, tile_cols, first, second, counts_all),
            (mine_shape, shape((n, 2 * levels, len(second) * cap), BF16), shape((n, n + EXTRA, cap), F32)),
            [SMEM] * 2 + [VMEM] * (3 + len(refs_all)),
        )(pos, lev, level_loc, slots, met, *refs_all)
        increment, grad_static = call(functools.partial(outputs_kernel, first, second), (flat, flat), [SMEM] * 2 + [VMEM] * 8)(
            pos, lev, slots, late, tables, static_control, diag, off, obs_weight, innovation
        )
    else:
        payload = call(
            band_kernel,
            shape((groups, n, levels + EXTRA, cap), F32),
            [SMEM] * 2 + [VMEM] * 7,
            [pltpu.VMEM((2 * levels, band_cols), BF16)],
        )(lev, counts, perturb, other_control, part, level_loc, static_control, send_src, send_wt)
        arrived = lax.all_to_all(
            payload.reshape(groups * n, levels + EXTRA, cap), ("grp", "tile"), split_axis=0, concat_axis=0, tiled=True
        ).reshape(groups, n, levels + EXTRA, cap)
        increment, partial, giving = call(
            tile_kernel, (flat, flat, shape((n, levels + EXTRA, cap), F32)), [SMEM] + [VMEM] * 7
        )(pos, arrived, recv_tgt, static_control, diag, off, obs_weight, innovation)
        returned = lax.all_to_all(giving, "tile", split_axis=0, concat_axis=0, tiled=True)
        grad_static, mine = call(adjoint_kernel, (flat, mine_shape), [SMEM, SMEM] + [VMEM] * 5)(
            pos, counts, returned, send_src, send_wt, partial, level_loc
        )
    theirs = lax.ppermute(mine, "lev", swap)
    grad_ens = call(ens_kernel, shape(control.shape, F32), [SMEM] + [VMEM] * 5)(
        lev, perturb, other_perturb, control, mine, theirs
    )
    return (increment, grad_static, grad_ens)


def solution(mesh):
    return jax.shard_map(
        body,
        mesh=mesh,
        in_specs=(
            P("lev", "grp", "tile"),
            P("lev", "grp", "tile"),
            P("lev", None),
            P("lev", "tile"),
            P("tile"),
            P("tile"),
            P("tile", None, None),
            P("tile", None, None),
            P("tile", None),
            P("tile", None, None),
            P("lev", "tile"),
            P("lev", "tile"),
        ),
        out_specs=(P("lev", "tile"), P("lev", "tile"), P("lev", "grp", "tile")),
        check_vma=False,
    )
```

```python
import functools

import jax
import jax.numpy as jnp
from jax import lax
from jax.experimental import pallas as pl
from jax.experimental.pallas import tpu as pltpu
from jax.sharding import PartitionSpec as P

F32 = jnp.float32
BF16 = jnp.bfloat16
SUB = 8
EXTRA = 8
VMEM = pl.BlockSpec(memory_space=pltpu.VMEM)
HBM = pl.BlockSpec(memory_space=pltpu.HBM)
SMEM = pl.BlockSpec(memory_space=pltpu.SMEM)
MIB = 1024 * 1024


def halves(values):
    high = values.astype(BF16)
    low = (values - high.astype(F32)).astype(BF16)
    return high, low


def product(a, b, dims=((1,), (0,))):
    return lax.dot_general(a, b, (dims, ((), ())), preferred_element_type=F32)


def select(values, chosen, dims=((1,), (0,))):
    rows = values.shape[0]
    both = product(jnp.concatenate(halves(values), axis=0), chosen, dims)
    return both[:rows] + both[rows:]


def spread(matrix, start, count):
    rows, cols = matrix.shape

    def iota(shape, axis):
        return lax.broadcasted_iota(jnp.int32, shape, axis)

    shape = (rows * SUB, count * SUB)
    tall = (iota((rows * SUB, rows), 0) // SUB == iota((rows * SUB, rows), 1)).astype(BF16)
    wide = (iota((cols, count * SUB), 1) // SUB + start == iota((cols, count * SUB), 0)).astype(BF16)
    same = iota(shape, 0) % SUB == iota(shape, 1) % SUB
    out = []
    for part in halves(matrix):
        filled = product(tall, product(part, wide).astype(BF16))
        out.append(jnp.where(same, filled, 0.0).astype(BF16))
    return out


def mix(weights, values):
    high, low = halves(values)
    return product(weights[0], high) + (product(weights[0], low) + product(weights[1], high))


def one_hot(index, size):
    rows = lax.broadcasted_iota(jnp.int32, (size, index.shape[1]), 0)
    return jnp.where(rows == index, 1.0, 0.0).astype(BF16)


def column_as_row(column, lane, offset):
    n = column.shape[0]
    place = lax.broadcasted_iota(jnp.int32, (n, 128), 1) == lax.broadcasted_iota(jnp.int32, (n, 128), 0) + offset
    return jnp.sum(jnp.where(place, column, 0.0), axis=0, keepdims=True)


def row_as_column(row, n, offset):
    place = lax.broadcasted_iota(jnp.int32, (n, 128), 1) == lax.broadcasted_iota(jnp.int32, (n, 128), 0) + offset
    return jnp.sum(jnp.where(place, row, 0.0), axis=1, keepdims=True)


def edge_rows(values):
    n = values.shape[0]
    row = column_as_row(values[:, -1:], None, 0) + column_as_row(values[:, :1], None, n)
    return jnp.broadcast_to(row, (EXTRA, 128))


def factor_of(counts_ref, weight_ref, d):
    slot = lax.broadcasted_iota(jnp.int32, (1, weight_ref.shape[2]), 1)
    return jnp.where(slot < counts_ref[0, d], weight_ref[0, pl.ds(d, 1), :], 0.0)


def loop(n, step, init):
    return lax.fori_loop(0, n, step, init, unroll=n if n <= 8 else 1)


def own_kernel(lev_ref, perturb_hbm, control_hbm, loc_hbm, part_ref, perturb_ref, control_ref, loc_ref, sems):
    levels, members, _ = perturb_ref.shape
    tiles = [slice(m, m + SUB) for m in range(0, members, SUB)]
    staged = [(loc_hbm, loc_ref), (perturb_hbm, perturb_ref)]
    staged += [(control_hbm.at[:, tile, :], control_ref.at[:, tile, :]) for tile in tiles]
    copies = [pltpu.make_async_copy(source, target, sems.at[i]) for i, (source, target) in enumerate(staged)]
    for copy in copies:
        copy.start()
    copies[0].wait()
    weights = spread(loc_ref[...], lev_ref[0] * levels, levels)
    copies[1].wait()
    part_ref[...] = mixed_sum(weights, perturb_ref, control_ref, [copy.wait for copy in copies[2:]])


def mixed_sum(weights, perturb_ref, control_ref, waits=()):
    levels, members, cols = perturb_ref.shape
    perturb = perturb_ref[...].astype(F32)
    total = jnp.zeros((levels, SUB, cols), F32)
    for i, m in enumerate(range(0, members, SUB)):
        if waits:
            waits[i]()
        tile = control_ref[:, m : m + SUB, :].reshape(levels * SUB, cols)
        total = total + perturb[:, m : m + SUB, :] * mix(weights, tile).reshape(levels, SUB, cols)
    return jnp.sum(total, axis=1)


def band_kernel(lev_ref, counts_ref, perturb_ref, other_ref, part_ref, loc_ref, static_ref, src_ref, weight_ref,
                out_ref, acc_ref):
    levels, members, cols = perturb_ref.shape
    weights = spread(loc_ref[...], (1 - lev_ref[0]) * levels, levels)
    band_sum = part_ref[...] + mixed_sum(weights, perturb_ref, other_ref)
    acc_ref[...] = jnp.concatenate(halves(band_sum), axis=0)
    n = src_ref.shape[1]
    edges = edge_rows(static_ref[...])

    def step(d, carry):
        chosen = one_hot(src_ref[0, pl.ds(d, 1), :], cols)
        both = product(acc_ref[...], chosen)
        payload = (both[:levels] + both[levels:]) * factor_of(counts_ref, weight_ref, d)
        for g in range(out_ref.shape[0]):
            out_ref[g, d, :levels, :] = payload
            out_ref[g, d, levels:, :] = edges
        return carry

    loop(n, step, 0)


def tile_kernel(pos_ref, arrived_ref, tgt_ref, static_ref, diag_ref, off_ref, obs_ref, innov_ref,
                increment_ref, partial_ref, out_ref):
    levels, cols = static_ref.shape
    groups, n = arrived_ref.shape[:2]
    me = pos_ref[0]

    def step(s, total):
        values = sum(arrived_ref[g, s, :levels, :] for g in range(groups))
        chosen = one_hot(tgt_ref[0, pl.ds(s, 1), :], cols)
        return total + select(values, chosen, ((1,), (1,)))

    remapped = loop(n, step, jnp.zeros((levels, cols), F32))
    before = arrived_ref[0, jnp.maximum(me - 1, 0), levels : levels + 1, :]
    after = arrived_ref[0, jnp.minimum(me + 1, n - 1), levels : levels + 1, :]
    before = jnp.where(me > 0, row_as_column(before, levels, 0), 0.0)
    after = jnp.where(me < n - 1, row_as_column(after, levels, levels), 0.0)
    static = static_ref[...]
    lane = lax.broadcasted_iota(jnp.int32, (levels, cols), 1)
    left = jnp.where(lane == 0, before, pltpu.roll(static, 1, 1))
    right = jnp.where(lane == cols - 1, after, pltpu.roll(static, cols - 1, 1))
    increment = remapped + diag_ref[...] * static + off_ref[...] * (left + right)
    increment_ref[...] = increment
    misfit = obs_ref[...] * (increment - innov_ref[...])
    coupled = off_ref[...] * misfit
    left = jnp.where(lane == 0, 0.0, pltpu.roll(coupled, 1, 1))
    right = jnp.where(lane == cols - 1, 0.0, pltpu.roll(coupled, cols - 1, 1))
    partial_ref[...] = static + diag_ref[...] * misfit + left + right
    edges = edge_rows(coupled)
    both = jnp.concatenate(halves(misfit), axis=0)

    def give(s, carry):
        chosen = one_hot(tgt_ref[0, pl.ds(s, 1), :], cols)
        picked = product(both, chosen)
        out_ref[s, :levels, :] = picked[:levels] + picked[levels:]
        out_ref[s, levels:, :] = edges
        return carry

    loop(n, give, 0)


def adjoint_kernel(pos_ref, counts_ref, returned_ref, src_ref, weight_ref, partial_ref, loc_ref, grad_ref, out_ref):
    levels, cols = partial_ref.shape
    n = returned_ref.shape[0]
    band = out_ref.shape[1] - 128
    me = pos_ref[0]

    def step(d, total):
        values = returned_ref[d, :levels, :] * factor_of(counts_ref, weight_ref, d)
        return total + select(values, one_hot(src_ref[0, pl.ds(d, 1), :], band), ((1,), (1,)))

    out_ref[:, :band] = loop(n, step, jnp.zeros((levels, band), F32))
    out_ref[:, band:] = jnp.concatenate([loc_ref[...], jnp.zeros((levels, 128 - loc_ref.shape[1]), F32)], axis=1)
    before = returned_ref[jnp.maximum(me - 1, 0), levels : levels + 1, :]
    after = returned_ref[jnp.minimum(me + 1, n - 1), levels : levels + 1, :]
    before = jnp.where(me > 0, row_as_column(before, levels, 0), 0.0)
    after = jnp.where(me < n - 1, row_as_column(after, levels, levels), 0.0)
    lane = lax.broadcasted_iota(jnp.int32, (levels, cols), 1)
    grad_ref[...] = partial_ref[...] + (jnp.where(lane == 0, before, 0.0) + jnp.where(lane == cols - 1, after, 0.0))


def ens_kernel(lev_ref, perturb_ref, other_ref, control_ref, mine_ref, theirs_ref, out_hbm, out_ref, sems):
    levels, members, cols = perturb_ref.shape
    mine, theirs = mine_ref[...], theirs_ref[...]
    loc = jnp.concatenate([mine[:, cols : cols + 2 * levels], theirs[:, cols : cols + 2 * levels]], axis=0)
    full = loc.shape[0]
    l_row = lax.broadcasted_iota(jnp.int32, (levels * SUB, full), 0) // SUB + lev_ref[0] * levels
    pick_l = (l_row == lax.broadcasted_iota(jnp.int32, (levels * SUB, full), 1)).astype(BF16)
    k_col = lax.broadcasted_iota(jnp.int32, (full, full * SUB), 1) // SUB
    pick_k = (k_col == lax.broadcasted_iota(jnp.int32, (full, full * SUB), 0)).astype(BF16)
    same = (
        lax.broadcasted_iota(jnp.int32, (levels * SUB, full * SUB), 0) % SUB
        == lax.broadcasted_iota(jnp.int32, (levels * SUB, full * SUB), 1) % SUB
    )
    weights = []
    for part in halves(loc):
        tall = product(pick_l, part, ((1,), (1,)))
        wide = product(tall.astype(BF16), pick_k)
        weights.append(jnp.where(same, wide, 0.0).astype(BF16))
    perturb = perturb_ref[...].astype(F32)
    other = other_ref[...].astype(F32)
    grad = jnp.concatenate([mine[:, :cols], theirs[:, :cols]], axis=0)[:, None, :]
    copies = []
    for i, m in enumerate(range(0, members, SUB)):
        tile = jnp.concatenate([perturb[:, m : m + SUB, :], other[:, m : m + SUB, :]], axis=0) * grad
        mixed = mix(weights, tile.reshape(full * SUB, cols)).reshape(levels, SUB, cols)
        place = (slice(None), slice(m, m + SUB), slice(None))
        out_ref[place] = control_ref[place] + mixed
        copies.append(pltpu.make_async_copy(out_ref.at[place], out_hbm.at[place], sems.at[i]))
        copies[-1].start()
    for copy in copies:
        copy.wait()


def relabel(r, n, lev):
    high, low = n // 2, n // 4
    if low == 0:
        return r
    both = high | low
    turned = (r & ~both) | ((r & low) << 1) | ((r & high) >> 1)
    return r + (turned - r) * lev


class Rows:
    def __init__(self, levels, n):
        self.weight = slice(0, levels)
        self.base = slice(levels, 2 * levels)
        at = 2 * levels
        self.factor, self.index, self.edge = at, at + n, at + 2 * n
        self.total = at + 2 * n + EXTRA


def static_kernel(band, pos_ref, lev_ref, counts_ref, static_ref, diag_ref, off_ref, obs_ref, innov_ref, src_ref, weight_ref, tgt_ref,
                  *out_refs):
    levels, cols = static_ref.shape
    n = len(out_refs)
    cap = src_ref.shape[2]
    rows = Rows(levels, n)
    peers = [pos_ref[0] ^ relabel(r, n, lev_ref[0]) for r in range(n)]
    static, off, obs = static_ref[...], off_ref[...], obs_ref[...]
    lane = lax.broadcasted_iota(jnp.int32, (levels, cols), 1)
    left = jnp.where(lane == 0, 0.0, pltpu.roll(static, 1, 1))
    right = jnp.where(lane == cols - 1, 0.0, pltpu.roll(static, cols - 1, 1))
    base = diag_ref[...] * static + off * (left + right) - innov_ref[...]
    coupled = off * obs
    ends = [v[:, i] for v in (static, coupled, base) for i in (slice(cols - 1, cols), slice(0, 1))]
    edge = sum(column_as_row(end, None, i * levels) for i, end in enumerate(ends))
    place = lax.broadcasted_iota(jnp.int32, (1, cap), 1)
    edge = edge + jnp.where(place == 6 * levels, off[:, cols - 1 :], 0.0)
    edge = edge + jnp.where(place == 6 * levels + 1, off[:, :1], 0.0)
    edge = jnp.broadcast_to(edge, (EXTRA, cap))
    both = jnp.concatenate(halves(jnp.concatenate([obs, base], axis=0)), axis=0)
    tgts = [tgt_ref[0, pl.ds(peer, 1), :] for peer in peers]
    src = jnp.concatenate([src_ref[0, pl.ds(peer, 1), :] for peer in peers], axis=0).astype(F32)
    index = jnp.concatenate(tgts, axis=0).astype(F32) * float(band) + src
    factor = jnp.concatenate([factor_of(counts_ref, weight_ref, peer) for peer in peers], axis=0)
    for r, out_ref in enumerate(out_refs):
        picked = product(both, one_hot(tgts[r], cols))
        out_ref[: 2 * levels, :] = picked[: 2 * levels] + picked[2 * levels :]
        out_ref[rows.factor : rows.factor + n, :] = factor
        out_ref[rows.index : rows.index + n, :] = index
        out_ref[rows.edge :, :] = edge


def sum_kernel(lev_ref, perturb_ref, other_ref, part_ref, loc_ref, out_ref):
    levels = perturb_ref.shape[0]
    weights = spread(loc_ref[...], (1 - lev_ref[0]) * levels, levels)
    out_ref[...] = part_ref[...] + mixed_sum(weights, perturb_ref, other_ref)


def blocks_kernel(groups, *refs):
    sums = refs[:groups]
    count = (len(refs) - groups - 1) // 2
    rests = refs[groups : groups + count]
    total_ref = refs[groups + count]
    out_refs = refs[groups + count + 1 :]
    total = sum(ref[...] for ref in sums)
    cap = total_ref.shape[1]
    total = jnp.concatenate([total[:, at : at + cap] for at in range(0, total.shape[1], cap)], axis=0)
    total_ref[...] = total
    for rest_ref, out_ref in zip(rests, out_refs):
        out_ref[: total.shape[0], :] = total
        out_ref[total.shape[0] :, :] = rest_ref[...]


class Block:
    def __init__(self, refs, n, levels, band):
        cap = refs[0].shape[1]
        self.levels, self.parts, self.cap = levels, band // cap, cap
        self.sums_ref, self.rest_ref = refs[0], refs[-1]
        self.head = 0 if len(refs) == 2 else self.parts * levels
        self.rows = Rows(levels, n)
        words = self.rest(self.rows.index, n)
        self.tgt = jnp.floor((words + 0.5) * (1.0 / band))
        self.src = words - self.tgt * float(band)
        self.factor = self.rest(self.rows.factor, n)

    def rest(self, at, size):
        return self.rest_ref[self.head + at : self.head + at + size, :]

    def sums(self):
        parts = [self.sums_ref[i * self.levels : (i + 1) * self.levels, :] for i in range(self.parts)]
        return jnp.concatenate(halves(jnp.concatenate(parts, axis=1)), axis=0)


def line(table, i):
    return table[i : i + 1]


def pick_source(block, r):
    band = block.parts * block.cap
    column = lax.broadcasted_iota(jnp.int32, (band, block.cap), 0).astype(F32)
    return jnp.where(column == line(block.src, r), 1.0, 0.0).astype(BF16)


def fill_slots(bands, blocks, n, slots_ref):
    for i, s in enumerate(bands):
        block = blocks[s]
        both = block.sums()
        for d in range(n):
            picked = product(both, pick_source(block, s ^ d))
            values = (picked[: block.levels] + picked[block.levels :]) * line(block.factor, s ^ d)
            slots_ref[d, :, i * block.cap : (i + 1) * block.cap] = jnp.concatenate(halves(values), axis=0)


def met_at(d, block, bands, slots_ref):
    own = jnp.broadcast_to(line(block.tgt, d), (block.cap, block.cap)).T
    same = [jnp.where(own == line(block.tgt, s ^ d), 1.0, 0.0).astype(BF16) for s in bands]
    met = product(slots_ref[d], jnp.concatenate(same, axis=1), ((1,), (1,)))
    return met[: block.levels] + met[block.levels :]


def land(table, bands, slots_ref, cols):
    cap = table.shape[1]
    row = lax.broadcasted_iota(jnp.int32, (cols, cap), 0).astype(F32)
    total = 0.0
    for i, s in enumerate(bands):
        landing = jnp.where(row == line(table, s), 1.0, 0.0).astype(BF16)
        total = total + product(slots_ref[0, :, i * cap : (i + 1) * cap], landing, ((1,), (1,)))
    levels = total.shape[0] // 2
    return total[:levels] + total[levels:]


def open_blocks(labels, refs, n, levels, band):
    blocks = {0: Block(refs[:2], n, levels, band)}
    refs = refs[2:]
    for i, r in enumerate(labels[1:]):
        blocks[r] = Block(refs[i : i + 1], n, levels, band)
    return blocks, refs[len(labels) - 1 :]


def stage_kernel(n, levels, band, cols, stages, *refs):
    known = sum(stages[:-1], [])
    blocks, refs = open_blocks(known + stages[-1], refs, n, levels, band)
    old, refs = refs[: len(stages) - 1], refs[len(stages) - 1 :]
    if known:
        met_old, remap_old, slots_ref, met_ref, remap_ref = refs
    else:
        slots_ref, met_ref, remap_ref, pick_ref = refs
        for d in range(n):
            pick_ref[d] = pick_source(blocks[0], d)
    fill_slots(stages[-1], blocks, n, slots_ref)
    for i, (d, block) in enumerate(blocks.items()):
        met = met_at(d, block, stages[-1], slots_ref)
        if d in known:
            met = met + met_old[i]
        else:
            for bands, ref in zip(stages, old):
                met = met + met_at(d, block, bands, ref)
        met_ref[i] = met
    landed = land(blocks[0].tgt, stages[-1], slots_ref, cols)
    remap_ref[...] = landed + remap_old[...] if known else landed


def shared_kernel(n, cols, stages, pos_ref, lev_ref, loc_ref, *refs):
    levels = loc_ref.shape[0]
    band = refs[-3].shape[1] - 128
    known = sum(stages[:-1], [])
    blocks, refs = open_blocks(known + stages[-1], refs, n, levels, band)
    old, refs = refs[: len(stages) - 1], refs[len(stages) - 1 :]
    met_old, pick_ref, out_ref, slots_ref, tables_ref = refs
    me = pos_ref[0]
    for r, block in blocks.items():
        there = me ^ relabel(r, n, lev_ref[0])
        tables_ref[there, :n, :] = block.tgt
        tables_ref[there, n:, :] = block.rest(block.rows.edge, EXTRA)
    fill_slots(stages[-1], blocks, n, slots_ref)
    last = cols - 1.0
    total = jnp.zeros((levels, band), F32)
    for i, (d, block) in enumerate(blocks.items()):
        value = met_at(d, block, stages[-1], slots_ref) + block.rest(levels, levels)
        if d in known:
            value = value + met_old[i]
        else:
            for bands, ref in zip(stages, old):
                value = value + met_at(d, block, bands, ref)
        edge = block.rest(block.rows.edge, 1)
        own = line(block.tgt, d)
        there = me ^ relabel(d, n, lev_ref[0])
        before = tables_ref[jnp.maximum(there - 1, 0), n : n + 1, :]
        near = jnp.where((own == 0.0) & (there > 0), edge[:, 6 * levels + 1 : 6 * levels + 2], 0.0)
        value = value + row_as_column(before, levels, 0) * near
        after = tables_ref[jnp.minimum(there + 1, n - 1), n : n + 1, :]
        near = jnp.where((own == last) & (there < n - 1), edge[:, 6 * levels : 6 * levels + 1], 0.0)
        value = value + row_as_column(after, levels, levels) * near
        given = block.rest(0, levels) * value * line(blocks[0].factor, d)
        total = total + select(given, pick_ref[d], ((1,), (1,)))
    out_ref[:, :band] = total
    out_ref[:, band:] = jnp.concatenate([loc_ref[...], jnp.zeros((levels, 128 - loc_ref.shape[1]), F32)], axis=1)


def outputs_kernel(stages, pos_ref, lev_ref, *refs):
    slots_refs, refs = refs[: len(stages)], refs[len(stages) :]
    remap_ref, tables_ref, static_ref, diag_ref, off_ref, obs_ref, innov_ref, increment_ref, grad_ref = refs
    levels, cols = static_ref.shape
    n = tables_ref.shape[0]
    cap = tables_ref.shape[2]
    me = pos_ref[0]
    given = [
        (s, ref, slice(i * cap, (i + 1) * cap)) for bands, ref in zip(stages, slots_refs) for i, s in enumerate(bands)
    ]
    remapped = remap_ref[...] + land(tables_ref[me, :n, :], stages[-1], slots_refs[-1], cols)
    static, off = static_ref[...], off_ref[...]
    lane = lax.broadcasted_iota(jnp.int32, (levels, cols), 1)

    def beside(there, exists, column, own_end, side):
        edge = tables_ref[there, n : n + 1, :]
        static_end, coupling, base = (row_as_column(edge, levels, (2 * i + side) * levels) for i in range(3))
        far = relabel(me ^ there, n, lev_ref[0])
        landed = []
        for s, ref, place in given:
            values = ref[far, :levels, place].astype(F32) + ref[far, levels:, place].astype(F32)
            landed.append(jnp.where(tables_ref[there, pl.ds(s ^ far, 1), :] == column, values, 0.0))
        remap_end = jnp.sum(sum(landed), axis=1, keepdims=True)
        off_end = edge[:, 6 * levels + side : 6 * levels + side + 1]
        coupled = coupling * (remap_end + base + off_end * own_end)
        return jnp.where(exists, static_end, 0.0), jnp.where(exists, coupled, 0.0)

    before, coupled_before = beside(jnp.maximum(me - 1, 0), me > 0, cols - 1.0, static[:, :1], 0)
    after, coupled_after = beside(jnp.minimum(me + 1, n - 1), me < n - 1, 0.0, static[:, cols - 1 :], 1)
    left = jnp.where(lane == 0, before, pltpu.roll(static, 1, 1))
    right = jnp.where(lane == cols - 1, after, pltpu.roll(static, cols - 1, 1))
    increment = remapped + diag_ref[...] * static + off * (left + right)
    increment_ref[...] = increment
    misfit = obs_ref[...] * (increment - innov_ref[...])
    coupled = off * misfit
    left = jnp.where(lane == 0, coupled_before, pltpu.roll(coupled, 1, 1))
    right = jnp.where(lane == cols - 1, coupled_after, pltpu.roll(coupled, cols - 1, 1))
    grad_ref[...] = static + diag_ref[...] * misfit + left + right


def call(kernel, out_shape, spaces, scratch=(), limit=40 * MIB, out=VMEM):
    return pl.pallas_call(
        kernel,
        out_shape=out_shape,
        in_specs=spaces,
        out_specs=jax.tree.map(lambda _: out, out_shape),
        scratch_shapes=scratch,
        compiler_params=pltpu.CompilerParams(vmem_limit_bytes=limit),
    )


def body(
    perturb,
    control,
    level_loc,
    static_control,
    filter_diag,
    filter_off,
    send_src,
    send_wt,
    counts,
    recv_tgt,
    obs_weight,
    innovation,
):
    levels, members, band_cols = control.shape
    tile_cols = static_control.shape[1]
    n = lax.axis_size("tile")
    groups = lax.axis_size("grp")
    cap = send_src.shape[2]
    shape = jax.ShapeDtypeStruct
    swap = [(0, 1), (1, 0)]
    lev = lax.axis_index("lev").astype(jnp.int32).reshape(1)
    pos = lax.axis_index("tile").astype(jnp.int32).reshape(1)
    other_control = lax.ppermute(control, "lev", swap)
    other_perturb = lax.ppermute(perturb, "lev", swap)
    part = call(
        own_kernel,
        shape((levels, band_cols), F32),
        [SMEM] + [HBM] * 3,
        [pltpu.VMEM(a.shape, a.dtype) for a in (perturb, control, level_loc)] + [pltpu.SemaphoreType.DMA((2 + members // SUB,))],
        limit=58 * MIB,
    )(lev, perturb, control, level_loc)
    flat = shape((levels, tile_cols), F32)
    mine_shape = shape((levels, band_cols + 128), F32)
    diag, off = filter_diag.reshape(1, -1), filter_off.reshape(1, -1)
    if n * cap <= tile_cols and n >= 8 and lax.axis_size("lev") == 2 and n & (n - 1) == 0 and band_cols * tile_cols <= 2**20:
        rows = Rows(levels, n)
        stacked = band_cols // cap * levels
        rests = call(functools.partial(static_kernel, band_cols), [shape((rows.total, cap), F32)] * n, [SMEM] * 3 + [VMEM] * 8)(
            pos, lev, counts, static_control, diag, off, obs_weight, innovation, send_src, send_wt, recv_tgt
        )
        sums = [
            call(sum_kernel, shape((levels, band_cols), F32), [SMEM] + [VMEM] * 4)(
                lev, perturb, other_control, part, level_loc
            )
        ]
        sums[0], other_perturb = lax.optimization_barrier((sums[0], other_perturb))
        for k in range(1, groups):
            sums.append(lax.ppermute(sums[0], "grp", [(g, (g + k) % groups) for g in range(groups)]))
        total, *blocks = call(
            functools.partial(blocks_kernel, groups),
            [shape((stacked, cap), F32)] + [shape((stacked + rows.total, cap), F32)] * (n - 1),
            [VMEM] * (groups + n - 1),
        )(*sums, *rests[1:])
        far = sorted(range(n // 2, n), key=lambda r: (relabel(r, n, 1) != r, r))
        far = far[: n // 4 // 2] + far[n // 4 :] + far[n // 4 // 2 : n // 4]
        stages = [[0] + far, list(range(2, n // 2)), [1]]
        levs = lax.axis_size("lev")
        arrived = {0: [total, rests[0]]}
        for r in sum(stages, [])[1:]:
            pairs = [(i * levs + v, (i ^ relabel(r, n, v)) * levs + v) for i in range(n) for v in range(levs)]
            arrived[r] = [lax.ppermute(blocks[r - 1], ("tile", "lev"), pairs)]
        slots, carried, picks = [], [], []
        for count in range(1, len(stages)):
            labels = sum(stages[:count], [])
            refs = [ref for r in labels for ref in arrived[r]]
            outs = [
                shape((n, 2 * levels, len(stages[count - 1]) * cap), BF16),
                shape((len(labels), levels, cap), F32),
                flat,
            ] + [shape((n, band_cols, cap), BF16)] * (count == 1)
            new, *carried = call(
                functools.partial(stage_kernel, n, levels, band_cols, tile_cols, stages[:count]),
                outs,
                [VMEM] * (len(refs) + len(slots) + len(carried)),
            )(*refs, *slots, *carried)
            slots.append(new)
            picks += carried[2:]
            carried = carried[:2]
        met, remap = carried
        refs = [ref for r in sum(stages, []) for ref in arrived[r]] + slots + [met] + picks
        mine, new, tables = call(
            functools.partial(shared_kernel, n, tile_cols, stages),
            (mine_shape, shape((n, 2 * levels, len(stages[-1]) * cap), BF16), shape((n, n + EXTRA, cap), F32)),
            [SMEM] * 2 + [VMEM] * (1 + len(refs)),
        )(pos, lev, level_loc, *refs)
        slots.append(new)
        increment, grad_static = call(
            functools.partial(outputs_kernel, stages), (flat, flat), [SMEM] * 2 + [VMEM] * (len(slots) + 7)
        )(pos, lev, *slots, remap, tables, static_control, diag, off, obs_weight, innovation)
    else:
        payload = call(
            band_kernel,
            shape((groups, n, levels + EXTRA, cap), F32),
            [SMEM] * 2 + [VMEM] * 7,
            [pltpu.VMEM((2 * levels, band_cols), BF16)],
        )(lev, counts, perturb, other_control, part, level_loc, static_control, send_src, send_wt)
        arrived = lax.all_to_all(
            payload.reshape(groups * n, levels + EXTRA, cap), ("grp", "tile"), split_axis=0, concat_axis=0, tiled=True
        ).reshape(groups, n, levels + EXTRA, cap)
        increment, partial, giving = call(
            tile_kernel, (flat, flat, shape((n, levels + EXTRA, cap), F32)), [SMEM] + [VMEM] * 7
        )(pos, arrived, recv_tgt, static_control, diag, off, obs_weight, innovation)
        returned = lax.all_to_all(giving, "tile", split_axis=0, concat_axis=0, tiled=True)
        grad_static, mine = call(adjoint_kernel, (flat, mine_shape), [SMEM, SMEM] + [VMEM] * 5)(
            pos, counts, returned, send_src, send_wt, partial, level_loc
        )
    theirs = lax.ppermute(mine, "lev", swap)
    grad_ens = call(
        ens_kernel,
        shape(control.shape, F32),
        [SMEM] + [VMEM] * 5,
        [pltpu.VMEM(control.shape, F32), pltpu.SemaphoreType.DMA((members // SUB,))],
        out=HBM,
    )(
        lev, perturb, other_perturb, control, mine, theirs
    )
    return (increment, grad_static, grad_ens)


def solution(mesh):
    return jax.shard_map(
        body,
        mesh=mesh,
        in_specs=(
            P("lev", "grp", "tile"),
            P("lev", "grp", "tile"),
            P("lev", None),
            P("lev", "tile"),
            P("tile"),
            P("tile"),
            P("tile", None, None),
            P("tile", None, None),
            P("tile", None),
            P("tile", None, None),
            P("lev", "tile"),
            P("lev", "tile"),
        ),
        out_specs=(P("lev", "tile"), P("lev", "tile"), P("lev", "grp", "tile")),
        check_vma=False,
    )
```

```python
import functools

import jax
import jax.numpy as jnp
from jax import lax
from jax.experimental import pallas as pl
from jax.experimental.pallas import tpu as pltpu
from jax.sharding import PartitionSpec as P

F32 = jnp.float32
BF16 = jnp.bfloat16
SUB = 8
EXTRA = 8
VMEM = pl.BlockSpec(memory_space=pltpu.VMEM)
HBM = pl.BlockSpec(memory_space=pltpu.HBM)
SMEM = pl.BlockSpec(memory_space=pltpu.SMEM)
MIB = 1024 * 1024


def halves(values):
    high = values.astype(BF16)
    low = (values - high.astype(F32)).astype(BF16)
    return high, low


def product(a, b, dims=((1,), (0,))):
    return lax.dot_general(a, b, (dims, ((), ())), preferred_element_type=F32)


def select(values, chosen, dims=((1,), (0,))):
    rows = values.shape[0]
    both = product(jnp.concatenate(halves(values), axis=0), chosen, dims)
    return both[:rows] + both[rows:]


def spread(matrix, start, count):
    rows, cols = matrix.shape

    def iota(shape, axis):
        return lax.broadcasted_iota(jnp.int32, shape, axis)

    shape = (rows * SUB, count * SUB)
    tall = (iota((rows * SUB, rows), 0) // SUB == iota((rows * SUB, rows), 1)).astype(BF16)
    wide = (iota((cols, count * SUB), 1) // SUB + start == iota((cols, count * SUB), 0)).astype(BF16)
    same = iota(shape, 0) % SUB == iota(shape, 1) % SUB
    out = []
    for part in halves(matrix):
        filled = product(tall, product(part, wide).astype(BF16))
        out.append(jnp.where(same, filled, 0.0).astype(BF16))
    return out


def mix(weights, values):
    high, low = halves(values)
    rows = weights[0].shape[0]
    both = product(jnp.concatenate(weights, axis=0), high)
    return both[:rows] + (product(weights[0], low) + both[rows:])


def one_hot(index, size):
    rows = lax.broadcasted_iota(jnp.int32, (size, index.shape[1]), 0)
    return jnp.where(rows == index, 1.0, 0.0).astype(BF16)


def column_as_row(column, lane, offset):
    n = column.shape[0]
    place = lax.broadcasted_iota(jnp.int32, (n, 128), 1) == lax.broadcasted_iota(jnp.int32, (n, 128), 0) + offset
    return jnp.sum(jnp.where(place, column, 0.0), axis=0, keepdims=True)


def row_as_column(row, n, offset):
    place = lax.broadcasted_iota(jnp.int32, (n, 128), 1) == lax.broadcasted_iota(jnp.int32, (n, 128), 0) + offset
    return jnp.sum(jnp.where(place, row, 0.0), axis=1, keepdims=True)


def edge_rows(values):
    n = values.shape[0]
    row = column_as_row(values[:, -1:], None, 0) + column_as_row(values[:, :1], None, n)
    return jnp.broadcast_to(row, (EXTRA, 128))


def factor_of(counts_ref, weight_ref, d):
    slot = lax.broadcasted_iota(jnp.int32, (1, weight_ref.shape[2]), 1)
    return jnp.where(slot < counts_ref[0, d], weight_ref[0, pl.ds(d, 1), :], 0.0)


def loop(n, step, init):
    return lax.fori_loop(0, n, step, init, unroll=n if n <= 8 else 1)


def own_kernel(lev_ref, perturb_hbm, control_hbm, loc_hbm, part_ref, perturb_ref, control_ref, loc_ref, sems):
    staged = [(loc_hbm, loc_ref), (control_hbm, control_ref), (perturb_hbm, perturb_ref)]
    copies = [pltpu.make_async_copy(source, target, sems.at[i]) for i, (source, target) in enumerate(staged)]
    for copy in copies:
        copy.start()
    levels = perturb_ref.shape[0]
    copies[0].wait()
    weights = spread(loc_ref[...], lev_ref[0] * levels, levels)
    copies[1].wait()
    copies[2].wait()
    part_ref[...] = mixed_sum(weights, perturb_ref, control_ref)


def mixed_sum(weights, perturb_ref, control_ref):
    levels, members, cols = perturb_ref.shape
    perturb = perturb_ref[...].astype(F32)
    total = jnp.zeros((levels, SUB, cols), F32)
    for m in range(0, members, SUB):
        tile = control_ref[:, m : m + SUB, :].reshape(levels * SUB, cols)
        total = total + perturb[:, m : m + SUB, :] * mix(weights, tile).reshape(levels, SUB, cols)
    return jnp.sum(total, axis=1)


def band_kernel(lev_ref, counts_ref, perturb_ref, other_ref, part_ref, loc_ref, static_ref, src_ref, weight_ref,
                out_ref, acc_ref):
    levels, members, cols = perturb_ref.shape
    weights = spread(loc_ref[...], (1 - lev_ref[0]) * levels, levels)
    band_sum = part_ref[...] + mixed_sum(weights, perturb_ref, other_ref)
    acc_ref[...] = jnp.concatenate(halves(band_sum), axis=0)
    n = src_ref.shape[1]
    edges = edge_rows(static_ref[...])

    def step(d, carry):
        chosen = one_hot(src_ref[0, pl.ds(d, 1), :], cols)
        both = product(acc_ref[...], chosen)
        payload = (both[:levels] + both[levels:]) * factor_of(counts_ref, weight_ref, d)
        for g in range(out_ref.shape[0]):
            out_ref[g, d, :levels, :] = payload
            out_ref[g, d, levels:, :] = edges
        return carry

    loop(n, step, 0)


def tile_kernel(pos_ref, arrived_ref, tgt_ref, static_ref, diag_ref, off_ref, obs_ref, innov_ref,
                increment_ref, partial_ref, out_ref):
    levels, cols = static_ref.shape
    groups, n = arrived_ref.shape[:2]
    me = pos_ref[0]

    def step(s, total):
        values = sum(arrived_ref[g, s, :levels, :] for g in range(groups))
        chosen = one_hot(tgt_ref[0, pl.ds(s, 1), :], cols)
        return total + select(values, chosen, ((1,), (1,)))

    remapped = loop(n, step, jnp.zeros((levels, cols), F32))
    before = arrived_ref[0, jnp.maximum(me - 1, 0), levels : levels + 1, :]
    after = arrived_ref[0, jnp.minimum(me + 1, n - 1), levels : levels + 1, :]
    before = jnp.where(me > 0, row_as_column(before, levels, 0), 0.0)
    after = jnp.where(me < n - 1, row_as_column(after, levels, levels), 0.0)
    static = static_ref[...]
    lane = lax.broadcasted_iota(jnp.int32, (levels, cols), 1)
    left = jnp.where(lane == 0, before, pltpu.roll(static, 1, 1))
    right = jnp.where(lane == cols - 1, after, pltpu.roll(static, cols - 1, 1))
    increment = remapped + diag_ref[...] * static + off_ref[...] * (left + right)
    increment_ref[...] = increment
    misfit = obs_ref[...] * (increment - innov_ref[...])
    coupled = off_ref[...] * misfit
    left = jnp.where(lane == 0, 0.0, pltpu.roll(coupled, 1, 1))
    right = jnp.where(lane == cols - 1, 0.0, pltpu.roll(coupled, cols - 1, 1))
    partial_ref[...] = static + diag_ref[...] * misfit + left + right
    edges = edge_rows(coupled)
    both = jnp.concatenate(halves(misfit), axis=0)

    def give(s, carry):
        chosen = one_hot(tgt_ref[0, pl.ds(s, 1), :], cols)
        picked = product(both, chosen)
        out_ref[s, :levels, :] = picked[:levels] + picked[levels:]
        out_ref[s, levels:, :] = edges
        return carry

    loop(n, give, 0)


def adjoint_kernel(pos_ref, counts_ref, returned_ref, src_ref, weight_ref, partial_ref, loc_ref, grad_ref, out_ref):
    levels, cols = partial_ref.shape
    n = returned_ref.shape[0]
    band = out_ref.shape[1] - 128
    me = pos_ref[0]

    def step(d, total):
        values = returned_ref[d, :levels, :] * factor_of(counts_ref, weight_ref, d)
        return total + select(values, one_hot(src_ref[0, pl.ds(d, 1), :], band), ((1,), (1,)))

    out_ref[:, :band] = loop(n, step, jnp.zeros((levels, band), F32))
    out_ref[:, band:] = jnp.concatenate([loc_ref[...], jnp.zeros((levels, 128 - loc_ref.shape[1]), F32)], axis=1)
    before = returned_ref[jnp.maximum(me - 1, 0), levels : levels + 1, :]
    after = returned_ref[jnp.minimum(me + 1, n - 1), levels : levels + 1, :]
    before = jnp.where(me > 0, row_as_column(before, levels, 0), 0.0)
    after = jnp.where(me < n - 1, row_as_column(after, levels, levels), 0.0)
    lane = lax.broadcasted_iota(jnp.int32, (levels, cols), 1)
    grad_ref[...] = partial_ref[...] + (jnp.where(lane == 0, before, 0.0) + jnp.where(lane == cols - 1, after, 0.0))


def ens_kernel(lev_ref, perturb_ref, other_ref, control_ref, mine_ref, theirs_ref, out_hbm, out_ref, sems):
    levels, members, cols = perturb_ref.shape
    mine, theirs = mine_ref[...], theirs_ref[...]
    loc = jnp.concatenate([mine[:, cols : cols + 2 * levels], theirs[:, cols : cols + 2 * levels]], axis=0)
    full = loc.shape[0]
    l_row = lax.broadcasted_iota(jnp.int32, (levels * SUB, full), 0) // SUB + lev_ref[0] * levels
    pick_l = (l_row == lax.broadcasted_iota(jnp.int32, (levels * SUB, full), 1)).astype(BF16)
    k_col = lax.broadcasted_iota(jnp.int32, (full, full * SUB), 1) // SUB
    pick_k = (k_col == lax.broadcasted_iota(jnp.int32, (full, full * SUB), 0)).astype(BF16)
    same = (
        lax.broadcasted_iota(jnp.int32, (levels * SUB, full * SUB), 0) % SUB
        == lax.broadcasted_iota(jnp.int32, (levels * SUB, full * SUB), 1) % SUB
    )
    weights = []
    for part in halves(loc):
        tall = product(pick_l, part, ((1,), (1,)))
        wide = product(tall.astype(BF16), pick_k)
        weights.append(jnp.where(same, wide, 0.0).astype(BF16))
    perturb = perturb_ref[...].astype(F32)
    other = other_ref[...].astype(F32)
    grad = jnp.concatenate([mine[:, :cols], theirs[:, :cols]], axis=0)[:, None, :]
    copies = []
    for i, m in enumerate(range(0, members, SUB)):
        tile = jnp.concatenate([perturb[:, m : m + SUB, :], other[:, m : m + SUB, :]], axis=0) * grad
        mixed = mix(weights, tile.reshape(full * SUB, cols)).reshape(levels, SUB, cols)
        place = (slice(None), slice(m, m + SUB), slice(None))
        out_ref[place] = control_ref[place] + mixed
        copies.append(pltpu.make_async_copy(out_ref.at[place], out_hbm.at[place], sems.at[i]))
        copies[-1].start()
    for copy in copies:
        copy.wait()


def relabel(r, n, lev):
    high, low = n // 2, n // 4
    if low == 0:
        return r
    both = high | low
    turned = (r & ~both) | ((r & low) << 1) | ((r & high) >> 1)
    return r + (turned - r) * lev


class Rows:
    def __init__(self, levels, n):
        self.weight = slice(0, levels)
        self.base = slice(levels, 2 * levels)
        at = 2 * levels
        self.factor, self.index, self.edge = at, at + n, at + 2 * n
        self.total = at + 2 * n + EXTRA


def static_kernel(band, pos_ref, lev_ref, counts_ref, static_ref, diag_ref, off_ref, obs_ref, innov_ref, src_ref, weight_ref, tgt_ref,
                  *out_refs):
    levels, cols = static_ref.shape
    n = len(out_refs)
    cap = src_ref.shape[2]
    rows = Rows(levels, n)
    peers = [pos_ref[0] ^ relabel(r, n, lev_ref[0]) for r in range(n)]
    static, off, obs = static_ref[...], off_ref[...], obs_ref[...]
    lane = lax.broadcasted_iota(jnp.int32, (levels, cols), 1)
    left = jnp.where(lane == 0, 0.0, pltpu.roll(static, 1, 1))
    right = jnp.where(lane == cols - 1, 0.0, pltpu.roll(static, cols - 1, 1))
    base = diag_ref[...] * static + off * (left + right) - innov_ref[...]
    coupled = off * obs
    ends = [v[:, i] for v in (static, coupled, base) for i in (slice(cols - 1, cols), slice(0, 1))]
    edge = sum(column_as_row(end, None, i * levels) for i, end in enumerate(ends))
    place = lax.broadcasted_iota(jnp.int32, (1, cap), 1)
    edge = edge + jnp.where(place == 6 * levels, off[:, cols - 1 :], 0.0)
    edge = edge + jnp.where(place == 6 * levels + 1, off[:, :1], 0.0)
    edge = jnp.broadcast_to(edge, (EXTRA, cap))
    both = jnp.concatenate(halves(jnp.concatenate([obs, base], axis=0)), axis=0)
    tgts = [tgt_ref[0, pl.ds(peer, 1), :] for peer in peers]
    src = jnp.concatenate([src_ref[0, pl.ds(peer, 1), :] for peer in peers], axis=0).astype(F32)
    index = jnp.concatenate(tgts, axis=0).astype(F32) * float(band) + src
    factor = jnp.concatenate([factor_of(counts_ref, weight_ref, peer) for peer in peers], axis=0)
    for r, out_ref in enumerate(out_refs):
        picked = product(both, one_hot(tgts[r], cols))
        out_ref[: 2 * levels, :] = picked[: 2 * levels] + picked[2 * levels :]
        out_ref[rows.factor : rows.factor + n, :] = factor
        out_ref[rows.index : rows.index + n, :] = index
        out_ref[rows.edge :, :] = edge


def other_kernel(lev_ref, perturb_ref, other_ref, loc_ref, out_ref):
    levels = perturb_ref.shape[0]
    weights = spread(loc_ref[...], (1 - lev_ref[0]) * levels, levels)
    out_ref[...] = mixed_sum(weights, perturb_ref, other_ref)


def add_kernel(a_ref, b_ref, out_ref):
    out_ref[...] = a_ref[...] + b_ref[...]


def blocks_kernel(groups, *refs):
    sums = refs[:groups]
    count = (len(refs) - groups - 1) // 2
    rests = refs[groups : groups + count]
    total_ref = refs[groups + count]
    out_refs = refs[groups + count + 1 :]
    total = sum(ref[...] for ref in sums)
    cap = total_ref.shape[1]
    total = jnp.concatenate([total[:, at : at + cap] for at in range(0, total.shape[1], cap)], axis=0)
    total_ref[...] = total
    for rest_ref, out_ref in zip(rests, out_refs):
        out_ref[: total.shape[0], :] = total
        out_ref[total.shape[0] :, :] = rest_ref[...]


class Block:
    def __init__(self, refs, n, levels, band):
        cap = refs[0].shape[1]
        self.levels, self.parts, self.cap = levels, band // cap, cap
        self.sums_ref, self.rest_ref = refs[0], refs[-1]
        self.head = 0 if len(refs) == 2 else self.parts * levels
        self.rows = Rows(levels, n)
        words = self.rest(self.rows.index, n)
        self.tgt = jnp.floor((words + 0.5) * (1.0 / band))
        self.src = words - self.tgt * float(band)
        self.factor = self.rest(self.rows.factor, n)

    def rest(self, at, size):
        return self.rest_ref[self.head + at : self.head + at + size, :]

    def sums(self):
        parts = [self.sums_ref[i * self.levels : (i + 1) * self.levels, :] for i in range(self.parts)]
        return jnp.concatenate(halves(jnp.concatenate(parts, axis=1)), axis=0)


def line(table, i):
    return table[i : i + 1]


def pick_source(block, r):
    band = block.parts * block.cap
    column = lax.broadcasted_iota(jnp.int32, (band, block.cap), 0).astype(F32)
    return jnp.where(column == line(block.src, r), 1.0, 0.0).astype(BF16)


def fill_slots(bands, blocks, n, slots_ref):
    for i, s in enumerate(bands):
        block = blocks[s]
        both = block.sums()
        for d in range(n):
            picked = product(both, pick_source(block, s ^ d))
            values = (picked[: block.levels] + picked[block.levels :]) * line(block.factor, s ^ d)
            slots_ref[d, :, i * block.cap : (i + 1) * block.cap] = jnp.concatenate(halves(values), axis=0)


def met_at(d, block, bands, slots_ref):
    own = jnp.broadcast_to(line(block.tgt, d), (block.cap, block.cap)).T
    same = [jnp.where(own == line(block.tgt, s ^ d), 1.0, 0.0).astype(BF16) for s in bands]
    met = product(slots_ref[d], jnp.concatenate(same, axis=1), ((1,), (1,)))
    return met[: block.levels] + met[block.levels :]


def land(table, bands, slots_ref, cols):
    cap = table.shape[1]
    row = lax.broadcasted_iota(jnp.int32, (cols, cap), 0).astype(F32)
    total = 0.0
    for i, s in enumerate(bands):
        landing = jnp.where(row == line(table, s), 1.0, 0.0).astype(BF16)
        total = total + product(slots_ref[0, :, i * cap : (i + 1) * cap], landing, ((1,), (1,)))
    levels = total.shape[0] // 2
    return total[:levels] + total[levels:]


def open_blocks(labels, refs, n, levels, band):
    blocks = {0: Block(refs[:2], n, levels, band)}
    refs = refs[2:]
    for i, r in enumerate(labels[1:]):
        blocks[r] = Block(refs[i : i + 1], n, levels, band)
    return blocks, refs[len(labels) - 1 :]


def stage_kernel(n, levels, band, cols, stages, *refs):
    known = sum(stages[:-1], [])
    blocks, refs = open_blocks(known + stages[-1], refs, n, levels, band)
    old, refs = refs[: len(stages) - 1], refs[len(stages) - 1 :]
    if known:
        met_old, remap_old, slots_ref, met_ref, remap_ref = refs
    else:
        slots_ref, met_ref, remap_ref, pick_ref = refs
        for d in range(n):
            pick_ref[d] = pick_source(blocks[0], d)
    fill_slots(stages[-1], blocks, n, slots_ref)
    for i, (d, block) in enumerate(blocks.items()):
        met = met_at(d, block, stages[-1], slots_ref)
        if d in known:
            met = met + met_old[i]
        else:
            for bands, ref in zip(stages, old):
                met = met + met_at(d, block, bands, ref)
        met_ref[i] = met
    landed = land(blocks[0].tgt, stages[-1], slots_ref, cols)
    remap_ref[...] = landed + remap_old[...] if known else landed


def shared_kernel(n, cols, stages, pos_ref, lev_ref, loc_ref, *refs):
    levels = loc_ref.shape[0]
    band = refs[-3].shape[1] - 128
    known = sum(stages[:-1], [])
    blocks, refs = open_blocks(known + stages[-1], refs, n, levels, band)
    old, refs = refs[: len(stages) - 1], refs[len(stages) - 1 :]
    met_old, pick_ref, out_ref, slots_ref, tables_ref = refs
    me = pos_ref[0]
    for r, block in blocks.items():
        there = me ^ relabel(r, n, lev_ref[0])
        tables_ref[there, :n, :] = block.tgt
        tables_ref[there, n:, :] = block.rest(block.rows.edge, EXTRA)
    fill_slots(stages[-1], blocks, n, slots_ref)
    last = cols - 1.0
    total = jnp.zeros((levels, band), F32)
    for i, (d, block) in enumerate(blocks.items()):
        value = met_at(d, block, stages[-1], slots_ref) + block.rest(levels, levels)
        if d in known:
            value = value + met_old[i]
        else:
            for bands, ref in zip(stages, old):
                value = value + met_at(d, block, bands, ref)
        edge = block.rest(block.rows.edge, 1)
        own = line(block.tgt, d)
        there = me ^ relabel(d, n, lev_ref[0])
        before = tables_ref[jnp.maximum(there - 1, 0), n : n + 1, :]
        near = jnp.where((own == 0.0) & (there > 0), edge[:, 6 * levels + 1 : 6 * levels + 2], 0.0)
        value = value + row_as_column(before, levels, 0) * near
        after = tables_ref[jnp.minimum(there + 1, n - 1), n : n + 1, :]
        near = jnp.where((own == last) & (there < n - 1), edge[:, 6 * levels : 6 * levels + 1], 0.0)
        value = value + row_as_column(after, levels, levels) * near
        given = block.rest(0, levels) * value * line(blocks[0].factor, d)
        total = total + select(given, pick_ref[d], ((1,), (1,)))
    out_ref[:, :band] = total
    out_ref[:, band:] = jnp.concatenate([loc_ref[...], jnp.zeros((levels, 128 - loc_ref.shape[1]), F32)], axis=1)


def outputs_kernel(stages, pos_ref, lev_ref, *refs):
    slots_refs, refs = refs[: len(stages)], refs[len(stages) :]
    remap_ref, tables_ref, static_ref, diag_ref, off_ref, obs_ref, innov_ref, increment_ref, grad_ref = refs
    levels, cols = static_ref.shape
    n = tables_ref.shape[0]
    cap = tables_ref.shape[2]
    me = pos_ref[0]
    given = [
        (s, ref, slice(i * cap, (i + 1) * cap)) for bands, ref in zip(stages, slots_refs) for i, s in enumerate(bands)
    ]
    remapped = remap_ref[...] + land(tables_ref[me, :n, :], stages[-1], slots_refs[-1], cols)
    static, off = static_ref[...], off_ref[...]
    lane = lax.broadcasted_iota(jnp.int32, (levels, cols), 1)

    def beside(there, exists, column, own_end, side):
        edge = tables_ref[there, n : n + 1, :]
        static_end, coupling, base = (row_as_column(edge, levels, (2 * i + side) * levels) for i in range(3))
        far = relabel(me ^ there, n, lev_ref[0])
        landed = []
        for s, ref, place in given:
            values = ref[far, :levels, place].astype(F32) + ref[far, levels:, place].astype(F32)
            landed.append(jnp.where(tables_ref[there, pl.ds(s ^ far, 1), :] == column, values, 0.0))
        remap_end = jnp.sum(sum(landed), axis=1, keepdims=True)
        off_end = edge[:, 6 * levels + side : 6 * levels + side + 1]
        coupled = coupling * (remap_end + base + off_end * own_end)
        return jnp.where(exists, static_end, 0.0), jnp.where(exists, coupled, 0.0)

    before, coupled_before = beside(jnp.maximum(me - 1, 0), me > 0, cols - 1.0, static[:, :1], 0)
    after, coupled_after = beside(jnp.minimum(me + 1, n - 1), me < n - 1, 0.0, static[:, cols - 1 :], 1)
    left = jnp.where(lane == 0, before, pltpu.roll(static, 1, 1))
    right = jnp.where(lane == cols - 1, after, pltpu.roll(static, cols - 1, 1))
    increment = remapped + diag_ref[...] * static + off * (left + right)
    increment_ref[...] = increment
    misfit = obs_ref[...] * (increment - innov_ref[...])
    coupled = off * misfit
    left = jnp.where(lane == 0, coupled_before, pltpu.roll(coupled, 1, 1))
    right = jnp.where(lane == cols - 1, coupled_after, pltpu.roll(coupled, cols - 1, 1))
    grad_ref[...] = static + diag_ref[...] * misfit + left + right


def call(kernel, out_shape, spaces, scratch=(), limit=40 * MIB, out=VMEM):
    return pl.pallas_call(
        kernel,
        out_shape=out_shape,
        in_specs=spaces,
        out_specs=jax.tree.map(lambda _: out, out_shape),
        scratch_shapes=scratch,
        compiler_params=pltpu.CompilerParams(vmem_limit_bytes=limit),
    )


def body(
    perturb,
    control,
    level_loc,
    static_control,
    filter_diag,
    filter_off,
    send_src,
    send_wt,
    counts,
    recv_tgt,
    obs_weight,
    innovation,
):
    levels, members, band_cols = control.shape
    tile_cols = static_control.shape[1]
    n = lax.axis_size("tile")
    groups = lax.axis_size("grp")
    cap = send_src.shape[2]
    shape = jax.ShapeDtypeStruct
    swap = [(0, 1), (1, 0)]
    lev = lax.axis_index("lev").astype(jnp.int32).reshape(1)
    pos = lax.axis_index("tile").astype(jnp.int32).reshape(1)
    other_control = lax.ppermute(control, "lev", swap)
    other_perturb = lax.ppermute(perturb, "lev", swap)
    part = call(
        own_kernel,
        shape((levels, band_cols), F32),
        [SMEM] + [HBM] * 3,
        [pltpu.VMEM(a.shape, a.dtype) for a in (perturb, control, level_loc)] + [pltpu.SemaphoreType.DMA((3,))],
        limit=58 * MIB,
    )(lev, perturb, control, level_loc)
    flat = shape((levels, tile_cols), F32)
    mine_shape = shape((levels, band_cols + 128), F32)
    diag, off = filter_diag.reshape(1, -1), filter_off.reshape(1, -1)
    if n * cap <= tile_cols and n >= 8 and lax.axis_size("lev") == 2 and n & (n - 1) == 0 and band_cols * tile_cols <= 2**20:
        rows = Rows(levels, n)
        stacked = band_cols // cap * levels
        rests = call(functools.partial(static_kernel, band_cols), [shape((rows.total, cap), F32)] * n, [SMEM] * 3 + [VMEM] * 8)(
            pos, lev, counts, static_control, diag, off, obs_weight, innovation, send_src, send_wt, recv_tgt
        )
        other_part = call(other_kernel, shape((levels, band_cols), F32), [SMEM] + [VMEM] * 3)(
            lev, perturb, other_control, level_loc
        )
        sums = [call(add_kernel, shape((levels, band_cols), F32), [VMEM] * 2)(part, other_part)]
        sums[0], other_perturb = lax.optimization_barrier((sums[0], other_perturb))
        for k in range(1, groups):
            sums.append(lax.ppermute(sums[0], "grp", [(g, (g + k) % groups) for g in range(groups)]))
        total, *blocks = call(
            functools.partial(blocks_kernel, groups),
            [shape((stacked, cap), F32)] + [shape((stacked + rows.total, cap), F32)] * (n - 1),
            [VMEM] * (groups + n - 1),
        )(*sums, *rests[1:])
        low, high = n // 4, n // 2
        both_far = [high + low + i for i in range(low)]
        mixed = [r for i in reversed(range(low)) for r in (high + i, low + i)]
        stages = [[0] + both_far + mixed[:low], mixed[low:], list(range(1, low))]
        levs = lax.axis_size("lev")
        arrived = {0: [total, rests[0]]}
        for r in sum(stages, [])[1:]:
            pairs = [(i * levs + v, (i ^ relabel(r, n, v)) * levs + v) for i in range(n) for v in range(levs)]
            arrived[r] = [lax.ppermute(blocks[r - 1], ("tile", "lev"), pairs)]
        slots, carried, picks = [], [], []
        for count in range(1, len(stages)):
            labels = sum(stages[:count], [])
            refs = [ref for r in labels for ref in arrived[r]]
            outs = [
                shape((n, 2 * levels, len(stages[count - 1]) * cap), BF16),
                shape((len(labels), levels, cap), F32),
                flat,
            ] + [shape((n, band_cols, cap), BF16)] * (count == 1)
            new, *carried = call(
                functools.partial(stage_kernel, n, levels, band_cols, tile_cols, stages[:count]),
                outs,
                [VMEM] * (len(refs) + len(slots) + len(carried)),
            )(*refs, *slots, *carried)
            slots.append(new)
            picks += carried[2:]
            carried = carried[:2]
        met, remap = carried
        refs = [ref for r in sum(stages, []) for ref in arrived[r]] + slots + [met] + picks
        mine, new, tables = call(
            functools.partial(shared_kernel, n, tile_cols, stages),
            (mine_shape, shape((n, 2 * levels, len(stages[-1]) * cap), BF16), shape((n, n + EXTRA, cap), F32)),
            [SMEM] * 2 + [VMEM] * (1 + len(refs)),
        )(pos, lev, level_loc, *refs)
        slots.append(new)
        increment, grad_static = call(
            functools.partial(outputs_kernel, stages), (flat, flat), [SMEM] * 2 + [VMEM] * (len(slots) + 7)
        )(pos, lev, *slots, remap, tables, static_control, diag, off, obs_weight, innovation)
    else:
        payload = call(
            band_kernel,
            shape((groups, n, levels + EXTRA, cap), F32),
            [SMEM] * 2 + [VMEM] * 7,
            [pltpu.VMEM((2 * levels, band_cols), BF16)],
        )(lev, counts, perturb, other_control, part, level_loc, static_control, send_src, send_wt)
        arrived = lax.all_to_all(
            payload.reshape(groups * n, levels + EXTRA, cap), ("grp", "tile"), split_axis=0, concat_axis=0, tiled=True
        ).reshape(groups, n, levels + EXTRA, cap)
        increment, partial, giving = call(
            tile_kernel, (flat, flat, shape((n, levels + EXTRA, cap), F32)), [SMEM] + [VMEM] * 7
        )(pos, arrived, recv_tgt, static_control, diag, off, obs_weight, innovation)
        returned = lax.all_to_all(giving, "tile", split_axis=0, concat_axis=0, tiled=True)
        grad_static, mine = call(adjoint_kernel, (flat, mine_shape), [SMEM, SMEM] + [VMEM] * 5)(
            pos, counts, returned, send_src, send_wt, partial, level_loc
        )
    theirs = lax.ppermute(mine, "lev", swap)
    grad_ens = call(
        ens_kernel,
        shape(control.shape, F32),
        [SMEM] + [VMEM] * 5,
        [pltpu.VMEM(control.shape, F32), pltpu.SemaphoreType.DMA((members // SUB,))],
        out=HBM,
    )(
        lev, perturb, other_perturb, control, mine, theirs
    )
    return (increment, grad_static, grad_ens)


def solution(mesh):
    return jax.shard_map(
        body,
        mesh=mesh,
        in_specs=(
            P("lev", "grp", "tile"),
            P("lev", "grp", "tile"),
            P("lev", None),
            P("lev", "tile"),
            P("tile"),
            P("tile"),
            P("tile", None, None),
            P("tile", None, None),
            P("tile", None),
            P("tile", None, None),
            P("lev", "tile"),
            P("lev", "tile"),
        ),
        out_specs=(P("lev", "tile"), P("lev", "tile"), P("lev", "grp", "tile")),
        check_vma=False,
    )
```

```python
import functools

import jax
import jax.numpy as jnp
from jax import lax
from jax.experimental import pallas as pl
from jax.experimental.pallas import tpu as pltpu
from jax.sharding import PartitionSpec as P

F32 = jnp.float32
BF16 = jnp.bfloat16
SUB = 8
EXTRA = 8
VMEM = pl.BlockSpec(memory_space=pltpu.VMEM)
HBM = pl.BlockSpec(memory_space=pltpu.HBM)
SMEM = pl.BlockSpec(memory_space=pltpu.SMEM)
MIB = 1024 * 1024


def halves(values):
    high = values.astype(BF16)
    low = (values - high.astype(F32)).astype(BF16)
    return high, low


def product(a, b, dims=((1,), (0,))):
    return lax.dot_general(a, b, (dims, ((), ())), preferred_element_type=F32)


def select(values, chosen, dims=((1,), (0,))):
    rows = values.shape[0]
    both = product(jnp.concatenate(halves(values), axis=0), chosen, dims)
    return both[:rows] + both[rows:]


def spread(matrix, start, count):
    rows, cols = matrix.shape

    def iota(shape, axis):
        return lax.broadcasted_iota(jnp.int32, shape, axis)

    shape = (rows * SUB, count * SUB)
    tall = (iota((rows * SUB, rows), 0) // SUB == iota((rows * SUB, rows), 1)).astype(BF16)
    wide = (iota((cols, count * SUB), 1) // SUB + start == iota((cols, count * SUB), 0)).astype(BF16)
    same = iota(shape, 0) % SUB == iota(shape, 1) % SUB
    out = []
    for part in halves(matrix):
        filled = product(tall, product(part, wide).astype(BF16))
        out.append(jnp.where(same, filled, 0.0).astype(BF16))
    return out


def mix(weights, values):
    high, low = halves(values)
    rows = weights[0].shape[0]
    both = product(jnp.concatenate(weights, axis=0), high)
    return both[:rows] + (product(weights[0], low) + both[rows:])


def one_hot(index, size):
    rows = lax.broadcasted_iota(jnp.int32, (size, index.shape[1]), 0)
    return jnp.where(rows == index, 1.0, 0.0).astype(BF16)


def column_as_row(column, lane, offset):
    n = column.shape[0]
    place = lax.broadcasted_iota(jnp.int32, (n, 128), 1) == lax.broadcasted_iota(jnp.int32, (n, 128), 0) + offset
    return jnp.sum(jnp.where(place, column, 0.0), axis=0, keepdims=True)


def row_as_column(row, n, offset):
    place = lax.broadcasted_iota(jnp.int32, (n, 128), 1) == lax.broadcasted_iota(jnp.int32, (n, 128), 0) + offset
    return jnp.sum(jnp.where(place, row, 0.0), axis=1, keepdims=True)


def edge_rows(values):
    n = values.shape[0]
    row = column_as_row(values[:, -1:], None, 0) + column_as_row(values[:, :1], None, n)
    return jnp.broadcast_to(row, (EXTRA, 128))


def factor_of(counts_ref, weight_ref, d):
    slot = lax.broadcasted_iota(jnp.int32, (1, weight_ref.shape[2]), 1)
    return jnp.where(slot < counts_ref[0, d], weight_ref[0, pl.ds(d, 1), :], 0.0)


def loop(n, step, init):
    return lax.fori_loop(0, n, step, init, unroll=n if n <= 8 else 1)


def own_kernel(lev_ref, perturb_hbm, control_hbm, loc_hbm, part_ref, perturb_ref, control_ref, loc_ref, sems):
    staged = [(loc_hbm, loc_ref), (control_hbm, control_ref), (perturb_hbm, perturb_ref)]
    copies = [pltpu.make_async_copy(source, target, sems.at[i]) for i, (source, target) in enumerate(staged)]
    for copy in copies:
        copy.start()
    levels = perturb_ref.shape[0]
    copies[0].wait()
    weights = spread(loc_ref[...], lev_ref[0] * levels, levels)
    copies[1].wait()
    copies[2].wait()
    part_ref[...] = mixed_sum(weights, perturb_ref, control_ref)


def mixed_sum(weights, perturb_ref, control_ref):
    levels, members, cols = perturb_ref.shape
    perturb = perturb_ref[...].astype(F32)
    total = jnp.zeros((levels, SUB, cols), F32)
    for m in range(0, members, SUB):
        tile = control_ref[:, m : m + SUB, :].reshape(levels * SUB, cols)
        total = total + perturb[:, m : m + SUB, :] * mix(weights, tile).reshape(levels, SUB, cols)
    return jnp.sum(total, axis=1)


def band_kernel(lev_ref, counts_ref, perturb_ref, other_ref, part_ref, loc_ref, static_ref, src_ref, weight_ref,
                out_ref, acc_ref):
    levels, members, cols = perturb_ref.shape
    weights = spread(loc_ref[...], (1 - lev_ref[0]) * levels, levels)
    band_sum = part_ref[...] + mixed_sum(weights, perturb_ref, other_ref)
    acc_ref[...] = jnp.concatenate(halves(band_sum), axis=0)
    n = src_ref.shape[1]
    edges = edge_rows(static_ref[...])

    def step(d, carry):
        chosen = one_hot(src_ref[0, pl.ds(d, 1), :], cols)
        both = product(acc_ref[...], chosen)
        payload = (both[:levels] + both[levels:]) * factor_of(counts_ref, weight_ref, d)
        for g in range(out_ref.shape[0]):
            out_ref[g, d, :levels, :] = payload
            out_ref[g, d, levels:, :] = edges
        return carry

    loop(n, step, 0)


def tile_kernel(pos_ref, arrived_ref, tgt_ref, static_ref, diag_ref, off_ref, obs_ref, innov_ref,
                increment_ref, partial_ref, out_ref):
    levels, cols = static_ref.shape
    groups, n = arrived_ref.shape[:2]
    me = pos_ref[0]

    def step(s, total):
        values = sum(arrived_ref[g, s, :levels, :] for g in range(groups))
        chosen = one_hot(tgt_ref[0, pl.ds(s, 1), :], cols)
        return total + select(values, chosen, ((1,), (1,)))

    remapped = loop(n, step, jnp.zeros((levels, cols), F32))
    before = arrived_ref[0, jnp.maximum(me - 1, 0), levels : levels + 1, :]
    after = arrived_ref[0, jnp.minimum(me + 1, n - 1), levels : levels + 1, :]
    before = jnp.where(me > 0, row_as_column(before, levels, 0), 0.0)
    after = jnp.where(me < n - 1, row_as_column(after, levels, levels), 0.0)
    static = static_ref[...]
    lane = lax.broadcasted_iota(jnp.int32, (levels, cols), 1)
    left = jnp.where(lane == 0, before, pltpu.roll(static, 1, 1))
    right = jnp.where(lane == cols - 1, after, pltpu.roll(static, cols - 1, 1))
    increment = remapped + diag_ref[...] * static + off_ref[...] * (left + right)
    increment_ref[...] = increment
    misfit = obs_ref[...] * (increment - innov_ref[...])
    coupled = off_ref[...] * misfit
    left = jnp.where(lane == 0, 0.0, pltpu.roll(coupled, 1, 1))
    right = jnp.where(lane == cols - 1, 0.0, pltpu.roll(coupled, cols - 1, 1))
    partial_ref[...] = static + diag_ref[...] * misfit + left + right
    edges = edge_rows(coupled)
    both = jnp.concatenate(halves(misfit), axis=0)

    def give(s, carry):
        chosen = one_hot(tgt_ref[0, pl.ds(s, 1), :], cols)
        picked = product(both, chosen)
        out_ref[s, :levels, :] = picked[:levels] + picked[levels:]
        out_ref[s, levels:, :] = edges
        return carry

    loop(n, give, 0)


def adjoint_kernel(pos_ref, counts_ref, returned_ref, src_ref, weight_ref, partial_ref, loc_ref, grad_ref, out_ref):
    levels, cols = partial_ref.shape
    n = returned_ref.shape[0]
    band = out_ref.shape[1] - 128
    me = pos_ref[0]

    def step(d, total):
        values = returned_ref[d, :levels, :] * factor_of(counts_ref, weight_ref, d)
        return total + select(values, one_hot(src_ref[0, pl.ds(d, 1), :], band), ((1,), (1,)))

    out_ref[:, :band] = loop(n, step, jnp.zeros((levels, band), F32))
    out_ref[:, band:] = jnp.concatenate([loc_ref[...], jnp.zeros((levels, 128 - loc_ref.shape[1]), F32)], axis=1)
    before = returned_ref[jnp.maximum(me - 1, 0), levels : levels + 1, :]
    after = returned_ref[jnp.minimum(me + 1, n - 1), levels : levels + 1, :]
    before = jnp.where(me > 0, row_as_column(before, levels, 0), 0.0)
    after = jnp.where(me < n - 1, row_as_column(after, levels, levels), 0.0)
    lane = lax.broadcasted_iota(jnp.int32, (levels, cols), 1)
    grad_ref[...] = partial_ref[...] + (jnp.where(lane == 0, before, 0.0) + jnp.where(lane == cols - 1, after, 0.0))


def ens_weights(loc, start, count):
    full = loc.shape[0]

    def iota(shape, axis):
        return lax.broadcasted_iota(jnp.int32, shape, axis)

    shape = (count * SUB, full * SUB)
    pick_l = (iota((count * SUB, loc.shape[1]), 0) // SUB + start == iota((count * SUB, loc.shape[1]), 1)).astype(BF16)
    pick_k = (iota((full, full * SUB), 1) // SUB == iota((full, full * SUB), 0)).astype(BF16)
    same = iota(shape, 0) % SUB == iota(shape, 1) % SUB
    weights = []
    for part in halves(loc):
        wide = product(product(pick_l, part, ((1,), (1,))).astype(BF16), pick_k)
        weights.append(jnp.where(same, wide, 0.0).astype(BF16))
    return weights


def ens_tiles(lev_ref, perturb_ref, band_ref, before_ref):
    levels, members, cols = perturb_ref.shape
    band = band_ref[...]
    weights = ens_weights(band[:, cols : cols + 2 * levels], lev_ref[0] * levels, levels)
    grad = band[:, :cols][:, None, :]
    perturb = perturb_ref[...].astype(F32)
    for m in range(0, members, SUB):
        place = (slice(None), slice(m, m + SUB), slice(None))
        tile = (perturb[place] * grad).reshape(levels * SUB, cols)
        yield place, before_ref[place] + mix(weights, tile).reshape(levels, SUB, cols)


def ens_own_kernel(lev_ref, perturb_ref, mine_ref, control_ref, out_ref):
    for place, values in ens_tiles(lev_ref, perturb_ref, mine_ref, control_ref):
        out_ref[place] = values


def ens_kernel(lev_ref, perturb_ref, theirs_ref, own_ref, *refs):
    count = (len(refs) - 3) // 2
    flats, (out_hbm, *flat_hbms), (out_ref, sems) = refs[:count], refs[count : 2 * count + 1], refs[2 * count + 1 :]
    copies = [pltpu.make_async_copy(a, b, sems.at[i]) for i, (a, b) in enumerate(zip(flats, flat_hbms))]
    for copy in copies:
        copy.start()
    for place, values in ens_tiles(lev_ref, perturb_ref, theirs_ref, own_ref):
        out_ref[place] = values
        copies.append(pltpu.make_async_copy(out_ref.at[place], out_hbm.at[place], sems.at[len(copies)]))
        copies[-1].start()
    for copy in copies:
        copy.wait()


def relabel(r, n, lev):
    high, low = n // 2, n // 4
    if low == 0:
        return r
    both = high | low
    turned = (r & ~both) | ((r & low) << 1) | ((r & high) >> 1)
    return r + (turned - r) * lev


class Rows:
    def __init__(self, levels, n):
        self.weight = slice(0, levels)
        self.base = slice(levels, 2 * levels)
        at = 2 * levels
        self.factor, self.index, self.edge = at, at + n, at + 2 * n
        self.total = at + 2 * n + EXTRA


def static_kernel(band, pos_ref, lev_ref, counts_ref, static_ref, diag_ref, off_ref, obs_ref, innov_ref, src_ref, weight_ref, tgt_ref,
                  *out_refs):
    levels, cols = static_ref.shape
    n = len(out_refs)
    cap = src_ref.shape[2]
    rows = Rows(levels, n)
    peers = [pos_ref[0] ^ relabel(r, n, lev_ref[0]) for r in range(n)]
    static, off, obs = static_ref[...], off_ref[...], obs_ref[...]
    lane = lax.broadcasted_iota(jnp.int32, (levels, cols), 1)
    left = jnp.where(lane == 0, 0.0, pltpu.roll(static, 1, 1))
    right = jnp.where(lane == cols - 1, 0.0, pltpu.roll(static, cols - 1, 1))
    base = diag_ref[...] * static + off * (left + right) - innov_ref[...]
    coupled = off * obs
    ends = [v[:, i] for v in (static, coupled, base) for i in (slice(cols - 1, cols), slice(0, 1))]
    edge = sum(column_as_row(end, None, i * levels) for i, end in enumerate(ends))
    place = lax.broadcasted_iota(jnp.int32, (1, cap), 1)
    edge = edge + jnp.where(place == 6 * levels, off[:, cols - 1 :], 0.0)
    edge = edge + jnp.where(place == 6 * levels + 1, off[:, :1], 0.0)
    edge = jnp.broadcast_to(edge, (EXTRA, cap))
    both = jnp.concatenate(halves(jnp.concatenate([obs, base], axis=0)), axis=0)
    tgts = [tgt_ref[0, pl.ds(peer, 1), :] for peer in peers]
    src = jnp.concatenate([src_ref[0, pl.ds(peer, 1), :] for peer in peers], axis=0).astype(F32)
    index = jnp.concatenate(tgts, axis=0).astype(F32) * float(band) + src
    factor = jnp.concatenate([factor_of(counts_ref, weight_ref, peer) for peer in peers], axis=0)
    for r, out_ref in enumerate(out_refs):
        picked = product(both, one_hot(tgts[r], cols))
        out_ref[: 2 * levels, :] = picked[: 2 * levels] + picked[2 * levels :]
        out_ref[rows.factor : rows.factor + n, :] = factor
        out_ref[rows.index : rows.index + n, :] = index
        out_ref[rows.edge :, :] = edge


def other_kernel(lev_ref, perturb_ref, other_ref, loc_ref, out_ref):
    levels = perturb_ref.shape[0]
    weights = spread(loc_ref[...], (1 - lev_ref[0]) * levels, levels)
    out_ref[...] = mixed_sum(weights, perturb_ref, other_ref)


def add_kernel(a_ref, b_ref, out_ref):
    out_ref[...] = a_ref[...] + b_ref[...]


def blocks_kernel(groups, *refs):
    sums = refs[:groups]
    count = (len(refs) - groups - 1) // 2
    rests = refs[groups : groups + count]
    total_ref = refs[groups + count]
    out_refs = refs[groups + count + 1 :]
    total = sum(ref[...] for ref in sums)
    cap = total_ref.shape[1]
    total = jnp.concatenate([total[:, at : at + cap] for at in range(0, total.shape[1], cap)], axis=0)
    total_ref[...] = total
    for rest_ref, out_ref in zip(rests, out_refs):
        out_ref[: total.shape[0], :] = total
        out_ref[total.shape[0] :, :] = rest_ref[...]


class Block:
    def __init__(self, refs, n, levels, band):
        cap = refs[0].shape[1]
        self.levels, self.parts, self.cap = levels, band // cap, cap
        self.sums_ref, self.rest_ref = refs[0], refs[-1]
        self.head = 0 if len(refs) == 2 else self.parts * levels
        self.rows = Rows(levels, n)
        words = self.rest(self.rows.index, n)
        self.tgt = jnp.floor((words + 0.5) * (1.0 / band))
        self.src = words - self.tgt * float(band)
        self.factor = self.rest(self.rows.factor, n)

    def rest(self, at, size):
        return self.rest_ref[self.head + at : self.head + at + size, :]

    def sums(self):
        parts = [self.sums_ref[i * self.levels : (i + 1) * self.levels, :] for i in range(self.parts)]
        return jnp.concatenate(halves(jnp.concatenate(parts, axis=1)), axis=0)


def line(table, i):
    return table[i : i + 1]


def pick_source(block, r):
    band = block.parts * block.cap
    column = lax.broadcasted_iota(jnp.int32, (band, block.cap), 0).astype(F32)
    return jnp.where(column == line(block.src, r), 1.0, 0.0).astype(BF16)


def fill_slots(bands, blocks, n, slots_ref):
    for i, s in enumerate(bands):
        block = blocks[s]
        both = block.sums()
        for d in range(n):
            picked = product(both, pick_source(block, s ^ d))
            values = (picked[: block.levels] + picked[block.levels :]) * line(block.factor, s ^ d)
            slots_ref[d, :, i * block.cap : (i + 1) * block.cap] = jnp.concatenate(halves(values), axis=0)


def met_at(d, block, bands, slots_ref):
    own = jnp.broadcast_to(line(block.tgt, d), (block.cap, block.cap)).T
    same = [jnp.where(own == line(block.tgt, s ^ d), 1.0, 0.0).astype(BF16) for s in bands]
    met = product(slots_ref[d], jnp.concatenate(same, axis=1), ((1,), (1,)))
    return met[: block.levels] + met[block.levels :]


def land(table, bands, slots_ref, cols):
    cap = table.shape[1]
    row = lax.broadcasted_iota(jnp.int32, (cols, cap), 0).astype(F32)
    total = 0.0
    for i, s in enumerate(bands):
        landing = jnp.where(row == line(table, s), 1.0, 0.0).astype(BF16)
        total = total + product(slots_ref[0, :, i * cap : (i + 1) * cap], landing, ((1,), (1,)))
    levels = total.shape[0] // 2
    return total[:levels] + total[levels:]


def open_blocks(labels, refs, n, levels, band):
    blocks = {0: Block(refs[:2], n, levels, band)}
    refs = refs[2:]
    for i, r in enumerate(labels[1:]):
        blocks[r] = Block(refs[i : i + 1], n, levels, band)
    return blocks, refs[len(labels) - 1 :]


def stage_kernel(n, levels, band, cols, stages, *refs):
    known = sum(stages[:-1], [])
    blocks, refs = open_blocks(known + stages[-1], refs, n, levels, band)
    old, refs = refs[: len(stages) - 1], refs[len(stages) - 1 :]
    if known:
        met_old, remap_old, slots_ref, met_ref, remap_ref = refs
    else:
        slots_ref, met_ref, remap_ref, pick_ref = refs
        for d in range(n):
            pick_ref[d] = pick_source(blocks[0], d)
    fill_slots(stages[-1], blocks, n, slots_ref)
    for i, (d, block) in enumerate(blocks.items()):
        met = met_at(d, block, stages[-1], slots_ref)
        if d in known:
            met = met + met_old[i]
        else:
            for bands, ref in zip(stages, old):
                met = met + met_at(d, block, bands, ref)
        met_ref[i] = met
    landed = land(blocks[0].tgt, stages[-1], slots_ref, cols)
    remap_ref[...] = landed + remap_old[...] if known else landed


def shared_kernel(n, cols, stages, pos_ref, lev_ref, loc_ref, *refs):
    levels = loc_ref.shape[0]
    band = refs[-3].shape[1] - 128
    known = sum(stages[:-1], [])
    blocks, refs = open_blocks(known + stages[-1], refs, n, levels, band)
    old, refs = refs[: len(stages) - 1], refs[len(stages) - 1 :]
    met_old, pick_ref, out_ref, slots_ref, tables_ref = refs
    me = pos_ref[0]
    for r, block in blocks.items():
        there = me ^ relabel(r, n, lev_ref[0])
        tables_ref[there, :n, :] = block.tgt
        tables_ref[there, n:, :] = block.rest(block.rows.edge, EXTRA)
    fill_slots(stages[-1], blocks, n, slots_ref)
    last = cols - 1.0
    total = jnp.zeros((levels, band), F32)
    for i, (d, block) in enumerate(blocks.items()):
        value = met_at(d, block, stages[-1], slots_ref) + block.rest(levels, levels)
        if d in known:
            value = value + met_old[i]
        else:
            for bands, ref in zip(stages, old):
                value = value + met_at(d, block, bands, ref)
        edge = block.rest(block.rows.edge, 1)
        own = line(block.tgt, d)
        there = me ^ relabel(d, n, lev_ref[0])
        before = tables_ref[jnp.maximum(there - 1, 0), n : n + 1, :]
        near = jnp.where((own == 0.0) & (there > 0), edge[:, 6 * levels + 1 : 6 * levels + 2], 0.0)
        value = value + row_as_column(before, levels, 0) * near
        after = tables_ref[jnp.minimum(there + 1, n - 1), n : n + 1, :]
        near = jnp.where((own == last) & (there < n - 1), edge[:, 6 * levels : 6 * levels + 1], 0.0)
        value = value + row_as_column(after, levels, levels) * near
        given = block.rest(0, levels) * value * line(blocks[0].factor, d)
        total = total + select(given, pick_ref[d], ((1,), (1,)))
    out_ref[:, :band] = total
    out_ref[:, band:] = jnp.concatenate([loc_ref[...], jnp.zeros((levels, 128 - loc_ref.shape[1]), F32)], axis=1)


def outputs_kernel(stages, pos_ref, lev_ref, *refs):
    slots_refs, refs = refs[: len(stages)], refs[len(stages) :]
    remap_ref, tables_ref, static_ref, diag_ref, off_ref, obs_ref, innov_ref, increment_ref, grad_ref = refs
    levels, cols = static_ref.shape
    n = tables_ref.shape[0]
    cap = tables_ref.shape[2]
    me = pos_ref[0]
    given = [
        (s, ref, slice(i * cap, (i + 1) * cap)) for bands, ref in zip(stages, slots_refs) for i, s in enumerate(bands)
    ]
    remapped = remap_ref[...] + land(tables_ref[me, :n, :], stages[-1], slots_refs[-1], cols)
    static, off = static_ref[...], off_ref[...]
    lane = lax.broadcasted_iota(jnp.int32, (levels, cols), 1)

    def beside(there, exists, column, own_end, side):
        edge = tables_ref[there, n : n + 1, :]
        static_end, coupling, base = (row_as_column(edge, levels, (2 * i + side) * levels) for i in range(3))
        far = relabel(me ^ there, n, lev_ref[0])
        landed = []
        for s, ref, place in given:
            values = ref[far, :levels, place].astype(F32) + ref[far, levels:, place].astype(F32)
            landed.append(jnp.where(tables_ref[there, pl.ds(s ^ far, 1), :] == column, values, 0.0))
        remap_end = jnp.sum(sum(landed), axis=1, keepdims=True)
        off_end = edge[:, 6 * levels + side : 6 * levels + side + 1]
        coupled = coupling * (remap_end + base + off_end * own_end)
        return jnp.where(exists, static_end, 0.0), jnp.where(exists, coupled, 0.0)

    before, coupled_before = beside(jnp.maximum(me - 1, 0), me > 0, cols - 1.0, static[:, :1], 0)
    after, coupled_after = beside(jnp.minimum(me + 1, n - 1), me < n - 1, 0.0, static[:, cols - 1 :], 1)
    left = jnp.where(lane == 0, before, pltpu.roll(static, 1, 1))
    right = jnp.where(lane == cols - 1, after, pltpu.roll(static, cols - 1, 1))
    increment = remapped + diag_ref[...] * static + off * (left + right)
    increment_ref[...] = increment
    misfit = obs_ref[...] * (increment - innov_ref[...])
    coupled = off * misfit
    left = jnp.where(lane == 0, coupled_before, pltpu.roll(coupled, 1, 1))
    right = jnp.where(lane == cols - 1, coupled_after, pltpu.roll(coupled, cols - 1, 1))
    grad_ref[...] = static + diag_ref[...] * misfit + left + right


def call(kernel, out_shape, spaces, scratch=(), limit=40 * MIB, out=VMEM):
    return pl.pallas_call(
        kernel,
        out_shape=out_shape,
        in_specs=spaces,
        out_specs=jax.tree.map(lambda _: out, out_shape),
        scratch_shapes=scratch,
        compiler_params=pltpu.CompilerParams(vmem_limit_bytes=limit),
    )


def body(
    perturb,
    control,
    level_loc,
    static_control,
    filter_diag,
    filter_off,
    send_src,
    send_wt,
    counts,
    recv_tgt,
    obs_weight,
    innovation,
):
    levels, members, band_cols = control.shape
    tile_cols = static_control.shape[1]
    n = lax.axis_size("tile")
    groups = lax.axis_size("grp")
    cap = send_src.shape[2]
    shape = jax.ShapeDtypeStruct
    swap = [(0, 1), (1, 0)]
    lev = lax.axis_index("lev").astype(jnp.int32).reshape(1)
    pos = lax.axis_index("tile").astype(jnp.int32).reshape(1)
    other_control = lax.ppermute(control, "lev", swap)
    part = call(
        own_kernel,
        shape((levels, band_cols), F32),
        [SMEM] + [HBM] * 3,
        [pltpu.VMEM(a.shape, a.dtype) for a in (perturb, control, level_loc)] + [pltpu.SemaphoreType.DMA((3,))],
        limit=58 * MIB,
    )(lev, perturb, control, level_loc)
    flat = shape((levels, tile_cols), F32)
    mine_shape = shape((levels, band_cols + 128), F32)
    diag, off = filter_diag.reshape(1, -1), filter_off.reshape(1, -1)
    if n * cap <= tile_cols and n >= 8 and lax.axis_size("lev") == 2 and n & (n - 1) == 0 and band_cols * tile_cols <= 2**20:
        rows = Rows(levels, n)
        stacked = band_cols // cap * levels
        rests = call(functools.partial(static_kernel, band_cols), [shape((rows.total, cap), F32)] * n, [SMEM] * 3 + [VMEM] * 8)(
            pos, lev, counts, static_control, diag, off, obs_weight, innovation, send_src, send_wt, recv_tgt
        )
        other_part = call(other_kernel, shape((levels, band_cols), F32), [SMEM] + [VMEM] * 3)(
            lev, perturb, other_control, level_loc
        )
        sums = [call(add_kernel, shape((levels, band_cols), F32), [VMEM] * 2)(part, other_part)]
        sums[0], other_perturb = lax.optimization_barrier((sums[0], lax.ppermute(perturb, "lev", swap)))
        for k in range(1, groups):
            sums.append(lax.ppermute(sums[0], "grp", [(g, (g + k) % groups) for g in range(groups)]))
        total, *blocks = call(
            functools.partial(blocks_kernel, groups),
            [shape((stacked, cap), F32)] + [shape((stacked + rows.total, cap), F32)] * (n - 1),
            [VMEM] * (groups + n - 1),
        )(*sums, *rests[1:])
        low, high = n // 4, n // 2
        both_far = [high + low + i for i in range(low)]
        mixed = [high + i for i in reversed(range(low))] + [low + i for i in reversed(range(low))]
        stages = [[0] + both_far + mixed[:low], mixed[low:], list(range(1, low))]
        levs = lax.axis_size("lev")
        arrived = {0: [total, rests[0]]}
        for r in sum(stages, [])[1:]:
            pairs = [(i * levs + v, (i ^ relabel(r, n, v)) * levs + v) for i in range(n) for v in range(levs)]
            arrived[r] = [lax.ppermute(blocks[r - 1], ("tile", "lev"), pairs)]
        slots, carried, picks = [], [], []
        for count in range(1, len(stages)):
            labels = sum(stages[:count], [])
            refs = [ref for r in labels for ref in arrived[r]]
            outs = [
                shape((n, 2 * levels, len(stages[count - 1]) * cap), BF16),
                shape((len(labels), levels, cap), F32),
                flat,
            ] + [shape((n, band_cols, cap), BF16)] * (count == 1)
            new, *carried = call(
                functools.partial(stage_kernel, n, levels, band_cols, tile_cols, stages[:count]),
                outs,
                [VMEM] * (len(refs) + len(slots) + len(carried)),
            )(*refs, *slots, *carried)
            slots.append(new)
            picks += carried[2:]
            carried = carried[:2]
        met, remap = carried
        refs = [ref for r in sum(stages, []) for ref in arrived[r]] + slots + [met] + picks
        mine, new, tables = call(
            functools.partial(shared_kernel, n, tile_cols, stages),
            (mine_shape, shape((n, 2 * levels, len(stages[-1]) * cap), BF16), shape((n, n + EXTRA, cap), F32)),
            [SMEM] * 2 + [VMEM] * (1 + len(refs)),
        )(pos, lev, level_loc, *refs)
        slots.append(new)
        increment, grad_static = call(
            functools.partial(outputs_kernel, stages), (flat, flat), [SMEM] * 2 + [VMEM] * (len(slots) + 7)
        )(pos, lev, *slots, remap, tables, static_control, diag, off, obs_weight, innovation)
    else:
        other_perturb = lax.ppermute(perturb, "lev", swap)
        payload = call(
            band_kernel,
            shape((groups, n, levels + EXTRA, cap), F32),
            [SMEM] * 2 + [VMEM] * 7,
            [pltpu.VMEM((2 * levels, band_cols), BF16)],
        )(lev, counts, perturb, other_control, part, level_loc, static_control, send_src, send_wt)
        arrived = lax.all_to_all(
            payload.reshape(groups * n, levels + EXTRA, cap), ("grp", "tile"), split_axis=0, concat_axis=0, tiled=True
        ).reshape(groups, n, levels + EXTRA, cap)
        increment, partial, giving = call(
            tile_kernel, (flat, flat, shape((n, levels + EXTRA, cap), F32)), [SMEM] + [VMEM] * 7
        )(pos, arrived, recv_tgt, static_control, diag, off, obs_weight, innovation)
        returned = lax.all_to_all(giving, "tile", split_axis=0, concat_axis=0, tiled=True)
        grad_static, mine = call(adjoint_kernel, (flat, mine_shape), [SMEM, SMEM] + [VMEM] * 5)(
            pos, counts, returned, send_src, send_wt, partial, level_loc
        )
    theirs = lax.ppermute(mine, "lev", swap)
    own = call(ens_own_kernel, shape(control.shape, F32), [SMEM] + [VMEM] * 3)(lev, perturb, mine, control)
    grad_ens, increment, grad_static = call(
        ens_kernel,
        (shape(control.shape, F32), flat, flat),
        [SMEM] + [VMEM] * 5,
        [pltpu.VMEM(control.shape, F32), pltpu.SemaphoreType.DMA((2 + members // SUB,))],
        out=HBM,
    )(lev, other_perturb, theirs, own, increment, grad_static)
    return (increment, grad_static, grad_ens)


def solution(mesh):
    return jax.shard_map(
        body,
        mesh=mesh,
        in_specs=(
            P("lev", "grp", "tile"),
            P("lev", "grp", "tile"),
            P("lev", None),
            P("lev", "tile"),
            P("tile"),
            P("tile"),
            P("tile", None, None),
            P("tile", None, None),
            P("tile", None),
            P("tile", None, None),
            P("lev", "tile"),
            P("lev", "tile"),
        ),
        out_specs=(P("lev", "tile"), P("lev", "tile"), P("lev", "grp", "tile")),
        check_vma=False,
    )
```

```python
import functools

import jax
import jax.numpy as jnp
from jax import lax
from jax.experimental import pallas as pl
from jax.experimental.pallas import tpu as pltpu
from jax.sharding import PartitionSpec as P

F32 = jnp.float32
BF16 = jnp.bfloat16
SUB = 8
EXTRA = 8
VMEM = pl.BlockSpec(memory_space=pltpu.VMEM)
HBM = pl.BlockSpec(memory_space=pltpu.HBM)
SMEM = pl.BlockSpec(memory_space=pltpu.SMEM)
MIB = 1024 * 1024


def halves(values):
    high = values.astype(BF16)
    low = (values - high.astype(F32)).astype(BF16)
    return high, low


def product(a, b, dims=((1,), (0,))):
    return lax.dot_general(a, b, (dims, ((), ())), preferred_element_type=F32)


def select(values, chosen, dims=((1,), (0,))):
    rows = values.shape[0]
    both = product(jnp.concatenate(halves(values), axis=0), chosen, dims)
    return both[:rows] + both[rows:]


def spread(matrix, start, count):
    rows, cols = matrix.shape

    def iota(shape, axis):
        return lax.broadcasted_iota(jnp.int32, shape, axis)

    shape = (rows * SUB, count * SUB)
    tall = (iota((rows * SUB, rows), 0) // SUB == iota((rows * SUB, rows), 1)).astype(BF16)
    wide = (iota((cols, count * SUB), 1) // SUB + start == iota((cols, count * SUB), 0)).astype(BF16)
    same = iota(shape, 0) % SUB == iota(shape, 1) % SUB
    out = []
    for part in halves(matrix):
        filled = product(tall, product(part, wide).astype(BF16))
        out.append(jnp.where(same, filled, 0.0).astype(BF16))
    return out


def mix(weights, values):
    high, low = halves(values)
    rows = weights[0].shape[0]
    both = product(jnp.concatenate(weights, axis=0), high)
    return both[:rows] + (product(weights[0], low) + both[rows:])


def one_hot(index, size):
    rows = lax.broadcasted_iota(jnp.int32, (size, index.shape[1]), 0)
    return jnp.where(rows == index, 1.0, 0.0).astype(BF16)


def column_as_row(column, lane, offset):
    n = column.shape[0]
    place = lax.broadcasted_iota(jnp.int32, (n, 128), 1) == lax.broadcasted_iota(jnp.int32, (n, 128), 0) + offset
    return jnp.sum(jnp.where(place, column, 0.0), axis=0, keepdims=True)


def row_as_column(row, n, offset):
    place = lax.broadcasted_iota(jnp.int32, (n, 128), 1) == lax.broadcasted_iota(jnp.int32, (n, 128), 0) + offset
    return jnp.sum(jnp.where(place, row, 0.0), axis=1, keepdims=True)


def edge_rows(values):
    n = values.shape[0]
    row = column_as_row(values[:, -1:], None, 0) + column_as_row(values[:, :1], None, n)
    return jnp.broadcast_to(row, (EXTRA, 128))


def factor_of(counts_ref, weight_ref, d):
    slot = lax.broadcasted_iota(jnp.int32, (1, weight_ref.shape[2]), 1)
    return jnp.where(slot < counts_ref[0, d], weight_ref[0, pl.ds(d, 1), :], 0.0)


def loop(n, step, init):
    return lax.fori_loop(0, n, step, init, unroll=n if n <= 8 else 1)


def own_kernel(lev_ref, perturb_hbm, control_hbm, loc_hbm, part_ref, perturb_ref, control_ref, loc_ref, sems):
    staged = [(loc_hbm, loc_ref), (control_hbm, control_ref), (perturb_hbm, perturb_ref)]
    copies = [pltpu.make_async_copy(source, target, sems.at[i]) for i, (source, target) in enumerate(staged)]
    for copy in copies:
        copy.start()
    levels = perturb_ref.shape[0]
    copies[0].wait()
    weights = spread(loc_ref[...], lev_ref[0] * levels, levels)
    copies[1].wait()
    copies[2].wait()
    part_ref[...] = mixed_sum(weights, perturb_ref, control_ref)


def mixed_sum(weights, perturb_ref, control_ref):
    levels, members, cols = perturb_ref.shape
    perturb = perturb_ref[...].astype(F32)
    total = jnp.zeros((levels, SUB, cols), F32)
    for m in range(0, members, SUB):
        tile = control_ref[:, m : m + SUB, :].reshape(levels * SUB, cols)
        total = total + perturb[:, m : m + SUB, :] * mix(weights, tile).reshape(levels, SUB, cols)
    return jnp.sum(total, axis=1)


def band_kernel(lev_ref, counts_ref, perturb_ref, other_ref, part_ref, loc_ref, static_ref, src_ref, weight_ref,
                out_ref, acc_ref):
    levels, members, cols = perturb_ref.shape
    weights = spread(loc_ref[...], (1 - lev_ref[0]) * levels, levels)
    band_sum = part_ref[...] + mixed_sum(weights, perturb_ref, other_ref)
    acc_ref[...] = jnp.concatenate(halves(band_sum), axis=0)
    n = src_ref.shape[1]
    edges = edge_rows(static_ref[...])

    def step(d, carry):
        chosen = one_hot(src_ref[0, pl.ds(d, 1), :], cols)
        both = product(acc_ref[...], chosen)
        payload = (both[:levels] + both[levels:]) * factor_of(counts_ref, weight_ref, d)
        for g in range(out_ref.shape[0]):
            out_ref[g, d, :levels, :] = payload
            out_ref[g, d, levels:, :] = edges
        return carry

    loop(n, step, 0)


def tile_kernel(pos_ref, arrived_ref, tgt_ref, static_ref, diag_ref, off_ref, obs_ref, innov_ref,
                increment_ref, partial_ref, out_ref):
    levels, cols = static_ref.shape
    groups, n = arrived_ref.shape[:2]
    me = pos_ref[0]

    def step(s, total):
        values = sum(arrived_ref[g, s, :levels, :] for g in range(groups))
        chosen = one_hot(tgt_ref[0, pl.ds(s, 1), :], cols)
        return total + select(values, chosen, ((1,), (1,)))

    remapped = loop(n, step, jnp.zeros((levels, cols), F32))
    before = arrived_ref[0, jnp.maximum(me - 1, 0), levels : levels + 1, :]
    after = arrived_ref[0, jnp.minimum(me + 1, n - 1), levels : levels + 1, :]
    before = jnp.where(me > 0, row_as_column(before, levels, 0), 0.0)
    after = jnp.where(me < n - 1, row_as_column(after, levels, levels), 0.0)
    static = static_ref[...]
    lane = lax.broadcasted_iota(jnp.int32, (levels, cols), 1)
    left = jnp.where(lane == 0, before, pltpu.roll(static, 1, 1))
    right = jnp.where(lane == cols - 1, after, pltpu.roll(static, cols - 1, 1))
    increment = remapped + diag_ref[...] * static + off_ref[...] * (left + right)
    increment_ref[...] = increment
    misfit = obs_ref[...] * (increment - innov_ref[...])
    coupled = off_ref[...] * misfit
    left = jnp.where(lane == 0, 0.0, pltpu.roll(coupled, 1, 1))
    right = jnp.where(lane == cols - 1, 0.0, pltpu.roll(coupled, cols - 1, 1))
    partial_ref[...] = static + diag_ref[...] * misfit + left + right
    edges = edge_rows(coupled)
    both = jnp.concatenate(halves(misfit), axis=0)

    def give(s, carry):
        chosen = one_hot(tgt_ref[0, pl.ds(s, 1), :], cols)
        picked = product(both, chosen)
        out_ref[s, :levels, :] = picked[:levels] + picked[levels:]
        out_ref[s, levels:, :] = edges
        return carry

    loop(n, give, 0)


def adjoint_kernel(band, pos_ref, counts_ref, returned_ref, src_ref, weight_ref, partial_ref, mix_ref, grad_ref, out_ref):
    levels, cols = partial_ref.shape
    n = returned_ref.shape[0]
    me = pos_ref[0]

    def step(d, total):
        values = returned_ref[d, :levels, :] * factor_of(counts_ref, weight_ref, d)
        return total + select(values, one_hot(src_ref[0, pl.ds(d, 1), :], band), ((1,), (1,)))

    out_ref[...] = band_rows(loop(n, step, jnp.zeros((levels, band), F32)), mix_ref[...])
    before = returned_ref[jnp.maximum(me - 1, 0), levels : levels + 1, :]
    after = returned_ref[jnp.minimum(me + 1, n - 1), levels : levels + 1, :]
    before = jnp.where(me > 0, row_as_column(before, levels, 0), 0.0)
    after = jnp.where(me < n - 1, row_as_column(after, levels, levels), 0.0)
    lane = lax.broadcasted_iota(jnp.int32, (levels, cols), 1)
    grad_ref[...] = partial_ref[...] + (jnp.where(lane == 0, before, 0.0) + jnp.where(lane == cols - 1, after, 0.0))


def ens_weights(loc, start, count):
    full = loc.shape[0]

    def iota(shape, axis):
        return lax.broadcasted_iota(jnp.int32, shape, axis)

    shape = (count * SUB, full * SUB)
    pick_l = (iota((count * SUB, loc.shape[1]), 0) // SUB + start == iota((count * SUB, loc.shape[1]), 1)).astype(BF16)
    pick_k = (iota((full, full * SUB), 1) // SUB == iota((full, full * SUB), 0)).astype(BF16)
    same = iota(shape, 0) % SUB == iota(shape, 1) % SUB
    weights = []
    for part in halves(loc):
        wide = product(product(pick_l, part, ((1,), (1,))).astype(BF16), pick_k)
        weights.append(jnp.where(same, wide, 0.0).astype(BF16))
    return weights


def mix_kernel(lev_ref, loc_ref, own_ref, given_ref):
    levels = loc_ref.shape[0]
    own_ref[0], own_ref[1] = ens_weights(loc_ref[...], lev_ref[0] * levels, levels)
    high, low = ens_weights(loc_ref[...], (1 - lev_ref[0]) * levels, levels)
    given_ref[...] = high.astype(F32) + low.astype(F32)


def band_rows(band, weights):
    width = weights.shape[1]
    return jnp.concatenate([band[:, at : at + width] for at in range(0, band.shape[1], width)] + [weights], axis=0)


def ens_tiles(perturb_ref, rows_ref, weights, before_ref):
    levels, members, cols = perturb_ref.shape
    width = rows_ref.shape[1]
    parts = [rows_ref[i * levels : (i + 1) * levels, :] for i in range(cols // width)]
    grad = jnp.concatenate(parts, axis=1)[:, None, :]
    perturb = perturb_ref[...].astype(F32)
    for m in range(0, members, SUB):
        place = (slice(None), slice(m, m + SUB), slice(None))
        tile = (perturb[place] * grad).reshape(levels * SUB, cols)
        yield place, before_ref[place] + mix(weights, tile).reshape(levels, SUB, cols)


def ens_own_kernel(perturb_ref, mine_ref, weights_ref, control_ref, out_ref):
    for place, values in ens_tiles(perturb_ref, mine_ref, (weights_ref[0], weights_ref[1]), control_ref):
        out_ref[place] = values


def ens_kernel(perturb_ref, theirs_ref, own_ref, *refs):
    count = (len(refs) - 3) // 2
    flats, (out_hbm, *flat_hbms), (out_ref, sems) = refs[:count], refs[count : 2 * count + 1], refs[2 * count + 1 :]
    copies = [pltpu.make_async_copy(a, b, sems.at[i]) for i, (a, b) in enumerate(zip(flats, flat_hbms))]
    for copy in copies:
        copy.start()
    weights = halves(theirs_ref[theirs_ref.shape[0] - theirs_ref.shape[1] :, :])
    for place, values in ens_tiles(perturb_ref, theirs_ref, weights, own_ref):
        out_ref[place] = values
        copies.append(pltpu.make_async_copy(out_ref.at[place], out_hbm.at[place], sems.at[len(copies)]))
        copies[-1].start()
    for copy in copies:
        copy.wait()


def relabel(r, n, lev):
    high, low = n // 2, n // 4
    if low == 0:
        return r
    both = high | low
    turned = (r & ~both) | ((r & low) << 1) | ((r & high) >> 1)
    return r + (turned - r) * lev


class Rows:
    def __init__(self, levels, n):
        self.weight = slice(0, levels)
        self.base = slice(levels, 2 * levels)
        at = 2 * levels
        self.factor, self.index, self.edge = at, at + n, at + 2 * n
        self.total = at + 2 * n + EXTRA


def static_kernel(band, pos_ref, lev_ref, counts_ref, static_ref, diag_ref, off_ref, obs_ref, innov_ref, src_ref, weight_ref, tgt_ref,
                  *out_refs):
    levels, cols = static_ref.shape
    n = len(out_refs)
    cap = src_ref.shape[2]
    rows = Rows(levels, n)
    peers = [pos_ref[0] ^ relabel(r, n, lev_ref[0]) for r in range(n)]
    static, off, obs = static_ref[...], off_ref[...], obs_ref[...]
    lane = lax.broadcasted_iota(jnp.int32, (levels, cols), 1)
    left = jnp.where(lane == 0, 0.0, pltpu.roll(static, 1, 1))
    right = jnp.where(lane == cols - 1, 0.0, pltpu.roll(static, cols - 1, 1))
    base = diag_ref[...] * static + off * (left + right) - innov_ref[...]
    coupled = off * obs
    ends = [v[:, i] for v in (static, coupled, base) for i in (slice(cols - 1, cols), slice(0, 1))]
    edge = sum(column_as_row(end, None, i * levels) for i, end in enumerate(ends))
    place = lax.broadcasted_iota(jnp.int32, (1, cap), 1)
    edge = edge + jnp.where(place == 6 * levels, off[:, cols - 1 :], 0.0)
    edge = edge + jnp.where(place == 6 * levels + 1, off[:, :1], 0.0)
    edge = jnp.broadcast_to(edge, (EXTRA, cap))
    both = jnp.concatenate(halves(jnp.concatenate([obs, base], axis=0)), axis=0)
    tgts = [tgt_ref[0, pl.ds(peer, 1), :] for peer in peers]
    src = jnp.concatenate([src_ref[0, pl.ds(peer, 1), :] for peer in peers], axis=0).astype(F32)
    index = jnp.concatenate(tgts, axis=0).astype(F32) * float(band) + src
    factor = jnp.concatenate([factor_of(counts_ref, weight_ref, peer) for peer in peers], axis=0)
    for r, out_ref in enumerate(out_refs):
        picked = product(both, one_hot(tgts[r], cols))
        out_ref[: 2 * levels, :] = picked[: 2 * levels] + picked[2 * levels :]
        out_ref[rows.factor : rows.factor + n, :] = factor
        out_ref[rows.index : rows.index + n, :] = index
        out_ref[rows.edge :, :] = edge


def other_kernel(lev_ref, perturb_ref, other_ref, loc_ref, out_ref):
    levels = perturb_ref.shape[0]
    weights = spread(loc_ref[...], (1 - lev_ref[0]) * levels, levels)
    out_ref[...] = mixed_sum(weights, perturb_ref, other_ref)


def add_kernel(a_ref, b_ref, out_ref):
    out_ref[...] = a_ref[...] + b_ref[...]


def blocks_kernel(groups, *refs):
    sums = refs[:groups]
    count = (len(refs) - groups - 1) // 2
    rests = refs[groups : groups + count]
    total_ref = refs[groups + count]
    out_refs = refs[groups + count + 1 :]
    total = sum(ref[...] for ref in sums)
    cap = total_ref.shape[1]
    total = jnp.concatenate([total[:, at : at + cap] for at in range(0, total.shape[1], cap)], axis=0)
    total_ref[...] = total
    for rest_ref, out_ref in zip(rests, out_refs):
        out_ref[: total.shape[0], :] = total
        out_ref[total.shape[0] :, :] = rest_ref[...]


class Block:
    def __init__(self, refs, n, levels, band):
        cap = refs[0].shape[1]
        self.levels, self.parts, self.cap = levels, band // cap, cap
        self.sums_ref, self.rest_ref = refs[0], refs[-1]
        self.head = 0 if len(refs) == 2 else self.parts * levels
        self.rows = Rows(levels, n)
        words = self.rest(self.rows.index, n)
        self.tgt = jnp.floor((words + 0.5) * (1.0 / band))
        self.src = words - self.tgt * float(band)
        self.factor = self.rest(self.rows.factor, n)

    def rest(self, at, size):
        return self.rest_ref[self.head + at : self.head + at + size, :]

    def sums(self):
        parts = [self.sums_ref[i * self.levels : (i + 1) * self.levels, :] for i in range(self.parts)]
        return jnp.concatenate(halves(jnp.concatenate(parts, axis=1)), axis=0)


def line(table, i):
    return table[i : i + 1]


def pick_source(block, r):
    band = block.parts * block.cap
    column = lax.broadcasted_iota(jnp.int32, (band, block.cap), 0).astype(F32)
    return jnp.where(column == line(block.src, r), 1.0, 0.0).astype(BF16)


def fill_slots(bands, blocks, n, slots_ref):
    for i, s in enumerate(bands):
        block = blocks[s]
        both = block.sums()
        for d in range(n):
            picked = product(both, pick_source(block, s ^ d))
            values = (picked[: block.levels] + picked[block.levels :]) * line(block.factor, s ^ d)
            slots_ref[d, :, i * block.cap : (i + 1) * block.cap] = jnp.concatenate(halves(values), axis=0)


def met_at(d, block, bands, slots_ref):
    own = jnp.broadcast_to(line(block.tgt, d), (block.cap, block.cap)).T
    same = [jnp.where(own == line(block.tgt, s ^ d), 1.0, 0.0).astype(BF16) for s in bands]
    met = product(slots_ref[d], jnp.concatenate(same, axis=1), ((1,), (1,)))
    return met[: block.levels] + met[block.levels :]


def land(table, bands, slots_ref, cols):
    cap = table.shape[1]
    row = lax.broadcasted_iota(jnp.int32, (cols, cap), 0).astype(F32)
    total = 0.0
    for i, s in enumerate(bands):
        landing = jnp.where(row == line(table, s), 1.0, 0.0).astype(BF16)
        total = total + product(slots_ref[0, :, i * cap : (i + 1) * cap], landing, ((1,), (1,)))
    levels = total.shape[0] // 2
    return total[:levels] + total[levels:]


def open_blocks(labels, refs, n, levels, band):
    blocks = {0: Block(refs[:2], n, levels, band)}
    refs = refs[2:]
    for i, r in enumerate(labels[1:]):
        blocks[r] = Block(refs[i : i + 1], n, levels, band)
    return blocks, refs[len(labels) - 1 :]


def stage_kernel(n, levels, band, cols, stages, lev_ref, loc_ref, *refs):
    known = sum(stages[:-1], [])
    blocks, refs = open_blocks(known + stages[-1], refs, n, levels, band)
    old, refs = refs[: len(stages) - 1], refs[len(stages) - 1 :]
    if known:
        met_old, remap_old, slots_ref, met_ref, remap_ref = refs
    else:
        slots_ref, met_ref, remap_ref, pick_ref, own_ref, given_ref = refs
        for d in range(n):
            pick_ref[d] = pick_source(blocks[0], d)
        mix_kernel(lev_ref, loc_ref, own_ref, given_ref)
    fill_slots(stages[-1], blocks, n, slots_ref)
    for i, (d, block) in enumerate(blocks.items()):
        met = met_at(d, block, stages[-1], slots_ref)
        if d in known:
            met = met + met_old[i]
        else:
            for bands, ref in zip(stages, old):
                met = met + met_at(d, block, bands, ref)
        met_ref[i] = met
    landed = land(blocks[0].tgt, stages[-1], slots_ref, cols)
    remap_ref[...] = landed + remap_old[...] if known else landed


def shared_kernel(n, levels, band, cols, stages, pos_ref, lev_ref, mix_ref, *refs):
    known = sum(stages[:-1], [])
    blocks, refs = open_blocks(known + stages[-1], refs, n, levels, band)
    old, refs = refs[: len(stages) - 1], refs[len(stages) - 1 :]
    met_old, pick_ref, out_ref, slots_ref, tables_ref = refs
    me = pos_ref[0]
    for r, block in blocks.items():
        there = me ^ relabel(r, n, lev_ref[0])
        tables_ref[there, :n, :] = block.tgt
        tables_ref[there, n:, :] = block.rest(block.rows.edge, EXTRA)
    fill_slots(stages[-1], blocks, n, slots_ref)
    last = cols - 1.0
    total = jnp.zeros((levels, band), F32)
    for i, (d, block) in enumerate(blocks.items()):
        value = met_at(d, block, stages[-1], slots_ref) + block.rest(levels, levels)
        if d in known:
            value = value + met_old[i]
        else:
            for bands, ref in zip(stages, old):
                value = value + met_at(d, block, bands, ref)
        edge = block.rest(block.rows.edge, 1)
        own = line(block.tgt, d)
        there = me ^ relabel(d, n, lev_ref[0])
        before = tables_ref[jnp.maximum(there - 1, 0), n : n + 1, :]
        near = jnp.where((own == 0.0) & (there > 0), edge[:, 6 * levels + 1 : 6 * levels + 2], 0.0)
        value = value + row_as_column(before, levels, 0) * near
        after = tables_ref[jnp.minimum(there + 1, n - 1), n : n + 1, :]
        near = jnp.where((own == last) & (there < n - 1), edge[:, 6 * levels : 6 * levels + 1], 0.0)
        value = value + row_as_column(after, levels, levels) * near
        given = block.rest(0, levels) * value * line(blocks[0].factor, d)
        total = total + select(given, pick_ref[d], ((1,), (1,)))
    out_ref[...] = band_rows(total, mix_ref[...])


def outputs_kernel(stages, pos_ref, lev_ref, *refs):
    slots_refs, refs = refs[: len(stages)], refs[len(stages) :]
    remap_ref, tables_ref, static_ref, diag_ref, off_ref, obs_ref, innov_ref, increment_ref, grad_ref = refs
    levels, cols = static_ref.shape
    n = tables_ref.shape[0]
    cap = tables_ref.shape[2]
    me = pos_ref[0]
    given = [
        (s, ref, slice(i * cap, (i + 1) * cap)) for bands, ref in zip(stages, slots_refs) for i, s in enumerate(bands)
    ]
    remapped = remap_ref[...] + land(tables_ref[me, :n, :], stages[-1], slots_refs[-1], cols)
    static, off = static_ref[...], off_ref[...]
    lane = lax.broadcasted_iota(jnp.int32, (levels, cols), 1)

    def beside(there, exists, column, own_end, side):
        edge = tables_ref[there, n : n + 1, :]
        static_end, coupling, base = (row_as_column(edge, levels, (2 * i + side) * levels) for i in range(3))
        far = relabel(me ^ there, n, lev_ref[0])
        landed = []
        for s, ref, place in given:
            values = ref[far, :levels, place].astype(F32) + ref[far, levels:, place].astype(F32)
            landed.append(jnp.where(tables_ref[there, pl.ds(s ^ far, 1), :] == column, values, 0.0))
        remap_end = jnp.sum(sum(landed), axis=1, keepdims=True)
        off_end = edge[:, 6 * levels + side : 6 * levels + side + 1]
        coupled = coupling * (remap_end + base + off_end * own_end)
        return jnp.where(exists, static_end, 0.0), jnp.where(exists, coupled, 0.0)

    before, coupled_before = beside(jnp.maximum(me - 1, 0), me > 0, cols - 1.0, static[:, :1], 0)
    after, coupled_after = beside(jnp.minimum(me + 1, n - 1), me < n - 1, 0.0, static[:, cols - 1 :], 1)
    left = jnp.where(lane == 0, before, pltpu.roll(static, 1, 1))
    right = jnp.where(lane == cols - 1, after, pltpu.roll(static, cols - 1, 1))
    increment = remapped + diag_ref[...] * static + off * (left + right)
    increment_ref[...] = increment
    misfit = obs_ref[...] * (increment - innov_ref[...])
    coupled = off * misfit
    left = jnp.where(lane == 0, coupled_before, pltpu.roll(coupled, 1, 1))
    right = jnp.where(lane == cols - 1, coupled_after, pltpu.roll(coupled, cols - 1, 1))
    grad_ref[...] = static + diag_ref[...] * misfit + left + right


def call(kernel, out_shape, spaces, scratch=(), limit=40 * MIB, out=VMEM):
    return pl.pallas_call(
        kernel,
        out_shape=out_shape,
        in_specs=spaces,
        out_specs=jax.tree.map(lambda _: out, out_shape),
        scratch_shapes=scratch,
        compiler_params=pltpu.CompilerParams(vmem_limit_bytes=limit),
    )


def body(
    perturb,
    control,
    level_loc,
    static_control,
    filter_diag,
    filter_off,
    send_src,
    send_wt,
    counts,
    recv_tgt,
    obs_weight,
    innovation,
):
    levels, members, band_cols = control.shape
    tile_cols = static_control.shape[1]
    n = lax.axis_size("tile")
    groups = lax.axis_size("grp")
    cap = send_src.shape[2]
    shape = jax.ShapeDtypeStruct
    swap = [(0, 1), (1, 0)]
    lev = lax.axis_index("lev").astype(jnp.int32).reshape(1)
    pos = lax.axis_index("tile").astype(jnp.int32).reshape(1)
    other_control = lax.ppermute(control, "lev", swap)
    part = call(
        own_kernel,
        shape((levels, band_cols), F32),
        [SMEM] + [HBM] * 3,
        [pltpu.VMEM(a.shape, a.dtype) for a in (perturb, control, level_loc)] + [pltpu.SemaphoreType.DMA((3,))],
        limit=58 * MIB,
    )(lev, perturb, control, level_loc)
    flat = shape((levels, tile_cols), F32)
    width = levels * SUB
    mine_shape = shape((band_cols // width * levels + width, width), F32)
    mix_shapes = [shape((2, width, width), BF16), shape((width, width), F32)]
    diag, off = filter_diag.reshape(1, -1), filter_off.reshape(1, -1)
    if n * cap <= tile_cols and n >= 8 and lax.axis_size("lev") == 2 and n & (n - 1) == 0 and band_cols * tile_cols <= 2**20:
        rows = Rows(levels, n)
        stacked = band_cols // cap * levels
        rests = call(functools.partial(static_kernel, band_cols), [shape((rows.total, cap), F32)] * n, [SMEM] * 3 + [VMEM] * 8)(
            pos, lev, counts, static_control, diag, off, obs_weight, innovation, send_src, send_wt, recv_tgt
        )
        other_part = call(other_kernel, shape((levels, band_cols), F32), [SMEM] + [VMEM] * 3)(
            lev, perturb, other_control, level_loc
        )
        sums = [call(add_kernel, shape((levels, band_cols), F32), [VMEM] * 2)(part, other_part)]
        sums[0], other_perturb = lax.optimization_barrier((sums[0], lax.ppermute(perturb, "lev", swap)))
        for k in range(1, groups):
            sums.append(lax.ppermute(sums[0], "grp", [(g, (g + k) % groups) for g in range(groups)]))
        total, *blocks = call(
            functools.partial(blocks_kernel, groups),
            [shape((stacked, cap), F32)] + [shape((stacked + rows.total, cap), F32)] * (n - 1),
            [VMEM] * (groups + n - 1),
        )(*sums, *rests[1:])
        low, high = n // 4, n // 2
        both_far = [high + low + i for i in range(low)]
        mixed = [high + i for i in reversed(range(low))] + [low + i for i in reversed(range(low))]
        stages = [[0] + both_far + mixed[: low // 2], mixed[low // 2 :], list(range(1, low))]
        levs = lax.axis_size("lev")
        arrived = {0: [total, rests[0]]}
        for r in sum(stages, [])[1:]:
            pairs = [(i * levs + v, (i ^ relabel(r, n, v)) * levs + v) for i in range(n) for v in range(levs)]
            arrived[r] = [lax.ppermute(blocks[r - 1], ("tile", "lev"), pairs)]
        slots, carried, made = [], [], []
        for count in range(1, len(stages)):
            labels = sum(stages[:count], [])
            refs = [ref for r in labels for ref in arrived[r]]
            outs = [
                shape((n, 2 * levels, len(stages[count - 1]) * cap), BF16),
                shape((len(labels), levels, cap), F32),
                flat,
            ] + [shape((n, band_cols, cap), BF16), *mix_shapes] * (count == 1)
            new, *carried = call(
                functools.partial(stage_kernel, n, levels, band_cols, tile_cols, stages[:count]),
                outs,
                [SMEM] + [VMEM] * (1 + len(refs) + len(slots) + len(carried)),
            )(lev, level_loc, *refs, *slots, *carried)
            slots.append(new)
            made += carried[2:]
            carried = carried[:2]
        met, remap = carried
        picks, own_mix, given_mix = made
        refs = [ref for r in sum(stages, []) for ref in arrived[r]] + slots + [met, picks]
        mine, new, tables = call(
            functools.partial(shared_kernel, n, levels, band_cols, tile_cols, stages),
            (mine_shape, shape((n, 2 * levels, len(stages[-1]) * cap), BF16), shape((n, n + EXTRA, cap), F32)),
            [SMEM] * 2 + [VMEM] * (1 + len(refs)),
        )(pos, lev, given_mix, *refs)
        slots.append(new)
        increment, grad_static = call(
            functools.partial(outputs_kernel, stages), (flat, flat), [SMEM] * 2 + [VMEM] * (len(slots) + 7)
        )(pos, lev, *slots, remap, tables, static_control, diag, off, obs_weight, innovation)
    else:
        other_perturb = lax.ppermute(perturb, "lev", swap)
        payload = call(
            band_kernel,
            shape((groups, n, levels + EXTRA, cap), F32),
            [SMEM] * 2 + [VMEM] * 7,
            [pltpu.VMEM((2 * levels, band_cols), BF16)],
        )(lev, counts, perturb, other_control, part, level_loc, static_control, send_src, send_wt)
        arrived = lax.all_to_all(
            payload.reshape(groups * n, levels + EXTRA, cap), ("grp", "tile"), split_axis=0, concat_axis=0, tiled=True
        ).reshape(groups, n, levels + EXTRA, cap)
        increment, partial, giving = call(
            tile_kernel, (flat, flat, shape((n, levels + EXTRA, cap), F32)), [SMEM] + [VMEM] * 7
        )(pos, arrived, recv_tgt, static_control, diag, off, obs_weight, innovation)
        returned = lax.all_to_all(giving, "tile", split_axis=0, concat_axis=0, tiled=True)
        own_mix, given_mix = call(mix_kernel, mix_shapes, [SMEM, VMEM])(lev, level_loc)
        grad_static, mine = call(
            functools.partial(adjoint_kernel, band_cols), (flat, mine_shape), [SMEM, SMEM] + [VMEM] * 5
        )(pos, counts, returned, send_src, send_wt, partial, given_mix)
    theirs = lax.ppermute(mine, "lev", swap)
    own = call(ens_own_kernel, shape(control.shape, F32), [VMEM] * 4)(perturb, mine, own_mix, control)
    grad_ens, increment, grad_static = call(
        ens_kernel,
        (shape(control.shape, F32), flat, flat),
        [VMEM] * 5,
        [pltpu.VMEM(control.shape, F32), pltpu.SemaphoreType.DMA((2 + members // SUB,))],
        out=HBM,
    )(other_perturb, theirs, own, increment, grad_static)
    return (increment, grad_static, grad_ens)


def solution(mesh):
    return jax.shard_map(
        body,
        mesh=mesh,
        in_specs=(
            P("lev", "grp", "tile"),
            P("lev", "grp", "tile"),
            P("lev", None),
            P("lev", "tile"),
            P("tile"),
            P("tile"),
            P("tile", None, None),
            P("tile", None, None),
            P("tile", None),
            P("tile", None, None),
            P("lev", "tile"),
            P("lev", "tile"),
        ),
        out_specs=(P("lev", "tile"), P("lev", "tile"), P("lev", "grp", "tile")),
        check_vma=False,
    )
```

```python
import functools

import jax
import jax.numpy as jnp
from jax import lax
from jax.experimental import pallas as pl
from jax.experimental.pallas import tpu as pltpu
from jax.sharding import PartitionSpec as P

F32 = jnp.float32
BF16 = jnp.bfloat16
SUB = 8
EXTRA = 8
VMEM = pl.BlockSpec(memory_space=pltpu.VMEM)
HBM = pl.BlockSpec(memory_space=pltpu.HBM)
SMEM = pl.BlockSpec(memory_space=pltpu.SMEM)
MIB = 1024 * 1024


def halves(values):
    high = values.astype(BF16)
    low = (values - high.astype(F32)).astype(BF16)
    return high, low


def product(a, b, dims=((1,), (0,))):
    return lax.dot_general(a, b, (dims, ((), ())), preferred_element_type=F32)


def select(values, chosen, dims=((1,), (0,))):
    rows = values.shape[0]
    both = product(jnp.concatenate(halves(values), axis=0), chosen, dims)
    return both[:rows] + both[rows:]


def iota(shape, axis):
    return lax.broadcasted_iota(jnp.int32, shape, axis)


def wide_rows(matrix, start, count):
    cols = matrix.shape[1]
    shape = (cols, count * SUB)
    place = (iota(shape, 1) // SUB + start) % cols
    pick = (place == iota(shape, 0)).astype(BF16)
    high, low = halves(matrix)
    return product(high, pick) + product(low, pick)


def spread(wide):
    rows, cols = wide.shape
    tall = jnp.broadcast_to(wide[:, None, :], (rows, SUB, cols)).reshape(rows * SUB, cols)
    return jnp.where(iota(tall.shape, 0) % SUB == iota(tall.shape, 1) % SUB, tall, 0.0)


def mix(weights, values):
    high, low = halves(values)
    rows = weights[0].shape[0]
    both = product(jnp.concatenate(weights, axis=0), high)
    return both[:rows] + (product(weights[0], low) + both[rows:])


def one_hot(index, size):
    rows = lax.broadcasted_iota(jnp.int32, (size, index.shape[1]), 0)
    return jnp.where(rows == index, 1.0, 0.0).astype(BF16)


def column_as_row(column, lane, offset):
    n = column.shape[0]
    place = lax.broadcasted_iota(jnp.int32, (n, 128), 1) == lax.broadcasted_iota(jnp.int32, (n, 128), 0) + offset
    return jnp.sum(jnp.where(place, column, 0.0), axis=0, keepdims=True)


def row_as_column(row, n, offset):
    place = lax.broadcasted_iota(jnp.int32, (n, 128), 1) == lax.broadcasted_iota(jnp.int32, (n, 128), 0) + offset
    return jnp.sum(jnp.where(place, row, 0.0), axis=1, keepdims=True)


def edge_rows(values):
    n = values.shape[0]
    row = column_as_row(values[:, -1:], None, 0) + column_as_row(values[:, :1], None, n)
    return jnp.broadcast_to(row, (EXTRA, 128))


def factor_of(counts_ref, weight_ref, d):
    slot = lax.broadcasted_iota(jnp.int32, (1, weight_ref.shape[2]), 1)
    return jnp.where(slot < counts_ref[0, d], weight_ref[0, pl.ds(d, 1), :], 0.0)


def loop(n, step, init):
    return lax.fori_loop(0, n, step, init, unroll=n if n <= 8 else 1)


def mix_kernel(lev_ref, loc_ref, mix_ref, own_ref, given_ref):
    levels = loc_ref.shape[0]
    start = lev_ref[0] * levels
    loc = loc_ref[...]
    mix_ref[0], mix_ref[1] = halves(spread(wide_rows(loc, start, 2 * levels)))
    own_ref[0], own_ref[1] = halves(spread(wide_rows(loc, start, levels)).T)
    given_ref[...] = wide_rows(loc, levels - start, levels)


def sum_kernel(perturb_ref, control_ref, other_ref, mix_ref, out_ref):
    levels, members, cols = perturb_ref.shape
    perturb = perturb_ref[...].astype(F32)
    total = jnp.zeros((levels, SUB, cols), F32)
    for m in range(0, members, SUB):
        tile = jnp.concatenate([control_ref[:, m : m + SUB, :], other_ref[:, m : m + SUB, :]], axis=0)
        mixed = mix((mix_ref[0], mix_ref[1]), tile.reshape(2 * levels * SUB, cols))
        total = total + perturb[:, m : m + SUB, :] * mixed.reshape(levels, SUB, cols)
    out_ref[...] = jnp.sum(total, axis=1)


def band_kernel(counts_ref, sum_ref, static_ref, src_ref, weight_ref, out_ref, acc_ref):
    levels, cols = sum_ref.shape
    acc_ref[...] = jnp.concatenate(halves(sum_ref[...]), axis=0)
    n = src_ref.shape[1]
    edges = edge_rows(static_ref[...])

    def step(d, carry):
        chosen = one_hot(src_ref[0, pl.ds(d, 1), :], cols)
        both = product(acc_ref[...], chosen)
        payload = (both[:levels] + both[levels:]) * factor_of(counts_ref, weight_ref, d)
        for g in range(out_ref.shape[0]):
            out_ref[g, d, :levels, :] = payload
            out_ref[g, d, levels:, :] = edges
        return carry

    loop(n, step, 0)


def tile_kernel(pos_ref, arrived_ref, tgt_ref, static_ref, diag_ref, off_ref, obs_ref, innov_ref,
                increment_ref, partial_ref, out_ref):
    levels, cols = static_ref.shape
    groups, n = arrived_ref.shape[:2]
    me = pos_ref[0]

    def step(s, total):
        values = sum(arrived_ref[g, s, :levels, :] for g in range(groups))
        chosen = one_hot(tgt_ref[0, pl.ds(s, 1), :], cols)
        return total + select(values, chosen, ((1,), (1,)))

    remapped = loop(n, step, jnp.zeros((levels, cols), F32))
    before = arrived_ref[0, jnp.maximum(me - 1, 0), levels : levels + 1, :]
    after = arrived_ref[0, jnp.minimum(me + 1, n - 1), levels : levels + 1, :]
    before = jnp.where(me > 0, row_as_column(before, levels, 0), 0.0)
    after = jnp.where(me < n - 1, row_as_column(after, levels, levels), 0.0)
    static = static_ref[...]
    lane = lax.broadcasted_iota(jnp.int32, (levels, cols), 1)
    left = jnp.where(lane == 0, before, pltpu.roll(static, 1, 1))
    right = jnp.where(lane == cols - 1, after, pltpu.roll(static, cols - 1, 1))
    increment = remapped + diag_ref[...] * static + off_ref[...] * (left + right)
    increment_ref[...] = increment
    misfit = obs_ref[...] * (increment - innov_ref[...])
    coupled = off_ref[...] * misfit
    left = jnp.where(lane == 0, 0.0, pltpu.roll(coupled, 1, 1))
    right = jnp.where(lane == cols - 1, 0.0, pltpu.roll(coupled, cols - 1, 1))
    partial_ref[...] = static + diag_ref[...] * misfit + left + right
    edges = edge_rows(coupled)
    both = jnp.concatenate(halves(misfit), axis=0)

    def give(s, carry):
        chosen = one_hot(tgt_ref[0, pl.ds(s, 1), :], cols)
        picked = product(both, chosen)
        out_ref[s, :levels, :] = picked[:levels] + picked[levels:]
        out_ref[s, levels:, :] = edges
        return carry

    loop(n, give, 0)


def adjoint_kernel(band, pos_ref, counts_ref, returned_ref, src_ref, weight_ref, partial_ref, mix_ref, grad_ref, out_ref):
    levels, cols = partial_ref.shape
    n = returned_ref.shape[0]
    me = pos_ref[0]

    def step(d, total):
        values = returned_ref[d, :levels, :] * factor_of(counts_ref, weight_ref, d)
        return total + select(values, one_hot(src_ref[0, pl.ds(d, 1), :], band), ((1,), (1,)))

    out_ref[...] = band_rows(loop(n, step, jnp.zeros((levels, band), F32)), mix_ref[...])
    before = returned_ref[jnp.maximum(me - 1, 0), levels : levels + 1, :]
    after = returned_ref[jnp.minimum(me + 1, n - 1), levels : levels + 1, :]
    before = jnp.where(me > 0, row_as_column(before, levels, 0), 0.0)
    after = jnp.where(me < n - 1, row_as_column(after, levels, levels), 0.0)
    lane = lax.broadcasted_iota(jnp.int32, (levels, cols), 1)
    grad_ref[...] = partial_ref[...] + (jnp.where(lane == 0, before, 0.0) + jnp.where(lane == cols - 1, after, 0.0))


def band_rows(band, weights):
    width = weights.shape[1]
    return jnp.concatenate([band[:, at : at + width] for at in range(0, band.shape[1], width)] + [weights], axis=0)


def ens_tiles(perturb_ref, rows_ref, weights, before_ref):
    levels, members, cols = perturb_ref.shape
    width = rows_ref.shape[1]
    parts = [rows_ref[i * levels : (i + 1) * levels, :] for i in range(cols // width)]
    grad = jnp.concatenate(parts, axis=1)[:, None, :]
    perturb = perturb_ref[...].astype(F32)
    for m in range(0, members, SUB):
        place = (slice(None), slice(m, m + SUB), slice(None))
        tile = (perturb[place] * grad).reshape(levels * SUB, cols)
        yield place, before_ref[place] + mix(weights, tile).reshape(levels, SUB, cols)


def ens_own_kernel(perturb_ref, mine_ref, weights_ref, control_ref, out_ref):
    for place, values in ens_tiles(perturb_ref, mine_ref, (weights_ref[0], weights_ref[1]), control_ref):
        out_ref[place] = values


def ens_kernel(perturb_ref, theirs_ref, own_ref, *refs):
    count = (len(refs) - 3) // 2
    flats, (out_hbm, *flat_hbms), (out_ref, sems) = refs[:count], refs[count : 2 * count + 1], refs[2 * count + 1 :]
    copies = [pltpu.make_async_copy(a, b, sems.at[i]) for i, (a, b) in enumerate(zip(flats, flat_hbms))]
    for copy in copies:
        copy.start()
    levels = perturb_ref.shape[0]
    weights = halves(spread(theirs_ref[theirs_ref.shape[0] - levels :, :]).T)
    for place, values in ens_tiles(perturb_ref, theirs_ref, weights, own_ref):
        out_ref[place] = values
        copies.append(pltpu.make_async_copy(out_ref.at[place], out_hbm.at[place], sems.at[len(copies)]))
        copies[-1].start()
    for copy in copies:
        copy.wait()


def relabel(r, n, lev):
    high, low = n // 2, n // 4
    if low == 0:
        return r
    both = high | low
    turned = (r & ~both) | ((r & low) << 1) | ((r & high) >> 1)
    return r + (turned - r) * lev


class Rows:
    def __init__(self, levels, n):
        self.weight = slice(0, levels)
        self.base = slice(levels, 2 * levels)
        at = 2 * levels
        self.factor, self.index, self.edge = at, at + n, at + 2 * n
        self.total = at + 2 * n + EXTRA


def static_kernel(band, pos_ref, lev_ref, counts_ref, static_ref, diag_ref, off_ref, obs_ref, innov_ref, src_ref, weight_ref, tgt_ref,
                  *out_refs):
    levels, cols = static_ref.shape
    n = len(out_refs)
    cap = src_ref.shape[2]
    rows = Rows(levels, n)
    peers = [pos_ref[0] ^ relabel(r, n, lev_ref[0]) for r in range(n)]
    static, off, obs = static_ref[...], off_ref[...], obs_ref[...]
    lane = lax.broadcasted_iota(jnp.int32, (levels, cols), 1)
    left = jnp.where(lane == 0, 0.0, pltpu.roll(static, 1, 1))
    right = jnp.where(lane == cols - 1, 0.0, pltpu.roll(static, cols - 1, 1))
    base = diag_ref[...] * static + off * (left + right) - innov_ref[...]
    coupled = off * obs
    ends = [v[:, i] for v in (static, coupled, base) for i in (slice(cols - 1, cols), slice(0, 1))]
    edge = sum(column_as_row(end, None, i * levels) for i, end in enumerate(ends))
    place = lax.broadcasted_iota(jnp.int32, (1, cap), 1)
    edge = edge + jnp.where(place == 6 * levels, off[:, cols - 1 :], 0.0)
    edge = edge + jnp.where(place == 6 * levels + 1, off[:, :1], 0.0)
    edge = jnp.broadcast_to(edge, (EXTRA, cap))
    both = jnp.concatenate(halves(jnp.concatenate([obs, base], axis=0)), axis=0)
    tgts = [tgt_ref[0, pl.ds(peer, 1), :] for peer in peers]
    src = jnp.concatenate([src_ref[0, pl.ds(peer, 1), :] for peer in peers], axis=0).astype(F32)
    index = jnp.concatenate(tgts, axis=0).astype(F32) * float(band) + src
    factor = jnp.concatenate([factor_of(counts_ref, weight_ref, peer) for peer in peers], axis=0)
    for r, out_ref in enumerate(out_refs):
        picked = product(both, one_hot(tgts[r], cols))
        out_ref[: 2 * levels, :] = picked[: 2 * levels] + picked[2 * levels :]
        out_ref[rows.factor : rows.factor + n, :] = factor
        out_ref[rows.index : rows.index + n, :] = index
        out_ref[rows.edge :, :] = edge


def blocks_kernel(groups, *refs):
    sums = refs[:groups]
    count = (len(refs) - groups - 1) // 2
    rests = refs[groups : groups + count]
    total_ref = refs[groups + count]
    out_refs = refs[groups + count + 1 :]
    total = sum(ref[...] for ref in sums)
    cap = total_ref.shape[1]
    total = jnp.concatenate([total[:, at : at + cap] for at in range(0, total.shape[1], cap)], axis=0)
    total_ref[...] = total
    for rest_ref, out_ref in zip(rests, out_refs):
        out_ref[: total.shape[0], :] = total
        out_ref[total.shape[0] :, :] = rest_ref[...]


class Block:
    def __init__(self, refs, n, levels, band):
        cap = refs[0].shape[1]
        self.levels, self.parts, self.cap = levels, band // cap, cap
        self.sums_ref, self.rest_ref = refs[0], refs[-1]
        self.head = 0 if len(refs) == 2 else self.parts * levels
        self.rows = Rows(levels, n)
        words = self.rest(self.rows.index, n)
        self.tgt = jnp.floor((words + 0.5) * (1.0 / band))
        self.src = words - self.tgt * float(band)
        self.factor = self.rest(self.rows.factor, n)

    def rest(self, at, size):
        return self.rest_ref[self.head + at : self.head + at + size, :]

    def sums(self):
        parts = [self.sums_ref[i * self.levels : (i + 1) * self.levels, :] for i in range(self.parts)]
        return jnp.concatenate(halves(jnp.concatenate(parts, axis=1)), axis=0)


def line(table, i):
    return table[i : i + 1]


def pick_source(block, r):
    band = block.parts * block.cap
    column = lax.broadcasted_iota(jnp.int32, (band, block.cap), 0).astype(F32)
    return jnp.where(column == line(block.src, r), 1.0, 0.0).astype(BF16)


def fill_slots(bands, blocks, n, slots_ref):
    for i, s in enumerate(bands):
        block = blocks[s]
        both = block.sums()
        for d in range(n):
            picked = product(both, pick_source(block, s ^ d))
            values = (picked[: block.levels] + picked[block.levels :]) * line(block.factor, s ^ d)
            slots_ref[d, :, i * block.cap : (i + 1) * block.cap] = jnp.concatenate(halves(values), axis=0)


def met_at(d, block, bands, slots_ref):
    own = jnp.broadcast_to(line(block.tgt, d), (block.cap, block.cap)).T
    same = [jnp.where(own == line(block.tgt, s ^ d), 1.0, 0.0).astype(BF16) for s in bands]
    met = product(slots_ref[d], jnp.concatenate(same, axis=1), ((1,), (1,)))
    return met[: block.levels] + met[block.levels :]


def land(table, bands, slots_ref, cols):
    cap = table.shape[1]
    row = lax.broadcasted_iota(jnp.int32, (cols, cap), 0).astype(F32)
    total = 0.0
    for i, s in enumerate(bands):
        landing = jnp.where(row == line(table, s), 1.0, 0.0).astype(BF16)
        total = total + product(slots_ref[0, :, i * cap : (i + 1) * cap], landing, ((1,), (1,)))
    levels = total.shape[0] // 2
    return total[:levels] + total[levels:]


def open_blocks(labels, refs, n, levels, band):
    blocks = {0: Block(refs[:2], n, levels, band)}
    refs = refs[2:]
    for i, r in enumerate(labels[1:]):
        blocks[r] = Block(refs[i : i + 1], n, levels, band)
    return blocks, refs[len(labels) - 1 :]


def stage_kernel(n, levels, band, cols, stages, *refs):
    known = sum(stages[:-1], [])
    blocks, refs = open_blocks(known + stages[-1], refs, n, levels, band)
    old, refs = refs[: len(stages) - 1], refs[len(stages) - 1 :]
    if known:
        met_old, remap_old, slots_ref, met_ref, remap_ref = refs
    else:
        slots_ref, met_ref, remap_ref, pick_ref = refs
        for d in range(n):
            pick_ref[d] = pick_source(blocks[0], d)
    fill_slots(stages[-1], blocks, n, slots_ref)
    for i, (d, block) in enumerate(blocks.items()):
        met = met_at(d, block, stages[-1], slots_ref)
        if d in known:
            met = met + met_old[i]
        else:
            for bands, ref in zip(stages, old):
                met = met + met_at(d, block, bands, ref)
        met_ref[i] = met
    landed = land(blocks[0].tgt, stages[-1], slots_ref, cols)
    remap_ref[...] = landed + remap_old[...] if known else landed


def shared_kernel(n, levels, band, cols, stages, pos_ref, lev_ref, mix_ref, *refs):
    known = sum(stages[:-1], [])
    blocks, refs = open_blocks(known + stages[-1], refs, n, levels, band)
    old, refs = refs[: len(stages) - 1], refs[len(stages) - 1 :]
    met_old, pick_ref, out_ref, slots_ref, tables_ref = refs
    me = pos_ref[0]
    for r, block in blocks.items():
        there = me ^ relabel(r, n, lev_ref[0])
        tables_ref[there, :n, :] = block.tgt
        tables_ref[there, n:, :] = block.rest(block.rows.edge, EXTRA)
    fill_slots(stages[-1], blocks, n, slots_ref)
    last = cols - 1.0
    total = jnp.zeros((levels, band), F32)
    for i, (d, block) in enumerate(blocks.items()):
        value = met_at(d, block, stages[-1], slots_ref) + block.rest(levels, levels)
        if d in known:
            value = value + met_old[i]
        else:
            for bands, ref in zip(stages, old):
                value = value + met_at(d, block, bands, ref)
        edge = block.rest(block.rows.edge, 1)
        own = line(block.tgt, d)
        there = me ^ relabel(d, n, lev_ref[0])
        before = tables_ref[jnp.maximum(there - 1, 0), n : n + 1, :]
        near = jnp.where((own == 0.0) & (there > 0), edge[:, 6 * levels + 1 : 6 * levels + 2], 0.0)
        value = value + row_as_column(before, levels, 0) * near
        after = tables_ref[jnp.minimum(there + 1, n - 1), n : n + 1, :]
        near = jnp.where((own == last) & (there < n - 1), edge[:, 6 * levels : 6 * levels + 1], 0.0)
        value = value + row_as_column(after, levels, levels) * near
        given = block.rest(0, levels) * value * line(blocks[0].factor, d)
        total = total + select(given, pick_ref[d], ((1,), (1,)))
    out_ref[...] = band_rows(total, mix_ref[...])


def outputs_kernel(stages, pos_ref, lev_ref, *refs):
    slots_refs, refs = refs[: len(stages)], refs[len(stages) :]
    remap_ref, tables_ref, static_ref, diag_ref, off_ref, obs_ref, innov_ref, increment_ref, grad_ref = refs
    levels, cols = static_ref.shape
    n = tables_ref.shape[0]
    cap = tables_ref.shape[2]
    me = pos_ref[0]
    given = [
        (s, ref, slice(i * cap, (i + 1) * cap)) for bands, ref in zip(stages, slots_refs) for i, s in enumerate(bands)
    ]
    remapped = remap_ref[...] + land(tables_ref[me, :n, :], stages[-1], slots_refs[-1], cols)
    static, off = static_ref[...], off_ref[...]
    lane = lax.broadcasted_iota(jnp.int32, (levels, cols), 1)

    def beside(there, exists, column, own_end, side):
        edge = tables_ref[there, n : n + 1, :]
        static_end, coupling, base = (row_as_column(edge, levels, (2 * i + side) * levels) for i in range(3))
        far = relabel(me ^ there, n, lev_ref[0])
        landed = []
        for s, ref, place in given:
            values = ref[far, :levels, place].astype(F32) + ref[far, levels:, place].astype(F32)
            landed.append(jnp.where(tables_ref[there, pl.ds(s ^ far, 1), :] == column, values, 0.0))
        remap_end = jnp.sum(sum(landed), axis=1, keepdims=True)
        off_end = edge[:, 6 * levels + side : 6 * levels + side + 1]
        coupled = coupling * (remap_end + base + off_end * own_end)
        return jnp.where(exists, static_end, 0.0), jnp.where(exists, coupled, 0.0)

    before, coupled_before = beside(jnp.maximum(me - 1, 0), me > 0, cols - 1.0, static[:, :1], 0)
    after, coupled_after = beside(jnp.minimum(me + 1, n - 1), me < n - 1, 0.0, static[:, cols - 1 :], 1)
    left = jnp.where(lane == 0, before, pltpu.roll(static, 1, 1))
    right = jnp.where(lane == cols - 1, after, pltpu.roll(static, cols - 1, 1))
    increment = remapped + diag_ref[...] * static + off * (left + right)
    increment_ref[...] = increment
    misfit = obs_ref[...] * (increment - innov_ref[...])
    coupled = off * misfit
    left = jnp.where(lane == 0, coupled_before, pltpu.roll(coupled, 1, 1))
    right = jnp.where(lane == cols - 1, coupled_after, pltpu.roll(coupled, cols - 1, 1))
    grad_ref[...] = static + diag_ref[...] * misfit + left + right


def call(kernel, out_shape, spaces, scratch=(), out=VMEM, cost=None):
    return pl.pallas_call(
        kernel,
        out_shape=out_shape,
        in_specs=spaces,
        out_specs=jax.tree.map(lambda _: out, out_shape),
        scratch_shapes=scratch,
        cost_estimate=cost,
        compiler_params=pltpu.CompilerParams(vmem_limit_bytes=40 * MIB),
    )


def body(
    perturb,
    control,
    level_loc,
    static_control,
    filter_diag,
    filter_off,
    send_src,
    send_wt,
    counts,
    recv_tgt,
    obs_weight,
    innovation,
):
    levels, members, band_cols = control.shape
    tile_cols = static_control.shape[1]
    n = lax.axis_size("tile")
    groups = lax.axis_size("grp")
    cap = send_src.shape[2]
    shape = jax.ShapeDtypeStruct
    swap = [(0, 1), (1, 0)]
    lev = lax.axis_index("lev").astype(jnp.int32).reshape(1)
    pos = lax.axis_index("tile").astype(jnp.int32).reshape(1)
    other_control = lax.ppermute(control, "lev", swap)
    width = levels * SUB
    level_mix, own_mix, given_mix = call(
        mix_kernel,
        (shape((2, width, 2 * width), BF16), shape((2, width, width), BF16), shape((levels, width), F32)),
        [SMEM, VMEM],
        cost=pl.CostEstimate(flops=10**9, bytes_accessed=0, transcendentals=0),
    )(lev, level_loc)
    own_sum = call(sum_kernel, shape((levels, band_cols), F32), [VMEM] * 4)(perturb, control, other_control, level_mix)
    flat = shape((levels, tile_cols), F32)
    mine_shape = shape((band_cols // width * levels + levels, width), F32)
    diag, off = filter_diag.reshape(1, -1), filter_off.reshape(1, -1)
    if n * cap <= tile_cols and n >= 8 and lax.axis_size("lev") == 2 and n & (n - 1) == 0 and band_cols * tile_cols <= 2**20:
        rows = Rows(levels, n)
        stacked = band_cols // cap * levels
        rests = call(functools.partial(static_kernel, band_cols), [shape((rows.total, cap), F32)] * n, [SMEM] * 3 + [VMEM] * 8)(
            pos, lev, counts, static_control, diag, off, obs_weight, innovation, send_src, send_wt, recv_tgt
        )
        sums = [own_sum]
        sums[0], other_perturb = lax.optimization_barrier((sums[0], lax.ppermute(perturb, "lev", swap)))
        for k in range(1, groups):
            sums.append(lax.ppermute(sums[0], "grp", [(g, (g + k) % groups) for g in range(groups)]))
        total, *blocks = call(
            functools.partial(blocks_kernel, groups),
            [shape((stacked, cap), F32)] + [shape((stacked + rows.total, cap), F32)] * (n - 1),
            [VMEM] * (groups + n - 1),
        )(*sums, *rests[1:])
        low, high = n // 4, n // 2
        both_far = [high + low + i for i in range(low)]
        mixed = [high + i for i in reversed(range(low))] + [low + i for i in reversed(range(low))]
        stages = [[0] + both_far + mixed[: low // 2], mixed[low // 2 :], list(range(1, low))]
        levs = lax.axis_size("lev")
        arrived = {0: [total, rests[0]]}
        for r in sum(stages, [])[1:]:
            pairs = [(i * levs + v, (i ^ relabel(r, n, v)) * levs + v) for i in range(n) for v in range(levs)]
            arrived[r] = [lax.ppermute(blocks[r - 1], ("tile", "lev"), pairs)]
        slots, carried, picks = [], [], []
        for count in range(1, len(stages)):
            labels = sum(stages[:count], [])
            refs = [ref for r in labels for ref in arrived[r]]
            outs = [
                shape((n, 2 * levels, len(stages[count - 1]) * cap), BF16),
                shape((len(labels), levels, cap), F32),
                flat,
            ] + [shape((n, band_cols, cap), BF16)] * (count == 1)
            new, *carried = call(
                functools.partial(stage_kernel, n, levels, band_cols, tile_cols, stages[:count]),
                outs,
                [VMEM] * (len(refs) + len(slots) + len(carried)),
            )(*refs, *slots, *carried)
            slots.append(new)
            picks += carried[2:]
            carried = carried[:2]
        met, remap = carried
        refs = [ref for r in sum(stages, []) for ref in arrived[r]] + slots + [met] + picks
        mine, new, tables = call(
            functools.partial(shared_kernel, n, levels, band_cols, tile_cols, stages),
            (mine_shape, shape((n, 2 * levels, len(stages[-1]) * cap), BF16), shape((n, n + EXTRA, cap), F32)),
            [SMEM] * 2 + [VMEM] * (1 + len(refs)),
        )(pos, lev, given_mix, *refs)
        slots.append(new)
        increment, grad_static = call(
            functools.partial(outputs_kernel, stages), (flat, flat), [SMEM] * 2 + [VMEM] * (len(slots) + 7)
        )(pos, lev, *slots, remap, tables, static_control, diag, off, obs_weight, innovation)
    else:
        other_perturb = lax.ppermute(perturb, "lev", swap)
        payload = call(
            band_kernel,
            shape((groups, n, levels + EXTRA, cap), F32),
            [SMEM] + [VMEM] * 4,
            [pltpu.VMEM((2 * levels, band_cols), BF16)],
        )(counts, own_sum, static_control, send_src, send_wt)
        arrived = lax.all_to_all(
            payload.reshape(groups * n, levels + EXTRA, cap), ("grp", "tile"), split_axis=0, concat_axis=0, tiled=True
        ).reshape(groups, n, levels + EXTRA, cap)
        increment, partial, giving = call(
            tile_kernel, (flat, flat, shape((n, levels + EXTRA, cap), F32)), [SMEM] + [VMEM] * 7
        )(pos, arrived, recv_tgt, static_control, diag, off, obs_weight, innovation)
        returned = lax.all_to_all(giving, "tile", split_axis=0, concat_axis=0, tiled=True)
        grad_static, mine = call(
            functools.partial(adjoint_kernel, band_cols), (flat, mine_shape), [SMEM, SMEM] + [VMEM] * 5
        )(pos, counts, returned, send_src, send_wt, partial, given_mix)
    theirs = lax.ppermute(mine, "lev", swap)
    own = call(ens_own_kernel, shape(control.shape, F32), [VMEM] * 4)(perturb, mine, own_mix, control)
    grad_ens, increment, grad_static = call(
        ens_kernel,
        (shape(control.shape, F32), flat, flat),
        [VMEM] * 5,
        [pltpu.VMEM(control.shape, F32), pltpu.SemaphoreType.DMA((2 + members // SUB,))],
        out=HBM,
    )(other_perturb, theirs, own, increment, grad_static)
    return (increment, grad_static, grad_ens)


def solution(mesh):
    return jax.shard_map(
        body,
        mesh=mesh,
        in_specs=(
            P("lev", "grp", "tile"),
            P("lev", "grp", "tile"),
            P("lev", None),
            P("lev", "tile"),
            P("tile"),
            P("tile"),
            P("tile", None, None),
            P("tile", None, None),
            P("tile", None),
            P("tile", None, None),
            P("lev", "tile"),
            P("lev", "tile"),
        ),
        out_specs=(P("lev", "tile"), P("lev", "tile"), P("lev", "grp", "tile")),
        check_vma=False,
    )
```

```python
import functools

import jax
import jax.numpy as jnp
from jax import lax
from jax.experimental import pallas as pl
from jax.experimental.pallas import tpu as pltpu
from jax.sharding import PartitionSpec as P

F32 = jnp.float32
BF16 = jnp.bfloat16
SUB = 8
EXTRA = 8
VMEM = pl.BlockSpec(memory_space=pltpu.VMEM)
HBM = pl.BlockSpec(memory_space=pltpu.HBM)
SMEM = pl.BlockSpec(memory_space=pltpu.SMEM)
MIB = 1024 * 1024


def halves(values):
    high = values.astype(BF16)
    low = (values - high.astype(F32)).astype(BF16)
    return high, low


def product(a, b, dims=((1,), (0,))):
    return lax.dot_general(a, b, (dims, ((), ())), preferred_element_type=F32)


def select(values, chosen, dims=((1,), (0,))):
    rows = values.shape[0]
    both = product(jnp.concatenate(halves(values), axis=0), chosen, dims)
    return both[:rows] + both[rows:]


def iota(shape, axis):
    return lax.broadcasted_iota(jnp.int32, shape, axis)


def wide_rows(matrix, start, count):
    cols = matrix.shape[1]
    shape = (cols, count * SUB)
    place = (iota(shape, 1) // SUB + start) % cols
    pick = (place == iota(shape, 0)).astype(BF16)
    high, low = halves(matrix)
    return product(high, pick) + product(low, pick)


def spread(wide):
    rows, cols = wide.shape
    tall = jnp.broadcast_to(wide[:, None, :], (rows, SUB, cols)).reshape(rows * SUB, cols)
    return jnp.where(iota(tall.shape, 0) % SUB == iota(tall.shape, 1) % SUB, tall, 0.0)


def mix(weights, values):
    high, low = halves(values)
    rows = weights[0].shape[0]
    both = product(jnp.concatenate(weights, axis=0), high)
    return both[:rows] + (product(weights[0], low) + both[rows:])


def one_hot(index, size):
    rows = lax.broadcasted_iota(jnp.int32, (size, index.shape[1]), 0)
    return jnp.where(rows == index, 1.0, 0.0).astype(BF16)


def column_as_row(column, lane, offset):
    n = column.shape[0]
    place = lax.broadcasted_iota(jnp.int32, (n, 128), 1) == lax.broadcasted_iota(jnp.int32, (n, 128), 0) + offset
    return jnp.sum(jnp.where(place, column, 0.0), axis=0, keepdims=True)


def row_as_column(row, n, offset):
    place = lax.broadcasted_iota(jnp.int32, (n, 128), 1) == lax.broadcasted_iota(jnp.int32, (n, 128), 0) + offset
    return jnp.sum(jnp.where(place, row, 0.0), axis=1, keepdims=True)


def edge_rows(values):
    n = values.shape[0]
    row = column_as_row(values[:, -1:], None, 0) + column_as_row(values[:, :1], None, n)
    return jnp.broadcast_to(row, (EXTRA, 128))


def factor_of(counts_ref, weight_ref, d):
    slot = lax.broadcasted_iota(jnp.int32, (1, weight_ref.shape[2]), 1)
    return jnp.where(slot < counts_ref[0, d], weight_ref[0, pl.ds(d, 1), :], 0.0)


def loop(n, step, init):
    return lax.fori_loop(0, n, step, init, unroll=n if n <= 8 else 1)


def mix_kernel(lev_ref, loc_ref, other_ref, sums_ref, ens_ref):
    levels = loc_ref.shape[0]
    start = lev_ref[0] * levels
    locs = loc_ref[...], other_ref[...]
    sums_ref[...] = jnp.concatenate(
        [term for both in zip(*(halves(spread(wide_rows(loc, start, 2 * levels))) for loc in locs)) for term in both]
    )
    for i, loc in enumerate(locs):
        ens_ref[2 * i], ens_ref[2 * i + 1] = halves(spread(wide_rows(loc, start, levels)).T)


def sum_kernel(perturb_ref, other_perturb_ref, control_ref, other_ref, mix_ref, out_ref):
    levels, members, cols = perturb_ref.shape
    perturb = jnp.concatenate([perturb_ref[...].astype(F32), other_perturb_ref[...].astype(F32)], axis=0)
    total = jnp.zeros((2 * levels, SUB, cols), F32)
    rows = mix_ref.shape[0] // 2
    for m in range(0, members, SUB):
        tile = jnp.concatenate([control_ref[:, m : m + SUB, :], other_ref[:, m : m + SUB, :]], axis=0)
        high, low = halves(tile.reshape(2 * levels * SUB, cols))
        both = product(mix_ref[...], high)
        mixed = both[:rows] + (product(mix_ref[:rows, :], low) + both[rows:])
        total = total + perturb[:, m : m + SUB, :] * mixed.reshape(2 * levels, SUB, cols)
    out_ref[: 2 * levels, :] = jnp.sum(total, axis=1)
    out_ref[2 * levels :, :] = jnp.zeros((SUB, cols), F32)


def band_kernel(counts_ref, sum_ref, static_ref, src_ref, weight_ref, out_ref, acc_ref):
    levels, cols = static_ref.shape[0], sum_ref.shape[1]
    acc_ref[...] = jnp.concatenate(halves(sum_ref[:levels, :]), axis=0)
    n = src_ref.shape[1]
    edges = edge_rows(static_ref[...])

    def step(d, carry):
        chosen = one_hot(src_ref[0, pl.ds(d, 1), :], cols)
        both = product(acc_ref[...], chosen)
        payload = (both[:levels] + both[levels:]) * factor_of(counts_ref, weight_ref, d)
        for g in range(out_ref.shape[0]):
            out_ref[g, d, :levels, :] = payload
            out_ref[g, d, levels:, :] = edges
        return carry

    loop(n, step, 0)


def tile_kernel(pos_ref, arrived_ref, tgt_ref, static_ref, diag_ref, off_ref, obs_ref, innov_ref,
                increment_ref, partial_ref, out_ref):
    levels, cols = static_ref.shape
    groups, n = arrived_ref.shape[:2]
    me = pos_ref[0]

    def step(s, total):
        values = sum(arrived_ref[g, s, :levels, :] for g in range(groups))
        chosen = one_hot(tgt_ref[0, pl.ds(s, 1), :], cols)
        return total + select(values, chosen, ((1,), (1,)))

    remapped = loop(n, step, jnp.zeros((levels, cols), F32))
    before = arrived_ref[0, jnp.maximum(me - 1, 0), levels : levels + 1, :]
    after = arrived_ref[0, jnp.minimum(me + 1, n - 1), levels : levels + 1, :]
    before = jnp.where(me > 0, row_as_column(before, levels, 0), 0.0)
    after = jnp.where(me < n - 1, row_as_column(after, levels, levels), 0.0)
    static = static_ref[...]
    lane = lax.broadcasted_iota(jnp.int32, (levels, cols), 1)
    left = jnp.where(lane == 0, before, pltpu.roll(static, 1, 1))
    right = jnp.where(lane == cols - 1, after, pltpu.roll(static, cols - 1, 1))
    increment = remapped + diag_ref[...] * static + off_ref[...] * (left + right)
    increment_ref[...] = increment
    misfit = obs_ref[...] * (increment - innov_ref[...])
    coupled = off_ref[...] * misfit
    left = jnp.where(lane == 0, 0.0, pltpu.roll(coupled, 1, 1))
    right = jnp.where(lane == cols - 1, 0.0, pltpu.roll(coupled, cols - 1, 1))
    partial_ref[...] = static + diag_ref[...] * misfit + left + right
    edges = edge_rows(coupled)
    both = jnp.concatenate(halves(misfit), axis=0)

    def give(s, carry):
        chosen = one_hot(tgt_ref[0, pl.ds(s, 1), :], cols)
        picked = product(both, chosen)
        out_ref[s, :levels, :] = picked[:levels] + picked[levels:]
        out_ref[s, levels:, :] = edges
        return carry

    loop(n, give, 0)


def adjoint_kernel(band, pos_ref, counts_ref, returned_ref, src_ref, weight_ref, partial_ref, grad_ref, out_ref):
    levels, cols = partial_ref.shape
    n = returned_ref.shape[0]
    me = pos_ref[0]

    def step(d, total):
        values = returned_ref[d, :levels, :] * factor_of(counts_ref, weight_ref, d)
        return total + select(values, one_hot(src_ref[0, pl.ds(d, 1), :], band), ((1,), (1,)))

    out_ref[...] = stack(loop(n, step, jnp.zeros((levels, band), F32)), out_ref.shape[1])
    before = returned_ref[jnp.maximum(me - 1, 0), levels : levels + 1, :]
    after = returned_ref[jnp.minimum(me + 1, n - 1), levels : levels + 1, :]
    before = jnp.where(me > 0, row_as_column(before, levels, 0), 0.0)
    after = jnp.where(me < n - 1, row_as_column(after, levels, levels), 0.0)
    lane = lax.broadcasted_iota(jnp.int32, (levels, cols), 1)
    grad_ref[...] = partial_ref[...] + (jnp.where(lane == 0, before, 0.0) + jnp.where(lane == cols - 1, after, 0.0))


def stack(values, width):
    return jnp.concatenate([values[:, at : at + width] for at in range(0, values.shape[1], width)], axis=0)


def ens_tiles(perturb_ref, rows_ref, weights, before_ref):
    levels, members, cols = perturb_ref.shape
    width = rows_ref.shape[1]
    parts = [rows_ref[i * levels : (i + 1) * levels, :] for i in range(cols // width)]
    grad = jnp.concatenate(parts, axis=1)[:, None, :]
    perturb = perturb_ref[...].astype(F32)
    for m in range(0, members, SUB):
        place = (slice(None), slice(m, m + SUB), slice(None))
        tile = (perturb[place] * grad).reshape(levels * SUB, cols)
        yield place, before_ref[place] + mix(weights, tile).reshape(levels, SUB, cols)


def ens_own_kernel(perturb_ref, mine_ref, weights_ref, control_ref, out_ref):
    for place, values in ens_tiles(perturb_ref, mine_ref, (weights_ref[0], weights_ref[1]), control_ref):
        out_ref[place] = values


def ens_kernel(perturb_ref, theirs_ref, weights_ref, own_ref, *refs):
    count = (len(refs) - 3) // 2
    flats, (out_hbm, *flat_hbms), (out_ref, sems) = refs[:count], refs[count : 2 * count + 1], refs[2 * count + 1 :]
    copies = [pltpu.make_async_copy(a, b, sems.at[i]) for i, (a, b) in enumerate(zip(flats, flat_hbms))]
    for copy in copies:
        copy.start()
    for place, values in ens_tiles(perturb_ref, theirs_ref, (weights_ref[2], weights_ref[3]), own_ref):
        out_ref[place] = values
        copies.append(pltpu.make_async_copy(out_ref.at[place], out_hbm.at[place], sems.at[len(copies)]))
        copies[-1].start()
    for copy in copies:
        copy.wait()


def relabel(r, n, lev):
    return r ^ (((r & (n // 2)) >> 1) * lev)


class Rows:
    def __init__(self, levels, n):
        self.weight = slice(0, levels)
        self.base = slice(levels, 2 * levels)
        at = 2 * levels
        self.factor, self.index, self.edge = at, at + n, at + 2 * n
        self.total = at + 2 * n + EXTRA


def static_kernel(n, band, pos_ref, lev_ref, counts_ref, static_ref, diag_ref, off_ref, obs_ref, innov_ref, src_ref,
                  weight_ref, tgt_ref, *out_refs):
    levels, cols = static_ref.shape
    cap = src_ref.shape[2]
    rows = Rows(levels, n)
    peers = [pos_ref[0] ^ r for r in range(n)]
    static, off, obs = static_ref[...], off_ref[...], obs_ref[...]
    lane = lax.broadcasted_iota(jnp.int32, (levels, cols), 1)
    left = jnp.where(lane == 0, 0.0, pltpu.roll(static, 1, 1))
    right = jnp.where(lane == cols - 1, 0.0, pltpu.roll(static, cols - 1, 1))
    base = diag_ref[...] * static + off * (left + right) - innov_ref[...]
    coupled = off * obs
    ends = [v[:, i] for v in (static, coupled, base) for i in (slice(cols - 1, cols), slice(0, 1))]
    edge = sum(column_as_row(end, None, i * levels) for i, end in enumerate(ends))
    place = lax.broadcasted_iota(jnp.int32, (1, cap), 1)
    edge = edge + jnp.where(place == 6 * levels, off[:, cols - 1 :], 0.0)
    edge = edge + jnp.where(place == 6 * levels + 1, off[:, :1], 0.0)
    edge = jnp.broadcast_to(edge, (EXTRA, cap))
    both = jnp.concatenate(halves(jnp.concatenate([obs, base], axis=0)), axis=0)
    tgts = [tgt_ref[0, pl.ds(peer, 1), :] for peer in peers]
    src = jnp.concatenate([src_ref[0, pl.ds(peer, 1), :] for peer in peers], axis=0).astype(F32)
    index = jnp.concatenate(tgts, axis=0).astype(F32) * float(band) + src
    factor = jnp.concatenate([factor_of(counts_ref, weight_ref, peer) for peer in peers], axis=0)
    picks = []
    for tgt in tgts:
        picked = product(both, one_hot(tgt, cols))
        picks.append(picked[: 2 * levels] + picked[2 * levels :])
    *block_refs, give_ref = out_refs
    low, high = n // 4, n // 2
    first = lev_ref[0] == 0
    for i in range(low):
        here, there = picks[high + i], picks[high + low + i]
        picks[high + i] = jnp.where(first, here, there)
        give_ref[2 * levels * i : 2 * levels * (i + 1), :] = jnp.where(first, there, here)
    give_ref[2 * levels * low :, :] = edge
    for picked, out_ref in zip(picks, block_refs):
        out_ref[: 2 * levels, :] = picked
        out_ref[rows.factor : rows.factor + n, :] = factor
        out_ref[rows.index : rows.index + n, :] = index
        out_ref[rows.edge :, :] = edge


def blocks_kernel(groups, near, levels, lev_ref, *refs):
    sums, refs = refs[:groups], refs[groups:]
    count = (len(refs) - 2) // 2
    rests, given_ref, total_ref, out_refs = refs[:count], refs[count], refs[count + 1], refs[count + 2 :]
    total = sum(ref[...] for ref in sums)
    cap = total_ref.shape[1]
    own, other = (stack(part, cap) for part in (total[:levels], total[levels : 2 * levels]))
    total_ref[...] = own
    for rest_ref, out_ref in zip(rests[:near], out_refs[:near]):
        out_ref[...] = jnp.concatenate([own, rest_ref[...]], axis=0)
    first = lev_ref[0] == 0
    for i, (rest_ref, out_ref) in enumerate(zip(rests[near:], out_refs[near:])):
        mine = jnp.concatenate([own, rest_ref[: 2 * levels, :], rest_ref[-EXTRA:, :]], axis=0)
        part = given_ref[2 * levels * i : 2 * levels * (i + 1), :]
        theirs = jnp.concatenate([other, part, given_ref[-EXTRA:, :]], axis=0)
        tables = rest_ref[2 * levels : -EXTRA, :]
        out_ref[...] = jnp.concatenate([jnp.where(first, mine, theirs), tables, jnp.where(first, theirs, mine)], axis=0)


class Block:
    def __init__(self, sums, weight, base, tables, edge, lev, n, band):
        self.levels, self.cap = weight.shape
        self.stacked, self.weight, self.base, self.edge = sums, weight, base, edge
        low, high = n // 4, n // 2
        turned = [tables[at : at + size] for k in (0, n) for at, size in ((k, high), (k + high + low, low), (k + high, low))]
        tables = jnp.where(lev == 1, jnp.concatenate(turned, axis=0), tables)
        self.factor, words = tables[:n], tables[n:]
        self.tgt = jnp.floor((words + 0.5) * (1.0 / band))
        self.src = words - self.tgt * float(band)

    def sums(self):
        parts = [self.stacked[at : at + self.levels] for at in range(0, self.stacked.shape[0], self.levels)]
        return jnp.concatenate(halves(jnp.concatenate(parts, axis=1)), axis=0)


def line(table, i):
    return table[i : i + 1]


def pick_source(block, r):
    band = block.stacked.shape[0] // block.levels * block.cap
    column = lax.broadcasted_iota(jnp.int32, (band, block.cap), 0).astype(F32)
    return jnp.where(column == line(block.src, r), 1.0, 0.0).astype(BF16)


def fill_slots(bands, blocks, n, slots_ref):
    for i, s in enumerate(bands):
        block = blocks[s]
        both = block.sums()
        for d in range(n):
            picked = product(both, pick_source(block, s ^ d))
            values = (picked[: block.levels] + picked[block.levels :]) * line(block.factor, s ^ d)
            slots_ref[d, :, i * block.cap : (i + 1) * block.cap] = jnp.concatenate(halves(values), axis=0)


def met_at(d, block, bands, slots_ref):
    own = jnp.broadcast_to(line(block.tgt, d), (block.cap, block.cap)).T
    same = [jnp.where(own == line(block.tgt, s ^ d), 1.0, 0.0).astype(BF16) for s in bands]
    met = product(slots_ref[d], jnp.concatenate(same, axis=1), ((1,), (1,)))
    return met[: block.levels] + met[block.levels :]


def land(table, bands, slots_ref, cols):
    cap = table.shape[1]
    row = lax.broadcasted_iota(jnp.int32, (cols, cap), 0).astype(F32)
    total = 0.0
    for i, s in enumerate(bands):
        landing = jnp.where(row == line(table, s), 1.0, 0.0).astype(BF16)
        total = total + product(slots_ref[0, :, i * cap : (i + 1) * cap], landing, ((1,), (1,)))
    levels = total.shape[0] // 2
    return total[:levels] + total[levels:]


def open_blocks(labels, refs, lev, n, levels, band):
    blocks = {}
    for r in labels:
        head = band // refs[0].shape[1] * levels
        if r == 0:
            whole = jnp.concatenate([refs[0][...], refs[1][...]], axis=0)
        else:
            whole = refs[0][...]
        refs = refs[1 + (r == 0) :]
        if r >= n // 2:
            size = (whole.shape[0] - 2 * n) // 2
            part = jnp.where(lev == 0, whole[:size], whole[size + 2 * n :])
            whole = jnp.concatenate([part[:-EXTRA], whole[size : size + 2 * n], part[-EXTRA:]], axis=0)
        at = head + 2 * levels
        weight, base = whole[head : head + levels], whole[head + levels : at]
        blocks[r] = Block(whole[:head], weight, base, whole[at : at + 2 * n], whole[at + 2 * n :], lev, n, band)
    return blocks, refs


def stage_kernel(n, levels, band, cols, stages, lev_ref, *refs):
    known = sum(stages[:-1], [])
    blocks, refs = open_blocks(known + stages[-1], refs, lev_ref[0], n, levels, band)
    old, refs = refs[: len(stages) - 1], refs[len(stages) - 1 :]
    if known:
        met_old, remap_old, slots_ref, met_ref, remap_ref = refs
    else:
        slots_ref, met_ref, remap_ref, pick_ref = refs
        for d in range(n):
            pick_ref[d] = pick_source(blocks[0], d)
    fill_slots(stages[-1], blocks, n, slots_ref)
    for i, (d, block) in enumerate(blocks.items()):
        met = met_at(d, block, stages[-1], slots_ref)
        if d in known:
            met = met + met_old[i]
        else:
            for bands, ref in zip(stages, old):
                met = met + met_at(d, block, bands, ref)
        met_ref[i] = met
    landed = land(blocks[0].tgt, stages[-1], slots_ref, cols)
    remap_ref[...] = landed + remap_old[...] if known else landed


def shared_kernel(n, levels, band, cols, stages, pos_ref, lev_ref, *refs):
    known = sum(stages[:-1], [])
    blocks, refs = open_blocks(known + stages[-1], refs, lev_ref[0], n, levels, band)
    old, refs = refs[: len(stages) - 1], refs[len(stages) - 1 :]
    met_old, pick_ref, out_ref, slots_ref, tables_ref = refs
    me = pos_ref[0]
    for r, block in blocks.items():
        there = me ^ relabel(r, n, lev_ref[0])
        tables_ref[there, :n, :] = block.tgt
        tables_ref[there, n:, :] = block.edge
    fill_slots(stages[-1], blocks, n, slots_ref)
    last = cols - 1.0
    total = jnp.zeros((levels, band), F32)
    for i, (d, block) in enumerate(blocks.items()):
        value = met_at(d, block, stages[-1], slots_ref) + block.base
        if d in known:
            value = value + met_old[i]
        else:
            for bands, ref in zip(stages, old):
                value = value + met_at(d, block, bands, ref)
        edge = line(block.edge, 0)
        own = line(block.tgt, d)
        there = me ^ relabel(d, n, lev_ref[0])
        before = tables_ref[jnp.maximum(there - 1, 0), n : n + 1, :]
        near = jnp.where((own == 0.0) & (there > 0), edge[:, 6 * levels + 1 : 6 * levels + 2], 0.0)
        value = value + row_as_column(before, levels, 0) * near
        after = tables_ref[jnp.minimum(there + 1, n - 1), n : n + 1, :]
        near = jnp.where((own == last) & (there < n - 1), edge[:, 6 * levels : 6 * levels + 1], 0.0)
        value = value + row_as_column(after, levels, levels) * near
        given = block.weight * value * line(blocks[0].factor, d)
        total = total + select(given, pick_ref[d], ((1,), (1,)))
    out_ref[...] = stack(total, out_ref.shape[1])


def outputs_kernel(stages, pos_ref, lev_ref, *refs):
    slots_refs, refs = refs[: len(stages)], refs[len(stages) :]
    remap_ref, tables_ref, static_ref, diag_ref, off_ref, obs_ref, innov_ref, increment_ref, grad_ref = refs
    levels, cols = static_ref.shape
    n = tables_ref.shape[0]
    cap = tables_ref.shape[2]
    me = pos_ref[0]
    given = [
        (s, ref, slice(i * cap, (i + 1) * cap)) for bands, ref in zip(stages, slots_refs) for i, s in enumerate(bands)
    ]
    remapped = remap_ref[...] + land(tables_ref[me, :n, :], stages[-1], slots_refs[-1], cols)
    static, off = static_ref[...], off_ref[...]
    lane = lax.broadcasted_iota(jnp.int32, (levels, cols), 1)

    def beside(there, exists, column, own_end, side):
        edge = tables_ref[there, n : n + 1, :]
        static_end, coupling, base = (row_as_column(edge, levels, (2 * i + side) * levels) for i in range(3))
        far = relabel(me ^ there, n, lev_ref[0])
        landed = []
        for s, ref, place in given:
            values = ref[far, :levels, place].astype(F32) + ref[far, levels:, place].astype(F32)
            landed.append(jnp.where(tables_ref[there, pl.ds(s ^ far, 1), :] == column, values, 0.0))
        remap_end = jnp.sum(sum(landed), axis=1, keepdims=True)
        off_end = edge[:, 6 * levels + side : 6 * levels + side + 1]
        coupled = coupling * (remap_end + base + off_end * own_end)
        return jnp.where(exists, static_end, 0.0), jnp.where(exists, coupled, 0.0)

    before, coupled_before = beside(jnp.maximum(me - 1, 0), me > 0, cols - 1.0, static[:, :1], 0)
    after, coupled_after = beside(jnp.minimum(me + 1, n - 1), me < n - 1, 0.0, static[:, cols - 1 :], 1)
    left = jnp.where(lane == 0, before, pltpu.roll(static, 1, 1))
    right = jnp.where(lane == cols - 1, after, pltpu.roll(static, cols - 1, 1))
    increment = remapped + diag_ref[...] * static + off * (left + right)
    increment_ref[...] = increment
    misfit = obs_ref[...] * (increment - innov_ref[...])
    coupled = off * misfit
    left = jnp.where(lane == 0, coupled_before, pltpu.roll(coupled, 1, 1))
    right = jnp.where(lane == cols - 1, coupled_after, pltpu.roll(coupled, cols - 1, 1))
    grad_ref[...] = static + diag_ref[...] * misfit + left + right


def call(kernel, out_shape, spaces, scratch=(), out=VMEM, cost=None):
    return pl.pallas_call(
        kernel,
        out_shape=out_shape,
        in_specs=spaces,
        out_specs=jax.tree.map(lambda _: out, out_shape),
        scratch_shapes=scratch,
        cost_estimate=cost,
        compiler_params=pltpu.CompilerParams(vmem_limit_bytes=40 * MIB),
    )


def body(
    perturb,
    control,
    level_loc,
    static_control,
    filter_diag,
    filter_off,
    send_src,
    send_wt,
    counts,
    recv_tgt,
    obs_weight,
    innovation,
):
    levels, members, band_cols = control.shape
    tile_cols = static_control.shape[1]
    n = lax.axis_size("tile")
    groups = lax.axis_size("grp")
    cap = send_src.shape[2]
    shape = jax.ShapeDtypeStruct
    swap = [(0, 1), (1, 0)]
    lev = lax.axis_index("lev").astype(jnp.int32).reshape(1)
    pos = lax.axis_index("tile").astype(jnp.int32).reshape(1)
    other_control = lax.ppermute(control, "lev", swap)
    other_perturb = lax.ppermute(perturb, "lev", swap)
    width = levels * SUB
    sum_mix, ens_mix = call(
        mix_kernel,
        (shape((4 * width, 2 * width), BF16), shape((4, width, width), BF16)),
        [SMEM] + [VMEM] * 2,
        cost=pl.CostEstimate(flops=10**9, bytes_accessed=0, transcendentals=0),
    )(lev, level_loc, lax.ppermute(level_loc, "lev", swap))
    sums = call(sum_kernel, shape((2 * levels + SUB, band_cols), F32), [VMEM] * 5)(
        perturb, other_perturb, control, other_control, sum_mix
    )
    flat = shape((levels, tile_cols), F32)
    mine_shape = shape((band_cols // cap * levels, cap), F32)
    diag, off = filter_diag.reshape(1, -1), filter_off.reshape(1, -1)
    if n * cap <= tile_cols and n >= 8 and lax.axis_size("lev") == 2 and n & (n - 1) == 0 and band_cols * tile_cols <= 2**20:
        rows = Rows(levels, n)
        stacked = band_cols // cap * levels
        low, high = n // 4, n // 2
        part = shape((rows.total, cap), F32)
        sums, counts = lax.optimization_barrier((sums, counts))
        *rests, give = call(
            functools.partial(static_kernel, n, band_cols),
            [part] * (high + low) + [shape((2 * levels * low + EXTRA, cap), F32)],
            [SMEM] * 3 + [VMEM] * 8,
        )(pos, lev, counts, static_control, diag, off, obs_weight, innovation, send_src, send_wt, recv_tgt)
        given = lax.ppermute(give, "lev", swap)
        sums = [sums]
        for k in range(1, groups):
            sums.append(lax.ppermute(sums[0], "grp", [(g, (g + k) % groups) for g in range(groups)]))
        total, *blocks = call(
            functools.partial(blocks_kernel, groups, high - 1, levels),
            [shape((stacked, cap), F32)]
            + [shape((stacked + rows.total, cap), F32)] * (high - 1)
            + [shape((2 * stacked + 4 * levels + 2 * n + 2 * EXTRA, cap), F32)] * low,
            [SMEM] + [VMEM] * (groups + high + low),
        )(lev, *sums, *rests[1:], given)
        arrived = {0: [total, rests[0]]}
        for r in range(high, high + low):
            pairs = [(i * 2 + v, (i ^ relabel(r, n, v)) * 2 + v) for i in range(n) for v in range(2)]
            arrived[r] = [lax.ppermute(blocks[r - 1], ("tile", "lev"), pairs)]
        for r in reversed(range(1, high)):
            arrived[r] = [lax.ppermute(blocks[r - 1], "tile", [(i, i ^ r) for i in range(n)])]
        for r in range(high, high + low):
            arrived[r + low] = [lax.ppermute(arrived[r][0], "lev", swap)]
        stages = [[0, high, high - 1], [*range(high + 1, n - 1), *range(2, high - 1)], [1, n - 1]]
        slots, carried, picks = [], [], []
        for count in range(1, len(stages)):
            labels = sum(stages[:count], [])
            refs = [ref for r in labels for ref in arrived[r]]
            outs = [
                shape((n, 2 * levels, len(stages[count - 1]) * cap), BF16),
                shape((len(labels), levels, cap), F32),
                flat,
            ] + [shape((n, band_cols, cap), BF16)] * (count == 1)
            new, *carried = call(
                functools.partial(stage_kernel, n, levels, band_cols, tile_cols, stages[:count]),
                outs,
                [SMEM] + [VMEM] * (len(refs) + len(slots) + len(carried)),
                cost=pl.CostEstimate(flops=10**9, bytes_accessed=0, transcendentals=0),
            )(lev, *refs, *slots, *carried)
            slots.append(new)
            picks += carried[2:]
            carried = carried[:2]
        met, remap = carried
        refs = [ref for r in sum(stages, []) for ref in arrived[r]] + slots + [met] + picks
        mine, new, tables = call(
            functools.partial(shared_kernel, n, levels, band_cols, tile_cols, stages),
            (mine_shape, shape((n, 2 * levels, len(stages[-1]) * cap), BF16), shape((n, n + EXTRA, cap), F32)),
            [SMEM] * 2 + [VMEM] * len(refs),
            cost=pl.CostEstimate(flops=10**9, bytes_accessed=0, transcendentals=0),
        )(pos, lev, *refs)
        slots.append(new)
        increment, grad_static = call(
            functools.partial(outputs_kernel, stages), (flat, flat), [SMEM] * 2 + [VMEM] * (len(slots) + 7)
        )(pos, lev, *slots, remap, tables, static_control, diag, off, obs_weight, innovation)
    else:
        payload = call(
            band_kernel,
            shape((groups, n, levels + EXTRA, cap), F32),
            [SMEM] + [VMEM] * 4,
            [pltpu.VMEM((2 * levels, band_cols), BF16)],
        )(counts, sums, static_control, send_src, send_wt)
        arrived = lax.all_to_all(
            payload.reshape(groups * n, levels + EXTRA, cap), ("grp", "tile"), split_axis=0, concat_axis=0, tiled=True
        ).reshape(groups, n, levels + EXTRA, cap)
        increment, partial, giving = call(
            tile_kernel, (flat, flat, shape((n, levels + EXTRA, cap), F32)), [SMEM] + [VMEM] * 7
        )(pos, arrived, recv_tgt, static_control, diag, off, obs_weight, innovation)
        returned = lax.all_to_all(giving, "tile", split_axis=0, concat_axis=0, tiled=True)
        grad_static, mine = call(
            functools.partial(adjoint_kernel, band_cols), (flat, mine_shape), [SMEM, SMEM] + [VMEM] * 4
        )(pos, counts, returned, send_src, send_wt, partial)
    theirs = lax.ppermute(mine, "lev", swap)
    own = call(ens_own_kernel, shape(control.shape, F32), [VMEM] * 4)(perturb, mine, ens_mix, control)
    grad_ens, increment, grad_static = call(
        ens_kernel,
        (shape(control.shape, F32), flat, flat),
        [VMEM] * 6,
        [pltpu.VMEM(control.shape, F32), pltpu.SemaphoreType.DMA((2 + members // SUB,))],
        out=HBM,
    )(other_perturb, theirs, ens_mix, own, increment, grad_static)
    return (increment, grad_static, grad_ens)


def solution(mesh):
    return jax.shard_map(
        body,
        mesh=mesh,
        in_specs=(
            P("lev", "grp", "tile"),
            P("lev", "grp", "tile"),
            P("lev", None),
            P("lev", "tile"),
            P("tile"),
            P("tile"),
            P("tile", None, None),
            P("tile", None, None),
            P("tile", None),
            P("tile", None, None),
            P("lev", "tile"),
            P("lev", "tile"),
        ),
        out_specs=(P("lev", "tile"), P("lev", "tile"), P("lev", "grp", "tile")),
        check_vma=False,
    )
```

```python
import functools

import jax
import jax.numpy as jnp
from jax import lax
from jax.experimental import pallas as pl
from jax.experimental.pallas import tpu as pltpu
from jax.sharding import PartitionSpec as P

F32 = jnp.float32
BF16 = jnp.bfloat16
SUB = 8
EXTRA = 8
VMEM = pl.BlockSpec(memory_space=pltpu.VMEM)
HBM = pl.BlockSpec(memory_space=pltpu.HBM)
SMEM = pl.BlockSpec(memory_space=pltpu.SMEM)
MIB = 1024 * 1024


def halves(values):
    high = values.astype(BF16)
    low = (values - high.astype(F32)).astype(BF16)
    return high, low


def product(a, b, dims=((1,), (0,))):
    return lax.dot_general(a, b, (dims, ((), ())), preferred_element_type=F32)


def select(values, chosen, dims=((1,), (0,))):
    rows = values.shape[0]
    both = product(jnp.concatenate(halves(values), axis=0), chosen, dims)
    return both[:rows] + both[rows:]


def iota(shape, axis):
    return lax.broadcasted_iota(jnp.int32, shape, axis)


def wide_rows(matrix, start, count):
    cols = matrix.shape[1]
    shape = (cols, count * SUB)
    place = (iota(shape, 1) // SUB + start) % cols
    pick = (place == iota(shape, 0)).astype(BF16)
    high, low = halves(matrix)
    return product(high, pick) + product(low, pick)


def spread(wide):
    rows, cols = wide.shape
    tall = jnp.broadcast_to(wide[:, None, :], (rows, SUB, cols)).reshape(rows * SUB, cols)
    return jnp.where(iota(tall.shape, 0) % SUB == iota(tall.shape, 1) % SUB, tall, 0.0)


def mix(weights, values):
    high, low = halves(values)
    rows = weights[0].shape[0]
    both = product(jnp.concatenate(weights, axis=0), high)
    return both[:rows] + (product(weights[0], low) + both[rows:])


def one_hot(index, size):
    rows = lax.broadcasted_iota(jnp.int32, (size, index.shape[1]), 0)
    return jnp.where(rows == index, 1.0, 0.0).astype(BF16)


def column_as_row(column, lane, offset):
    n = column.shape[0]
    place = lax.broadcasted_iota(jnp.int32, (n, 128), 1) == lax.broadcasted_iota(jnp.int32, (n, 128), 0) + offset
    return jnp.sum(jnp.where(place, column, 0.0), axis=0, keepdims=True)


def row_as_column(row, n, offset):
    place = lax.broadcasted_iota(jnp.int32, (n, 128), 1) == lax.broadcasted_iota(jnp.int32, (n, 128), 0) + offset
    return jnp.sum(jnp.where(place, row, 0.0), axis=1, keepdims=True)


def edge_rows(values):
    n = values.shape[0]
    row = column_as_row(values[:, -1:], None, 0) + column_as_row(values[:, :1], None, n)
    return jnp.broadcast_to(row, (EXTRA, 128))


def factor_of(counts_ref, weight_ref, d):
    slot = lax.broadcasted_iota(jnp.int32, (1, weight_ref.shape[2]), 1)
    return jnp.where(slot < counts_ref[0, d], weight_ref[0, pl.ds(d, 1), :], 0.0)


def loop(n, step, init):
    return lax.fori_loop(0, n, step, init, unroll=n if n <= 8 else 1)


def mix_kernel(lev_ref, loc_ref, mix_ref, own_ref, given_ref):
    levels = loc_ref.shape[0]
    start = lev_ref[0] * levels
    loc = loc_ref[...]
    mix_ref[0], mix_ref[1] = halves(spread(wide_rows(loc, start, 2 * levels)))
    own_ref[0], own_ref[1] = halves(spread(wide_rows(loc, start, levels)).T)
    given_ref[...] = wide_rows(loc, levels - start, levels)


def sum_kernel(perturb_ref, control_ref, other_ref, mix_ref, out_ref):
    levels, members, cols = perturb_ref.shape
    perturb = perturb_ref[...].astype(F32)
    total = jnp.zeros((levels, SUB, cols), F32)
    for m in range(0, members, SUB):
        tile = jnp.concatenate([control_ref[:, m : m + SUB, :], other_ref[:, m : m + SUB, :]], axis=0)
        mixed = mix((mix_ref[0], mix_ref[1]), tile.reshape(2 * levels * SUB, cols))
        total = total + perturb[:, m : m + SUB, :] * mixed.reshape(levels, SUB, cols)
    out_ref[...] = jnp.sum(total, axis=1)


def band_kernel(counts_ref, sum_ref, static_ref, src_ref, weight_ref, out_ref, acc_ref):
    levels, cols = sum_ref.shape
    acc_ref[...] = jnp.concatenate(halves(sum_ref[...]), axis=0)
    n = src_ref.shape[1]
    edges = edge_rows(static_ref[...])

    def step(d, carry):
        chosen = one_hot(src_ref[0, pl.ds(d, 1), :], cols)
        both = product(acc_ref[...], chosen)
        payload = (both[:levels] + both[levels:]) * factor_of(counts_ref, weight_ref, d)
        for g in range(out_ref.shape[0]):
            out_ref[g, d, :levels, :] = payload
            out_ref[g, d, levels:, :] = edges
        return carry

    loop(n, step, 0)


def tile_kernel(pos_ref, arrived_ref, tgt_ref, static_ref, diag_ref, off_ref, obs_ref, innov_ref,
                increment_ref, partial_ref, out_ref):
    levels, cols = static_ref.shape
    groups, n = arrived_ref.shape[:2]
    me = pos_ref[0]

    def step(s, total):
        values = sum(arrived_ref[g, s, :levels, :] for g in range(groups))
        chosen = one_hot(tgt_ref[0, pl.ds(s, 1), :], cols)
        return total + select(values, chosen, ((1,), (1,)))

    remapped = loop(n, step, jnp.zeros((levels, cols), F32))
    before = arrived_ref[0, jnp.maximum(me - 1, 0), levels : levels + 1, :]
    after = arrived_ref[0, jnp.minimum(me + 1, n - 1), levels : levels + 1, :]
    before = jnp.where(me > 0, row_as_column(before, levels, 0), 0.0)
    after = jnp.where(me < n - 1, row_as_column(after, levels, levels), 0.0)
    static = static_ref[...]
    lane = lax.broadcasted_iota(jnp.int32, (levels, cols), 1)
    left = jnp.where(lane == 0, before, pltpu.roll(static, 1, 1))
    right = jnp.where(lane == cols - 1, after, pltpu.roll(static, cols - 1, 1))
    increment = remapped + diag_ref[...] * static + off_ref[...] * (left + right)
    increment_ref[...] = increment
    misfit = obs_ref[...] * (increment - innov_ref[...])
    coupled = off_ref[...] * misfit
    left = jnp.where(lane == 0, 0.0, pltpu.roll(coupled, 1, 1))
    right = jnp.where(lane == cols - 1, 0.0, pltpu.roll(coupled, cols - 1, 1))
    partial_ref[...] = static + diag_ref[...] * misfit + left + right
    edges = edge_rows(coupled)
    both = jnp.concatenate(halves(misfit), axis=0)

    def give(s, carry):
        chosen = one_hot(tgt_ref[0, pl.ds(s, 1), :], cols)
        picked = product(both, chosen)
        out_ref[s, :levels, :] = picked[:levels] + picked[levels:]
        out_ref[s, levels:, :] = edges
        return carry

    loop(n, give, 0)


def adjoint_kernel(band, pos_ref, counts_ref, returned_ref, src_ref, weight_ref, partial_ref, mix_ref, grad_ref, out_ref):
    levels, cols = partial_ref.shape
    n = returned_ref.shape[0]
    me = pos_ref[0]

    def step(d, total):
        values = returned_ref[d, :levels, :] * factor_of(counts_ref, weight_ref, d)
        return total + select(values, one_hot(src_ref[0, pl.ds(d, 1), :], band), ((1,), (1,)))

    out_ref[...] = band_rows(loop(n, step, jnp.zeros((levels, band), F32)), mix_ref[...])
    before = returned_ref[jnp.maximum(me - 1, 0), levels : levels + 1, :]
    after = returned_ref[jnp.minimum(me + 1, n - 1), levels : levels + 1, :]
    before = jnp.where(me > 0, row_as_column(before, levels, 0), 0.0)
    after = jnp.where(me < n - 1, row_as_column(after, levels, levels), 0.0)
    lane = lax.broadcasted_iota(jnp.int32, (levels, cols), 1)
    grad_ref[...] = partial_ref[...] + (jnp.where(lane == 0, before, 0.0) + jnp.where(lane == cols - 1, after, 0.0))


def band_rows(band, weights):
    width = weights.shape[1]
    return jnp.concatenate([band[:, at : at + width] for at in range(0, band.shape[1], width)] + [weights], axis=0)


def ens_tiles(perturb_ref, rows_ref, weights, before_ref):
    levels, members, cols = perturb_ref.shape
    width = rows_ref.shape[1]
    parts = [rows_ref[i * levels : (i + 1) * levels, :] for i in range(cols // width)]
    grad = jnp.concatenate(parts, axis=1)[:, None, :]
    perturb = perturb_ref[...].astype(F32)
    for m in range(0, members, SUB):
        place = (slice(None), slice(m, m + SUB), slice(None))
        tile = (perturb[place] * grad).reshape(levels * SUB, cols)
        yield place, before_ref[place] + mix(weights, tile).reshape(levels, SUB, cols)


def ens_own_kernel(perturb_ref, mine_ref, weights_ref, control_ref, out_ref):
    for place, values in ens_tiles(perturb_ref, mine_ref, (weights_ref[0], weights_ref[1]), control_ref):
        out_ref[place] = values


def ens_kernel(perturb_ref, theirs_ref, own_ref, *refs):
    count = (len(refs) - 3) // 2
    flats, (out_hbm, *flat_hbms), (out_ref, sems) = refs[:count], refs[count : 2 * count + 1], refs[2 * count + 1 :]
    copies = [pltpu.make_async_copy(a, b, sems.at[i]) for i, (a, b) in enumerate(zip(flats, flat_hbms))]
    for copy in copies:
        copy.start()
    levels = perturb_ref.shape[0]
    weights = halves(spread(theirs_ref[theirs_ref.shape[0] - levels :, :]).T)
    for place, values in ens_tiles(perturb_ref, theirs_ref, weights, own_ref):
        out_ref[place] = values
        copies.append(pltpu.make_async_copy(out_ref.at[place], out_hbm.at[place], sems.at[len(copies)]))
        copies[-1].start()
    for copy in copies:
        copy.wait()


def relabel(r, n, lev):
    high, low = n // 2, n // 4
    if low == 0:
        return r
    both = high | low
    turned = (r & ~both) | ((r & low) << 1) | ((r & high) >> 1)
    return r + (turned - r) * lev


class Rows:
    def __init__(self, levels, n):
        self.weight = slice(0, levels)
        self.base = slice(levels, 2 * levels)
        at = 2 * levels
        self.factor, self.index, self.edge = at, at + n, at + 2 * n
        self.total = at + 2 * n + EXTRA


def static_kernel(band, pos_ref, lev_ref, counts_ref, static_ref, diag_ref, off_ref, obs_ref, innov_ref, src_ref, weight_ref, tgt_ref,
                  *out_refs):
    levels, cols = static_ref.shape
    n = len(out_refs)
    cap = src_ref.shape[2]
    rows = Rows(levels, n)
    peers = [pos_ref[0] ^ relabel(r, n, lev_ref[0]) for r in range(n)]
    static, off, obs = static_ref[...], off_ref[...], obs_ref[...]
    lane = lax.broadcasted_iota(jnp.int32, (levels, cols), 1)
    left = jnp.where(lane == 0, 0.0, pltpu.roll(static, 1, 1))
    right = jnp.where(lane == cols - 1, 0.0, pltpu.roll(static, cols - 1, 1))
    base = diag_ref[...] * static + off * (left + right) - innov_ref[...]
    coupled = off * obs
    ends = [v[:, i] for v in (static, coupled, base) for i in (slice(cols - 1, cols), slice(0, 1))]
    edge = sum(column_as_row(end, None, i * levels) for i, end in enumerate(ends))
    place = lax.broadcasted_iota(jnp.int32, (1, cap), 1)
    edge = edge + jnp.where(place == 6 * levels, off[:, cols - 1 :], 0.0)
    edge = edge + jnp.where(place == 6 * levels + 1, off[:, :1], 0.0)
    edge = jnp.broadcast_to(edge, (EXTRA, cap))
    both = jnp.concatenate(halves(jnp.concatenate([obs, base], axis=0)), axis=0)
    tgts = [tgt_ref[0, pl.ds(peer, 1), :] for peer in peers]
    src = jnp.concatenate([src_ref[0, pl.ds(peer, 1), :] for peer in peers], axis=0).astype(F32)
    index = jnp.concatenate(tgts, axis=0).astype(F32) * float(band) + src
    factor = jnp.concatenate([factor_of(counts_ref, weight_ref, peer) for peer in peers], axis=0)
    for r, out_ref in enumerate(out_refs):
        picked = product(both, one_hot(tgts[r], cols))
        out_ref[: 2 * levels, :] = picked[: 2 * levels] + picked[2 * levels :]
        out_ref[rows.factor : rows.factor + n, :] = factor
        out_ref[rows.index : rows.index + n, :] = index
        out_ref[rows.edge :, :] = edge


def blocks_kernel(groups, *refs):
    sums = refs[:groups]
    count = (len(refs) - groups - 1) // 2
    rests = refs[groups : groups + count]
    total_ref = refs[groups + count]
    out_refs = refs[groups + count + 1 :]
    total = sum(ref[...] for ref in sums)
    cap = total_ref.shape[1]
    total = jnp.concatenate([total[:, at : at + cap] for at in range(0, total.shape[1], cap)], axis=0)
    total_ref[...] = total
    for rest_ref, out_ref in zip(rests, out_refs):
        out_ref[: total.shape[0], :] = total
        out_ref[total.shape[0] :, :] = rest_ref[...]


class Block:
    def __init__(self, refs, n, levels, band):
        cap = refs[0].shape[1]
        self.levels, self.parts, self.cap = levels, band // cap, cap
        self.sums_ref, self.rest_ref = refs[0], refs[-1]
        self.head = 0 if len(refs) == 2 else self.parts * levels
        self.rows = Rows(levels, n)
        words = self.rest(self.rows.index, n)
        self.tgt = jnp.floor((words + 0.5) * (1.0 / band))
        self.src = words - self.tgt * float(band)
        self.factor = self.rest(self.rows.factor, n)

    def rest(self, at, size):
        return self.rest_ref[self.head + at : self.head + at + size, :]

    def sums(self):
        parts = [self.sums_ref[i * self.levels : (i + 1) * self.levels, :] for i in range(self.parts)]
        return jnp.concatenate(halves(jnp.concatenate(parts, axis=1)), axis=0)


def line(table, i):
    return table[i : i + 1]


def pick_source(block, r):
    band = block.parts * block.cap
    column = lax.broadcasted_iota(jnp.int32, (band, block.cap), 0).astype(F32)
    return jnp.where(column == line(block.src, r), 1.0, 0.0).astype(BF16)


def fill_slots(bands, blocks, n, slots_ref):
    for i, s in enumerate(bands):
        block = blocks[s]
        both = block.sums()
        for d in range(n):
            picked = product(both, pick_source(block, s ^ d))
            values = (picked[: block.levels] + picked[block.levels :]) * line(block.factor, s ^ d)
            slots_ref[d, :, i * block.cap : (i + 1) * block.cap] = jnp.concatenate(halves(values), axis=0)


def met_at(d, block, bands, slots_ref):
    own = jnp.broadcast_to(line(block.tgt, d), (block.cap, block.cap)).T
    same = [jnp.where(own == line(block.tgt, s ^ d), 1.0, 0.0).astype(BF16) for s in bands]
    met = product(slots_ref[d], jnp.concatenate(same, axis=1), ((1,), (1,)))
    return met[: block.levels] + met[block.levels :]


def land(table, bands, slots_ref, cols):
    cap = table.shape[1]
    row = lax.broadcasted_iota(jnp.int32, (cols, cap), 0).astype(F32)
    total = 0.0
    for i, s in enumerate(bands):
        landing = jnp.where(row == line(table, s), 1.0, 0.0).astype(BF16)
        total = total + product(slots_ref[0, :, i * cap : (i + 1) * cap], landing, ((1,), (1,)))
    levels = total.shape[0] // 2
    return total[:levels] + total[levels:]


def open_blocks(labels, refs, n, levels, band):
    blocks = {0: Block(refs[:2], n, levels, band)}
    refs = refs[2:]
    for i, r in enumerate(labels[1:]):
        blocks[r] = Block(refs[i : i + 1], n, levels, band)
    return blocks, refs[len(labels) - 1 :]


def stage_kernel(n, levels, band, cols, stages, *refs):
    known = sum(stages[:-1], [])
    blocks, refs = open_blocks(known + stages[-1], refs, n, levels, band)
    old, refs = refs[: len(stages) - 1], refs[len(stages) - 1 :]
    if known:
        met_old, remap_old, slots_ref, met_ref, remap_ref = refs
    else:
        slots_ref, met_ref, remap_ref, pick_ref = refs
        for d in range(n):
            pick_ref[d] = pick_source(blocks[0], d)
    fill_slots(stages[-1], blocks, n, slots_ref)
    for i, (d, block) in enumerate(blocks.items()):
        met = met_at(d, block, stages[-1], slots_ref)
        if d in known:
            met = met + met_old[i]
        else:
            for bands, ref in zip(stages, old):
                met = met + met_at(d, block, bands, ref)
        met_ref[i] = met
    landed = land(blocks[0].tgt, stages[-1], slots_ref, cols)
    remap_ref[...] = landed + remap_old[...] if known else landed


def shared_kernel(n, levels, band, cols, stages, pos_ref, lev_ref, mix_ref, *refs):
    known = sum(stages[:-1], [])
    blocks, refs = open_blocks(known + stages[-1], refs, n, levels, band)
    old, refs = refs[: len(stages) - 1], refs[len(stages) - 1 :]
    met_old, pick_ref, out_ref, slots_ref, tables_ref = refs
    me = pos_ref[0]
    for r, block in blocks.items():
        there = me ^ relabel(r, n, lev_ref[0])
        tables_ref[there, :n, :] = block.tgt
        tables_ref[there, n:, :] = block.rest(block.rows.edge, EXTRA)
    fill_slots(stages[-1], blocks, n, slots_ref)
    last = cols - 1.0
    total = jnp.zeros((levels, band), F32)
    for i, (d, block) in enumerate(blocks.items()):
        value = met_at(d, block, stages[-1], slots_ref) + block.rest(levels, levels)
        if d in known:
            value = value + met_old[i]
        else:
            for bands, ref in zip(stages, old):
                value = value + met_at(d, block, bands, ref)
        edge = block.rest(block.rows.edge, 1)
        own = line(block.tgt, d)
        there = me ^ relabel(d, n, lev_ref[0])
        before = tables_ref[jnp.maximum(there - 1, 0), n : n + 1, :]
        near = jnp.where((own == 0.0) & (there > 0), edge[:, 6 * levels + 1 : 6 * levels + 2], 0.0)
        value = value + row_as_column(before, levels, 0) * near
        after = tables_ref[jnp.minimum(there + 1, n - 1), n : n + 1, :]
        near = jnp.where((own == last) & (there < n - 1), edge[:, 6 * levels : 6 * levels + 1], 0.0)
        value = value + row_as_column(after, levels, levels) * near
        given = block.rest(0, levels) * value * line(blocks[0].factor, d)
        total = total + select(given, pick_ref[d], ((1,), (1,)))
    out_ref[...] = band_rows(total, mix_ref[...])


def outputs_kernel(stages, pos_ref, lev_ref, *refs):
    slots_refs, refs = refs[: len(stages)], refs[len(stages) :]
    remap_ref, tables_ref, static_ref, diag_ref, off_ref, obs_ref, innov_ref, increment_ref, grad_ref = refs
    levels, cols = static_ref.shape
    n = tables_ref.shape[0]
    cap = tables_ref.shape[2]
    me = pos_ref[0]
    given = [
        (s, ref, slice(i * cap, (i + 1) * cap)) for bands, ref in zip(stages, slots_refs) for i, s in enumerate(bands)
    ]
    remapped = remap_ref[...] + land(tables_ref[me, :n, :], stages[-1], slots_refs[-1], cols)
    static, off = static_ref[...], off_ref[...]
    lane = lax.broadcasted_iota(jnp.int32, (levels, cols), 1)

    def beside(there, exists, column, own_end, side):
        edge = tables_ref[there, n : n + 1, :]
        static_end, coupling, base = (row_as_column(edge, levels, (2 * i + side) * levels) for i in range(3))
        far = relabel(me ^ there, n, lev_ref[0])
        landed = []
        for s, ref, place in given:
            values = ref[far, :levels, place].astype(F32) + ref[far, levels:, place].astype(F32)
            landed.append(jnp.where(tables_ref[there, pl.ds(s ^ far, 1), :] == column, values, 0.0))
        remap_end = jnp.sum(sum(landed), axis=1, keepdims=True)
        off_end = edge[:, 6 * levels + side : 6 * levels + side + 1]
        coupled = coupling * (remap_end + base + off_end * own_end)
        return jnp.where(exists, static_end, 0.0), jnp.where(exists, coupled, 0.0)

    before, coupled_before = beside(jnp.maximum(me - 1, 0), me > 0, cols - 1.0, static[:, :1], 0)
    after, coupled_after = beside(jnp.minimum(me + 1, n - 1), me < n - 1, 0.0, static[:, cols - 1 :], 1)
    left = jnp.where(lane == 0, before, pltpu.roll(static, 1, 1))
    right = jnp.where(lane == cols - 1, after, pltpu.roll(static, cols - 1, 1))
    increment = remapped + diag_ref[...] * static + off * (left + right)
    increment_ref[...] = increment
    misfit = obs_ref[...] * (increment - innov_ref[...])
    coupled = off * misfit
    left = jnp.where(lane == 0, coupled_before, pltpu.roll(coupled, 1, 1))
    right = jnp.where(lane == cols - 1, coupled_after, pltpu.roll(coupled, cols - 1, 1))
    grad_ref[...] = static + diag_ref[...] * misfit + left + right


def call(kernel, out_shape, spaces, scratch=(), out=VMEM, cost=None):
    return pl.pallas_call(
        kernel,
        out_shape=out_shape,
        in_specs=spaces,
        out_specs=jax.tree.map(lambda _: out, out_shape),
        scratch_shapes=scratch,
        cost_estimate=cost,
        compiler_params=pltpu.CompilerParams(vmem_limit_bytes=40 * MIB),
    )


def body(
    perturb,
    control,
    level_loc,
    static_control,
    filter_diag,
    filter_off,
    send_src,
    send_wt,
    counts,
    recv_tgt,
    obs_weight,
    innovation,
):
    levels, members, band_cols = control.shape
    tile_cols = static_control.shape[1]
    n = lax.axis_size("tile")
    groups = lax.axis_size("grp")
    cap = send_src.shape[2]
    shape = jax.ShapeDtypeStruct
    swap = [(0, 1), (1, 0)]
    lev = lax.axis_index("lev").astype(jnp.int32).reshape(1)
    pos = lax.axis_index("tile").astype(jnp.int32).reshape(1)
    other_control = lax.ppermute(control, "lev", swap)
    width = levels * SUB
    level_mix, own_mix, given_mix = call(
        mix_kernel,
        (shape((2, width, 2 * width), BF16), shape((2, width, width), BF16), shape((levels, width), F32)),
        [SMEM, VMEM],
        cost=pl.CostEstimate(flops=10**9, bytes_accessed=0, transcendentals=0),
    )(lev, level_loc)
    own_sum = call(sum_kernel, shape((levels, band_cols), F32), [VMEM] * 4)(perturb, control, other_control, level_mix)
    flat = shape((levels, tile_cols), F32)
    mine_shape = shape((band_cols // width * levels + levels, width), F32)
    diag, off = filter_diag.reshape(1, -1), filter_off.reshape(1, -1)
    if n * cap <= tile_cols and n >= 8 and lax.axis_size("lev") == 2 and n & (n - 1) == 0 and band_cols * tile_cols <= 2**20:
        rows = Rows(levels, n)
        stacked = band_cols // cap * levels
        rests = call(functools.partial(static_kernel, band_cols), [shape((rows.total, cap), F32)] * n, [SMEM] * 3 + [VMEM] * 8)(
            pos, lev, counts, static_control, diag, off, obs_weight, innovation, send_src, send_wt, recv_tgt
        )
        sums = [own_sum]
        sums[0], other_perturb = lax.optimization_barrier((sums[0], lax.ppermute(perturb, "lev", swap)))
        for k in range(1, groups):
            sums.append(lax.ppermute(sums[0], "grp", [(g, (g + k) % groups) for g in range(groups)]))
        total, *blocks = call(
            functools.partial(blocks_kernel, groups),
            [shape((stacked, cap), F32)] + [shape((stacked + rows.total, cap), F32)] * (n - 1),
            [VMEM] * (groups + n - 1),
        )(*sums, *rests[1:])
        low, high = n // 4, n // 2
        mixed = [r for i in reversed(range(low)) for r in (high + i, low + i)]
        order = [high + low, mixed[0], *range(high + low + 1, n), *mixed[1:], *range(1, low)]
        stages = [[0] + order[: high - 1], order[high - 1 : n - low], order[n - low :]]
        levs = lax.axis_size("lev")
        arrived = {0: [total, rests[0]]}
        for r in sum(stages, [])[1:]:
            pairs = [(i * levs + v, (i ^ relabel(r, n, v)) * levs + v) for i in range(n) for v in range(levs)]
            arrived[r] = [lax.ppermute(blocks[r - 1], ("tile", "lev"), pairs)]
        slots, carried, picks = [], [], []
        for count in range(1, len(stages)):
            labels = sum(stages[:count], [])
            refs = [ref for r in labels for ref in arrived[r]]
            outs = [
                shape((n, 2 * levels, len(stages[count - 1]) * cap), BF16),
                shape((len(labels), levels, cap), F32),
                flat,
            ] + [shape((n, band_cols, cap), BF16)] * (count == 1)
            new, *carried = call(
                functools.partial(stage_kernel, n, levels, band_cols, tile_cols, stages[:count]),
                outs,
                [VMEM] * (len(refs) + len(slots) + len(carried)),
            )(*refs, *slots, *carried)
            slots.append(new)
            picks += carried[2:]
            carried = carried[:2]
        met, remap = carried
        refs = [ref for r in sum(stages, []) for ref in arrived[r]] + slots + [met] + picks
        mine, new, tables = call(
            functools.partial(shared_kernel, n, levels, band_cols, tile_cols, stages),
            (mine_shape, shape((n, 2 * levels, len(stages[-1]) * cap), BF16), shape((n, n + EXTRA, cap), F32)),
            [SMEM] * 2 + [VMEM] * (1 + len(refs)),
        )(pos, lev, given_mix, *refs)
        slots.append(new)
        increment, grad_static = call(
            functools.partial(outputs_kernel, stages), (flat, flat), [SMEM] * 2 + [VMEM] * (len(slots) + 7)
        )(pos, lev, *slots, remap, tables, static_control, diag, off, obs_weight, innovation)
    else:
        other_perturb = lax.ppermute(perturb, "lev", swap)
        payload = call(
            band_kernel,
            shape((groups, n, levels + EXTRA, cap), F32),
            [SMEM] + [VMEM] * 4,
            [pltpu.VMEM((2 * levels, band_cols), BF16)],
        )(counts, own_sum, static_control, send_src, send_wt)
        arrived = lax.all_to_all(
            payload.reshape(groups * n, levels + EXTRA, cap), ("grp", "tile"), split_axis=0, concat_axis=0, tiled=True
        ).reshape(groups, n, levels + EXTRA, cap)
        increment, partial, giving = call(
            tile_kernel, (flat, flat, shape((n, levels + EXTRA, cap), F32)), [SMEM] + [VMEM] * 7
        )(pos, arrived, recv_tgt, static_control, diag, off, obs_weight, innovation)
        returned = lax.all_to_all(giving, "tile", split_axis=0, concat_axis=0, tiled=True)
        grad_static, mine = call(
            functools.partial(adjoint_kernel, band_cols), (flat, mine_shape), [SMEM, SMEM] + [VMEM] * 5
        )(pos, counts, returned, send_src, send_wt, partial, given_mix)
    theirs = lax.ppermute(mine, "lev", swap)
    own = call(ens_own_kernel, shape(control.shape, F32), [VMEM] * 4)(perturb, mine, own_mix, control)
    grad_ens, increment, grad_static = call(
        ens_kernel,
        (shape(control.shape, F32), flat, flat),
        [VMEM] * 5,
        [pltpu.VMEM(control.shape, F32), pltpu.SemaphoreType.DMA((2 + members // SUB,))],
        out=HBM,
    )(other_perturb, theirs, own, increment, grad_static)
    return (increment, grad_static, grad_ens)


def solution(mesh):
    return jax.shard_map(
        body,
        mesh=mesh,
        in_specs=(
            P("lev", "grp", "tile"),
            P("lev", "grp", "tile"),
            P("lev", None),
            P("lev", "tile"),
            P("tile"),
            P("tile"),
            P("tile", None, None),
            P("tile", None, None),
            P("tile", None),
            P("tile", None, None),
            P("lev", "tile"),
            P("lev", "tile"),
        ),
        out_specs=(P("lev", "tile"), P("lev", "tile"), P("lev", "grp", "tile")),
        check_vma=False,
    )
```

```python
import functools

import jax
import jax.numpy as jnp
from jax import lax
from jax.experimental import pallas as pl
from jax.experimental.pallas import tpu as pltpu
from jax.sharding import PartitionSpec as P

F32 = jnp.float32
BF16 = jnp.bfloat16
SUB = 8
EXTRA = 8
VMEM = pl.BlockSpec(memory_space=pltpu.VMEM)
HBM = pl.BlockSpec(memory_space=pltpu.HBM)
SMEM = pl.BlockSpec(memory_space=pltpu.SMEM)
MIB = 1024 * 1024


def halves(values):
    high = values.astype(BF16)
    low = (values - high.astype(F32)).astype(BF16)
    return high, low


def product(a, b, dims=((1,), (0,))):
    return lax.dot_general(a, b, (dims, ((), ())), preferred_element_type=F32)


def select(values, chosen, dims=((1,), (0,))):
    rows = values.shape[0]
    both = product(jnp.concatenate(halves(values), axis=0), chosen, dims)
    return both[:rows] + both[rows:]


def iota(shape, axis):
    return lax.broadcasted_iota(jnp.int32, shape, axis)


def wide_rows(matrix, start, count):
    cols = matrix.shape[1]
    shape = (cols, count * SUB)
    place = (iota(shape, 1) // SUB + start) % cols
    pick = (place == iota(shape, 0)).astype(BF16)
    high, low = halves(matrix)
    return product(high, pick) + product(low, pick)


def spread(wide):
    rows, cols = wide.shape
    tall = jnp.broadcast_to(wide[:, None, :], (rows, SUB, cols)).reshape(rows * SUB, cols)
    return jnp.where(iota(tall.shape, 0) % SUB == iota(tall.shape, 1) % SUB, tall, 0.0)


def mix(weights, values):
    high, low = halves(values)
    rows = weights[0].shape[0]
    both = product(jnp.concatenate(weights, axis=0), high)
    return both[:rows] + (product(weights[0], low) + both[rows:])


def one_hot(index, size):
    rows = lax.broadcasted_iota(jnp.int32, (size, index.shape[1]), 0)
    return jnp.where(rows == index, 1.0, 0.0).astype(BF16)


def column_as_row(column, lane, offset):
    n = column.shape[0]
    place = lax.broadcasted_iota(jnp.int32, (n, 128), 1) == lax.broadcasted_iota(jnp.int32, (n, 128), 0) + offset
    return jnp.sum(jnp.where(place, column, 0.0), axis=0, keepdims=True)


def row_as_column(row, n, offset):
    place = lax.broadcasted_iota(jnp.int32, (n, 128), 1) == lax.broadcasted_iota(jnp.int32, (n, 128), 0) + offset
    return jnp.sum(jnp.where(place, row, 0.0), axis=1, keepdims=True)


def edge_rows(values):
    n = values.shape[0]
    row = column_as_row(values[:, -1:], None, 0) + column_as_row(values[:, :1], None, n)
    return jnp.broadcast_to(row, (EXTRA, 128))


def factor_of(counts_ref, weight_ref, d):
    slot = lax.broadcasted_iota(jnp.int32, (1, weight_ref.shape[2]), 1)
    return jnp.where(slot < counts_ref[0, d], weight_ref[0, pl.ds(d, 1), :], 0.0)


def loop(n, step, init):
    return lax.fori_loop(0, n, step, init, unroll=n if n <= 8 else 1)


def mix_kernel(lev_ref, loc_ref, mix_ref, own_ref, given_ref):
    levels = loc_ref.shape[0]
    start = lev_ref[0] * levels
    loc = loc_ref[...]
    mix_ref[0], mix_ref[1] = halves(spread(wide_rows(loc, start, 2 * levels)))
    own_ref[0], own_ref[1] = halves(spread(wide_rows(loc, start, levels)).T)
    given_ref[...] = wide_rows(loc, levels - start, levels)


def sum_kernel(perturb_ref, control_ref, other_ref, mix_ref, out_ref):
    levels, members, cols = perturb_ref.shape
    perturb = perturb_ref[...].astype(F32)
    total = jnp.zeros((levels, SUB, cols), F32)
    for m in range(0, members, SUB):
        tile = jnp.concatenate([control_ref[:, m : m + SUB, :], other_ref[:, m : m + SUB, :]], axis=0)
        mixed = mix((mix_ref[0], mix_ref[1]), tile.reshape(2 * levels * SUB, cols))
        total = total + perturb[:, m : m + SUB, :] * mixed.reshape(levels, SUB, cols)
    out_ref[...] = jnp.sum(total, axis=1)


def band_kernel(counts_ref, sum_ref, static_ref, src_ref, weight_ref, out_ref, acc_ref):
    levels, cols = sum_ref.shape
    acc_ref[...] = jnp.concatenate(halves(sum_ref[...]), axis=0)
    n = src_ref.shape[1]
    edges = edge_rows(static_ref[...])

    def step(d, carry):
        chosen = one_hot(src_ref[0, pl.ds(d, 1), :], cols)
        both = product(acc_ref[...], chosen)
        payload = (both[:levels] + both[levels:]) * factor_of(counts_ref, weight_ref, d)
        for g in range(out_ref.shape[0]):
            out_ref[g, d, :levels, :] = payload
            out_ref[g, d, levels:, :] = edges
        return carry

    loop(n, step, 0)


def tile_kernel(pos_ref, arrived_ref, tgt_ref, static_ref, diag_ref, off_ref, obs_ref, innov_ref,
                increment_ref, partial_ref, out_ref):
    levels, cols = static_ref.shape
    groups, n = arrived_ref.shape[:2]
    me = pos_ref[0]

    def step(s, total):
        values = sum(arrived_ref[g, s, :levels, :] for g in range(groups))
        chosen = one_hot(tgt_ref[0, pl.ds(s, 1), :], cols)
        return total + select(values, chosen, ((1,), (1,)))

    remapped = loop(n, step, jnp.zeros((levels, cols), F32))
    before = arrived_ref[0, jnp.maximum(me - 1, 0), levels : levels + 1, :]
    after = arrived_ref[0, jnp.minimum(me + 1, n - 1), levels : levels + 1, :]
    before = jnp.where(me > 0, row_as_column(before, levels, 0), 0.0)
    after = jnp.where(me < n - 1, row_as_column(after, levels, levels), 0.0)
    static = static_ref[...]
    lane = lax.broadcasted_iota(jnp.int32, (levels, cols), 1)
    left = jnp.where(lane == 0, before, pltpu.roll(static, 1, 1))
    right = jnp.where(lane == cols - 1, after, pltpu.roll(static, cols - 1, 1))
    increment = remapped + diag_ref[...] * static + off_ref[...] * (left + right)
    increment_ref[...] = increment
    misfit = obs_ref[...] * (increment - innov_ref[...])
    coupled = off_ref[...] * misfit
    left = jnp.where(lane == 0, 0.0, pltpu.roll(coupled, 1, 1))
    right = jnp.where(lane == cols - 1, 0.0, pltpu.roll(coupled, cols - 1, 1))
    partial_ref[...] = static + diag_ref[...] * misfit + left + right
    edges = edge_rows(coupled)
    both = jnp.concatenate(halves(misfit), axis=0)

    def give(s, carry):
        chosen = one_hot(tgt_ref[0, pl.ds(s, 1), :], cols)
        picked = product(both, chosen)
        out_ref[s, :levels, :] = picked[:levels] + picked[levels:]
        out_ref[s, levels:, :] = edges
        return carry

    loop(n, give, 0)


def adjoint_kernel(band, pos_ref, counts_ref, returned_ref, src_ref, weight_ref, partial_ref, mix_ref, grad_ref, out_ref):
    levels, cols = partial_ref.shape
    n = returned_ref.shape[0]
    me = pos_ref[0]

    def step(d, total):
        values = returned_ref[d, :levels, :] * factor_of(counts_ref, weight_ref, d)
        return total + select(values, one_hot(src_ref[0, pl.ds(d, 1), :], band), ((1,), (1,)))

    out_ref[...] = band_rows(loop(n, step, jnp.zeros((levels, band), F32)), mix_ref[...])
    before = returned_ref[jnp.maximum(me - 1, 0), levels : levels + 1, :]
    after = returned_ref[jnp.minimum(me + 1, n - 1), levels : levels + 1, :]
    before = jnp.where(me > 0, row_as_column(before, levels, 0), 0.0)
    after = jnp.where(me < n - 1, row_as_column(after, levels, levels), 0.0)
    lane = lax.broadcasted_iota(jnp.int32, (levels, cols), 1)
    grad_ref[...] = partial_ref[...] + (jnp.where(lane == 0, before, 0.0) + jnp.where(lane == cols - 1, after, 0.0))


def band_rows(band, weights):
    width = weights.shape[1]
    return jnp.concatenate([band[:, at : at + width] for at in range(0, band.shape[1], width)] + [weights], axis=0)


def ens_tiles(perturb_ref, rows_ref, weights, before_ref):
    levels, members, cols = perturb_ref.shape
    width = rows_ref.shape[1]
    parts = [rows_ref[i * levels : (i + 1) * levels, :] for i in range(cols // width)]
    grad = jnp.concatenate(parts, axis=1)[:, None, :]
    perturb = perturb_ref[...].astype(F32)
    for m in range(0, members, SUB):
        place = (slice(None), slice(m, m + SUB), slice(None))
        tile = (perturb[place] * grad).reshape(levels * SUB, cols)
        yield place, before_ref[place] + mix(weights, tile).reshape(levels, SUB, cols)


def ens_own_kernel(perturb_ref, mine_ref, weights_ref, control_ref, out_ref):
    for place, values in ens_tiles(perturb_ref, mine_ref, (weights_ref[0], weights_ref[1]), control_ref):
        out_ref[place] = values


def ens_kernel(perturb_ref, theirs_ref, own_ref, *refs):
    count = (len(refs) - 3) // 2
    flats, (out_hbm, *flat_hbms), (out_ref, sems) = refs[:count], refs[count : 2 * count + 1], refs[2 * count + 1 :]
    copies = [pltpu.make_async_copy(a, b, sems.at[i]) for i, (a, b) in enumerate(zip(flats, flat_hbms))]
    for copy in copies:
        copy.start()
    levels = perturb_ref.shape[0]
    weights = halves(spread(theirs_ref[theirs_ref.shape[0] - levels :, :]).T)
    for place, values in ens_tiles(perturb_ref, theirs_ref, weights, own_ref):
        out_ref[place] = values
        copies.append(pltpu.make_async_copy(out_ref.at[place], out_hbm.at[place], sems.at[len(copies)]))
        copies[-1].start()
    for copy in copies:
        copy.wait()


def relabel(r, n, lev):
    high, low = n // 2, n // 4
    if low == 0:
        return r
    both = high | low
    turned = (r & ~both) | ((r & low) << 1) | ((r & high) >> 1)
    return r + (turned - r) * lev


class Rows:
    def __init__(self, levels, n):
        self.weight = slice(0, levels)
        self.base = slice(levels, 2 * levels)
        at = 2 * levels
        self.factor, self.index, self.edge = at, at + n, at + 2 * n
        self.total = at + 2 * n + EXTRA


def static_kernel(band, pos_ref, lev_ref, counts_ref, static_ref, diag_ref, off_ref, obs_ref, innov_ref, src_ref, weight_ref, tgt_ref,
                  *out_refs):
    levels, cols = static_ref.shape
    n = len(out_refs)
    cap = src_ref.shape[2]
    rows = Rows(levels, n)
    peers = [pos_ref[0] ^ relabel(r, n, lev_ref[0]) for r in range(n)]
    static, off, obs = static_ref[...], off_ref[...], obs_ref[...]
    lane = lax.broadcasted_iota(jnp.int32, (levels, cols), 1)
    left = jnp.where(lane == 0, 0.0, pltpu.roll(static, 1, 1))
    right = jnp.where(lane == cols - 1, 0.0, pltpu.roll(static, cols - 1, 1))
    base = diag_ref[...] * static + off * (left + right) - innov_ref[...]
    coupled = off * obs
    ends = [v[:, i] for v in (static, coupled, base) for i in (slice(cols - 1, cols), slice(0, 1))]
    edge = sum(column_as_row(end, None, i * levels) for i, end in enumerate(ends))
    place = lax.broadcasted_iota(jnp.int32, (1, cap), 1)
    edge = edge + jnp.where(place == 6 * levels, off[:, cols - 1 :], 0.0)
    edge = edge + jnp.where(place == 6 * levels + 1, off[:, :1], 0.0)
    edge = jnp.broadcast_to(edge, (EXTRA, cap))
    both = jnp.concatenate(halves(jnp.concatenate([obs, base], axis=0)), axis=0)
    tgts = [tgt_ref[0, pl.ds(peer, 1), :] for peer in peers]
    src = jnp.concatenate([src_ref[0, pl.ds(peer, 1), :] for peer in peers], axis=0).astype(F32)
    index = jnp.concatenate(tgts, axis=0).astype(F32) * float(band) + src
    factor = jnp.concatenate([factor_of(counts_ref, weight_ref, peer) for peer in peers], axis=0)
    for r, out_ref in enumerate(out_refs):
        picked = product(both, one_hot(tgts[r], cols))
        out_ref[: 2 * levels, :] = picked[: 2 * levels] + picked[2 * levels :]
        out_ref[rows.factor : rows.factor + n, :] = factor
        out_ref[rows.index : rows.index + n, :] = index
        out_ref[rows.edge :, :] = edge


def blocks_kernel(groups, levels, *refs):
    sums = refs[:groups]
    count = (len(refs) - groups - 1) // 2
    rests = refs[groups : groups + count]
    total_ref, *out_refs = refs[groups + count :]
    total = sum(ref[...] for ref in sums)
    cap = total_ref.shape[1]
    total = jnp.concatenate([total[:, at : at + cap] for at in range(0, total.shape[1], cap)], axis=0)
    total_ref[...] = total
    for rest_ref, out_ref in zip(rests[:-1], out_refs[:-1]):
        out_ref[: total.shape[0], :] = total
        out_ref[total.shape[0] :, :] = rest_ref[...]
    out_refs[-1][...] = jnp.concatenate([total, rests[-1][: 2 * levels, :], rests[-1][-EXTRA:, :]], axis=0)


def pair_kernel(levels, total_ref, rest_ref, given_ref, out_ref):
    head = total_ref.shape[0] + 2 * levels
    out_ref[...] = jnp.concatenate(
        [given_ref[:head, :], rest_ref[2 * levels : -EXTRA, :], given_ref[head:, :]]
        + [total_ref[...], rest_ref[: 2 * levels, :], rest_ref[-EXTRA:, :]],
        axis=0,
    )


class Block:
    def __init__(self, sums, rest, n, levels, band):
        self.levels, self.parts, self.cap = levels, sums.shape[0] // levels, sums.shape[1]
        rows = Rows(levels, n)
        self.stacked = sums
        self.weight, self.base = rest[rows.weight], rest[rows.base]
        self.factor = rest[rows.factor : rows.factor + n]
        self.edge = rest[rows.edge :]
        words = rest[rows.index : rows.index + n]
        self.tgt = jnp.floor((words + 0.5) * (1.0 / band))
        self.src = words - self.tgt * float(band)

    def sums(self):
        parts = [self.stacked[i * self.levels : (i + 1) * self.levels, :] for i in range(self.parts)]
        return jnp.concatenate(halves(jnp.concatenate(parts, axis=1)), axis=0)


def line(table, i):
    return table[i : i + 1]


def pick_source(block, r):
    band = block.parts * block.cap
    column = lax.broadcasted_iota(jnp.int32, (band, block.cap), 0).astype(F32)
    return jnp.where(column == line(block.src, r), 1.0, 0.0).astype(BF16)


def fill_slots(bands, blocks, n, slots_ref):
    for i, s in enumerate(bands):
        block = blocks[s]
        both = block.sums()
        for d in range(n):
            picked = product(both, pick_source(block, s ^ d))
            values = (picked[: block.levels] + picked[block.levels :]) * line(block.factor, s ^ d)
            slots_ref[d, :, i * block.cap : (i + 1) * block.cap] = jnp.concatenate(halves(values), axis=0)


def met_at(d, block, bands, slots_ref):
    own = jnp.broadcast_to(line(block.tgt, d), (block.cap, block.cap)).T
    same = [jnp.where(own == line(block.tgt, s ^ d), 1.0, 0.0).astype(BF16) for s in bands]
    met = product(slots_ref[d], jnp.concatenate(same, axis=1), ((1,), (1,)))
    return met[: block.levels] + met[block.levels :]


def land(table, bands, slots_ref, cols):
    cap = table.shape[1]
    row = lax.broadcasted_iota(jnp.int32, (cols, cap), 0).astype(F32)
    total = 0.0
    for i, s in enumerate(bands):
        landing = jnp.where(row == line(table, s), 1.0, 0.0).astype(BF16)
        total = total + product(slots_ref[0, :, i * cap : (i + 1) * cap], landing, ((1,), (1,)))
    levels = total.shape[0] // 2
    return total[:levels] + total[levels:]


def open_blocks(labels, refs, lev, n, levels, band):
    blocks = {0: Block(refs[0][...], refs[1][...], n, levels, band)}
    head, total = refs[0].shape[0], refs[1].shape[0]
    refs = refs[2:]
    for r in labels[1:]:
        if r < n - 1:
            blocks[r] = Block(refs[0][:head, :], refs[0][head:, :], n, levels, band)
            refs = refs[1:]
            continue
        both = jnp.where(lev == 1, refs[0][...], refs[1][...])
        refs = refs[2:]
        first, second = both[: head + total], both[head + total :]
        at = head + 2 * levels
        tables = first[at : at + 2 * n]
        turned = [tables[i + relabel(q, n, 1)][None] for i in (0, n) for q in range(n)]
        tables = jnp.where(lev == 1, tables, jnp.concatenate(turned, axis=0))
        first = jnp.concatenate([first[:at], first[at + 2 * n :]], axis=0)
        mine = jnp.where(lev == 1, second, first)
        blocks[r] = Block(mine[:head], jnp.concatenate([mine[head:at], tables, mine[at:]], axis=0), n, levels, band)
    return blocks, refs


def stage_kernel(n, levels, band, cols, stages, lev_ref, *refs):
    known = sum(stages[:-1], [])
    blocks, refs = open_blocks(known + stages[-1], refs, lev_ref[0], n, levels, band)
    old, refs = refs[: len(stages) - 1], refs[len(stages) - 1 :]
    if known:
        met_old, remap_old, slots_ref, met_ref, remap_ref = refs
    else:
        slots_ref, met_ref, remap_ref, pick_ref = refs
        for d in range(n):
            pick_ref[d] = pick_source(blocks[0], d)
    fill_slots(stages[-1], blocks, n, slots_ref)
    for i, (d, block) in enumerate(blocks.items()):
        met = met_at(d, block, stages[-1], slots_ref)
        if d in known:
            met = met + met_old[i]
        else:
            for bands, ref in zip(stages, old):
                met = met + met_at(d, block, bands, ref)
        met_ref[i] = met
    landed = land(blocks[0].tgt, stages[-1], slots_ref, cols)
    remap_ref[...] = landed + remap_old[...] if known else landed


def shared_kernel(n, levels, band, cols, stages, pos_ref, lev_ref, mix_ref, *refs):
    known = sum(stages[:-1], [])
    blocks, refs = open_blocks(known + stages[-1], refs, lev_ref[0], n, levels, band)
    old, refs = refs[: len(stages) - 1], refs[len(stages) - 1 :]
    met_old, pick_ref, out_ref, slots_ref, tables_ref = refs
    me = pos_ref[0]
    for r, block in blocks.items():
        there = me ^ relabel(r, n, lev_ref[0])
        tables_ref[there, :n, :] = block.tgt
        tables_ref[there, n:, :] = block.edge
    fill_slots(stages[-1], blocks, n, slots_ref)
    last = cols - 1.0
    total = jnp.zeros((levels, band), F32)
    for i, (d, block) in enumerate(blocks.items()):
        value = met_at(d, block, stages[-1], slots_ref) + block.base
        if d in known:
            value = value + met_old[i]
        else:
            for bands, ref in zip(stages, old):
                value = value + met_at(d, block, bands, ref)
        edge = line(block.edge, 0)
        own = line(block.tgt, d)
        there = me ^ relabel(d, n, lev_ref[0])
        before = tables_ref[jnp.maximum(there - 1, 0), n : n + 1, :]
        near = jnp.where((own == 0.0) & (there > 0), edge[:, 6 * levels + 1 : 6 * levels + 2], 0.0)
        value = value + row_as_column(before, levels, 0) * near
        after = tables_ref[jnp.minimum(there + 1, n - 1), n : n + 1, :]
        near = jnp.where((own == last) & (there < n - 1), edge[:, 6 * levels : 6 * levels + 1], 0.0)
        value = value + row_as_column(after, levels, levels) * near
        given = block.weight * value * line(blocks[0].factor, d)
        total = total + select(given, pick_ref[d], ((1,), (1,)))
    out_ref[...] = band_rows(total, mix_ref[...])


def outputs_kernel(stages, pos_ref, lev_ref, *refs):
    slots_refs, refs = refs[: len(stages)], refs[len(stages) :]
    remap_ref, tables_ref, static_ref, diag_ref, off_ref, obs_ref, innov_ref, increment_ref, grad_ref = refs
    levels, cols = static_ref.shape
    n = tables_ref.shape[0]
    cap = tables_ref.shape[2]
    me = pos_ref[0]
    given = [
        (s, ref, slice(i * cap, (i + 1) * cap)) for bands, ref in zip(stages, slots_refs) for i, s in enumerate(bands)
    ]
    remapped = remap_ref[...] + land(tables_ref[me, :n, :], stages[-1], slots_refs[-1], cols)
    static, off = static_ref[...], off_ref[...]
    lane = lax.broadcasted_iota(jnp.int32, (levels, cols), 1)

    def beside(there, exists, column, own_end, side):
        edge = tables_ref[there, n : n + 1, :]
        static_end, coupling, base = (row_as_column(edge, levels, (2 * i + side) * levels) for i in range(3))
        far = relabel(me ^ there, n, lev_ref[0])
        landed = []
        for s, ref, place in given:
            values = ref[far, :levels, place].astype(F32) + ref[far, levels:, place].astype(F32)
            landed.append(jnp.where(tables_ref[there, pl.ds(s ^ far, 1), :] == column, values, 0.0))
        remap_end = jnp.sum(sum(landed), axis=1, keepdims=True)
        off_end = edge[:, 6 * levels + side : 6 * levels + side + 1]
        coupled = coupling * (remap_end + base + off_end * own_end)
        return jnp.where(exists, static_end, 0.0), jnp.where(exists, coupled, 0.0)

    before, coupled_before = beside(jnp.maximum(me - 1, 0), me > 0, cols - 1.0, static[:, :1], 0)
    after, coupled_after = beside(jnp.minimum(me + 1, n - 1), me < n - 1, 0.0, static[:, cols - 1 :], 1)
    left = jnp.where(lane == 0, before, pltpu.roll(static, 1, 1))
    right = jnp.where(lane == cols - 1, after, pltpu.roll(static, cols - 1, 1))
    increment = remapped + diag_ref[...] * static + off * (left + right)
    increment_ref[...] = increment
    misfit = obs_ref[...] * (increment - innov_ref[...])
    coupled = off * misfit
    left = jnp.where(lane == 0, coupled_before, pltpu.roll(coupled, 1, 1))
    right = jnp.where(lane == cols - 1, coupled_after, pltpu.roll(coupled, cols - 1, 1))
    grad_ref[...] = static + diag_ref[...] * misfit + left + right


def call(kernel, out_shape, spaces, scratch=(), out=VMEM, cost=None):
    return pl.pallas_call(
        kernel,
        out_shape=out_shape,
        in_specs=spaces,
        out_specs=jax.tree.map(lambda _: out, out_shape),
        scratch_shapes=scratch,
        cost_estimate=cost,
        compiler_params=pltpu.CompilerParams(vmem_limit_bytes=40 * MIB),
    )


def body(
    perturb,
    control,
    level_loc,
    static_control,
    filter_diag,
    filter_off,
    send_src,
    send_wt,
    counts,
    recv_tgt,
    obs_weight,
    innovation,
):
    levels, members, band_cols = control.shape
    tile_cols = static_control.shape[1]
    n = lax.axis_size("tile")
    groups = lax.axis_size("grp")
    cap = send_src.shape[2]
    shape = jax.ShapeDtypeStruct
    swap = [(0, 1), (1, 0)]
    lev = lax.axis_index("lev").astype(jnp.int32).reshape(1)
    pos = lax.axis_index("tile").astype(jnp.int32).reshape(1)
    other_control = lax.ppermute(control, "lev", swap)
    width = levels * SUB
    level_mix, own_mix, given_mix = call(
        mix_kernel,
        (shape((2, width, 2 * width), BF16), shape((2, width, width), BF16), shape((levels, width), F32)),
        [SMEM, VMEM],
        cost=pl.CostEstimate(flops=10**9, bytes_accessed=0, transcendentals=0),
    )(lev, level_loc)
    own_sum = call(sum_kernel, shape((levels, band_cols), F32), [VMEM] * 4)(perturb, control, other_control, level_mix)
    flat = shape((levels, tile_cols), F32)
    mine_shape = shape((band_cols // width * levels + levels, width), F32)
    diag, off = filter_diag.reshape(1, -1), filter_off.reshape(1, -1)
    if n * cap <= tile_cols and n >= 8 and lax.axis_size("lev") == 2 and n & (n - 1) == 0 and band_cols * tile_cols <= 2**20:
        rows = Rows(levels, n)
        stacked = band_cols // cap * levels
        rests = call(functools.partial(static_kernel, band_cols), [shape((rows.total, cap), F32)] * n, [SMEM] * 3 + [VMEM] * 8)(
            pos, lev, counts, static_control, diag, off, obs_weight, innovation, send_src, send_wt, recv_tgt
        )
        sums = [own_sum]
        sums[0], other_perturb = lax.optimization_barrier((sums[0], lax.ppermute(perturb, "lev", swap)))
        for k in range(1, groups):
            sums.append(lax.ppermute(sums[0], "grp", [(g, (g + k) % groups) for g in range(groups)]))
        low, high = n // 4, n // 2
        order = [low, n - 1, *range(high + 1, n - 1), *range(low + 1, high), high, *range(1, low)]
        stages = [[0, order[0], *order[2:4]], [n - 1, *order[4:-1]], order[-1:]]
        direct = [r for r in order if r < n - 1]
        total, *blocks, give = call(
            functools.partial(blocks_kernel, groups, levels),
            [shape((stacked, cap), F32)]
            + [shape((stacked + rows.total, cap), F32)] * len(direct)
            + [shape((stacked + 2 * levels + EXTRA, cap), F32)],
            [VMEM] * (groups + n - 1),
        )(*sums, *[rests[r] for r in direct], rests[n - 1])
        given = lax.ppermute(give, "lev", [(0, 1)])
        pair = call(
            functools.partial(pair_kernel, levels),
            shape((2 * stacked + rows.total + 2 * levels + EXTRA, cap), F32),
            [VMEM] * 3,
        )(total, rests[n - 1], given)
        blocks = dict(zip(direct, blocks)) | {n - 1: pair}
        arrived = {0: [total, rests[0]]}
        for k, r in enumerate(order):
            if k == 3:
                arrived[order[0]][0], blocks[r] = lax.optimization_barrier((arrived[order[0]][0], blocks[r]))
            pairs = [(i * 2 + v, (i ^ relabel(r, n, v)) * 2 + v) for i in range(n) for v in range(2) if v or r < n - 1]
            arrived[r] = [lax.ppermute(blocks[r], ("tile", "lev"), pairs)]
        arrived[n - 1].append(lax.ppermute(arrived[n - 1][0], "lev", [(1, 0)]))
        slots, carried, picks = [], [], []
        for count in range(1, len(stages)):
            labels = sum(stages[:count], [])
            refs = [ref for r in labels for ref in arrived[r]]
            outs = [
                shape((n, 2 * levels, len(stages[count - 1]) * cap), BF16),
                shape((len(labels), levels, cap), F32),
                flat,
            ] + [shape((n, band_cols, cap), BF16)] * (count == 1)
            new, *carried = call(
                functools.partial(stage_kernel, n, levels, band_cols, tile_cols, stages[:count]),
                outs,
                [SMEM] + [VMEM] * (len(refs) + len(slots) + len(carried)),
                cost=pl.CostEstimate(flops=10**9, bytes_accessed=0, transcendentals=0),
            )(lev, *refs, *slots, *carried)
            slots.append(new)
            picks += carried[2:]
            carried = carried[:2]
        met, remap = carried
        refs = [ref for r in sum(stages, []) for ref in arrived[r]] + slots + [met] + picks
        mine, new, tables = call(
            functools.partial(shared_kernel, n, levels, band_cols, tile_cols, stages),
            (mine_shape, shape((n, 2 * levels, len(stages[-1]) * cap), BF16), shape((n, n + EXTRA, cap), F32)),
            [SMEM] * 2 + [VMEM] * (1 + len(refs)),
            cost=pl.CostEstimate(flops=10**9, bytes_accessed=0, transcendentals=0),
        )(pos, lev, given_mix, *refs)
        slots.append(new)
        increment, grad_static = call(
            functools.partial(outputs_kernel, stages), (flat, flat), [SMEM] * 2 + [VMEM] * (len(slots) + 7)
        )(pos, lev, *slots, remap, tables, static_control, diag, off, obs_weight, innovation)
    else:
        other_perturb = lax.ppermute(perturb, "lev", swap)
        payload = call(
            band_kernel,
            shape((groups, n, levels + EXTRA, cap), F32),
            [SMEM] + [VMEM] * 4,
            [pltpu.VMEM((2 * levels, band_cols), BF16)],
        )(counts, own_sum, static_control, send_src, send_wt)
        arrived = lax.all_to_all(
            payload.reshape(groups * n, levels + EXTRA, cap), ("grp", "tile"), split_axis=0, concat_axis=0, tiled=True
        ).reshape(groups, n, levels + EXTRA, cap)
        increment, partial, giving = call(
            tile_kernel, (flat, flat, shape((n, levels + EXTRA, cap), F32)), [SMEM] + [VMEM] * 7
        )(pos, arrived, recv_tgt, static_control, diag, off, obs_weight, innovation)
        returned = lax.all_to_all(giving, "tile", split_axis=0, concat_axis=0, tiled=True)
        grad_static, mine = call(
            functools.partial(adjoint_kernel, band_cols), (flat, mine_shape), [SMEM, SMEM] + [VMEM] * 5
        )(pos, counts, returned, send_src, send_wt, partial, given_mix)
    theirs = lax.ppermute(mine, "lev", swap)
    own = call(ens_own_kernel, shape(control.shape, F32), [VMEM] * 4)(perturb, mine, own_mix, control)
    grad_ens, increment, grad_static = call(
        ens_kernel,
        (shape(control.shape, F32), flat, flat),
        [VMEM] * 5,
        [pltpu.VMEM(control.shape, F32), pltpu.SemaphoreType.DMA((2 + members // SUB,))],
        out=HBM,
    )(other_perturb, theirs, own, increment, grad_static)
    return (increment, grad_static, grad_ens)


def solution(mesh):
    return jax.shard_map(
        body,
        mesh=mesh,
        in_specs=(
            P("lev", "grp", "tile"),
            P("lev", "grp", "tile"),
            P("lev", None),
            P("lev", "tile"),
            P("tile"),
            P("tile"),
            P("tile", None, None),
            P("tile", None, None),
            P("tile", None),
            P("tile", None, None),
            P("lev", "tile"),
            P("lev", "tile"),
        ),
        out_specs=(P("lev", "tile"), P("lev", "tile"), P("lev", "grp", "tile")),
        check_vma=False,
    )
```

```python
import functools

import jax
import jax.numpy as jnp
from jax import lax
from jax.experimental import pallas as pl
from jax.experimental.pallas import tpu as pltpu
from jax.sharding import PartitionSpec as P

F32 = jnp.float32
BF16 = jnp.bfloat16
SUB = 8
EXTRA = 8
VMEM = pl.BlockSpec(memory_space=pltpu.VMEM)
HBM = pl.BlockSpec(memory_space=pltpu.HBM)
SMEM = pl.BlockSpec(memory_space=pltpu.SMEM)
MIB = 1024 * 1024


def halves(values):
    high = values.astype(BF16)
    low = (values - high.astype(F32)).astype(BF16)
    return high, low


def product(a, b, dims=((1,), (0,))):
    return lax.dot_general(a, b, (dims, ((), ())), preferred_element_type=F32)


def select(values, chosen, dims=((1,), (0,))):
    rows = values.shape[0]
    both = product(jnp.concatenate(halves(values), axis=0), chosen, dims)
    return both[:rows] + both[rows:]


def iota(shape, axis):
    return lax.broadcasted_iota(jnp.int32, shape, axis)


def wide_rows(matrix, start, count):
    cols = matrix.shape[1]
    shape = (cols, count * SUB)
    place = (iota(shape, 1) // SUB + start) % cols
    pick = (place == iota(shape, 0)).astype(BF16)
    high, low = halves(matrix)
    return product(high, pick) + product(low, pick)


def spread(wide):
    rows, cols = wide.shape
    tall = jnp.broadcast_to(wide[:, None, :], (rows, SUB, cols)).reshape(rows * SUB, cols)
    return jnp.where(iota(tall.shape, 0) % SUB == iota(tall.shape, 1) % SUB, tall, 0.0)


def mix(weights, values):
    high, low = halves(values)
    rows = weights[0].shape[0]
    both = product(jnp.concatenate(weights, axis=0), high)
    return both[:rows] + (product(weights[0], low) + both[rows:])


def one_hot(index, size):
    rows = lax.broadcasted_iota(jnp.int32, (size, index.shape[1]), 0)
    return jnp.where(rows == index, 1.0, 0.0).astype(BF16)


def column_as_row(column, lane, offset):
    n = column.shape[0]
    place = lax.broadcasted_iota(jnp.int32, (n, 128), 1) == lax.broadcasted_iota(jnp.int32, (n, 128), 0) + offset
    return jnp.sum(jnp.where(place, column, 0.0), axis=0, keepdims=True)


def row_as_column(row, n, offset):
    place = lax.broadcasted_iota(jnp.int32, (n, 128), 1) == lax.broadcasted_iota(jnp.int32, (n, 128), 0) + offset
    return jnp.sum(jnp.where(place, row, 0.0), axis=1, keepdims=True)


def edge_rows(values):
    n = values.shape[0]
    row = column_as_row(values[:, -1:], None, 0) + column_as_row(values[:, :1], None, n)
    return jnp.broadcast_to(row, (EXTRA, 128))


def factor_of(counts_ref, weight_ref, d):
    slot = lax.broadcasted_iota(jnp.int32, (1, weight_ref.shape[2]), 1)
    return jnp.where(slot < counts_ref[0, d], weight_ref[0, pl.ds(d, 1), :], 0.0)


def loop(n, step, init):
    return lax.fori_loop(0, n, step, init, unroll=n if n <= 8 else 1)


def mix_kernel(lev_ref, loc_ref, mix_ref, own_ref, given_ref):
    levels = loc_ref.shape[0]
    start = lev_ref[0] * levels
    loc = loc_ref[...]
    mix_ref[0], mix_ref[1] = halves(spread(wide_rows(loc, start, 2 * levels)))
    own_ref[0], own_ref[1] = halves(spread(wide_rows(loc, start, levels)).T)
    given_ref[...] = wide_rows(loc, levels - start, levels)


def sum_kernel(perturb_ref, control_ref, other_ref, mix_ref, out_ref):
    levels, members, cols = perturb_ref.shape
    perturb = perturb_ref[...].astype(F32)
    total = jnp.zeros((levels, SUB, cols), F32)
    for m in range(0, members, SUB):
        tile = jnp.concatenate([control_ref[:, m : m + SUB, :], other_ref[:, m : m + SUB, :]], axis=0)
        mixed = mix((mix_ref[0], mix_ref[1]), tile.reshape(2 * levels * SUB, cols))
        total = total + perturb[:, m : m + SUB, :] * mixed.reshape(levels, SUB, cols)
    out_ref[...] = jnp.sum(total, axis=1)


def band_kernel(counts_ref, sum_ref, static_ref, src_ref, weight_ref, out_ref, acc_ref):
    levels, cols = sum_ref.shape
    acc_ref[...] = jnp.concatenate(halves(sum_ref[...]), axis=0)
    n = src_ref.shape[1]
    edges = edge_rows(static_ref[...])

    def step(d, carry):
        chosen = one_hot(src_ref[0, pl.ds(d, 1), :], cols)
        both = product(acc_ref[...], chosen)
        payload = (both[:levels] + both[levels:]) * factor_of(counts_ref, weight_ref, d)
        for g in range(out_ref.shape[0]):
            out_ref[g, d, :levels, :] = payload
            out_ref[g, d, levels:, :] = edges
        return carry

    loop(n, step, 0)


def tile_kernel(pos_ref, arrived_ref, tgt_ref, static_ref, diag_ref, off_ref, obs_ref, innov_ref,
                increment_ref, partial_ref, out_ref):
    levels, cols = static_ref.shape
    groups, n = arrived_ref.shape[:2]
    me = pos_ref[0]

    def step(s, total):
        values = sum(arrived_ref[g, s, :levels, :] for g in range(groups))
        chosen = one_hot(tgt_ref[0, pl.ds(s, 1), :], cols)
        return total + select(values, chosen, ((1,), (1,)))

    remapped = loop(n, step, jnp.zeros((levels, cols), F32))
    before = arrived_ref[0, jnp.maximum(me - 1, 0), levels : levels + 1, :]
    after = arrived_ref[0, jnp.minimum(me + 1, n - 1), levels : levels + 1, :]
    before = jnp.where(me > 0, row_as_column(before, levels, 0), 0.0)
    after = jnp.where(me < n - 1, row_as_column(after, levels, levels), 0.0)
    static = static_ref[...]
    lane = lax.broadcasted_iota(jnp.int32, (levels, cols), 1)
    left = jnp.where(lane == 0, before, pltpu.roll(static, 1, 1))
    right = jnp.where(lane == cols - 1, after, pltpu.roll(static, cols - 1, 1))
    increment = remapped + diag_ref[...] * static + off_ref[...] * (left + right)
    increment_ref[...] = increment
    misfit = obs_ref[...] * (increment - innov_ref[...])
    coupled = off_ref[...] * misfit
    left = jnp.where(lane == 0, 0.0, pltpu.roll(coupled, 1, 1))
    right = jnp.where(lane == cols - 1, 0.0, pltpu.roll(coupled, cols - 1, 1))
    partial_ref[...] = static + diag_ref[...] * misfit + left + right
    edges = edge_rows(coupled)
    both = jnp.concatenate(halves(misfit), axis=0)

    def give(s, carry):
        chosen = one_hot(tgt_ref[0, pl.ds(s, 1), :], cols)
        picked = product(both, chosen)
        out_ref[s, :levels, :] = picked[:levels] + picked[levels:]
        out_ref[s, levels:, :] = edges
        return carry

    loop(n, give, 0)


def adjoint_kernel(band, pos_ref, counts_ref, returned_ref, src_ref, weight_ref, partial_ref, mix_ref, grad_ref, out_ref):
    levels, cols = partial_ref.shape
    n = returned_ref.shape[0]
    me = pos_ref[0]

    def step(d, total):
        values = returned_ref[d, :levels, :] * factor_of(counts_ref, weight_ref, d)
        return total + select(values, one_hot(src_ref[0, pl.ds(d, 1), :], band), ((1,), (1,)))

    out_ref[...] = band_rows(loop(n, step, jnp.zeros((levels, band), F32)), mix_ref[...])
    before = returned_ref[jnp.maximum(me - 1, 0), levels : levels + 1, :]
    after = returned_ref[jnp.minimum(me + 1, n - 1), levels : levels + 1, :]
    before = jnp.where(me > 0, row_as_column(before, levels, 0), 0.0)
    after = jnp.where(me < n - 1, row_as_column(after, levels, levels), 0.0)
    lane = lax.broadcasted_iota(jnp.int32, (levels, cols), 1)
    grad_ref[...] = partial_ref[...] + (jnp.where(lane == 0, before, 0.0) + jnp.where(lane == cols - 1, after, 0.0))


def band_rows(band, weights):
    width = weights.shape[1]
    return jnp.concatenate([band[:, at : at + width] for at in range(0, band.shape[1], width)] + [weights], axis=0)


def ens_tiles(perturb_ref, rows_ref, weights, before_ref):
    levels, members, cols = perturb_ref.shape
    width = rows_ref.shape[1]
    parts = [rows_ref[i * levels : (i + 1) * levels, :] for i in range(cols // width)]
    grad = jnp.concatenate(parts, axis=1)[:, None, :]
    perturb = perturb_ref[...].astype(F32)
    for m in range(0, members, SUB):
        place = (slice(None), slice(m, m + SUB), slice(None))
        tile = (perturb[place] * grad).reshape(levels * SUB, cols)
        yield place, before_ref[place] + mix(weights, tile).reshape(levels, SUB, cols)


def ens_own_kernel(perturb_ref, mine_ref, weights_ref, control_ref, out_ref):
    for place, values in ens_tiles(perturb_ref, mine_ref, (weights_ref[0], weights_ref[1]), control_ref):
        out_ref[place] = values


def ens_kernel(perturb_ref, theirs_ref, own_ref, *refs):
    count = (len(refs) - 3) // 2
    flats, (out_hbm, *flat_hbms), (out_ref, sems) = refs[:count], refs[count : 2 * count + 1], refs[2 * count + 1 :]
    copies = [pltpu.make_async_copy(a, b, sems.at[i]) for i, (a, b) in enumerate(zip(flats, flat_hbms))]
    for copy in copies:
        copy.start()
    levels = perturb_ref.shape[0]
    weights = halves(spread(theirs_ref[theirs_ref.shape[0] - levels :, :]).T)
    for place, values in ens_tiles(perturb_ref, theirs_ref, weights, own_ref):
        out_ref[place] = values
        copies.append(pltpu.make_async_copy(out_ref.at[place], out_hbm.at[place], sems.at[len(copies)]))
        copies[-1].start()
    for copy in copies:
        copy.wait()


def relabel(r, n, lev):
    high, low = n // 2, n // 4
    if low == 0:
        return r
    both = high | low
    turned = (r & ~both) | ((r & low) << 1) | ((r & high) >> 1)
    return r + (turned - r) * lev


class Rows:
    def __init__(self, levels, n):
        self.weight = slice(0, levels)
        self.base = slice(levels, 2 * levels)
        at = 2 * levels
        self.factor, self.index, self.edge = at, at + n, at + 2 * n
        self.total = at + 2 * n + EXTRA


def static_kernel(band, pos_ref, lev_ref, counts_ref, static_ref, diag_ref, off_ref, obs_ref, innov_ref, src_ref, weight_ref, tgt_ref,
                  *out_refs):
    levels, cols = static_ref.shape
    n = len(out_refs)
    cap = src_ref.shape[2]
    rows = Rows(levels, n)
    peers = [pos_ref[0] ^ relabel(r, n, lev_ref[0]) for r in range(n)]
    static, off, obs = static_ref[...], off_ref[...], obs_ref[...]
    lane = lax.broadcasted_iota(jnp.int32, (levels, cols), 1)
    left = jnp.where(lane == 0, 0.0, pltpu.roll(static, 1, 1))
    right = jnp.where(lane == cols - 1, 0.0, pltpu.roll(static, cols - 1, 1))
    base = diag_ref[...] * static + off * (left + right) - innov_ref[...]
    coupled = off * obs
    ends = [v[:, i] for v in (static, coupled, base) for i in (slice(cols - 1, cols), slice(0, 1))]
    edge = sum(column_as_row(end, None, i * levels) for i, end in enumerate(ends))
    place = lax.broadcasted_iota(jnp.int32, (1, cap), 1)
    edge = edge + jnp.where(place == 6 * levels, off[:, cols - 1 :], 0.0)
    edge = edge + jnp.where(place == 6 * levels + 1, off[:, :1], 0.0)
    edge = jnp.broadcast_to(edge, (EXTRA, cap))
    both = jnp.concatenate(halves(jnp.concatenate([obs, base], axis=0)), axis=0)
    tgts = [tgt_ref[0, pl.ds(peer, 1), :] for peer in peers]
    src = jnp.concatenate([src_ref[0, pl.ds(peer, 1), :] for peer in peers], axis=0).astype(F32)
    index = jnp.concatenate(tgts, axis=0).astype(F32) * float(band) + src
    factor = jnp.concatenate([factor_of(counts_ref, weight_ref, peer) for peer in peers], axis=0)
    for r, out_ref in enumerate(out_refs):
        picked = product(both, one_hot(tgts[r], cols))
        out_ref[: 2 * levels, :] = picked[: 2 * levels] + picked[2 * levels :]
        out_ref[rows.factor : rows.factor + n, :] = factor
        out_ref[rows.index : rows.index + n, :] = index
        out_ref[rows.edge :, :] = edge


def blocks_kernel(groups, levels, *refs):
    sums = refs[:groups]
    count = (len(refs) - groups - 1) // 2
    rests = refs[groups : groups + count]
    total_ref, *out_refs = refs[groups + count :]
    total = sum(ref[...] for ref in sums)
    cap = total_ref.shape[1]
    total = jnp.concatenate([total[:, at : at + cap] for at in range(0, total.shape[1], cap)], axis=0)
    total_ref[...] = total
    for rest_ref, out_ref in zip(rests[:-1], out_refs[:-1]):
        out_ref[: total.shape[0], :] = total
        out_ref[total.shape[0] :, :] = rest_ref[...]
    out_refs[-1][...] = jnp.concatenate([total, rests[-1][: 2 * levels, :], rests[-1][-EXTRA:, :]], axis=0)


def pair_kernel(levels, total_ref, rest_ref, given_ref, out_ref):
    head = total_ref.shape[0] + 2 * levels
    out_ref[...] = jnp.concatenate(
        [given_ref[:head, :], rest_ref[2 * levels : -EXTRA, :], given_ref[head:, :]]
        + [total_ref[...], rest_ref[: 2 * levels, :], rest_ref[-EXTRA:, :]],
        axis=0,
    )


class Block:
    def __init__(self, sums, rest, n, levels, band):
        self.levels, self.parts, self.cap = levels, sums.shape[0] // levels, sums.shape[1]
        rows = Rows(levels, n)
        self.stacked = sums
        self.weight, self.base = rest[rows.weight], rest[rows.base]
        self.factor = rest[rows.factor : rows.factor + n]
        self.edge = rest[rows.edge :]
        words = rest[rows.index : rows.index + n]
        self.tgt = jnp.floor((words + 0.5) * (1.0 / band))
        self.src = words - self.tgt * float(band)

    def sums(self):
        parts = [self.stacked[i * self.levels : (i + 1) * self.levels, :] for i in range(self.parts)]
        return jnp.concatenate(halves(jnp.concatenate(parts, axis=1)), axis=0)


def line(table, i):
    return table[i : i + 1]


def pick_source(block, r):
    band = block.parts * block.cap
    column = lax.broadcasted_iota(jnp.int32, (band, block.cap), 0).astype(F32)
    return jnp.where(column == line(block.src, r), 1.0, 0.0).astype(BF16)


def fill_slots(bands, blocks, n, slots_ref):
    for i, s in enumerate(bands):
        block = blocks[s]
        both = block.sums()
        for d in range(n):
            picked = product(both, pick_source(block, s ^ d))
            values = (picked[: block.levels] + picked[block.levels :]) * line(block.factor, s ^ d)
            slots_ref[d, :, i * block.cap : (i + 1) * block.cap] = jnp.concatenate(halves(values), axis=0)


def met_at(d, block, bands, slots_ref):
    own = jnp.broadcast_to(line(block.tgt, d), (block.cap, block.cap)).T
    same = [jnp.where(own == line(block.tgt, s ^ d), 1.0, 0.0).astype(BF16) for s in bands]
    met = product(slots_ref[d], jnp.concatenate(same, axis=1), ((1,), (1,)))
    return met[: block.levels] + met[block.levels :]


def land(table, bands, slots_ref, cols):
    cap = table.shape[1]
    row = lax.broadcasted_iota(jnp.int32, (cols, cap), 0).astype(F32)
    total = 0.0
    for i, s in enumerate(bands):
        landing = jnp.where(row == line(table, s), 1.0, 0.0).astype(BF16)
        total = total + product(slots_ref[0, :, i * cap : (i + 1) * cap], landing, ((1,), (1,)))
    levels = total.shape[0] // 2
    return total[:levels] + total[levels:]


def open_blocks(labels, refs, lev, n, levels, band):
    blocks = {0: Block(refs[0][...], refs[1][...], n, levels, band)}
    head, total = refs[0].shape[0], refs[1].shape[0]
    refs = refs[2:]
    for r in labels[1:]:
        if r < n - 1:
            blocks[r] = Block(refs[0][:head, :], refs[0][head:, :], n, levels, band)
            refs = refs[1:]
            continue
        both = jnp.where(lev == 1, refs[0][...], refs[1][...])
        refs = refs[2:]
        first, second = both[: head + total], both[head + total :]
        at = head + 2 * levels
        tables = first[at : at + 2 * n]
        turned = [tables[i + relabel(q, n, 1)][None] for i in (0, n) for q in range(n)]
        tables = jnp.where(lev == 1, tables, jnp.concatenate(turned, axis=0))
        first = jnp.concatenate([first[:at], first[at + 2 * n :]], axis=0)
        mine = jnp.where(lev == 1, second, first)
        blocks[r] = Block(mine[:head], jnp.concatenate([mine[head:at], tables, mine[at:]], axis=0), n, levels, band)
    return blocks, refs


def stage_kernel(n, levels, band, cols, stages, lev_ref, *refs):
    known = sum(stages[:-1], [])
    blocks, refs = open_blocks(known + stages[-1], refs, lev_ref[0], n, levels, band)
    old, refs = refs[: len(stages) - 1], refs[len(stages) - 1 :]
    if known:
        met_old, remap_old, slots_ref, met_ref, remap_ref = refs
    else:
        slots_ref, met_ref, remap_ref, pick_ref = refs
        for d in range(n):
            pick_ref[d] = pick_source(blocks[0], d)
    fill_slots(stages[-1], blocks, n, slots_ref)
    for i, (d, block) in enumerate(blocks.items()):
        met = met_at(d, block, stages[-1], slots_ref)
        if d in known:
            met = met + met_old[i]
        else:
            for bands, ref in zip(stages, old):
                met = met + met_at(d, block, bands, ref)
        met_ref[i] = met
    landed = land(blocks[0].tgt, stages[-1], slots_ref, cols)
    remap_ref[...] = landed + remap_old[...] if known else landed


def shared_kernel(n, levels, band, cols, stages, pos_ref, lev_ref, mix_ref, *refs):
    known = sum(stages[:-1], [])
    blocks, refs = open_blocks(known + stages[-1], refs, lev_ref[0], n, levels, band)
    old, refs = refs[: len(stages) - 1], refs[len(stages) - 1 :]
    met_old, pick_ref, out_ref, slots_ref, tables_ref = refs
    me = pos_ref[0]
    for r, block in blocks.items():
        there = me ^ relabel(r, n, lev_ref[0])
        tables_ref[there, :n, :] = block.tgt
        tables_ref[there, n:, :] = block.edge
    fill_slots(stages[-1], blocks, n, slots_ref)
    last = cols - 1.0
    total = jnp.zeros((levels, band), F32)
    for i, (d, block) in enumerate(blocks.items()):
        value = met_at(d, block, stages[-1], slots_ref) + block.base
        if d in known:
            value = value + met_old[i]
        else:
            for bands, ref in zip(stages, old):
                value = value + met_at(d, block, bands, ref)
        edge = line(block.edge, 0)
        own = line(block.tgt, d)
        there = me ^ relabel(d, n, lev_ref[0])
        before = tables_ref[jnp.maximum(there - 1, 0), n : n + 1, :]
        near = jnp.where((own == 0.0) & (there > 0), edge[:, 6 * levels + 1 : 6 * levels + 2], 0.0)
        value = value + row_as_column(before, levels, 0) * near
        after = tables_ref[jnp.minimum(there + 1, n - 1), n : n + 1, :]
        near = jnp.where((own == last) & (there < n - 1), edge[:, 6 * levels : 6 * levels + 1], 0.0)
        value = value + row_as_column(after, levels, levels) * near
        given = block.weight * value * line(blocks[0].factor, d)
        total = total + select(given, pick_ref[d], ((1,), (1,)))
    out_ref[...] = band_rows(total, mix_ref[...])


def outputs_kernel(stages, pos_ref, lev_ref, *refs):
    slots_refs, refs = refs[: len(stages)], refs[len(stages) :]
    remap_ref, tables_ref, static_ref, diag_ref, off_ref, obs_ref, innov_ref, increment_ref, grad_ref = refs
    levels, cols = static_ref.shape
    n = tables_ref.shape[0]
    cap = tables_ref.shape[2]
    me = pos_ref[0]
    given = [
        (s, ref, slice(i * cap, (i + 1) * cap)) for bands, ref in zip(stages, slots_refs) for i, s in enumerate(bands)
    ]
    remapped = remap_ref[...] + land(tables_ref[me, :n, :], stages[-1], slots_refs[-1], cols)
    static, off = static_ref[...], off_ref[...]
    lane = lax.broadcasted_iota(jnp.int32, (levels, cols), 1)

    def beside(there, exists, column, own_end, side):
        edge = tables_ref[there, n : n + 1, :]
        static_end, coupling, base = (row_as_column(edge, levels, (2 * i + side) * levels) for i in range(3))
        far = relabel(me ^ there, n, lev_ref[0])
        landed = []
        for s, ref, place in given:
            values = ref[far, :levels, place].astype(F32) + ref[far, levels:, place].astype(F32)
            landed.append(jnp.where(tables_ref[there, pl.ds(s ^ far, 1), :] == column, values, 0.0))
        remap_end = jnp.sum(sum(landed), axis=1, keepdims=True)
        off_end = edge[:, 6 * levels + side : 6 * levels + side + 1]
        coupled = coupling * (remap_end + base + off_end * own_end)
        return jnp.where(exists, static_end, 0.0), jnp.where(exists, coupled, 0.0)

    before, coupled_before = beside(jnp.maximum(me - 1, 0), me > 0, cols - 1.0, static[:, :1], 0)
    after, coupled_after = beside(jnp.minimum(me + 1, n - 1), me < n - 1, 0.0, static[:, cols - 1 :], 1)
    left = jnp.where(lane == 0, before, pltpu.roll(static, 1, 1))
    right = jnp.where(lane == cols - 1, after, pltpu.roll(static, cols - 1, 1))
    increment = remapped + diag_ref[...] * static + off * (left + right)
    increment_ref[...] = increment
    misfit = obs_ref[...] * (increment - innov_ref[...])
    coupled = off * misfit
    left = jnp.where(lane == 0, coupled_before, pltpu.roll(coupled, 1, 1))
    right = jnp.where(lane == cols - 1, coupled_after, pltpu.roll(coupled, cols - 1, 1))
    grad_ref[...] = static + diag_ref[...] * misfit + left + right


def call(kernel, out_shape, spaces, scratch=(), out=VMEM, cost=None):
    return pl.pallas_call(
        kernel,
        out_shape=out_shape,
        in_specs=spaces,
        out_specs=jax.tree.map(lambda _: out, out_shape),
        scratch_shapes=scratch,
        cost_estimate=cost,
        compiler_params=pltpu.CompilerParams(vmem_limit_bytes=40 * MIB),
    )


def body(
    perturb,
    control,
    level_loc,
    static_control,
    filter_diag,
    filter_off,
    send_src,
    send_wt,
    counts,
    recv_tgt,
    obs_weight,
    innovation,
):
    levels, members, band_cols = control.shape
    tile_cols = static_control.shape[1]
    n = lax.axis_size("tile")
    groups = lax.axis_size("grp")
    cap = send_src.shape[2]
    shape = jax.ShapeDtypeStruct
    swap = [(0, 1), (1, 0)]
    lev = lax.axis_index("lev").astype(jnp.int32).reshape(1)
    pos = lax.axis_index("tile").astype(jnp.int32).reshape(1)
    other_control = lax.ppermute(control, "lev", swap)
    width = levels * SUB
    level_mix, own_mix, given_mix = call(
        mix_kernel,
        (shape((2, width, 2 * width), BF16), shape((2, width, width), BF16), shape((levels, width), F32)),
        [SMEM, VMEM],
        cost=pl.CostEstimate(flops=10**9, bytes_accessed=0, transcendentals=0),
    )(lev, level_loc)
    own_sum = call(sum_kernel, shape((levels, band_cols), F32), [VMEM] * 4)(perturb, control, other_control, level_mix)
    flat = shape((levels, tile_cols), F32)
    mine_shape = shape((band_cols // width * levels + levels, width), F32)
    diag, off = filter_diag.reshape(1, -1), filter_off.reshape(1, -1)
    if n * cap <= tile_cols and n >= 8 and lax.axis_size("lev") == 2 and n & (n - 1) == 0 and band_cols * tile_cols <= 2**20:
        rows = Rows(levels, n)
        stacked = band_cols // cap * levels
        rests = call(functools.partial(static_kernel, band_cols), [shape((rows.total, cap), F32)] * n, [SMEM] * 3 + [VMEM] * 8)(
            pos, lev, counts, static_control, diag, off, obs_weight, innovation, send_src, send_wt, recv_tgt
        )
        sums = [own_sum]
        sums[0], other_perturb = lax.optimization_barrier((sums[0], lax.ppermute(perturb, "lev", swap)))
        for k in range(1, groups):
            sums.append(lax.ppermute(sums[0], "grp", [(g, (g + k) % groups) for g in range(groups)]))
        low, high = n // 4, n // 2
        order = [low, n - 1, *range(high + 1, n - 1), *range(low + 1, high), high, *range(1, low)]
        stages = [[0, order[0], *order[2:4]], [n - 1, *order[4:-1]], order[-1:]]
        direct = [r for r in order if r < n - 1]
        total, *blocks, give = call(
            functools.partial(blocks_kernel, groups, levels),
            [shape((stacked, cap), F32)]
            + [shape((stacked + rows.total, cap), F32)] * len(direct)
            + [shape((stacked + 2 * levels + EXTRA, cap), F32)],
            [VMEM] * (groups + n - 1),
        )(*sums, *[rests[r] for r in direct], rests[n - 1])
        given = lax.ppermute(give, "lev", swap)
        pair = call(
            functools.partial(pair_kernel, levels),
            shape((2 * stacked + rows.total + 2 * levels + EXTRA, cap), F32),
            [VMEM] * 3,
        )(total, rests[n - 1], given)
        blocks = dict(zip(direct, blocks)) | {n - 1: pair}
        arrived = {0: [total, rests[0]]}
        for k, r in enumerate(order):
            if k == 3:
                arrived[order[0]][0], blocks[r] = lax.optimization_barrier((arrived[order[0]][0], blocks[r]))
            pairs = [(i * 2 + v, (i ^ (relabel(r, n, v) * (v or r < n - 1))) * 2 + v) for i in range(n) for v in range(2)]
            arrived[r] = [lax.ppermute(blocks[r], ("tile", "lev"), pairs)]
        arrived[n - 1].append(lax.ppermute(arrived[n - 1][0], "lev", swap))
        slots, carried, picks = [], [], []
        for count in range(1, len(stages)):
            labels = sum(stages[:count], [])
            refs = [ref for r in labels for ref in arrived[r]]
            outs = [
                shape((n, 2 * levels, len(stages[count - 1]) * cap), BF16),
                shape((len(labels), levels, cap), F32),
                flat,
            ] + [shape((n, band_cols, cap), BF16)] * (count == 1)
            new, *carried = call(
                functools.partial(stage_kernel, n, levels, band_cols, tile_cols, stages[:count]),
                outs,
                [SMEM] + [VMEM] * (len(refs) + len(slots) + len(carried)),
                cost=pl.CostEstimate(flops=10**9, bytes_accessed=0, transcendentals=0),
            )(lev, *refs, *slots, *carried)
            slots.append(new)
            picks += carried[2:]
            carried = carried[:2]
        met, remap = carried
        refs = [ref for r in sum(stages, []) for ref in arrived[r]] + slots + [met] + picks
        mine, new, tables = call(
            functools.partial(shared_kernel, n, levels, band_cols, tile_cols, stages),
            (mine_shape, shape((n, 2 * levels, len(stages[-1]) * cap), BF16), shape((n, n + EXTRA, cap), F32)),
            [SMEM] * 2 + [VMEM] * (1 + len(refs)),
            cost=pl.CostEstimate(flops=10**9, bytes_accessed=0, transcendentals=0),
        )(pos, lev, given_mix, *refs)
        slots.append(new)
        increment, grad_static = call(
            functools.partial(outputs_kernel, stages), (flat, flat), [SMEM] * 2 + [VMEM] * (len(slots) + 7)
        )(pos, lev, *slots, remap, tables, static_control, diag, off, obs_weight, innovation)
    else:
        other_perturb = lax.ppermute(perturb, "lev", swap)
        payload = call(
            band_kernel,
            shape((groups, n, levels + EXTRA, cap), F32),
            [SMEM] + [VMEM] * 4,
            [pltpu.VMEM((2 * levels, band_cols), BF16)],
        )(counts, own_sum, static_control, send_src, send_wt)
        arrived = lax.all_to_all(
            payload.reshape(groups * n, levels + EXTRA, cap), ("grp", "tile"), split_axis=0, concat_axis=0, tiled=True
        ).reshape(groups, n, levels + EXTRA, cap)
        increment, partial, giving = call(
            tile_kernel, (flat, flat, shape((n, levels + EXTRA, cap), F32)), [SMEM] + [VMEM] * 7
        )(pos, arrived, recv_tgt, static_control, diag, off, obs_weight, innovation)
        returned = lax.all_to_all(giving, "tile", split_axis=0, concat_axis=0, tiled=True)
        grad_static, mine = call(
            functools.partial(adjoint_kernel, band_cols), (flat, mine_shape), [SMEM, SMEM] + [VMEM] * 5
        )(pos, counts, returned, send_src, send_wt, partial, given_mix)
    theirs = lax.ppermute(mine, "lev", swap)
    own = call(ens_own_kernel, shape(control.shape, F32), [VMEM] * 4)(perturb, mine, own_mix, control)
    grad_ens, increment, grad_static = call(
        ens_kernel,
        (shape(control.shape, F32), flat, flat),
        [VMEM] * 5,
        [pltpu.VMEM(control.shape, F32), pltpu.SemaphoreType.DMA((2 + members // SUB,))],
        out=HBM,
    )(other_perturb, theirs, own, increment, grad_static)
    return (increment, grad_static, grad_ens)


def solution(mesh):
    return jax.shard_map(
        body,
        mesh=mesh,
        in_specs=(
            P("lev", "grp", "tile"),
            P("lev", "grp", "tile"),
            P("lev", None),
            P("lev", "tile"),
            P("tile"),
            P("tile"),
            P("tile", None, None),
            P("tile", None, None),
            P("tile", None),
            P("tile", None, None),
            P("lev", "tile"),
            P("lev", "tile"),
        ),
        out_specs=(P("lev", "tile"), P("lev", "tile"), P("lev", "grp", "tile")),
        check_vma=False,
    )
```

```python
import functools

import jax
import jax.numpy as jnp
from jax import lax
from jax.experimental import pallas as pl
from jax.experimental.pallas import tpu as pltpu
from jax.sharding import PartitionSpec as P

F32 = jnp.float32
BF16 = jnp.bfloat16
SUB = 8
EXTRA = 8
VMEM = pl.BlockSpec(memory_space=pltpu.VMEM)
HBM = pl.BlockSpec(memory_space=pltpu.HBM)
SMEM = pl.BlockSpec(memory_space=pltpu.SMEM)
MIB = 1024 * 1024


def halves(values):
    high = values.astype(BF16)
    low = (values - high.astype(F32)).astype(BF16)
    return high, low


def product(a, b, dims=((1,), (0,))):
    return lax.dot_general(a, b, (dims, ((), ())), preferred_element_type=F32)


def select(values, chosen, dims=((1,), (0,))):
    rows = values.shape[0]
    both = product(jnp.concatenate(halves(values), axis=0), chosen, dims)
    return both[:rows] + both[rows:]


def iota(shape, axis):
    return lax.broadcasted_iota(jnp.int32, shape, axis)


def wide_rows(matrix, start, count):
    cols = matrix.shape[1]
    shape = (cols, count * SUB)
    place = (iota(shape, 1) // SUB + start) % cols
    pick = (place == iota(shape, 0)).astype(BF16)
    high, low = halves(matrix)
    return product(high, pick) + product(low, pick)


def spread(wide):
    rows, cols = wide.shape
    tall = jnp.broadcast_to(wide[:, None, :], (rows, SUB, cols)).reshape(rows * SUB, cols)
    return jnp.where(iota(tall.shape, 0) % SUB == iota(tall.shape, 1) % SUB, tall, 0.0)


def mix(weights, values):
    high, low = halves(values)
    rows = weights[0].shape[0]
    both = product(jnp.concatenate(weights, axis=0), high)
    return both[:rows] + (product(weights[0], low) + both[rows:])


def one_hot(index, size):
    rows = lax.broadcasted_iota(jnp.int32, (size, index.shape[1]), 0)
    return jnp.where(rows == index, 1.0, 0.0).astype(BF16)


def column_as_row(column, lane, offset):
    n = column.shape[0]
    place = lax.broadcasted_iota(jnp.int32, (n, 128), 1) == lax.broadcasted_iota(jnp.int32, (n, 128), 0) + offset
    return jnp.sum(jnp.where(place, column, 0.0), axis=0, keepdims=True)


def row_as_column(row, n, offset):
    place = lax.broadcasted_iota(jnp.int32, (n, 128), 1) == lax.broadcasted_iota(jnp.int32, (n, 128), 0) + offset
    return jnp.sum(jnp.where(place, row, 0.0), axis=1, keepdims=True)


def edge_rows(values):
    n = values.shape[0]
    row = column_as_row(values[:, -1:], None, 0) + column_as_row(values[:, :1], None, n)
    return jnp.broadcast_to(row, (EXTRA, 128))


def factor_of(counts_ref, weight_ref, d):
    slot = lax.broadcasted_iota(jnp.int32, (1, weight_ref.shape[2]), 1)
    return jnp.where(slot < counts_ref[0, d], weight_ref[0, pl.ds(d, 1), :], 0.0)


def loop(n, step, init):
    return lax.fori_loop(0, n, step, init, unroll=n if n <= 8 else 1)


def mix_kernel(lev_ref, loc_ref, mix_ref, own_ref, given_ref):
    levels = loc_ref.shape[0]
    start = lev_ref[0] * levels
    loc = loc_ref[...]
    mix_ref[0], mix_ref[1] = halves(spread(wide_rows(loc, start, 2 * levels)))
    own_ref[0], own_ref[1] = halves(spread(wide_rows(loc, start, levels)).T)
    given_ref[...] = wide_rows(loc, levels - start, levels)


def sum_kernel(perturb_ref, control_ref, other_ref, mix_ref, out_ref):
    levels, members, cols = perturb_ref.shape
    perturb = perturb_ref[...].astype(F32)
    total = jnp.zeros((levels, SUB, cols), F32)
    for m in range(0, members, SUB):
        tile = jnp.concatenate([control_ref[:, m : m + SUB, :], other_ref[:, m : m + SUB, :]], axis=0)
        mixed = mix((mix_ref[0], mix_ref[1]), tile.reshape(2 * levels * SUB, cols))
        total = total + perturb[:, m : m + SUB, :] * mixed.reshape(levels, SUB, cols)
    out_ref[...] = jnp.sum(total, axis=1)


def band_kernel(counts_ref, sum_ref, static_ref, src_ref, weight_ref, out_ref, acc_ref):
    levels, cols = sum_ref.shape
    acc_ref[...] = jnp.concatenate(halves(sum_ref[...]), axis=0)
    n = src_ref.shape[1]
    edges = edge_rows(static_ref[...])

    def step(d, carry):
        chosen = one_hot(src_ref[0, pl.ds(d, 1), :], cols)
        both = product(acc_ref[...], chosen)
        payload = (both[:levels] + both[levels:]) * factor_of(counts_ref, weight_ref, d)
        for g in range(out_ref.shape[0]):
            out_ref[g, d, :levels, :] = payload
            out_ref[g, d, levels:, :] = edges
        return carry

    loop(n, step, 0)


def tile_kernel(pos_ref, arrived_ref, tgt_ref, static_ref, diag_ref, off_ref, obs_ref, innov_ref,
                increment_ref, partial_ref, out_ref):
    levels, cols = static_ref.shape
    groups, n = arrived_ref.shape[:2]
    me = pos_ref[0]

    def step(s, total):
        values = sum(arrived_ref[g, s, :levels, :] for g in range(groups))
        chosen = one_hot(tgt_ref[0, pl.ds(s, 1), :], cols)
        return total + select(values, chosen, ((1,), (1,)))

    remapped = loop(n, step, jnp.zeros((levels, cols), F32))
    before = arrived_ref[0, jnp.maximum(me - 1, 0), levels : levels + 1, :]
    after = arrived_ref[0, jnp.minimum(me + 1, n - 1), levels : levels + 1, :]
    before = jnp.where(me > 0, row_as_column(before, levels, 0), 0.0)
    after = jnp.where(me < n - 1, row_as_column(after, levels, levels), 0.0)
    static = static_ref[...]
    lane = lax.broadcasted_iota(jnp.int32, (levels, cols), 1)
    left = jnp.where(lane == 0, before, pltpu.roll(static, 1, 1))
    right = jnp.where(lane == cols - 1, after, pltpu.roll(static, cols - 1, 1))
    increment = remapped + diag_ref[...] * static + off_ref[...] * (left + right)
    increment_ref[...] = increment
    misfit = obs_ref[...] * (increment - innov_ref[...])
    coupled = off_ref[...] * misfit
    left = jnp.where(lane == 0, 0.0, pltpu.roll(coupled, 1, 1))
    right = jnp.where(lane == cols - 1, 0.0, pltpu.roll(coupled, cols - 1, 1))
    partial_ref[...] = static + diag_ref[...] * misfit + left + right
    edges = edge_rows(coupled)
    both = jnp.concatenate(halves(misfit), axis=0)

    def give(s, carry):
        chosen = one_hot(tgt_ref[0, pl.ds(s, 1), :], cols)
        picked = product(both, chosen)
        out_ref[s, :levels, :] = picked[:levels] + picked[levels:]
        out_ref[s, levels:, :] = edges
        return carry

    loop(n, give, 0)


def adjoint_kernel(band, pos_ref, counts_ref, returned_ref, src_ref, weight_ref, partial_ref, mix_ref, grad_ref, out_ref):
    levels, cols = partial_ref.shape
    n = returned_ref.shape[0]
    me = pos_ref[0]

    def step(d, total):
        values = returned_ref[d, :levels, :] * factor_of(counts_ref, weight_ref, d)
        return total + select(values, one_hot(src_ref[0, pl.ds(d, 1), :], band), ((1,), (1,)))

    out_ref[...] = band_rows(loop(n, step, jnp.zeros((levels, band), F32)), mix_ref[...])
    before = returned_ref[jnp.maximum(me - 1, 0), levels : levels + 1, :]
    after = returned_ref[jnp.minimum(me + 1, n - 1), levels : levels + 1, :]
    before = jnp.where(me > 0, row_as_column(before, levels, 0), 0.0)
    after = jnp.where(me < n - 1, row_as_column(after, levels, levels), 0.0)
    lane = lax.broadcasted_iota(jnp.int32, (levels, cols), 1)
    grad_ref[...] = partial_ref[...] + (jnp.where(lane == 0, before, 0.0) + jnp.where(lane == cols - 1, after, 0.0))


def band_rows(band, weights):
    width = weights.shape[1]
    return jnp.concatenate([band[:, at : at + width] for at in range(0, band.shape[1], width)] + [weights], axis=0)


def ens_tiles(perturb_ref, rows_ref, weights, before_ref):
    levels, members, cols = perturb_ref.shape
    width = rows_ref.shape[1]
    parts = [rows_ref[i * levels : (i + 1) * levels, :] for i in range(cols // width)]
    grad = jnp.concatenate(parts, axis=1)[:, None, :]
    perturb = perturb_ref[...].astype(F32)
    for m in range(0, members, SUB):
        place = (slice(None), slice(m, m + SUB), slice(None))
        tile = (perturb[place] * grad).reshape(levels * SUB, cols)
        yield place, before_ref[place] + mix(weights, tile).reshape(levels, SUB, cols)


def ens_own_kernel(perturb_ref, mine_ref, weights_ref, control_ref, out_ref):
    for place, values in ens_tiles(perturb_ref, mine_ref, (weights_ref[0], weights_ref[1]), control_ref):
        out_ref[place] = values


def ens_kernel(perturb_ref, theirs_ref, own_ref, *refs):
    count = (len(refs) - 3) // 2
    flats, (out_hbm, *flat_hbms), (out_ref, sems) = refs[:count], refs[count : 2 * count + 1], refs[2 * count + 1 :]
    copies = [pltpu.make_async_copy(a, b, sems.at[i]) for i, (a, b) in enumerate(zip(flats, flat_hbms))]
    for copy in copies:
        copy.start()
    levels = perturb_ref.shape[0]
    weights = halves(spread(theirs_ref[theirs_ref.shape[0] - levels :, :]).T)
    for place, values in ens_tiles(perturb_ref, theirs_ref, weights, own_ref):
        out_ref[place] = values
        copies.append(pltpu.make_async_copy(out_ref.at[place], out_hbm.at[place], sems.at[len(copies)]))
        copies[-1].start()
    for copy in copies:
        copy.wait()


def relabel(r, n, lev):
    high, low = n // 2, n // 4
    if low == 0:
        return r
    both = high | low
    turned = (r & ~both) | ((r & low) << 1) | ((r & high) >> 1)
    return r + (turned - r) * lev


class Rows:
    def __init__(self, levels, n):
        self.weight = slice(0, levels)
        self.base = slice(levels, 2 * levels)
        at = 2 * levels
        self.factor, self.index, self.edge = at, at + n, at + 2 * n
        self.total = at + 2 * n + EXTRA


def static_kernel(band, pos_ref, lev_ref, counts_ref, static_ref, diag_ref, off_ref, obs_ref, innov_ref, src_ref, weight_ref, tgt_ref,
                  *out_refs):
    levels, cols = static_ref.shape
    n = len(out_refs)
    cap = src_ref.shape[2]
    rows = Rows(levels, n)
    peers = [pos_ref[0] ^ relabel(r, n, lev_ref[0]) for r in range(n)]
    static, off, obs = static_ref[...], off_ref[...], obs_ref[...]
    lane = lax.broadcasted_iota(jnp.int32, (levels, cols), 1)
    left = jnp.where(lane == 0, 0.0, pltpu.roll(static, 1, 1))
    right = jnp.where(lane == cols - 1, 0.0, pltpu.roll(static, cols - 1, 1))
    base = diag_ref[...] * static + off * (left + right) - innov_ref[...]
    coupled = off * obs
    ends = [v[:, i] for v in (static, coupled, base) for i in (slice(cols - 1, cols), slice(0, 1))]
    edge = sum(column_as_row(end, None, i * levels) for i, end in enumerate(ends))
    place = lax.broadcasted_iota(jnp.int32, (1, cap), 1)
    edge = edge + jnp.where(place == 6 * levels, off[:, cols - 1 :], 0.0)
    edge = edge + jnp.where(place == 6 * levels + 1, off[:, :1], 0.0)
    edge = jnp.broadcast_to(edge, (EXTRA, cap))
    both = jnp.concatenate(halves(jnp.concatenate([obs, base], axis=0)), axis=0)
    tgts = [tgt_ref[0, pl.ds(peer, 1), :] for peer in peers]
    src = jnp.concatenate([src_ref[0, pl.ds(peer, 1), :] for peer in peers], axis=0).astype(F32)
    index = jnp.concatenate(tgts, axis=0).astype(F32) * float(band) + src
    factor = jnp.concatenate([factor_of(counts_ref, weight_ref, peer) for peer in peers], axis=0)
    for r, out_ref in enumerate(out_refs):
        picked = product(both, one_hot(tgts[r], cols))
        out_ref[: 2 * levels, :] = picked[: 2 * levels] + picked[2 * levels :]
        out_ref[rows.factor : rows.factor + n, :] = factor
        out_ref[rows.index : rows.index + n, :] = index
        out_ref[rows.edge :, :] = edge


def blocks_kernel(groups, *refs):
    sums = refs[:groups]
    count = (len(refs) - groups - 1) // 2
    rests = refs[groups : groups + count]
    total_ref = refs[groups + count]
    out_refs = refs[groups + count + 1 :]
    total = sum(ref[...] for ref in sums)
    cap = total_ref.shape[1]
    total = jnp.concatenate([total[:, at : at + cap] for at in range(0, total.shape[1], cap)], axis=0)
    total_ref[...] = total
    for rest_ref, out_ref in zip(rests, out_refs):
        out_ref[: total.shape[0], :] = total
        out_ref[total.shape[0] :, :] = rest_ref[...]


class Block:
    def __init__(self, refs, n, levels, band):
        cap = refs[0].shape[1]
        self.levels, self.parts, self.cap = levels, band // cap, cap
        self.sums_ref, self.rest_ref = refs[0], refs[-1]
        self.head = 0 if len(refs) == 2 else self.parts * levels
        self.rows = Rows(levels, n)
        words = self.rest(self.rows.index, n)
        self.tgt = jnp.floor((words + 0.5) * (1.0 / band))
        self.src = words - self.tgt * float(band)
        self.factor = self.rest(self.rows.factor, n)

    def rest(self, at, size):
        return self.rest_ref[self.head + at : self.head + at + size, :]

    def sums(self):
        parts = [self.sums_ref[i * self.levels : (i + 1) * self.levels, :] for i in range(self.parts)]
        return jnp.concatenate(halves(jnp.concatenate(parts, axis=1)), axis=0)


def line(table, i):
    return table[i : i + 1]


def pick_source(block, r):
    band = block.parts * block.cap
    column = lax.broadcasted_iota(jnp.int32, (band, block.cap), 0).astype(F32)
    return jnp.where(column == line(block.src, r), 1.0, 0.0).astype(BF16)


def fill_slots(bands, blocks, n, slots_ref):
    for i, s in enumerate(bands):
        block = blocks[s]
        both = block.sums()
        for d in range(n):
            picked = product(both, pick_source(block, s ^ d))
            values = (picked[: block.levels] + picked[block.levels :]) * line(block.factor, s ^ d)
            slots_ref[d, :, i * block.cap : (i + 1) * block.cap] = jnp.concatenate(halves(values), axis=0)


def met_at(d, block, bands, slots_ref):
    own = jnp.broadcast_to(line(block.tgt, d), (block.cap, block.cap)).T
    same = [jnp.where(own == line(block.tgt, s ^ d), 1.0, 0.0).astype(BF16) for s in bands]
    met = product(slots_ref[d], jnp.concatenate(same, axis=1), ((1,), (1,)))
    return met[: block.levels] + met[block.levels :]


def land(table, bands, slots_ref, cols):
    cap = table.shape[1]
    row = lax.broadcasted_iota(jnp.int32, (cols, cap), 0).astype(F32)
    total = 0.0
    for i, s in enumerate(bands):
        landing = jnp.where(row == line(table, s), 1.0, 0.0).astype(BF16)
        total = total + product(slots_ref[0, :, i * cap : (i + 1) * cap], landing, ((1,), (1,)))
    levels = total.shape[0] // 2
    return total[:levels] + total[levels:]


def open_blocks(labels, refs, n, levels, band):
    blocks = {0: Block(refs[:2], n, levels, band)}
    refs = refs[2:]
    for i, r in enumerate(labels[1:]):
        blocks[r] = Block(refs[i : i + 1], n, levels, band)
    return blocks, refs[len(labels) - 1 :]


def stage_kernel(n, levels, band, cols, stages, *refs):
    known = sum(stages[:-1], [])
    blocks, refs = open_blocks(known + stages[-1], refs, n, levels, band)
    old, refs = refs[: len(stages) - 1], refs[len(stages) - 1 :]
    if known:
        met_old, remap_old, slots_ref, met_ref, remap_ref = refs
    else:
        slots_ref, met_ref, remap_ref, pick_ref = refs
        for d in range(n):
            pick_ref[d] = pick_source(blocks[0], d)
    fill_slots(stages[-1], blocks, n, slots_ref)
    for i, (d, block) in enumerate(blocks.items()):
        met = met_at(d, block, stages[-1], slots_ref)
        if d in known:
            met = met + met_old[i]
        else:
            for bands, ref in zip(stages, old):
                met = met + met_at(d, block, bands, ref)
        met_ref[i] = met
    landed = land(blocks[0].tgt, stages[-1], slots_ref, cols)
    remap_ref[...] = landed + remap_old[...] if known else landed


def shared_kernel(n, levels, band, cols, stages, pos_ref, lev_ref, mix_ref, *refs):
    known = sum(stages[:-1], [])
    blocks, refs = open_blocks(known + stages[-1], refs, n, levels, band)
    old, refs = refs[: len(stages) - 1], refs[len(stages) - 1 :]
    met_old, pick_ref, out_ref, slots_ref, tables_ref = refs
    me = pos_ref[0]
    for r, block in blocks.items():
        there = me ^ relabel(r, n, lev_ref[0])
        tables_ref[there, :n, :] = block.tgt
        tables_ref[there, n:, :] = block.rest(block.rows.edge, EXTRA)
    fill_slots(stages[-1], blocks, n, slots_ref)
    last = cols - 1.0
    total = jnp.zeros((levels, band), F32)
    for i, (d, block) in enumerate(blocks.items()):
        value = met_at(d, block, stages[-1], slots_ref) + block.rest(levels, levels)
        if d in known:
            value = value + met_old[i]
        else:
            for bands, ref in zip(stages, old):
                value = value + met_at(d, block, bands, ref)
        edge = block.rest(block.rows.edge, 1)
        own = line(block.tgt, d)
        there = me ^ relabel(d, n, lev_ref[0])
        before = tables_ref[jnp.maximum(there - 1, 0), n : n + 1, :]
        near = jnp.where((own == 0.0) & (there > 0), edge[:, 6 * levels + 1 : 6 * levels + 2], 0.0)
        value = value + row_as_column(before, levels, 0) * near
        after = tables_ref[jnp.minimum(there + 1, n - 1), n : n + 1, :]
        near = jnp.where((own == last) & (there < n - 1), edge[:, 6 * levels : 6 * levels + 1], 0.0)
        value = value + row_as_column(after, levels, levels) * near
        given = block.rest(0, levels) * value * line(blocks[0].factor, d)
        total = total + select(given, pick_ref[d], ((1,), (1,)))
    out_ref[...] = band_rows(total, mix_ref[...])


def outputs_kernel(stages, pos_ref, lev_ref, *refs):
    slots_refs, refs = refs[: len(stages)], refs[len(stages) :]
    remap_ref, tables_ref, static_ref, diag_ref, off_ref, obs_ref, innov_ref, increment_ref, grad_ref = refs
    levels, cols = static_ref.shape
    n = tables_ref.shape[0]
    cap = tables_ref.shape[2]
    me = pos_ref[0]
    given = [
        (s, ref, slice(i * cap, (i + 1) * cap)) for bands, ref in zip(stages, slots_refs) for i, s in enumerate(bands)
    ]
    remapped = remap_ref[...] + land(tables_ref[me, :n, :], stages[-1], slots_refs[-1], cols)
    static, off = static_ref[...], off_ref[...]
    lane = lax.broadcasted_iota(jnp.int32, (levels, cols), 1)

    def beside(there, exists, column, own_end, side):
        edge = tables_ref[there, n : n + 1, :]
        static_end, coupling, base = (row_as_column(edge, levels, (2 * i + side) * levels) for i in range(3))
        far = relabel(me ^ there, n, lev_ref[0])
        landed = []
        for s, ref, place in given:
            values = ref[far, :levels, place].astype(F32) + ref[far, levels:, place].astype(F32)
            landed.append(jnp.where(tables_ref[there, pl.ds(s ^ far, 1), :] == column, values, 0.0))
        remap_end = jnp.sum(sum(landed), axis=1, keepdims=True)
        off_end = edge[:, 6 * levels + side : 6 * levels + side + 1]
        coupled = coupling * (remap_end + base + off_end * own_end)
        return jnp.where(exists, static_end, 0.0), jnp.where(exists, coupled, 0.0)

    before, coupled_before = beside(jnp.maximum(me - 1, 0), me > 0, cols - 1.0, static[:, :1], 0)
    after, coupled_after = beside(jnp.minimum(me + 1, n - 1), me < n - 1, 0.0, static[:, cols - 1 :], 1)
    left = jnp.where(lane == 0, before, pltpu.roll(static, 1, 1))
    right = jnp.where(lane == cols - 1, after, pltpu.roll(static, cols - 1, 1))
    increment = remapped + diag_ref[...] * static + off * (left + right)
    increment_ref[...] = increment
    misfit = obs_ref[...] * (increment - innov_ref[...])
    coupled = off * misfit
    left = jnp.where(lane == 0, coupled_before, pltpu.roll(coupled, 1, 1))
    right = jnp.where(lane == cols - 1, coupled_after, pltpu.roll(coupled, cols - 1, 1))
    grad_ref[...] = static + diag_ref[...] * misfit + left + right


def call(kernel, out_shape, spaces, scratch=(), out=VMEM, cost=None):
    return pl.pallas_call(
        kernel,
        out_shape=out_shape,
        in_specs=spaces,
        out_specs=jax.tree.map(lambda _: out, out_shape),
        scratch_shapes=scratch,
        cost_estimate=cost,
        compiler_params=pltpu.CompilerParams(vmem_limit_bytes=40 * MIB),
    )


def body(
    perturb,
    control,
    level_loc,
    static_control,
    filter_diag,
    filter_off,
    send_src,
    send_wt,
    counts,
    recv_tgt,
    obs_weight,
    innovation,
):
    levels, members, band_cols = control.shape
    tile_cols = static_control.shape[1]
    n = lax.axis_size("tile")
    groups = lax.axis_size("grp")
    cap = send_src.shape[2]
    shape = jax.ShapeDtypeStruct
    swap = [(0, 1), (1, 0)]
    lev = lax.axis_index("lev").astype(jnp.int32).reshape(1)
    pos = lax.axis_index("tile").astype(jnp.int32).reshape(1)
    other_control = lax.ppermute(control, "lev", swap)
    width = levels * SUB
    level_mix, own_mix, given_mix = call(
        mix_kernel,
        (shape((2, width, 2 * width), BF16), shape((2, width, width), BF16), shape((levels, width), F32)),
        [SMEM, VMEM],
        cost=pl.CostEstimate(flops=10**9, bytes_accessed=0, transcendentals=0),
    )(lev, level_loc)
    own_sum = call(sum_kernel, shape((levels, band_cols), F32), [VMEM] * 4)(perturb, control, other_control, level_mix)
    flat = shape((levels, tile_cols), F32)
    mine_shape = shape((band_cols // width * levels + levels, width), F32)
    diag, off = filter_diag.reshape(1, -1), filter_off.reshape(1, -1)
    if n * cap <= tile_cols and n >= 8 and lax.axis_size("lev") == 2 and n & (n - 1) == 0 and band_cols * tile_cols <= 2**20:
        rows = Rows(levels, n)
        stacked = band_cols // cap * levels
        rests = call(functools.partial(static_kernel, band_cols), [shape((rows.total, cap), F32)] * n, [SMEM] * 3 + [VMEM] * 8)(
            pos, lev, counts, static_control, diag, off, obs_weight, innovation, send_src, send_wt, recv_tgt
        )
        sums = [own_sum]
        sums[0], other_perturb = lax.optimization_barrier((sums[0], lax.ppermute(perturb, "lev", swap)))
        for k in range(1, groups):
            sums.append(lax.ppermute(sums[0], "grp", [(g, (g + k) % groups) for g in range(groups)]))
        total, *blocks = call(
            functools.partial(blocks_kernel, groups),
            [shape((stacked, cap), F32)] + [shape((stacked + rows.total, cap), F32)] * (n - 1),
            [VMEM] * (groups + n - 1),
        )(*sums, *rests[1:])
        low, high = n // 4, n // 2
        mixed = [r for i in reversed(range(low)) for r in (high + i, low + i)]
        order = [high + low, mixed[0], *range(high + low + 1, n), *mixed[1:], *range(1, low)]
        late = [mixed[2 * low - 2], *order[n - low :]]
        stages = [[0] + order[: high - 1], [r for r in order[high - 1 :] if r not in late], late]
        levs = lax.axis_size("lev")
        arrived = {0: [total, rests[0]]}
        for r in sum(stages, [])[1:]:
            pairs = [(i * levs + v, (i ^ relabel(r, n, v)) * levs + v) for i in range(n) for v in range(levs)]
            arrived[r] = [lax.ppermute(blocks[r - 1], ("tile", "lev"), pairs)]
        slots, carried, picks = [], [], []
        for count in range(1, len(stages)):
            labels = sum(stages[:count], [])
            refs = [ref for r in labels for ref in arrived[r]]
            outs = [
                shape((n, 2 * levels, len(stages[count - 1]) * cap), BF16),
                shape((len(labels), levels, cap), F32),
                flat,
            ] + [shape((n, band_cols, cap), BF16)] * (count == 1)
            new, *carried = call(
                functools.partial(stage_kernel, n, levels, band_cols, tile_cols, stages[:count]),
                outs,
                [VMEM] * (len(refs) + len(slots) + len(carried)),
            )(*refs, *slots, *carried)
            slots.append(new)
            picks += carried[2:]
            carried = carried[:2]
        met, remap = carried
        refs = [ref for r in sum(stages, []) for ref in arrived[r]] + slots + [met] + picks
        mine, new, tables = call(
            functools.partial(shared_kernel, n, levels, band_cols, tile_cols, stages),
            (mine_shape, shape((n, 2 * levels, len(stages[-1]) * cap), BF16), shape((n, n + EXTRA, cap), F32)),
            [SMEM] * 2 + [VMEM] * (1 + len(refs)),
        )(pos, lev, given_mix, *refs)
        slots.append(new)
        increment, grad_static = call(
            functools.partial(outputs_kernel, stages), (flat, flat), [SMEM] * 2 + [VMEM] * (len(slots) + 7)
        )(pos, lev, *slots, remap, tables, static_control, diag, off, obs_weight, innovation)
    else:
        other_perturb = lax.ppermute(perturb, "lev", swap)
        payload = call(
            band_kernel,
            shape((groups, n, levels + EXTRA, cap), F32),
            [SMEM] + [VMEM] * 4,
            [pltpu.VMEM((2 * levels, band_cols), BF16)],
        )(counts, own_sum, static_control, send_src, send_wt)
        arrived = lax.all_to_all(
            payload.reshape(groups * n, levels + EXTRA, cap), ("grp", "tile"), split_axis=0, concat_axis=0, tiled=True
        ).reshape(groups, n, levels + EXTRA, cap)
        increment, partial, giving = call(
            tile_kernel, (flat, flat, shape((n, levels + EXTRA, cap), F32)), [SMEM] + [VMEM] * 7
        )(pos, arrived, recv_tgt, static_control, diag, off, obs_weight, innovation)
        returned = lax.all_to_all(giving, "tile", split_axis=0, concat_axis=0, tiled=True)
        grad_static, mine = call(
            functools.partial(adjoint_kernel, band_cols), (flat, mine_shape), [SMEM, SMEM] + [VMEM] * 5
        )(pos, counts, returned, send_src, send_wt, partial, given_mix)
    theirs = lax.ppermute(mine, "lev", swap)
    own = call(ens_own_kernel, shape(control.shape, F32), [VMEM] * 4)(perturb, mine, own_mix, control)
    grad_ens, increment, grad_static = call(
        ens_kernel,
        (shape(control.shape, F32), flat, flat),
        [VMEM] * 5,
        [pltpu.VMEM(control.shape, F32), pltpu.SemaphoreType.DMA((2 + members // SUB,))],
        out=HBM,
    )(other_perturb, theirs, own, increment, grad_static)
    return (increment, grad_static, grad_ens)


def solution(mesh):
    return jax.shard_map(
        body,
        mesh=mesh,
        in_specs=(
            P("lev", "grp", "tile"),
            P("lev", "grp", "tile"),
            P("lev", None),
            P("lev", "tile"),
            P("tile"),
            P("tile"),
            P("tile", None, None),
            P("tile", None, None),
            P("tile", None),
            P("tile", None, None),
            P("lev", "tile"),
            P("lev", "tile"),
        ),
        out_specs=(P("lev", "tile"), P("lev", "tile"), P("lev", "grp", "tile")),
        check_vma=False,
    )
```

```python
import functools

import jax
import jax.numpy as jnp
from jax import lax
from jax.experimental import pallas as pl
from jax.experimental.pallas import tpu as pltpu
from jax.sharding import PartitionSpec as P

F32 = jnp.float32
BF16 = jnp.bfloat16
SUB = 8
EXTRA = 8
VMEM = pl.BlockSpec(memory_space=pltpu.VMEM)
HBM = pl.BlockSpec(memory_space=pltpu.HBM)
SMEM = pl.BlockSpec(memory_space=pltpu.SMEM)
MIB = 1024 * 1024


def halves(values):
    high = values.astype(BF16)
    low = (values - high.astype(F32)).astype(BF16)
    return high, low


def product(a, b, dims=((1,), (0,))):
    return lax.dot_general(a, b, (dims, ((), ())), preferred_element_type=F32)


def select(values, chosen, dims=((1,), (0,))):
    rows = values.shape[0]
    both = product(jnp.concatenate(halves(values), axis=0), chosen, dims)
    return both[:rows] + both[rows:]


def iota(shape, axis):
    return lax.broadcasted_iota(jnp.int32, shape, axis)


def wide_rows(matrix, start, count):
    cols = matrix.shape[1]
    shape = (cols, count * SUB)
    place = (iota(shape, 1) // SUB + start) % cols
    pick = (place == iota(shape, 0)).astype(BF16)
    high, low = halves(matrix)
    return product(high, pick) + product(low, pick)


def spread(wide):
    rows, cols = wide.shape
    tall = jnp.broadcast_to(wide[:, None, :], (rows, SUB, cols)).reshape(rows * SUB, cols)
    return jnp.where(iota(tall.shape, 0) % SUB == iota(tall.shape, 1) % SUB, tall, 0.0)


def mix(weights, values):
    high, low = halves(values)
    rows = weights[0].shape[0]
    both = product(jnp.concatenate(weights, axis=0), high)
    return both[:rows] + (product(weights[0], low) + both[rows:])


def one_hot(index, size):
    rows = lax.broadcasted_iota(jnp.int32, (size, index.shape[1]), 0)
    return jnp.where(rows == index, 1.0, 0.0).astype(BF16)


def column_as_row(column, lane, offset):
    n = column.shape[0]
    place = lax.broadcasted_iota(jnp.int32, (n, 128), 1) == lax.broadcasted_iota(jnp.int32, (n, 128), 0) + offset
    return jnp.sum(jnp.where(place, column, 0.0), axis=0, keepdims=True)


def row_as_column(row, n, offset):
    place = lax.broadcasted_iota(jnp.int32, (n, 128), 1) == lax.broadcasted_iota(jnp.int32, (n, 128), 0) + offset
    return jnp.sum(jnp.where(place, row, 0.0), axis=1, keepdims=True)


def edge_rows(values):
    n = values.shape[0]
    row = column_as_row(values[:, -1:], None, 0) + column_as_row(values[:, :1], None, n)
    return jnp.broadcast_to(row, (EXTRA, 128))


def factor_of(counts_ref, weight_ref, d):
    slot = lax.broadcasted_iota(jnp.int32, (1, weight_ref.shape[2]), 1)
    return jnp.where(slot < counts_ref[0, d], weight_ref[0, pl.ds(d, 1), :], 0.0)


def loop(n, step, init):
    return lax.fori_loop(0, n, step, init, unroll=n if n <= 8 else 1)


def mix_kernel(lev_ref, loc_ref, mix_ref, own_ref, given_ref):
    levels = loc_ref.shape[0]
    start = lev_ref[0] * levels
    loc = loc_ref[...]
    mix_ref[0], mix_ref[1] = halves(spread(wide_rows(loc, start, 2 * levels)))
    own_ref[0], own_ref[1] = halves(spread(wide_rows(loc, start, levels)).T)
    given_ref[...] = wide_rows(loc, levels - start, levels)


def sum_kernel(perturb_ref, control_ref, other_ref, mix_ref, out_ref):
    levels, members, cols = perturb_ref.shape
    perturb = perturb_ref[...].astype(F32)
    total = jnp.zeros((levels, SUB, cols), F32)
    for m in range(0, members, SUB):
        tile = jnp.concatenate([control_ref[:, m : m + SUB, :], other_ref[:, m : m + SUB, :]], axis=0)
        mixed = mix((mix_ref[0], mix_ref[1]), tile.reshape(2 * levels * SUB, cols))
        total = total + perturb[:, m : m + SUB, :] * mixed.reshape(levels, SUB, cols)
    out_ref[...] = jnp.sum(total, axis=1)


def band_kernel(counts_ref, sum_ref, static_ref, src_ref, weight_ref, out_ref, acc_ref):
    levels, cols = sum_ref.shape
    acc_ref[...] = jnp.concatenate(halves(sum_ref[...]), axis=0)
    n = src_ref.shape[1]
    edges = edge_rows(static_ref[...])

    def step(d, carry):
        chosen = one_hot(src_ref[0, pl.ds(d, 1), :], cols)
        both = product(acc_ref[...], chosen)
        payload = (both[:levels] + both[levels:]) * factor_of(counts_ref, weight_ref, d)
        for g in range(out_ref.shape[0]):
            out_ref[g, d, :levels, :] = payload
            out_ref[g, d, levels:, :] = edges
        return carry

    loop(n, step, 0)


def tile_kernel(pos_ref, arrived_ref, tgt_ref, static_ref, diag_ref, off_ref, obs_ref, innov_ref,
                increment_ref, partial_ref, out_ref):
    levels, cols = static_ref.shape
    groups, n = arrived_ref.shape[:2]
    me = pos_ref[0]

    def step(s, total):
        values = sum(arrived_ref[g, s, :levels, :] for g in range(groups))
        chosen = one_hot(tgt_ref[0, pl.ds(s, 1), :], cols)
        return total + select(values, chosen, ((1,), (1,)))

    remapped = loop(n, step, jnp.zeros((levels, cols), F32))
    before = arrived_ref[0, jnp.maximum(me - 1, 0), levels : levels + 1, :]
    after = arrived_ref[0, jnp.minimum(me + 1, n - 1), levels : levels + 1, :]
    before = jnp.where(me > 0, row_as_column(before, levels, 0), 0.0)
    after = jnp.where(me < n - 1, row_as_column(after, levels, levels), 0.0)
    static = static_ref[...]
    lane = lax.broadcasted_iota(jnp.int32, (levels, cols), 1)
    left = jnp.where(lane == 0, before, pltpu.roll(static, 1, 1))
    right = jnp.where(lane == cols - 1, after, pltpu.roll(static, cols - 1, 1))
    increment = remapped + diag_ref[...] * static + off_ref[...] * (left + right)
    increment_ref[...] = increment
    misfit = obs_ref[...] * (increment - innov_ref[...])
    coupled = off_ref[...] * misfit
    left = jnp.where(lane == 0, 0.0, pltpu.roll(coupled, 1, 1))
    right = jnp.where(lane == cols - 1, 0.0, pltpu.roll(coupled, cols - 1, 1))
    partial_ref[...] = static + diag_ref[...] * misfit + left + right
    edges = edge_rows(coupled)
    both = jnp.concatenate(halves(misfit), axis=0)

    def give(s, carry):
        chosen = one_hot(tgt_ref[0, pl.ds(s, 1), :], cols)
        picked = product(both, chosen)
        out_ref[s, :levels, :] = picked[:levels] + picked[levels:]
        out_ref[s, levels:, :] = edges
        return carry

    loop(n, give, 0)


def adjoint_kernel(band, pos_ref, counts_ref, returned_ref, src_ref, weight_ref, partial_ref, mix_ref, grad_ref, out_ref):
    levels, cols = partial_ref.shape
    n = returned_ref.shape[0]
    me = pos_ref[0]

    def step(d, total):
        values = returned_ref[d, :levels, :] * factor_of(counts_ref, weight_ref, d)
        return total + select(values, one_hot(src_ref[0, pl.ds(d, 1), :], band), ((1,), (1,)))

    out_ref[...] = band_rows(loop(n, step, jnp.zeros((levels, band), F32)), mix_ref[...])
    before = returned_ref[jnp.maximum(me - 1, 0), levels : levels + 1, :]
    after = returned_ref[jnp.minimum(me + 1, n - 1), levels : levels + 1, :]
    before = jnp.where(me > 0, row_as_column(before, levels, 0), 0.0)
    after = jnp.where(me < n - 1, row_as_column(after, levels, levels), 0.0)
    lane = lax.broadcasted_iota(jnp.int32, (levels, cols), 1)
    grad_ref[...] = partial_ref[...] + (jnp.where(lane == 0, before, 0.0) + jnp.where(lane == cols - 1, after, 0.0))


def band_rows(band, weights):
    width = weights.shape[1]
    return jnp.concatenate([band[:, at : at + width] for at in range(0, band.shape[1], width)] + [weights], axis=0)


def ens_tiles(perturb_ref, rows_ref, weights, before_ref):
    levels, members, cols = perturb_ref.shape
    width = rows_ref.shape[1]
    parts = [rows_ref[i * levels : (i + 1) * levels, :] for i in range(cols // width)]
    grad = jnp.concatenate(parts, axis=1)[:, None, :]
    perturb = perturb_ref[...].astype(F32)
    for m in range(0, members, SUB):
        place = (slice(None), slice(m, m + SUB), slice(None))
        tile = (perturb[place] * grad).reshape(levels * SUB, cols)
        yield place, before_ref[place] + mix(weights, tile).reshape(levels, SUB, cols)


def ens_own_kernel(perturb_ref, mine_ref, weights_ref, control_ref, out_ref):
    for place, values in ens_tiles(perturb_ref, mine_ref, (weights_ref[0], weights_ref[1]), control_ref):
        out_ref[place] = values


def ens_kernel(perturb_ref, theirs_ref, own_ref, *refs):
    count = (len(refs) - 3) // 2
    flats, (out_hbm, *flat_hbms), (out_ref, sems) = refs[:count], refs[count : 2 * count + 1], refs[2 * count + 1 :]
    copies = [pltpu.make_async_copy(a, b, sems.at[i]) for i, (a, b) in enumerate(zip(flats, flat_hbms))]
    for copy in copies:
        copy.start()
    levels = perturb_ref.shape[0]
    weights = halves(spread(theirs_ref[theirs_ref.shape[0] - levels :, :]).T)
    for place, values in ens_tiles(perturb_ref, theirs_ref, weights, own_ref):
        out_ref[place] = values
        copies.append(pltpu.make_async_copy(out_ref.at[place], out_hbm.at[place], sems.at[len(copies)]))
        copies[-1].start()
    for copy in copies:
        copy.wait()


def relabel(r, n, lev):
    high, low = n // 2, n // 4
    if low == 0:
        return r
    both = high | low
    turned = (r & ~both) | ((r & low) << 1) | ((r & high) >> 1)
    return r + (turned - r) * lev


class Rows:
    def __init__(self, levels, n):
        self.weight = slice(0, levels)
        self.base = slice(levels, 2 * levels)
        at = 2 * levels
        self.factor, self.index, self.edge = at, at + n, at + 2 * n
        self.total = at + 2 * n + EXTRA


def static_kernel(band, pos_ref, lev_ref, counts_ref, static_ref, diag_ref, off_ref, obs_ref, innov_ref, src_ref, weight_ref, tgt_ref,
                  *out_refs):
    levels, cols = static_ref.shape
    n = len(out_refs)
    cap = src_ref.shape[2]
    rows = Rows(levels, n)
    peers = [pos_ref[0] ^ relabel(r, n, lev_ref[0]) for r in range(n)]
    static, off, obs = static_ref[...], off_ref[...], obs_ref[...]
    lane = lax.broadcasted_iota(jnp.int32, (levels, cols), 1)
    left = jnp.where(lane == 0, 0.0, pltpu.roll(static, 1, 1))
    right = jnp.where(lane == cols - 1, 0.0, pltpu.roll(static, cols - 1, 1))
    base = diag_ref[...] * static + off * (left + right) - innov_ref[...]
    coupled = off * obs
    ends = [v[:, i] for v in (static, coupled, base) for i in (slice(cols - 1, cols), slice(0, 1))]
    edge = sum(column_as_row(end, None, i * levels) for i, end in enumerate(ends))
    place = lax.broadcasted_iota(jnp.int32, (1, cap), 1)
    edge = edge + jnp.where(place == 6 * levels, off[:, cols - 1 :], 0.0)
    edge = edge + jnp.where(place == 6 * levels + 1, off[:, :1], 0.0)
    edge = jnp.broadcast_to(edge, (EXTRA, cap))
    both = jnp.concatenate(halves(jnp.concatenate([obs, base], axis=0)), axis=0)
    tgts = [tgt_ref[0, pl.ds(peer, 1), :] for peer in peers]
    src = jnp.concatenate([src_ref[0, pl.ds(peer, 1), :] for peer in peers], axis=0).astype(F32)
    index = jnp.concatenate(tgts, axis=0).astype(F32) * float(band) + src
    factor = jnp.concatenate([factor_of(counts_ref, weight_ref, peer) for peer in peers], axis=0)
    for r, out_ref in enumerate(out_refs):
        picked = product(both, one_hot(tgts[r], cols))
        out_ref[: 2 * levels, :] = picked[: 2 * levels] + picked[2 * levels :]
        out_ref[rows.factor : rows.factor + n, :] = factor
        out_ref[rows.index : rows.index + n, :] = index
        out_ref[rows.edge :, :] = edge


def blocks_kernel(groups, *refs):
    sums = refs[:groups]
    count = (len(refs) - groups - 1) // 2
    rests = refs[groups : groups + count]
    total_ref = refs[groups + count]
    out_refs = refs[groups + count + 1 :]
    total = sum(ref[...] for ref in sums)
    cap = total_ref.shape[1]
    total = jnp.concatenate([total[:, at : at + cap] for at in range(0, total.shape[1], cap)], axis=0)
    total_ref[...] = total
    for rest_ref, out_ref in zip(rests, out_refs):
        out_ref[: total.shape[0], :] = total
        out_ref[total.shape[0] :, :] = rest_ref[...]


class Block:
    def __init__(self, refs, n, levels, band):
        cap = refs[0].shape[1]
        self.levels, self.parts, self.cap = levels, band // cap, cap
        self.sums_ref, self.rest_ref = refs[0], refs[-1]
        self.head = 0 if len(refs) == 2 else self.parts * levels
        self.rows = Rows(levels, n)
        words = self.rest(self.rows.index, n)
        self.tgt = jnp.floor((words + 0.5) * (1.0 / band))
        self.src = words - self.tgt * float(band)
        self.factor = self.rest(self.rows.factor, n)

    def rest(self, at, size):
        return self.rest_ref[self.head + at : self.head + at + size, :]

    def sums(self):
        parts = [self.sums_ref[i * self.levels : (i + 1) * self.levels, :] for i in range(self.parts)]
        return jnp.concatenate(halves(jnp.concatenate(parts, axis=1)), axis=0)


def line(table, i):
    return table[i : i + 1]


def pick_source(block, r):
    band = block.parts * block.cap
    column = lax.broadcasted_iota(jnp.int32, (band, block.cap), 0).astype(F32)
    return jnp.where(column == line(block.src, r), 1.0, 0.0).astype(BF16)


def fill_slots(bands, blocks, n, slots_ref):
    for i, s in enumerate(bands):
        block = blocks[s]
        both = block.sums()
        for d in range(n):
            picked = product(both, pick_source(block, s ^ d))
            values = (picked[: block.levels] + picked[block.levels :]) * line(block.factor, s ^ d)
            slots_ref[d, :, i * block.cap : (i + 1) * block.cap] = jnp.concatenate(halves(values), axis=0)


def met_at(d, block, bands, slots_ref):
    own = jnp.broadcast_to(line(block.tgt, d), (block.cap, block.cap)).T
    same = [jnp.where(own == line(block.tgt, s ^ d), 1.0, 0.0).astype(BF16) for s in bands]
    met = product(slots_ref[d], jnp.concatenate(same, axis=1), ((1,), (1,)))
    return met[: block.levels] + met[block.levels :]


def land(table, bands, slots_ref, cols):
    cap = table.shape[1]
    row = lax.broadcasted_iota(jnp.int32, (cols, cap), 0).astype(F32)
    total = 0.0
    for i, s in enumerate(bands):
        landing = jnp.where(row == line(table, s), 1.0, 0.0).astype(BF16)
        total = total + product(slots_ref[0, :, i * cap : (i + 1) * cap], landing, ((1,), (1,)))
    levels = total.shape[0] // 2
    return total[:levels] + total[levels:]


def open_blocks(labels, refs, n, levels, band):
    blocks = {0: Block(refs[:2], n, levels, band)}
    refs = refs[2:]
    for i, r in enumerate(labels[1:]):
        blocks[r] = Block(refs[i : i + 1], n, levels, band)
    return blocks, refs[len(labels) - 1 :]


def stage_kernel(n, levels, band, cols, stages, *refs):
    known = sum(stages[:-1], [])
    blocks, refs = open_blocks(known + stages[-1], refs, n, levels, band)
    old, refs = refs[: len(stages) - 1], refs[len(stages) - 1 :]
    if known:
        met_old, remap_old, slots_ref, met_ref, remap_ref = refs
    else:
        slots_ref, met_ref, remap_ref, pick_ref = refs
        for d in range(n):
            pick_ref[d] = pick_source(blocks[0], d)
    fill_slots(stages[-1], blocks, n, slots_ref)
    for i, (d, block) in enumerate(blocks.items()):
        met = met_at(d, block, stages[-1], slots_ref)
        if d in known:
            met = met + met_old[i]
        else:
            for bands, ref in zip(stages, old):
                met = met + met_at(d, block, bands, ref)
        met_ref[i] = met
    landed = land(blocks[0].tgt, stages[-1], slots_ref, cols)
    remap_ref[...] = landed + remap_old[...] if known else landed


def shared_kernel(n, levels, band, cols, stages, pos_ref, lev_ref, mix_ref, *refs):
    known = sum(stages[:-1], [])
    blocks, refs = open_blocks(known + stages[-1], refs, n, levels, band)
    old, refs = refs[: len(stages) - 1], refs[len(stages) - 1 :]
    met_old, pick_ref, out_ref, slots_ref, tables_ref = refs
    me = pos_ref[0]
    for r, block in blocks.items():
        there = me ^ relabel(r, n, lev_ref[0])
        tables_ref[there, :n, :] = block.tgt
        tables_ref[there, n:, :] = block.rest(block.rows.edge, EXTRA)
    fill_slots(stages[-1], blocks, n, slots_ref)
    last = cols - 1.0
    total = jnp.zeros((levels, band), F32)
    for i, (d, block) in enumerate(blocks.items()):
        value = met_at(d, block, stages[-1], slots_ref) + block.rest(levels, levels)
        if d in known:
            value = value + met_old[i]
        else:
            for bands, ref in zip(stages, old):
                value = value + met_at(d, block, bands, ref)
        edge = block.rest(block.rows.edge, 1)
        own = line(block.tgt, d)
        there = me ^ relabel(d, n, lev_ref[0])
        before = tables_ref[jnp.maximum(there - 1, 0), n : n + 1, :]
        near = jnp.where((own == 0.0) & (there > 0), edge[:, 6 * levels + 1 : 6 * levels + 2], 0.0)
        value = value + row_as_column(before, levels, 0) * near
        after = tables_ref[jnp.minimum(there + 1, n - 1), n : n + 1, :]
        near = jnp.where((own == last) & (there < n - 1), edge[:, 6 * levels : 6 * levels + 1], 0.0)
        value = value + row_as_column(after, levels, levels) * near
        given = block.rest(0, levels) * value * line(blocks[0].factor, d)
        total = total + select(given, pick_ref[d], ((1,), (1,)))
    out_ref[...] = band_rows(total, mix_ref[...])


def outputs_kernel(stages, pos_ref, lev_ref, *refs):
    slots_refs, refs = refs[: len(stages)], refs[len(stages) :]
    remap_ref, tables_ref, static_ref, diag_ref, off_ref, obs_ref, innov_ref, increment_ref, grad_ref = refs
    levels, cols = static_ref.shape
    n = tables_ref.shape[0]
    cap = tables_ref.shape[2]
    me = pos_ref[0]
    given = [
        (s, ref, slice(i * cap, (i + 1) * cap)) for bands, ref in zip(stages, slots_refs) for i, s in enumerate(bands)
    ]
    remapped = remap_ref[...] + land(tables_ref[me, :n, :], stages[-1], slots_refs[-1], cols)
    static, off = static_ref[...], off_ref[...]
    lane = lax.broadcasted_iota(jnp.int32, (levels, cols), 1)

    def beside(there, exists, column, own_end, side):
        edge = tables_ref[there, n : n + 1, :]
        static_end, coupling, base = (row_as_column(edge, levels, (2 * i + side) * levels) for i in range(3))
        far = relabel(me ^ there, n, lev_ref[0])
        landed = []
        for s, ref, place in given:
            values = ref[far, :levels, place].astype(F32) + ref[far, levels:, place].astype(F32)
            landed.append(jnp.where(tables_ref[there, pl.ds(s ^ far, 1), :] == column, values, 0.0))
        remap_end = jnp.sum(sum(landed), axis=1, keepdims=True)
        off_end = edge[:, 6 * levels + side : 6 * levels + side + 1]
        coupled = coupling * (remap_end + base + off_end * own_end)
        return jnp.where(exists, static_end, 0.0), jnp.where(exists, coupled, 0.0)

    before, coupled_before = beside(jnp.maximum(me - 1, 0), me > 0, cols - 1.0, static[:, :1], 0)
    after, coupled_after = beside(jnp.minimum(me + 1, n - 1), me < n - 1, 0.0, static[:, cols - 1 :], 1)
    left = jnp.where(lane == 0, before, pltpu.roll(static, 1, 1))
    right = jnp.where(lane == cols - 1, after, pltpu.roll(static, cols - 1, 1))
    increment = remapped + diag_ref[...] * static + off * (left + right)
    increment_ref[...] = increment
    misfit = obs_ref[...] * (increment - innov_ref[...])
    coupled = off * misfit
    left = jnp.where(lane == 0, coupled_before, pltpu.roll(coupled, 1, 1))
    right = jnp.where(lane == cols - 1, coupled_after, pltpu.roll(coupled, cols - 1, 1))
    grad_ref[...] = static + diag_ref[...] * misfit + left + right


def call(kernel, out_shape, spaces, scratch=(), out=VMEM, cost=None):
    return pl.pallas_call(
        kernel,
        out_shape=out_shape,
        in_specs=spaces,
        out_specs=jax.tree.map(lambda _: out, out_shape),
        scratch_shapes=scratch,
        cost_estimate=cost,
        compiler_params=pltpu.CompilerParams(vmem_limit_bytes=40 * MIB),
    )


def body(
    perturb,
    control,
    level_loc,
    static_control,
    filter_diag,
    filter_off,
    send_src,
    send_wt,
    counts,
    recv_tgt,
    obs_weight,
    innovation,
):
    levels, members, band_cols = control.shape
    tile_cols = static_control.shape[1]
    n = lax.axis_size("tile")
    groups = lax.axis_size("grp")
    cap = send_src.shape[2]
    shape = jax.ShapeDtypeStruct
    swap = [(0, 1), (1, 0)]
    lev = lax.axis_index("lev").astype(jnp.int32).reshape(1)
    pos = lax.axis_index("tile").astype(jnp.int32).reshape(1)
    other_control = lax.ppermute(control, "lev", swap)
    width = levels * SUB
    level_mix, own_mix, given_mix = call(
        mix_kernel,
        (shape((2, width, 2 * width), BF16), shape((2, width, width), BF16), shape((levels, width), F32)),
        [SMEM, VMEM],
        cost=pl.CostEstimate(flops=10**9, bytes_accessed=0, transcendentals=0),
    )(lev, level_loc)
    own_sum = call(sum_kernel, shape((levels, band_cols), F32), [VMEM] * 4)(perturb, control, other_control, level_mix)
    flat = shape((levels, tile_cols), F32)
    mine_shape = shape((band_cols // width * levels + levels, width), F32)
    diag, off = filter_diag.reshape(1, -1), filter_off.reshape(1, -1)
    if n * cap <= tile_cols and n >= 8 and lax.axis_size("lev") == 2 and n & (n - 1) == 0 and band_cols * tile_cols <= 2**20:
        rows = Rows(levels, n)
        stacked = band_cols // cap * levels
        rests = call(functools.partial(static_kernel, band_cols), [shape((rows.total, cap), F32)] * n, [SMEM] * 3 + [VMEM] * 8)(
            pos, lev, counts, static_control, diag, off, obs_weight, innovation, send_src, send_wt, recv_tgt
        )
        sums = [own_sum]
        sums[0], other_perturb = lax.optimization_barrier((sums[0], lax.ppermute(perturb, "lev", swap)))
        for k in range(1, groups):
            sums.append(lax.ppermute(sums[0], "grp", [(g, (g + k) % groups) for g in range(groups)]))
        total, *blocks = call(
            functools.partial(blocks_kernel, groups),
            [shape((stacked, cap), F32)] + [shape((stacked + rows.total, cap), F32)] * (n - 1),
            [VMEM] * (groups + n - 1),
        )(*sums, *rests[1:])
        low, high = n // 4, n // 2
        mixed = [r for i in reversed(range(low)) for r in (high + i, low + i)]
        order = [high + low, mixed[0], *range(high + low + 1, n), *mixed[1:], *range(1, low)]
        stages = [[0] + order[: high - 1], order[high - 1 : high], order[high:]]
        levs = lax.axis_size("lev")
        arrived = {0: [total, rests[0]]}
        for r in sum(stages, [])[1:]:
            pairs = [(i * levs + v, (i ^ relabel(r, n, v)) * levs + v) for i in range(n) for v in range(levs)]
            arrived[r] = [lax.ppermute(blocks[r - 1], ("tile", "lev"), pairs)]
        slots, carried, picks = [], [], []
        for count in range(1, len(stages)):
            labels = sum(stages[:count], [])
            refs = [ref for r in labels for ref in arrived[r]]
            outs = [
                shape((n, 2 * levels, len(stages[count - 1]) * cap), BF16),
                shape((len(labels), levels, cap), F32),
                flat,
            ] + [shape((n, band_cols, cap), BF16)] * (count == 1)
            new, *carried = call(
                functools.partial(stage_kernel, n, levels, band_cols, tile_cols, stages[:count]),
                outs,
                [VMEM] * (len(refs) + len(slots) + len(carried)),
            )(*refs, *slots, *carried)
            slots.append(new)
            picks += carried[2:]
            carried = carried[:2]
        met, remap = carried
        refs = [ref for r in sum(stages, []) for ref in arrived[r]] + slots + [met] + picks
        mine, new, tables = call(
            functools.partial(shared_kernel, n, levels, band_cols, tile_cols, stages),
            (mine_shape, shape((n, 2 * levels, len(stages[-1]) * cap), BF16), shape((n, n + EXTRA, cap), F32)),
            [SMEM] * 2 + [VMEM] * (1 + len(refs)),
        )(pos, lev, given_mix, *refs)
        slots.append(new)
        increment, grad_static = call(
            functools.partial(outputs_kernel, stages), (flat, flat), [SMEM] * 2 + [VMEM] * (len(slots) + 7)
        )(pos, lev, *slots, remap, tables, static_control, diag, off, obs_weight, innovation)
    else:
        other_perturb = lax.ppermute(perturb, "lev", swap)
        payload = call(
            band_kernel,
            shape((groups, n, levels + EXTRA, cap), F32),
            [SMEM] + [VMEM] * 4,
            [pltpu.VMEM((2 * levels, band_cols), BF16)],
        )(counts, own_sum, static_control, send_src, send_wt)
        arrived = lax.all_to_all(
            payload.reshape(groups * n, levels + EXTRA, cap), ("grp", "tile"), split_axis=0, concat_axis=0, tiled=True
        ).reshape(groups, n, levels + EXTRA, cap)
        increment, partial, giving = call(
            tile_kernel, (flat, flat, shape((n, levels + EXTRA, cap), F32)), [SMEM] + [VMEM] * 7
        )(pos, arrived, recv_tgt, static_control, diag, off, obs_weight, innovation)
        returned = lax.all_to_all(giving, "tile", split_axis=0, concat_axis=0, tiled=True)
        grad_static, mine = call(
            functools.partial(adjoint_kernel, band_cols), (flat, mine_shape), [SMEM, SMEM] + [VMEM] * 5
        )(pos, counts, returned, send_src, send_wt, partial, given_mix)
    theirs = lax.ppermute(mine, "lev", swap)
    own = call(ens_own_kernel, shape(control.shape, F32), [VMEM] * 4)(perturb, mine, own_mix, control)
    grad_ens, increment, grad_static = call(
        ens_kernel,
        (shape(control.shape, F32), flat, flat),
        [VMEM] * 5,
        [pltpu.VMEM(control.shape, F32), pltpu.SemaphoreType.DMA((2 + members // SUB,))],
        out=HBM,
    )(other_perturb, theirs, own, increment, grad_static)
    return (increment, grad_static, grad_ens)


def solution(mesh):
    return jax.shard_map(
        body,
        mesh=mesh,
        in_specs=(
            P("lev", "grp", "tile"),
            P("lev", "grp", "tile"),
            P("lev", None),
            P("lev", "tile"),
            P("tile"),
            P("tile"),
            P("tile", None, None),
            P("tile", None, None),
            P("tile", None),
            P("tile", None, None),
            P("lev", "tile"),
            P("lev", "tile"),
        ),
        out_specs=(P("lev", "tile"), P("lev", "tile"), P("lev", "grp", "tile")),
        check_vma=False,
    )
```

```python
import functools

import jax
import jax.numpy as jnp
from jax import lax
from jax.experimental import pallas as pl
from jax.experimental.pallas import tpu as pltpu
from jax.sharding import PartitionSpec as P

F32 = jnp.float32
BF16 = jnp.bfloat16
SUB = 8
EXTRA = 8
VMEM = pl.BlockSpec(memory_space=pltpu.VMEM)
HBM = pl.BlockSpec(memory_space=pltpu.HBM)
SMEM = pl.BlockSpec(memory_space=pltpu.SMEM)
MIB = 1024 * 1024


def halves(values):
    high = values.astype(BF16)
    low = (values - high.astype(F32)).astype(BF16)
    return high, low


def product(a, b, dims=((1,), (0,))):
    return lax.dot_general(a, b, (dims, ((), ())), preferred_element_type=F32)


def select(values, chosen, dims=((1,), (0,))):
    rows = values.shape[0]
    both = product(jnp.concatenate(halves(values), axis=0), chosen, dims)
    return both[:rows] + both[rows:]


def iota(shape, axis):
    return lax.broadcasted_iota(jnp.int32, shape, axis)


def wide_rows(matrix, start, count):
    cols = matrix.shape[1]
    shape = (cols, count * SUB)
    place = (iota(shape, 1) // SUB + start) % cols
    pick = (place == iota(shape, 0)).astype(BF16)
    high, low = halves(matrix)
    return product(high, pick) + product(low, pick)


def spread(wide):
    rows, cols = wide.shape
    tall = jnp.broadcast_to(wide[:, None, :], (rows, SUB, cols)).reshape(rows * SUB, cols)
    return jnp.where(iota(tall.shape, 0) % SUB == iota(tall.shape, 1) % SUB, tall, 0.0)


def mix(weights, values):
    high, low = halves(values)
    rows = weights[0].shape[0]
    both = product(jnp.concatenate(weights, axis=0), high)
    return both[:rows] + (product(weights[0], low) + both[rows:])


def one_hot(index, size):
    rows = lax.broadcasted_iota(jnp.int32, (size, index.shape[1]), 0)
    return jnp.where(rows == index, 1.0, 0.0).astype(BF16)


def column_as_row(column, lane, offset):
    n = column.shape[0]
    place = lax.broadcasted_iota(jnp.int32, (n, 128), 1) == lax.broadcasted_iota(jnp.int32, (n, 128), 0) + offset
    return jnp.sum(jnp.where(place, column, 0.0), axis=0, keepdims=True)


def row_as_column(row, n, offset):
    place = lax.broadcasted_iota(jnp.int32, (n, 128), 1) == lax.broadcasted_iota(jnp.int32, (n, 128), 0) + offset
    return jnp.sum(jnp.where(place, row, 0.0), axis=1, keepdims=True)


def edge_rows(values):
    n = values.shape[0]
    row = column_as_row(values[:, -1:], None, 0) + column_as_row(values[:, :1], None, n)
    return jnp.broadcast_to(row, (EXTRA, 128))


def factor_of(counts_ref, weight_ref, d):
    slot = lax.broadcasted_iota(jnp.int32, (1, weight_ref.shape[2]), 1)
    return jnp.where(slot < counts_ref[0, d], weight_ref[0, pl.ds(d, 1), :], 0.0)


def loop(n, step, init):
    return lax.fori_loop(0, n, step, init, unroll=n if n <= 8 else 1)


def mix_kernel(lev_ref, loc_ref, mix_ref, own_ref, given_ref):
    levels = loc_ref.shape[0]
    start = lev_ref[0] * levels
    loc = loc_ref[...]
    mix_ref[0], mix_ref[1] = halves(spread(wide_rows(loc, start, 2 * levels)))
    own_ref[0], own_ref[1] = halves(spread(wide_rows(loc, start, levels)).T)
    given_ref[...] = wide_rows(loc, levels - start, levels)


def sum_kernel(perturb_ref, control_ref, other_ref, mix_ref, out_ref):
    levels, members, cols = perturb_ref.shape
    perturb = perturb_ref[...].astype(F32)
    total = jnp.zeros((levels, SUB, cols), F32)
    for m in range(0, members, SUB):
        tile = jnp.concatenate([control_ref[:, m : m + SUB, :], other_ref[:, m : m + SUB, :]], axis=0)
        mixed = mix((mix_ref[0], mix_ref[1]), tile.reshape(2 * levels * SUB, cols))
        total = total + perturb[:, m : m + SUB, :] * mixed.reshape(levels, SUB, cols)
    out_ref[...] = jnp.sum(total, axis=1)


def band_kernel(counts_ref, sum_ref, static_ref, src_ref, weight_ref, out_ref, acc_ref):
    levels, cols = sum_ref.shape
    acc_ref[...] = jnp.concatenate(halves(sum_ref[...]), axis=0)
    n = src_ref.shape[1]
    edges = edge_rows(static_ref[...])

    def step(d, carry):
        chosen = one_hot(src_ref[0, pl.ds(d, 1), :], cols)
        both = product(acc_ref[...], chosen)
        payload = (both[:levels] + both[levels:]) * factor_of(counts_ref, weight_ref, d)
        for g in range(out_ref.shape[0]):
            out_ref[g, d, :levels, :] = payload
            out_ref[g, d, levels:, :] = edges
        return carry

    loop(n, step, 0)


def tile_kernel(pos_ref, arrived_ref, tgt_ref, static_ref, diag_ref, off_ref, obs_ref, innov_ref,
                increment_ref, partial_ref, out_ref):
    levels, cols = static_ref.shape
    groups, n = arrived_ref.shape[:2]
    me = pos_ref[0]

    def step(s, total):
        values = sum(arrived_ref[g, s, :levels, :] for g in range(groups))
        chosen = one_hot(tgt_ref[0, pl.ds(s, 1), :], cols)
        return total + select(values, chosen, ((1,), (1,)))

    remapped = loop(n, step, jnp.zeros((levels, cols), F32))
    before = arrived_ref[0, jnp.maximum(me - 1, 0), levels : levels + 1, :]
    after = arrived_ref[0, jnp.minimum(me + 1, n - 1), levels : levels + 1, :]
    before = jnp.where(me > 0, row_as_column(before, levels, 0), 0.0)
    after = jnp.where(me < n - 1, row_as_column(after, levels, levels), 0.0)
    static = static_ref[...]
    lane = lax.broadcasted_iota(jnp.int32, (levels, cols), 1)
    left = jnp.where(lane == 0, before, pltpu.roll(static, 1, 1))
    right = jnp.where(lane == cols - 1, after, pltpu.roll(static, cols - 1, 1))
    increment = remapped + diag_ref[...] * static + off_ref[...] * (left + right)
    increment_ref[...] = increment
    misfit = obs_ref[...] * (increment - innov_ref[...])
    coupled = off_ref[...] * misfit
    left = jnp.where(lane == 0, 0.0, pltpu.roll(coupled, 1, 1))
    right = jnp.where(lane == cols - 1, 0.0, pltpu.roll(coupled, cols - 1, 1))
    partial_ref[...] = static + diag_ref[...] * misfit + left + right
    edges = edge_rows(coupled)
    both = jnp.concatenate(halves(misfit), axis=0)

    def give(s, carry):
        chosen = one_hot(tgt_ref[0, pl.ds(s, 1), :], cols)
        picked = product(both, chosen)
        out_ref[s, :levels, :] = picked[:levels] + picked[levels:]
        out_ref[s, levels:, :] = edges
        return carry

    loop(n, give, 0)


def adjoint_kernel(band, pos_ref, counts_ref, returned_ref, src_ref, weight_ref, partial_ref, mix_ref, grad_ref, out_ref):
    levels, cols = partial_ref.shape
    n = returned_ref.shape[0]
    me = pos_ref[0]

    def step(d, total):
        values = returned_ref[d, :levels, :] * factor_of(counts_ref, weight_ref, d)
        return total + select(values, one_hot(src_ref[0, pl.ds(d, 1), :], band), ((1,), (1,)))

    out_ref[...] = band_rows(loop(n, step, jnp.zeros((levels, band), F32)), mix_ref[...])
    before = returned_ref[jnp.maximum(me - 1, 0), levels : levels + 1, :]
    after = returned_ref[jnp.minimum(me + 1, n - 1), levels : levels + 1, :]
    before = jnp.where(me > 0, row_as_column(before, levels, 0), 0.0)
    after = jnp.where(me < n - 1, row_as_column(after, levels, levels), 0.0)
    lane = lax.broadcasted_iota(jnp.int32, (levels, cols), 1)
    grad_ref[...] = partial_ref[...] + (jnp.where(lane == 0, before, 0.0) + jnp.where(lane == cols - 1, after, 0.0))


def band_rows(band, weights):
    width = weights.shape[1]
    return jnp.concatenate([band[:, at : at + width] for at in range(0, band.shape[1], width)] + [weights], axis=0)


def ens_tiles(perturb_ref, rows_ref, weights, before_ref):
    levels, members, cols = perturb_ref.shape
    width = rows_ref.shape[1]
    parts = [rows_ref[i * levels : (i + 1) * levels, :] for i in range(cols // width)]
    grad = jnp.concatenate(parts, axis=1)[:, None, :]
    perturb = perturb_ref[...].astype(F32)
    for m in range(0, members, SUB):
        place = (slice(None), slice(m, m + SUB), slice(None))
        tile = (perturb[place] * grad).reshape(levels * SUB, cols)
        yield place, before_ref[place] + mix(weights, tile).reshape(levels, SUB, cols)


def ens_own_kernel(perturb_ref, mine_ref, weights_ref, control_ref, out_ref):
    for place, values in ens_tiles(perturb_ref, mine_ref, (weights_ref[0], weights_ref[1]), control_ref):
        out_ref[place] = values


def ens_kernel(perturb_ref, theirs_ref, own_ref, *refs):
    count = (len(refs) - 3) // 2
    flats, (out_hbm, *flat_hbms), (out_ref, sems) = refs[:count], refs[count : 2 * count + 1], refs[2 * count + 1 :]
    copies = [pltpu.make_async_copy(a, b, sems.at[i]) for i, (a, b) in enumerate(zip(flats, flat_hbms))]
    for copy in copies:
        copy.start()
    levels = perturb_ref.shape[0]
    weights = halves(spread(theirs_ref[theirs_ref.shape[0] - levels :, :]).T)
    for place, values in ens_tiles(perturb_ref, theirs_ref, weights, own_ref):
        out_ref[place] = values
        copies.append(pltpu.make_async_copy(out_ref.at[place], out_hbm.at[place], sems.at[len(copies)]))
        copies[-1].start()
    for copy in copies:
        copy.wait()


class Rows:
    def __init__(self, levels, n):
        self.weight = slice(0, levels)
        self.base = slice(levels, 2 * levels)
        at = 2 * levels
        self.factor, self.index, self.edge = at, at + n, at + 2 * n
        self.total = at + 2 * n + EXTRA


def static_kernel(band, pos_ref, counts_ref, static_ref, diag_ref, off_ref, obs_ref, innov_ref, src_ref, weight_ref, tgt_ref,
                  *out_refs):
    levels, cols = static_ref.shape
    n = len(out_refs)
    cap = src_ref.shape[2]
    rows = Rows(levels, n)
    peers = [pos_ref[0] ^ r for r in range(n)]
    static, off, obs = static_ref[...], off_ref[...], obs_ref[...]
    lane = lax.broadcasted_iota(jnp.int32, (levels, cols), 1)
    left = jnp.where(lane == 0, 0.0, pltpu.roll(static, 1, 1))
    right = jnp.where(lane == cols - 1, 0.0, pltpu.roll(static, cols - 1, 1))
    base = diag_ref[...] * static + off * (left + right) - innov_ref[...]
    coupled = off * obs
    ends = [v[:, i] for v in (static, coupled, base) for i in (slice(cols - 1, cols), slice(0, 1))]
    edge = sum(column_as_row(end, None, i * levels) for i, end in enumerate(ends))
    place = lax.broadcasted_iota(jnp.int32, (1, cap), 1)
    edge = edge + jnp.where(place == 6 * levels, off[:, cols - 1 :], 0.0)
    edge = edge + jnp.where(place == 6 * levels + 1, off[:, :1], 0.0)
    edge = jnp.broadcast_to(edge, (EXTRA, cap))
    both = jnp.concatenate(halves(jnp.concatenate([obs, base], axis=0)), axis=0)
    tgts = [tgt_ref[0, pl.ds(peer, 1), :] for peer in peers]
    src = jnp.concatenate([src_ref[0, pl.ds(peer, 1), :] for peer in peers], axis=0).astype(F32)
    index = jnp.concatenate(tgts, axis=0).astype(F32) * float(band) + src
    factor = jnp.concatenate([factor_of(counts_ref, weight_ref, peer) for peer in peers], axis=0)
    for r, out_ref in enumerate(out_refs):
        picked = product(both, one_hot(tgts[r], cols))
        out_ref[: 2 * levels, :] = picked[: 2 * levels] + picked[2 * levels :]
        out_ref[rows.factor : rows.factor + n, :] = factor
        out_ref[rows.index : rows.index + n, :] = index
        out_ref[rows.edge :, :] = edge


def blocks_kernel(groups, levels, relayed, *refs):
    sums, refs = refs[:groups], refs[groups:]
    count = (len(refs) - 1 - relayed) // 2
    rests, relays, total_ref, out_refs = refs[:count], refs[count : count + relayed], refs[count + relayed], refs[-count:]
    total = sum(ref[...] for ref in sums)
    cap = total_ref.shape[1]
    total = jnp.concatenate([total[:, at : at + cap] for at in range(0, total.shape[1], cap)], axis=0)
    total_ref[...] = total
    for i, (rest_ref, out_ref) in enumerate(zip(rests, out_refs)):
        parts = [total, rest_ref[...]]
        if i == count - 1:
            parts += [ref[: 2 * levels, :] for ref in relays]
        out_ref[...] = jnp.concatenate(parts, axis=0)


def relay_kernel(levels, stacked, got_ref, *refs):
    count = len(refs) // 2
    head = refs[0].shape[0]
    for i, (block_ref, out_ref) in enumerate(zip(refs[:count], refs[count:])):
        at = head + 2 * levels * i
        out_ref[...] = jnp.concatenate(
            [block_ref[...], got_ref[:stacked, :], got_ref[at : at + 2 * levels, :], got_ref[stacked + 2 * levels : head, :]],
            axis=0,
        )


class Block:
    def __init__(self, refs, n, levels, band, base=0):
        cap = refs[0].shape[1]
        self.levels, self.parts, self.cap = levels, band // cap, cap
        self.sums_ref, self.rest_ref = refs[0], refs[-1]
        self.base = base
        self.head = 0 if len(refs) == 2 else base + self.parts * levels
        self.rows = Rows(levels, n)
        words = self.rest(self.rows.index, n)
        self.tgt = jnp.floor((words + 0.5) * (1.0 / band))
        self.src = words - self.tgt * float(band)
        self.factor = self.rest(self.rows.factor, n)

    def rest(self, at, size):
        return self.rest_ref[self.head + at : self.head + at + size, :]

    def sums(self):
        parts = [self.sums_ref[self.base + i * self.levels : self.base + (i + 1) * self.levels, :] for i in range(self.parts)]
        return jnp.concatenate(halves(jnp.concatenate(parts, axis=1)), axis=0)


def line(table, i):
    return table[i : i + 1]


def pick_source(block, r):
    band = block.parts * block.cap
    column = lax.broadcasted_iota(jnp.int32, (band, block.cap), 0).astype(F32)
    return jnp.where(column == line(block.src, r), 1.0, 0.0).astype(BF16)


def fill_slots(bands, blocks, n, slots_ref):
    for i, s in enumerate(bands):
        block = blocks[s]
        both = block.sums()
        for d in range(n):
            picked = product(both, pick_source(block, s ^ d))
            values = (picked[: block.levels] + picked[block.levels :]) * line(block.factor, s ^ d)
            slots_ref[d, :, i * block.cap : (i + 1) * block.cap] = jnp.concatenate(halves(values), axis=0)


def met_at(d, block, bands, slots_ref):
    own = jnp.broadcast_to(line(block.tgt, d), (block.cap, block.cap)).T
    same = [jnp.where(own == line(block.tgt, s ^ d), 1.0, 0.0).astype(BF16) for s in bands]
    met = product(slots_ref[d], jnp.concatenate(same, axis=1), ((1,), (1,)))
    return met[: block.levels] + met[block.levels :]


def land(table, bands, slots_ref, cols):
    cap = table.shape[1]
    row = lax.broadcasted_iota(jnp.int32, (cols, cap), 0).astype(F32)
    total = 0.0
    for i, s in enumerate(bands):
        landing = jnp.where(row == line(table, s), 1.0, 0.0).astype(BF16)
        total = total + product(slots_ref[0, :, i * cap : (i + 1) * cap], landing, ((1,), (1,)))
    levels = total.shape[0] // 2
    return total[:levels] + total[levels:]


def open_blocks(labels, refs, n, levels, band):
    blocks = {0: Block(refs[:2], n, levels, band)}
    refs = refs[2:]
    for i, r in enumerate(labels[1:]):
        base = refs[i].shape[0] // 2 if r >= n // 2 + n // 4 else 0
        blocks[r] = Block(refs[i : i + 1], n, levels, band, base)
    return blocks, refs[len(labels) - 1 :]


def stage_kernel(n, levels, band, cols, stages, *refs):
    known = sum(stages[:-1], [])
    blocks, refs = open_blocks(known + stages[-1], refs, n, levels, band)
    old, refs = refs[: len(stages) - 1], refs[len(stages) - 1 :]
    if known:
        met_old, remap_old, slots_ref, met_ref, remap_ref = refs
    else:
        slots_ref, met_ref, remap_ref, pick_ref = refs
        for d in range(n):
            pick_ref[d] = pick_source(blocks[0], d)
    fill_slots(stages[-1], blocks, n, slots_ref)
    for i, (d, block) in enumerate(blocks.items()):
        met = met_at(d, block, stages[-1], slots_ref)
        if d in known:
            met = met + met_old[i]
        else:
            for bands, ref in zip(stages, old):
                met = met + met_at(d, block, bands, ref)
        met_ref[i] = met
    landed = land(blocks[0].tgt, stages[-1], slots_ref, cols)
    remap_ref[...] = landed + remap_old[...] if known else landed


def shared_kernel(n, levels, band, cols, stages, pos_ref, mix_ref, *refs):
    known = sum(stages[:-1], [])
    blocks, refs = open_blocks(known + stages[-1], refs, n, levels, band)
    old, refs = refs[: len(stages) - 1], refs[len(stages) - 1 :]
    met_old, pick_ref, out_ref, slots_ref, tables_ref = refs
    me = pos_ref[0]
    for r, block in blocks.items():
        there = me ^ r
        tables_ref[there, :n, :] = block.tgt
        tables_ref[there, n:, :] = block.rest(block.rows.edge, EXTRA)
    fill_slots(stages[-1], blocks, n, slots_ref)
    last = cols - 1.0
    total = jnp.zeros((levels, band), F32)
    for i, (d, block) in enumerate(blocks.items()):
        value = met_at(d, block, stages[-1], slots_ref) + block.rest(levels, levels)
        if d in known:
            value = value + met_old[i]
        else:
            for bands, ref in zip(stages, old):
                value = value + met_at(d, block, bands, ref)
        edge = block.rest(block.rows.edge, 1)
        own = line(block.tgt, d)
        there = me ^ d
        before = tables_ref[jnp.maximum(there - 1, 0), n : n + 1, :]
        near = jnp.where((own == 0.0) & (there > 0), edge[:, 6 * levels + 1 : 6 * levels + 2], 0.0)
        value = value + row_as_column(before, levels, 0) * near
        after = tables_ref[jnp.minimum(there + 1, n - 1), n : n + 1, :]
        near = jnp.where((own == last) & (there < n - 1), edge[:, 6 * levels : 6 * levels + 1], 0.0)
        value = value + row_as_column(after, levels, levels) * near
        given = block.rest(0, levels) * value * line(blocks[0].factor, d)
        total = total + select(given, pick_ref[d], ((1,), (1,)))
    out_ref[...] = band_rows(total, mix_ref[...])


def outputs_kernel(stages, pos_ref, *refs):
    slots_refs, refs = refs[: len(stages)], refs[len(stages) :]
    remap_ref, tables_ref, static_ref, diag_ref, off_ref, obs_ref, innov_ref, increment_ref, grad_ref = refs
    levels, cols = static_ref.shape
    n = tables_ref.shape[0]
    cap = tables_ref.shape[2]
    me = pos_ref[0]
    given = [
        (s, ref, slice(i * cap, (i + 1) * cap)) for bands, ref in zip(stages, slots_refs) for i, s in enumerate(bands)
    ]
    remapped = remap_ref[...] + land(tables_ref[me, :n, :], stages[-1], slots_refs[-1], cols)
    static, off = static_ref[...], off_ref[...]
    lane = lax.broadcasted_iota(jnp.int32, (levels, cols), 1)

    def beside(there, exists, column, own_end, side):
        edge = tables_ref[there, n : n + 1, :]
        static_end, coupling, base = (row_as_column(edge, levels, (2 * i + side) * levels) for i in range(3))
        far = me ^ there
        landed = []
        for s, ref, place in given:
            values = ref[far, :levels, place].astype(F32) + ref[far, levels:, place].astype(F32)
            landed.append(jnp.where(tables_ref[there, pl.ds(s ^ far, 1), :] == column, values, 0.0))
        remap_end = jnp.sum(sum(landed), axis=1, keepdims=True)
        off_end = edge[:, 6 * levels + side : 6 * levels + side + 1]
        coupled = coupling * (remap_end + base + off_end * own_end)
        return jnp.where(exists, static_end, 0.0), jnp.where(exists, coupled, 0.0)

    before, coupled_before = beside(jnp.maximum(me - 1, 0), me > 0, cols - 1.0, static[:, :1], 0)
    after, coupled_after = beside(jnp.minimum(me + 1, n - 1), me < n - 1, 0.0, static[:, cols - 1 :], 1)
    left = jnp.where(lane == 0, before, pltpu.roll(static, 1, 1))
    right = jnp.where(lane == cols - 1, after, pltpu.roll(static, cols - 1, 1))
    increment = remapped + diag_ref[...] * static + off * (left + right)
    increment_ref[...] = increment
    misfit = obs_ref[...] * (increment - innov_ref[...])
    coupled = off * misfit
    left = jnp.where(lane == 0, coupled_before, pltpu.roll(coupled, 1, 1))
    right = jnp.where(lane == cols - 1, coupled_after, pltpu.roll(coupled, cols - 1, 1))
    grad_ref[...] = static + diag_ref[...] * misfit + left + right


def call(kernel, out_shape, spaces, scratch=(), out=VMEM, cost=None):
    return pl.pallas_call(
        kernel,
        out_shape=out_shape,
        in_specs=spaces,
        out_specs=jax.tree.map(lambda _: out, out_shape),
        scratch_shapes=scratch,
        cost_estimate=cost,
        compiler_params=pltpu.CompilerParams(vmem_limit_bytes=40 * MIB),
    )


def body(
    perturb,
    control,
    level_loc,
    static_control,
    filter_diag,
    filter_off,
    send_src,
    send_wt,
    counts,
    recv_tgt,
    obs_weight,
    innovation,
):
    levels, members, band_cols = control.shape
    tile_cols = static_control.shape[1]
    n = lax.axis_size("tile")
    groups = lax.axis_size("grp")
    cap = send_src.shape[2]
    shape = jax.ShapeDtypeStruct
    swap = [(0, 1), (1, 0)]
    lev = lax.axis_index("lev").astype(jnp.int32).reshape(1)
    pos = lax.axis_index("tile").astype(jnp.int32).reshape(1)
    other_control = lax.ppermute(control, "lev", swap)
    width = levels * SUB
    level_mix, own_mix, given_mix = call(
        mix_kernel,
        (shape((2, width, 2 * width), BF16), shape((2, width, width), BF16), shape((levels, width), F32)),
        [SMEM, VMEM],
        cost=pl.CostEstimate(flops=10**9, bytes_accessed=0, transcendentals=0),
    )(lev, level_loc)
    own_sum = call(sum_kernel, shape((levels, band_cols), F32), [VMEM] * 4)(perturb, control, other_control, level_mix)
    flat = shape((levels, tile_cols), F32)
    mine_shape = shape((band_cols // width * levels + levels, width), F32)
    diag, off = filter_diag.reshape(1, -1), filter_off.reshape(1, -1)
    if n * cap <= tile_cols and n >= 8 and lax.axis_size("lev") == 2 and n & (n - 1) == 0 and band_cols * tile_cols <= 2**20:
        rows = Rows(levels, n)
        stacked = band_cols // cap * levels
        rests = call(functools.partial(static_kernel, band_cols), [shape((rows.total, cap), F32)] * n, [SMEM] * 2 + [VMEM] * 8)(
            pos, counts, static_control, diag, off, obs_weight, innovation, send_src, send_wt, recv_tgt
        )
        sums = [own_sum]
        sums[0], other_perturb = lax.optimization_barrier((sums[0], lax.ppermute(perturb, "lev", swap)))
        for k in range(1, groups):
            sums.append(lax.ppermute(sums[0], "grp", [(g, (g + k) % groups) for g in range(groups)]))
        low, high = n // 4, n // 2
        order = [high, *range(1, low), *range(high + 1, high + low), *reversed(range(low, high))]
        stages = [[0] + order[: -low], *([r, r + high] for r in order[-low:])]
        direct = order[::-1]
        total, *blocks = call(
            functools.partial(blocks_kernel, groups, levels, low),
            [shape((stacked, cap), F32)]
            + [shape((stacked + rows.total + (r == high) * 2 * levels * low, cap), F32) for r in direct],
            [VMEM] * (groups + len(direct) + low),
        )(*sums, *[rests[r] for r in direct], *rests[high + low :])
        blocks = dict(zip(direct, blocks))

        def to(r):
            return lax.ppermute(blocks[r], "tile", [(i, i ^ r) for i in range(n)])

        arrived = {0: [total, rests[0]]} | {r: [to(r)] for r in order[:-low]}
        carriers = list(range(low, high))
        joined = call(
            functools.partial(relay_kernel, levels, stacked),
            [shape((2 * (stacked + rows.total), cap), F32)] * low,
            [VMEM] * (1 + low),
        )(arrived[high][0], *[blocks[r] for r in carriers])
        blocks |= dict(zip(carriers, joined))
        for r in order[-low:]:
            arrived[r] = arrived[r + high] = [to(r)]
        slots, carried, picks = [], [], []
        for count in range(1, len(stages)):
            labels = sum(stages[:count], [])
            refs = [ref for r in labels for ref in arrived[r]]
            outs = [
                shape((n, 2 * levels, len(stages[count - 1]) * cap), BF16),
                shape((len(labels), levels, cap), F32),
                flat,
            ] + [shape((n, band_cols, cap), BF16)] * (count == 1)
            new, *carried = call(
                functools.partial(stage_kernel, n, levels, band_cols, tile_cols, stages[:count]),
                outs,
                [VMEM] * (len(refs) + len(slots) + len(carried)),
                cost=pl.CostEstimate(flops=10**9, bytes_accessed=0, transcendentals=0),
            )(*refs, *slots, *carried)
            slots.append(new)
            picks += carried[2:]
            carried = carried[:2]
        met, remap = carried
        refs = [ref for r in sum(stages, []) for ref in arrived[r]] + slots + [met] + picks
        mine, new, tables = call(
            functools.partial(shared_kernel, n, levels, band_cols, tile_cols, stages),
            (mine_shape, shape((n, 2 * levels, len(stages[-1]) * cap), BF16), shape((n, n + EXTRA, cap), F32)),
            [SMEM] + [VMEM] * (1 + len(refs)),
            cost=pl.CostEstimate(flops=10**9, bytes_accessed=0, transcendentals=0),
        )(pos, given_mix, *refs)
        slots.append(new)
        increment, grad_static = call(
            functools.partial(outputs_kernel, stages), (flat, flat), [SMEM] + [VMEM] * (len(slots) + 7)
        )(pos, *slots, remap, tables, static_control, diag, off, obs_weight, innovation)
    else:
        other_perturb = lax.ppermute(perturb, "lev", swap)
        payload = call(
            band_kernel,
            shape((groups, n, levels + EXTRA, cap), F32),
            [SMEM] + [VMEM] * 4,
            [pltpu.VMEM((2 * levels, band_cols), BF16)],
        )(counts, own_sum, static_control, send_src, send_wt)
        arrived = lax.all_to_all(
            payload.reshape(groups * n, levels + EXTRA, cap), ("grp", "tile"), split_axis=0, concat_axis=0, tiled=True
        ).reshape(groups, n, levels + EXTRA, cap)
        increment, partial, giving = call(
            tile_kernel, (flat, flat, shape((n, levels + EXTRA, cap), F32)), [SMEM] + [VMEM] * 7
        )(pos, arrived, recv_tgt, static_control, diag, off, obs_weight, innovation)
        returned = lax.all_to_all(giving, "tile", split_axis=0, concat_axis=0, tiled=True)
        grad_static, mine = call(
            functools.partial(adjoint_kernel, band_cols), (flat, mine_shape), [SMEM, SMEM] + [VMEM] * 5
        )(pos, counts, returned, send_src, send_wt, partial, given_mix)
    theirs = lax.ppermute(mine, "lev", swap)
    own = call(ens_own_kernel, shape(control.shape, F32), [VMEM] * 4)(perturb, mine, own_mix, control)
    grad_ens, increment, grad_static = call(
        ens_kernel,
        (shape(control.shape, F32), flat, flat),
        [VMEM] * 5,
        [pltpu.VMEM(control.shape, F32), pltpu.SemaphoreType.DMA((2 + members // SUB,))],
        out=HBM,
    )(other_perturb, theirs, own, increment, grad_static)
    return (increment, grad_static, grad_ens)


def solution(mesh):
    return jax.shard_map(
        body,
        mesh=mesh,
        in_specs=(
            P("lev", "grp", "tile"),
            P("lev", "grp", "tile"),
            P("lev", None),
            P("lev", "tile"),
            P("tile"),
            P("tile"),
            P("tile", None, None),
            P("tile", None, None),
            P("tile", None),
            P("tile", None, None),
            P("lev", "tile"),
            P("lev", "tile"),
        ),
        out_specs=(P("lev", "tile"), P("lev", "tile"), P("lev", "grp", "tile")),
        check_vma=False,
    )
```

```python
import functools

import jax
import jax.numpy as jnp
from jax import lax
from jax.experimental import pallas as pl
from jax.experimental.pallas import tpu as pltpu
from jax.sharding import PartitionSpec as P

F32 = jnp.float32
BF16 = jnp.bfloat16
SUB = 8
EXTRA = 8
VMEM = pl.BlockSpec(memory_space=pltpu.VMEM)
HBM = pl.BlockSpec(memory_space=pltpu.HBM)
SMEM = pl.BlockSpec(memory_space=pltpu.SMEM)
MIB = 1024 * 1024


def halves(values):
    high = values.astype(BF16)
    low = (values - high.astype(F32)).astype(BF16)
    return high, low


def product(a, b, dims=((1,), (0,))):
    return lax.dot_general(a, b, (dims, ((), ())), preferred_element_type=F32)


def select(values, chosen, dims=((1,), (0,))):
    rows = values.shape[0]
    both = product(jnp.concatenate(halves(values), axis=0), chosen, dims)
    return both[:rows] + both[rows:]


def iota(shape, axis):
    return lax.broadcasted_iota(jnp.int32, shape, axis)


def wide_rows(matrix, start, count):
    cols = matrix.shape[1]
    shape = (cols, count * SUB)
    place = (iota(shape, 1) // SUB + start) % cols
    pick = (place == iota(shape, 0)).astype(BF16)
    high, low = halves(matrix)
    return product(high, pick) + product(low, pick)


def spread(wide):
    rows, cols = wide.shape
    tall = jnp.broadcast_to(wide[:, None, :], (rows, SUB, cols)).reshape(rows * SUB, cols)
    return jnp.where(iota(tall.shape, 0) % SUB == iota(tall.shape, 1) % SUB, tall, 0.0)


def mix(weights, values):
    high, low = halves(values)
    rows = weights[0].shape[0]
    both = product(jnp.concatenate(weights, axis=0), high)
    return both[:rows] + (product(weights[0], low) + both[rows:])


def one_hot(index, size):
    rows = lax.broadcasted_iota(jnp.int32, (size, index.shape[1]), 0)
    return jnp.where(rows == index, 1.0, 0.0).astype(BF16)


def column_as_row(column, lane, offset):
    n = column.shape[0]
    place = lax.broadcasted_iota(jnp.int32, (n, 128), 1) == lax.broadcasted_iota(jnp.int32, (n, 128), 0) + offset
    return jnp.sum(jnp.where(place, column, 0.0), axis=0, keepdims=True)


def row_as_column(row, n, offset):
    place = lax.broadcasted_iota(jnp.int32, (n, 128), 1) == lax.broadcasted_iota(jnp.int32, (n, 128), 0) + offset
    return jnp.sum(jnp.where(place, row, 0.0), axis=1, keepdims=True)


def edge_rows(values):
    n = values.shape[0]
    row = column_as_row(values[:, -1:], None, 0) + column_as_row(values[:, :1], None, n)
    return jnp.broadcast_to(row, (EXTRA, 128))


def factor_of(counts_ref, weight_ref, d):
    slot = lax.broadcasted_iota(jnp.int32, (1, weight_ref.shape[2]), 1)
    return jnp.where(slot < counts_ref[0, d], weight_ref[0, pl.ds(d, 1), :], 0.0)


def loop(n, step, init):
    return lax.fori_loop(0, n, step, init, unroll=n if n <= 8 else 1)


def mix_kernel(lev_ref, loc_ref, mix_ref, own_ref, given_ref):
    levels = loc_ref.shape[0]
    start = lev_ref[0] * levels
    loc = loc_ref[...]
    mix_ref[0], mix_ref[1] = halves(spread(wide_rows(loc, start, 2 * levels)))
    own_ref[0], own_ref[1] = halves(spread(wide_rows(loc, start, levels)).T)
    given_ref[...] = wide_rows(loc, levels - start, levels)


def sum_kernel(perturb_ref, control_ref, other_ref, mix_ref, out_ref):
    levels, members, cols = perturb_ref.shape
    perturb = perturb_ref[...].astype(F32)
    total = jnp.zeros((levels, SUB, cols), F32)
    for m in range(0, members, SUB):
        tile = jnp.concatenate([control_ref[:, m : m + SUB, :], other_ref[:, m : m + SUB, :]], axis=0)
        mixed = mix((mix_ref[0], mix_ref[1]), tile.reshape(2 * levels * SUB, cols))
        total = total + perturb[:, m : m + SUB, :] * mixed.reshape(levels, SUB, cols)
    out_ref[...] = jnp.sum(total, axis=1)


def band_kernel(counts_ref, sum_ref, static_ref, src_ref, weight_ref, out_ref, acc_ref):
    levels, cols = sum_ref.shape
    acc_ref[...] = jnp.concatenate(halves(sum_ref[...]), axis=0)
    n = src_ref.shape[1]
    edges = edge_rows(static_ref[...])

    def step(d, carry):
        chosen = one_hot(src_ref[0, pl.ds(d, 1), :], cols)
        both = product(acc_ref[...], chosen)
        payload = (both[:levels] + both[levels:]) * factor_of(counts_ref, weight_ref, d)
        for g in range(out_ref.shape[0]):
            out_ref[g, d, :levels, :] = payload
            out_ref[g, d, levels:, :] = edges
        return carry

    loop(n, step, 0)


def tile_kernel(pos_ref, arrived_ref, tgt_ref, static_ref, diag_ref, off_ref, obs_ref, innov_ref,
                increment_ref, partial_ref, out_ref):
    levels, cols = static_ref.shape
    groups, n = arrived_ref.shape[:2]
    me = pos_ref[0]

    def step(s, total):
        values = sum(arrived_ref[g, s, :levels, :] for g in range(groups))
        chosen = one_hot(tgt_ref[0, pl.ds(s, 1), :], cols)
        return total + select(values, chosen, ((1,), (1,)))

    remapped = loop(n, step, jnp.zeros((levels, cols), F32))
    before = arrived_ref[0, jnp.maximum(me - 1, 0), levels : levels + 1, :]
    after = arrived_ref[0, jnp.minimum(me + 1, n - 1), levels : levels + 1, :]
    before = jnp.where(me > 0, row_as_column(before, levels, 0), 0.0)
    after = jnp.where(me < n - 1, row_as_column(after, levels, levels), 0.0)
    static = static_ref[...]
    lane = lax.broadcasted_iota(jnp.int32, (levels, cols), 1)
    left = jnp.where(lane == 0, before, pltpu.roll(static, 1, 1))
    right = jnp.where(lane == cols - 1, after, pltpu.roll(static, cols - 1, 1))
    increment = remapped + diag_ref[...] * static + off_ref[...] * (left + right)
    increment_ref[...] = increment
    misfit = obs_ref[...] * (increment - innov_ref[...])
    coupled = off_ref[...] * misfit
    left = jnp.where(lane == 0, 0.0, pltpu.roll(coupled, 1, 1))
    right = jnp.where(lane == cols - 1, 0.0, pltpu.roll(coupled, cols - 1, 1))
    partial_ref[...] = static + diag_ref[...] * misfit + left + right
    edges = edge_rows(coupled)
    both = jnp.concatenate(halves(misfit), axis=0)

    def give(s, carry):
        chosen = one_hot(tgt_ref[0, pl.ds(s, 1), :], cols)
        picked = product(both, chosen)
        out_ref[s, :levels, :] = picked[:levels] + picked[levels:]
        out_ref[s, levels:, :] = edges
        return carry

    loop(n, give, 0)


def adjoint_kernel(band, pos_ref, counts_ref, returned_ref, src_ref, weight_ref, partial_ref, mix_ref, grad_ref, out_ref):
    levels, cols = partial_ref.shape
    n = returned_ref.shape[0]
    me = pos_ref[0]

    def step(d, total):
        values = returned_ref[d, :levels, :] * factor_of(counts_ref, weight_ref, d)
        return total + select(values, one_hot(src_ref[0, pl.ds(d, 1), :], band), ((1,), (1,)))

    out_ref[...] = band_rows(loop(n, step, jnp.zeros((levels, band), F32)), mix_ref[...])
    before = returned_ref[jnp.maximum(me - 1, 0), levels : levels + 1, :]
    after = returned_ref[jnp.minimum(me + 1, n - 1), levels : levels + 1, :]
    before = jnp.where(me > 0, row_as_column(before, levels, 0), 0.0)
    after = jnp.where(me < n - 1, row_as_column(after, levels, levels), 0.0)
    lane = lax.broadcasted_iota(jnp.int32, (levels, cols), 1)
    grad_ref[...] = partial_ref[...] + (jnp.where(lane == 0, before, 0.0) + jnp.where(lane == cols - 1, after, 0.0))


def band_rows(band, weights):
    width = weights.shape[1]
    return jnp.concatenate([band[:, at : at + width] for at in range(0, band.shape[1], width)] + [weights], axis=0)


def ens_tiles(perturb_ref, rows_ref, weights, before_ref):
    levels, members, cols = perturb_ref.shape
    width = rows_ref.shape[1]
    parts = [rows_ref[i * levels : (i + 1) * levels, :] for i in range(cols // width)]
    grad = jnp.concatenate(parts, axis=1)[:, None, :]
    perturb = perturb_ref[...].astype(F32)
    for m in range(0, members, SUB):
        place = (slice(None), slice(m, m + SUB), slice(None))
        tile = (perturb[place] * grad).reshape(levels * SUB, cols)
        yield place, before_ref[place] + mix(weights, tile).reshape(levels, SUB, cols)


def ens_own_kernel(perturb_ref, mine_ref, weights_ref, control_ref, out_ref):
    for place, values in ens_tiles(perturb_ref, mine_ref, (weights_ref[0], weights_ref[1]), control_ref):
        out_ref[place] = values


def ens_kernel(perturb_ref, theirs_ref, own_ref, *refs):
    count = (len(refs) - 3) // 2
    flats, (out_hbm, *flat_hbms), (out_ref, sems) = refs[:count], refs[count : 2 * count + 1], refs[2 * count + 1 :]
    copies = [pltpu.make_async_copy(a, b, sems.at[i]) for i, (a, b) in enumerate(zip(flats, flat_hbms))]
    for copy in copies:
        copy.start()
    levels = perturb_ref.shape[0]
    weights = halves(spread(theirs_ref[theirs_ref.shape[0] - levels :, :]).T)
    for place, values in ens_tiles(perturb_ref, theirs_ref, weights, own_ref):
        out_ref[place] = values
        copies.append(pltpu.make_async_copy(out_ref.at[place], out_hbm.at[place], sems.at[len(copies)]))
        copies[-1].start()
    for copy in copies:
        copy.wait()


class Rows:
    def __init__(self, levels, n):
        self.weight = slice(0, levels)
        self.base = slice(levels, 2 * levels)
        at = 2 * levels
        self.factor, self.index, self.edge = at, at + n, at + 2 * n
        self.total = at + 2 * n + EXTRA


def static_kernel(band, pos_ref, counts_ref, static_ref, diag_ref, off_ref, obs_ref, innov_ref, src_ref, weight_ref, tgt_ref,
                  *out_refs):
    levels, cols = static_ref.shape
    n = len(out_refs)
    cap = src_ref.shape[2]
    rows = Rows(levels, n)
    peers = [pos_ref[0] ^ r for r in range(n)]
    static, off, obs = static_ref[...], off_ref[...], obs_ref[...]
    lane = lax.broadcasted_iota(jnp.int32, (levels, cols), 1)
    left = jnp.where(lane == 0, 0.0, pltpu.roll(static, 1, 1))
    right = jnp.where(lane == cols - 1, 0.0, pltpu.roll(static, cols - 1, 1))
    base = diag_ref[...] * static + off * (left + right) - innov_ref[...]
    coupled = off * obs
    ends = [v[:, i] for v in (static, coupled, base) for i in (slice(cols - 1, cols), slice(0, 1))]
    edge = sum(column_as_row(end, None, i * levels) for i, end in enumerate(ends))
    place = lax.broadcasted_iota(jnp.int32, (1, cap), 1)
    edge = edge + jnp.where(place == 6 * levels, off[:, cols - 1 :], 0.0)
    edge = edge + jnp.where(place == 6 * levels + 1, off[:, :1], 0.0)
    edge = jnp.broadcast_to(edge, (EXTRA, cap))
    both = jnp.concatenate(halves(jnp.concatenate([obs, base], axis=0)), axis=0)
    tgts = [tgt_ref[0, pl.ds(peer, 1), :] for peer in peers]
    src = jnp.concatenate([src_ref[0, pl.ds(peer, 1), :] for peer in peers], axis=0).astype(F32)
    index = jnp.concatenate(tgts, axis=0).astype(F32) * float(band) + src
    factor = jnp.concatenate([factor_of(counts_ref, weight_ref, peer) for peer in peers], axis=0)
    for r, out_ref in enumerate(out_refs):
        picked = product(both, one_hot(tgts[r], cols))
        out_ref[: 2 * levels, :] = picked[: 2 * levels] + picked[2 * levels :]
        out_ref[rows.factor : rows.factor + n, :] = factor
        out_ref[rows.index : rows.index + n, :] = index
        out_ref[rows.edge :, :] = edge


def blocks_kernel(groups, levels, relayed, *refs):
    sums, refs = refs[:groups], refs[groups:]
    count = (len(refs) - 1 - relayed) // 2
    rests, relays, total_ref, out_refs = refs[:count], refs[count : count + relayed], refs[count + relayed], refs[-count:]
    total = sum(ref[...] for ref in sums)
    cap = total_ref.shape[1]
    total = jnp.concatenate([total[:, at : at + cap] for at in range(0, total.shape[1], cap)], axis=0)
    total_ref[...] = total
    for i, (rest_ref, out_ref) in enumerate(zip(rests, out_refs)):
        parts = [total, rest_ref[...]]
        if i == count - 1:
            parts += [ref[: 2 * levels, :] for ref in relays]
        out_ref[...] = jnp.concatenate(parts, axis=0)


def relay_kernel(levels, stacked, got_ref, *out_refs):
    head = got_ref.shape[0] - len(out_refs) * 2 * levels
    for i, out_ref in enumerate(out_refs):
        at = head + 2 * levels * i
        out_ref[...] = jnp.concatenate(
            [got_ref[:stacked, :], got_ref[at : at + 2 * levels, :], got_ref[stacked + 2 * levels : head, :]], axis=0
        )


class Block:
    def __init__(self, refs, n, levels, band):
        cap = refs[0].shape[1]
        self.levels, self.parts, self.cap = levels, band // cap, cap
        self.sums_ref, self.rest_ref = refs[0], refs[-1]
        self.head = 0 if len(refs) == 2 else self.parts * levels
        self.rows = Rows(levels, n)
        words = self.rest(self.rows.index, n)
        self.tgt = jnp.floor((words + 0.5) * (1.0 / band))
        self.src = words - self.tgt * float(band)
        self.factor = self.rest(self.rows.factor, n)

    def rest(self, at, size):
        return self.rest_ref[self.head + at : self.head + at + size, :]

    def sums(self):
        parts = [self.sums_ref[i * self.levels : (i + 1) * self.levels, :] for i in range(self.parts)]
        return jnp.concatenate(halves(jnp.concatenate(parts, axis=1)), axis=0)


def line(table, i):
    return table[i : i + 1]


def pick_source(block, r):
    band = block.parts * block.cap
    column = lax.broadcasted_iota(jnp.int32, (band, block.cap), 0).astype(F32)
    return jnp.where(column == line(block.src, r), 1.0, 0.0).astype(BF16)


def fill_slots(bands, blocks, n, slots_ref):
    for i, s in enumerate(bands):
        block = blocks[s]
        both = block.sums()
        for d in range(n):
            picked = product(both, pick_source(block, s ^ d))
            values = (picked[: block.levels] + picked[block.levels :]) * line(block.factor, s ^ d)
            slots_ref[d, :, i * block.cap : (i + 1) * block.cap] = jnp.concatenate(halves(values), axis=0)


def met_at(d, block, bands, slots_ref):
    own = jnp.broadcast_to(line(block.tgt, d), (block.cap, block.cap)).T
    same = [jnp.where(own == line(block.tgt, s ^ d), 1.0, 0.0).astype(BF16) for s in bands]
    met = product(slots_ref[d], jnp.concatenate(same, axis=1), ((1,), (1,)))
    return met[: block.levels] + met[block.levels :]


def land(table, bands, slots_ref, cols):
    cap = table.shape[1]
    row = lax.broadcasted_iota(jnp.int32, (cols, cap), 0).astype(F32)
    total = 0.0
    for i, s in enumerate(bands):
        landing = jnp.where(row == line(table, s), 1.0, 0.0).astype(BF16)
        total = total + product(slots_ref[0, :, i * cap : (i + 1) * cap], landing, ((1,), (1,)))
    levels = total.shape[0] // 2
    return total[:levels] + total[levels:]


def open_blocks(labels, refs, n, levels, band):
    blocks = {0: Block(refs[:2], n, levels, band)}
    refs = refs[2:]
    for i, r in enumerate(labels[1:]):
        blocks[r] = Block(refs[i : i + 1], n, levels, band)
    return blocks, refs[len(labels) - 1 :]


def stage_kernel(n, levels, band, cols, stages, *refs):
    known = sum(stages[:-1], [])
    blocks, refs = open_blocks(known + stages[-1], refs, n, levels, band)
    old, refs = refs[: len(stages) - 1], refs[len(stages) - 1 :]
    if known:
        met_old, remap_old, slots_ref, met_ref, remap_ref = refs
    else:
        slots_ref, met_ref, remap_ref, pick_ref = refs
        for d in range(n):
            pick_ref[d] = pick_source(blocks[0], d)
    fill_slots(stages[-1], blocks, n, slots_ref)
    for i, (d, block) in enumerate(blocks.items()):
        met = met_at(d, block, stages[-1], slots_ref)
        if d in known:
            met = met + met_old[i]
        else:
            for bands, ref in zip(stages, old):
                met = met + met_at(d, block, bands, ref)
        met_ref[i] = met
    landed = land(blocks[0].tgt, stages[-1], slots_ref, cols)
    remap_ref[...] = landed + remap_old[...] if known else landed


def shared_kernel(n, levels, band, cols, stages, pos_ref, mix_ref, *refs):
    known = sum(stages[:-1], [])
    blocks, refs = open_blocks(known + stages[-1], refs, n, levels, band)
    old, refs = refs[: len(stages) - 1], refs[len(stages) - 1 :]
    met_old, pick_ref, out_ref, slots_ref, tables_ref = refs
    me = pos_ref[0]
    for r, block in blocks.items():
        there = me ^ r
        tables_ref[there, :n, :] = block.tgt
        tables_ref[there, n:, :] = block.rest(block.rows.edge, EXTRA)
    fill_slots(stages[-1], blocks, n, slots_ref)
    last = cols - 1.0
    total = jnp.zeros((levels, band), F32)
    for i, (d, block) in enumerate(blocks.items()):
        value = met_at(d, block, stages[-1], slots_ref) + block.rest(levels, levels)
        if d in known:
            value = value + met_old[i]
        else:
            for bands, ref in zip(stages, old):
                value = value + met_at(d, block, bands, ref)
        edge = block.rest(block.rows.edge, 1)
        own = line(block.tgt, d)
        there = me ^ d
        before = tables_ref[jnp.maximum(there - 1, 0), n : n + 1, :]
        near = jnp.where((own == 0.0) & (there > 0), edge[:, 6 * levels + 1 : 6 * levels + 2], 0.0)
        value = value + row_as_column(before, levels, 0) * near
        after = tables_ref[jnp.minimum(there + 1, n - 1), n : n + 1, :]
        near = jnp.where((own == last) & (there < n - 1), edge[:, 6 * levels : 6 * levels + 1], 0.0)
        value = value + row_as_column(after, levels, levels) * near
        given = block.rest(0, levels) * value * line(blocks[0].factor, d)
        total = total + select(given, pick_ref[d], ((1,), (1,)))
    out_ref[...] = band_rows(total, mix_ref[...])


def outputs_kernel(stages, pos_ref, *refs):
    slots_refs, refs = refs[: len(stages)], refs[len(stages) :]
    remap_ref, tables_ref, static_ref, diag_ref, off_ref, obs_ref, innov_ref, increment_ref, grad_ref = refs
    levels, cols = static_ref.shape
    n = tables_ref.shape[0]
    cap = tables_ref.shape[2]
    me = pos_ref[0]
    given = [
        (s, ref, slice(i * cap, (i + 1) * cap)) for bands, ref in zip(stages, slots_refs) for i, s in enumerate(bands)
    ]
    remapped = remap_ref[...] + land(tables_ref[me, :n, :], stages[-1], slots_refs[-1], cols)
    static, off = static_ref[...], off_ref[...]
    lane = lax.broadcasted_iota(jnp.int32, (levels, cols), 1)

    def beside(there, exists, column, own_end, side):
        edge = tables_ref[there, n : n + 1, :]
        static_end, coupling, base = (row_as_column(edge, levels, (2 * i + side) * levels) for i in range(3))
        far = me ^ there
        landed = []
        for s, ref, place in given:
            values = ref[far, :levels, place].astype(F32) + ref[far, levels:, place].astype(F32)
            landed.append(jnp.where(tables_ref[there, pl.ds(s ^ far, 1), :] == column, values, 0.0))
        remap_end = jnp.sum(sum(landed), axis=1, keepdims=True)
        off_end = edge[:, 6 * levels + side : 6 * levels + side + 1]
        coupled = coupling * (remap_end + base + off_end * own_end)
        return jnp.where(exists, static_end, 0.0), jnp.where(exists, coupled, 0.0)

    before, coupled_before = beside(jnp.maximum(me - 1, 0), me > 0, cols - 1.0, static[:, :1], 0)
    after, coupled_after = beside(jnp.minimum(me + 1, n - 1), me < n - 1, 0.0, static[:, cols - 1 :], 1)
    left = jnp.where(lane == 0, before, pltpu.roll(static, 1, 1))
    right = jnp.where(lane == cols - 1, after, pltpu.roll(static, cols - 1, 1))
    increment = remapped + diag_ref[...] * static + off * (left + right)
    increment_ref[...] = increment
    misfit = obs_ref[...] * (increment - innov_ref[...])
    coupled = off * misfit
    left = jnp.where(lane == 0, coupled_before, pltpu.roll(coupled, 1, 1))
    right = jnp.where(lane == cols - 1, coupled_after, pltpu.roll(coupled, cols - 1, 1))
    grad_ref[...] = static + diag_ref[...] * misfit + left + right


def call(kernel, out_shape, spaces, scratch=(), out=VMEM, cost=None):
    return pl.pallas_call(
        kernel,
        out_shape=out_shape,
        in_specs=spaces,
        out_specs=jax.tree.map(lambda _: out, out_shape),
        scratch_shapes=scratch,
        cost_estimate=cost,
        compiler_params=pltpu.CompilerParams(vmem_limit_bytes=40 * MIB),
    )


def body(
    perturb,
    control,
    level_loc,
    static_control,
    filter_diag,
    filter_off,
    send_src,
    send_wt,
    counts,
    recv_tgt,
    obs_weight,
    innovation,
):
    levels, members, band_cols = control.shape
    tile_cols = static_control.shape[1]
    n = lax.axis_size("tile")
    groups = lax.axis_size("grp")
    cap = send_src.shape[2]
    shape = jax.ShapeDtypeStruct
    swap = [(0, 1), (1, 0)]
    lev = lax.axis_index("lev").astype(jnp.int32).reshape(1)
    pos = lax.axis_index("tile").astype(jnp.int32).reshape(1)
    other_control = lax.ppermute(control, "lev", swap)
    width = levels * SUB
    level_mix, own_mix, given_mix = call(
        mix_kernel,
        (shape((2, width, 2 * width), BF16), shape((2, width, width), BF16), shape((levels, width), F32)),
        [SMEM, VMEM],
        cost=pl.CostEstimate(flops=10**9, bytes_accessed=0, transcendentals=0),
    )(lev, level_loc)
    own_sum = call(sum_kernel, shape((levels, band_cols), F32), [VMEM] * 4)(perturb, control, other_control, level_mix)
    flat = shape((levels, tile_cols), F32)
    mine_shape = shape((band_cols // width * levels + levels, width), F32)
    diag, off = filter_diag.reshape(1, -1), filter_off.reshape(1, -1)
    if n * cap <= tile_cols and n >= 4 and lax.axis_size("lev") == 2 and n & (n - 1) == 0 and band_cols * tile_cols <= 2**20:
        rows = Rows(levels, n)
        stacked = band_cols // cap * levels
        rests = call(functools.partial(static_kernel, band_cols), [shape((rows.total, cap), F32)] * n, [SMEM] * 2 + [VMEM] * 8)(
            pos, counts, static_control, diag, off, obs_weight, innovation, send_src, send_wt, recv_tgt
        )
        sums = [own_sum]
        sums[0], other_perturb = lax.optimization_barrier((sums[0], lax.ppermute(perturb, "lev", swap)))
        for k in range(1, groups):
            sums.append(lax.ppermute(sums[0], "grp", [(g, (g + k) % groups) for g in range(groups)]))
        high = n // 2
        near = list(range(1, high))
        stages = [[0, *near], [high, *(r + high for r in reversed(near[1:]))], [high + 1]]
        block = stacked + rows.total
        total, *blocks = call(
            functools.partial(blocks_kernel, groups, levels, high - 1),
            [shape((stacked, cap), F32)]
            + [shape((block, cap), F32)] * (high - 1)
            + [shape((block + 2 * levels * (high - 1), cap), F32)],
            [VMEM] * (groups + n - 1),
        )(*sums, *rests[1:])

        def to(r, block):
            return [lax.ppermute(block, "tile", [(i, i ^ r) for i in range(n)])]

        arrived = {0: [total, rests[0]]} | {r: to(r, blocks[r - 1]) for r in (high, *near)}
        passed = call(
            functools.partial(relay_kernel, levels, stacked), [shape((block, cap), F32)] * (high - 1), [VMEM]
        )(*arrived[high])
        for r in reversed(near):
            arrived[r + high] = to(r, passed[r - 1])
        slots, carried, picks = [], [], []
        for count in range(1, len(stages)):
            labels = sum(stages[:count], [])
            refs = [ref for r in labels for ref in arrived[r]]
            outs = [
                shape((n, 2 * levels, len(stages[count - 1]) * cap), BF16),
                shape((len(labels), levels, cap), F32),
                flat,
            ] + [shape((n, band_cols, cap), BF16)] * (count == 1)
            new, *carried = call(
                functools.partial(stage_kernel, n, levels, band_cols, tile_cols, stages[:count]),
                outs,
                [VMEM] * (len(refs) + len(slots) + len(carried)),
                cost=pl.CostEstimate(flops=(10**9, 10**6)[count - 1], bytes_accessed=0, transcendentals=0),
            )(*refs, *slots, *carried)
            slots.append(new)
            picks += carried[2:]
            carried = carried[:2]
        met, remap = carried
        refs = [ref for r in sum(stages, []) for ref in arrived[r]] + slots + [met] + picks
        mine, new, tables = call(
            functools.partial(shared_kernel, n, levels, band_cols, tile_cols, stages),
            (mine_shape, shape((n, 2 * levels, len(stages[-1]) * cap), BF16), shape((n, n + EXTRA, cap), F32)),
            [SMEM] + [VMEM] * (1 + len(refs)),
            cost=pl.CostEstimate(flops=10**9, bytes_accessed=0, transcendentals=0),
        )(pos, given_mix, *refs)
        slots.append(new)
        increment, grad_static = call(
            functools.partial(outputs_kernel, stages), (flat, flat), [SMEM] + [VMEM] * (len(slots) + 7)
        )(pos, *slots, remap, tables, static_control, diag, off, obs_weight, innovation)
    else:
        other_perturb = lax.ppermute(perturb, "lev", swap)
        payload = call(
            band_kernel,
            shape((groups, n, levels + EXTRA, cap), F32),
            [SMEM] + [VMEM] * 4,
            [pltpu.VMEM((2 * levels, band_cols), BF16)],
        )(counts, own_sum, static_control, send_src, send_wt)
        arrived = lax.all_to_all(
            payload.reshape(groups * n, levels + EXTRA, cap), ("grp", "tile"), split_axis=0, concat_axis=0, tiled=True
        ).reshape(groups, n, levels + EXTRA, cap)
        increment, partial, giving = call(
            tile_kernel, (flat, flat, shape((n, levels + EXTRA, cap), F32)), [SMEM] + [VMEM] * 7
        )(pos, arrived, recv_tgt, static_control, diag, off, obs_weight, innovation)
        returned = lax.all_to_all(giving, "tile", split_axis=0, concat_axis=0, tiled=True)
        grad_static, mine = call(
            functools.partial(adjoint_kernel, band_cols), (flat, mine_shape), [SMEM, SMEM] + [VMEM] * 5
        )(pos, counts, returned, send_src, send_wt, partial, given_mix)
    theirs = lax.ppermute(mine, "lev", swap)
    own = call(ens_own_kernel, shape(control.shape, F32), [VMEM] * 4)(perturb, mine, own_mix, control)
    grad_ens, increment, grad_static = call(
        ens_kernel,
        (shape(control.shape, F32), flat, flat),
        [VMEM] * 5,
        [pltpu.VMEM(control.shape, F32), pltpu.SemaphoreType.DMA((2 + members // SUB,))],
        out=HBM,
    )(other_perturb, theirs, own, increment, grad_static)
    return (increment, grad_static, grad_ens)


def solution(mesh):
    return jax.shard_map(
        body,
        mesh=mesh,
        in_specs=(
            P("lev", "grp", "tile"),
            P("lev", "grp", "tile"),
            P("lev", None),
            P("lev", "tile"),
            P("tile"),
            P("tile"),
            P("tile", None, None),
            P("tile", None, None),
            P("tile", None),
            P("tile", None, None),
            P("lev", "tile"),
            P("lev", "tile"),
        ),
        out_specs=(P("lev", "tile"), P("lev", "tile"), P("lev", "grp", "tile")),
        check_vma=False,
    )
```

```python
import functools

import jax
import jax.numpy as jnp
from jax import lax
from jax.experimental import pallas as pl
from jax.experimental.pallas import tpu as pltpu
from jax.sharding import PartitionSpec as P

F32 = jnp.float32
BF16 = jnp.bfloat16
SUB = 8
EXTRA = 8
VMEM = pl.BlockSpec(memory_space=pltpu.VMEM)
HBM = pl.BlockSpec(memory_space=pltpu.HBM)
SMEM = pl.BlockSpec(memory_space=pltpu.SMEM)
MIB = 1024 * 1024


def halves(values):
    high = values.astype(BF16)
    low = (values - high.astype(F32)).astype(BF16)
    return high, low


def product(a, b, dims=((1,), (0,))):
    return lax.dot_general(a, b, (dims, ((), ())), preferred_element_type=F32)


def select(values, chosen, dims=((1,), (0,))):
    rows = values.shape[0]
    both = product(jnp.concatenate(halves(values), axis=0), chosen, dims)
    return both[:rows] + both[rows:]


def iota(shape, axis):
    return lax.broadcasted_iota(jnp.int32, shape, axis)


def wide_rows(matrix, start, count):
    cols = matrix.shape[1]
    shape = (cols, count * SUB)
    place = (iota(shape, 1) // SUB + start) % cols
    pick = (place == iota(shape, 0)).astype(BF16)
    high, low = halves(matrix)
    return product(high, pick) + product(low, pick)


def spread(wide):
    rows, cols = wide.shape
    tall = jnp.broadcast_to(wide[:, None, :], (rows, SUB, cols)).reshape(rows * SUB, cols)
    return jnp.where(iota(tall.shape, 0) % SUB == iota(tall.shape, 1) % SUB, tall, 0.0)


def mix(weights, values):
    high, low = halves(values)
    rows = weights[0].shape[0]
    both = product(jnp.concatenate(weights, axis=0), high)
    return both[:rows] + (product(weights[0], low) + both[rows:])


def one_hot(index, size):
    rows = lax.broadcasted_iota(jnp.int32, (size, index.shape[1]), 0)
    return jnp.where(rows == index, 1.0, 0.0).astype(BF16)


def column_as_row(column, lane, offset):
    n = column.shape[0]
    place = lax.broadcasted_iota(jnp.int32, (n, 128), 1) == lax.broadcasted_iota(jnp.int32, (n, 128), 0) + offset
    return jnp.sum(jnp.where(place, column, 0.0), axis=0, keepdims=True)


def row_as_column(row, n, offset):
    place = lax.broadcasted_iota(jnp.int32, (n, 128), 1) == lax.broadcasted_iota(jnp.int32, (n, 128), 0) + offset
    return jnp.sum(jnp.where(place, row, 0.0), axis=1, keepdims=True)


def edge_rows(values):
    n = values.shape[0]
    row = column_as_row(values[:, -1:], None, 0) + column_as_row(values[:, :1], None, n)
    return jnp.broadcast_to(row, (EXTRA, 128))


def factor_of(counts_ref, weight_ref, d):
    slot = lax.broadcasted_iota(jnp.int32, (1, weight_ref.shape[2]), 1)
    return jnp.where(slot < counts_ref[0, d], weight_ref[0, pl.ds(d, 1), :], 0.0)


def loop(n, step, init):
    return lax.fori_loop(0, n, step, init, unroll=n if n <= 8 else 1)


def mix_kernel(lev_ref, loc_ref, mix_ref, own_ref, given_ref):
    levels = loc_ref.shape[0]
    start = lev_ref[0] * levels
    loc = loc_ref[...]
    mix_ref[0], mix_ref[1] = halves(spread(wide_rows(loc, start, 2 * levels)))
    own_ref[0], own_ref[1] = halves(spread(wide_rows(loc, start, levels)).T)
    given_ref[...] = wide_rows(loc, levels - start, levels)


def sum_kernel(perturb_ref, control_ref, other_ref, mix_ref, out_ref):
    levels, members, cols = perturb_ref.shape
    perturb = perturb_ref[...].astype(F32)
    total = jnp.zeros((levels, SUB, cols), F32)
    for m in range(0, members, SUB):
        tile = jnp.concatenate([control_ref[:, m : m + SUB, :], other_ref[:, m : m + SUB, :]], axis=0)
        mixed = mix((mix_ref[0], mix_ref[1]), tile.reshape(2 * levels * SUB, cols))
        total = total + perturb[:, m : m + SUB, :] * mixed.reshape(levels, SUB, cols)
    out_ref[...] = jnp.sum(total, axis=1)


def band_kernel(counts_ref, sum_ref, static_ref, src_ref, weight_ref, out_ref, acc_ref):
    levels, cols = sum_ref.shape
    acc_ref[...] = jnp.concatenate(halves(sum_ref[...]), axis=0)
    n = src_ref.shape[1]
    edges = edge_rows(static_ref[...])

    def step(d, carry):
        chosen = one_hot(src_ref[0, pl.ds(d, 1), :], cols)
        both = product(acc_ref[...], chosen)
        payload = (both[:levels] + both[levels:]) * factor_of(counts_ref, weight_ref, d)
        for g in range(out_ref.shape[0]):
            out_ref[g, d, :levels, :] = payload
            out_ref[g, d, levels:, :] = edges
        return carry

    loop(n, step, 0)


def tile_kernel(pos_ref, arrived_ref, tgt_ref, static_ref, diag_ref, off_ref, obs_ref, innov_ref,
                increment_ref, partial_ref, out_ref):
    levels, cols = static_ref.shape
    groups, n = arrived_ref.shape[:2]
    me = pos_ref[0]

    def step(s, total):
        values = sum(arrived_ref[g, s, :levels, :] for g in range(groups))
        chosen = one_hot(tgt_ref[0, pl.ds(s, 1), :], cols)
        return total + select(values, chosen, ((1,), (1,)))

    remapped = loop(n, step, jnp.zeros((levels, cols), F32))
    before = arrived_ref[0, jnp.maximum(me - 1, 0), levels : levels + 1, :]
    after = arrived_ref[0, jnp.minimum(me + 1, n - 1), levels : levels + 1, :]
    before = jnp.where(me > 0, row_as_column(before, levels, 0), 0.0)
    after = jnp.where(me < n - 1, row_as_column(after, levels, levels), 0.0)
    static = static_ref[...]
    lane = lax.broadcasted_iota(jnp.int32, (levels, cols), 1)
    left = jnp.where(lane == 0, before, pltpu.roll(static, 1, 1))
    right = jnp.where(lane == cols - 1, after, pltpu.roll(static, cols - 1, 1))
    increment = remapped + diag_ref[...] * static + off_ref[...] * (left + right)
    increment_ref[...] = increment
    misfit = obs_ref[...] * (increment - innov_ref[...])
    coupled = off_ref[...] * misfit
    left = jnp.where(lane == 0, 0.0, pltpu.roll(coupled, 1, 1))
    right = jnp.where(lane == cols - 1, 0.0, pltpu.roll(coupled, cols - 1, 1))
    partial_ref[...] = static + diag_ref[...] * misfit + left + right
    edges = edge_rows(coupled)
    both = jnp.concatenate(halves(misfit), axis=0)

    def give(s, carry):
        chosen = one_hot(tgt_ref[0, pl.ds(s, 1), :], cols)
        picked = product(both, chosen)
        out_ref[s, :levels, :] = picked[:levels] + picked[levels:]
        out_ref[s, levels:, :] = edges
        return carry

    loop(n, give, 0)


def adjoint_kernel(band, pos_ref, counts_ref, returned_ref, src_ref, weight_ref, partial_ref, mix_ref, grad_ref, out_ref):
    levels, cols = partial_ref.shape
    n = returned_ref.shape[0]
    me = pos_ref[0]

    def step(d, total):
        values = returned_ref[d, :levels, :] * factor_of(counts_ref, weight_ref, d)
        return total + select(values, one_hot(src_ref[0, pl.ds(d, 1), :], band), ((1,), (1,)))

    out_ref[...] = band_rows(loop(n, step, jnp.zeros((levels, band), F32)), mix_ref[...])
    before = returned_ref[jnp.maximum(me - 1, 0), levels : levels + 1, :]
    after = returned_ref[jnp.minimum(me + 1, n - 1), levels : levels + 1, :]
    before = jnp.where(me > 0, row_as_column(before, levels, 0), 0.0)
    after = jnp.where(me < n - 1, row_as_column(after, levels, levels), 0.0)
    lane = lax.broadcasted_iota(jnp.int32, (levels, cols), 1)
    grad_ref[...] = partial_ref[...] + (jnp.where(lane == 0, before, 0.0) + jnp.where(lane == cols - 1, after, 0.0))


def band_rows(band, weights):
    width = weights.shape[1]
    return jnp.concatenate([band[:, at : at + width] for at in range(0, band.shape[1], width)] + [weights], axis=0)


def ens_tiles(perturb_ref, rows_ref, weights, before_ref):
    levels, members, cols = perturb_ref.shape
    width = rows_ref.shape[1]
    parts = [rows_ref[i * levels : (i + 1) * levels, :] for i in range(cols // width)]
    grad = jnp.concatenate(parts, axis=1)[:, None, :]
    perturb = perturb_ref[...].astype(F32)
    for m in range(0, members, SUB):
        place = (slice(None), slice(m, m + SUB), slice(None))
        tile = (perturb[place] * grad).reshape(levels * SUB, cols)
        yield place, before_ref[place] + mix(weights, tile).reshape(levels, SUB, cols)


def ens_own_kernel(perturb_ref, mine_ref, weights_ref, control_ref, out_ref):
    for place, values in ens_tiles(perturb_ref, mine_ref, (weights_ref[0], weights_ref[1]), control_ref):
        out_ref[place] = values


def ens_kernel(perturb_ref, theirs_ref, own_ref, *refs):
    count = (len(refs) - 3) // 2
    flats, (out_hbm, *flat_hbms), (out_ref, sems) = refs[:count], refs[count : 2 * count + 1], refs[2 * count + 1 :]
    copies = [pltpu.make_async_copy(a, b, sems.at[i]) for i, (a, b) in enumerate(zip(flats, flat_hbms))]
    for copy in copies:
        copy.start()
    levels = perturb_ref.shape[0]
    weights = halves(spread(theirs_ref[theirs_ref.shape[0] - levels :, :]).T)
    for place, values in ens_tiles(perturb_ref, theirs_ref, weights, own_ref):
        out_ref[place] = values
        copies.append(pltpu.make_async_copy(out_ref.at[place], out_hbm.at[place], sems.at[len(copies)]))
        copies[-1].start()
    for copy in copies:
        copy.wait()


def relabel(r, n, lev):
    high, low = n // 2, n // 4
    both = high | low
    turned = (r & ~both) | ((r & low) << 1) | ((r & high) >> 1)
    return r + (turned - r) * lev


class Rows:
    def __init__(self, levels, n):
        self.weight = slice(0, levels)
        self.base = slice(levels, 2 * levels)
        at = 2 * levels
        self.factor, self.index, self.edge = at, at + n, at + 2 * n
        self.total = at + 2 * n + EXTRA


def static_kernel(band, pos_ref, lev_ref, counts_ref, static_ref, diag_ref, off_ref, obs_ref, innov_ref, src_ref, weight_ref, tgt_ref,
                  *out_refs):
    levels, cols = static_ref.shape
    n = len(out_refs)
    cap = src_ref.shape[2]
    rows = Rows(levels, n)
    peers = [pos_ref[0] ^ relabel(r, n, lev_ref[0]) for r in range(n)]
    static, off, obs = static_ref[...], off_ref[...], obs_ref[...]
    lane = lax.broadcasted_iota(jnp.int32, (levels, cols), 1)
    left = jnp.where(lane == 0, 0.0, pltpu.roll(static, 1, 1))
    right = jnp.where(lane == cols - 1, 0.0, pltpu.roll(static, cols - 1, 1))
    base = diag_ref[...] * static + off * (left + right) - innov_ref[...]
    coupled = off * obs
    ends = [v[:, i] for v in (static, coupled, base) for i in (slice(cols - 1, cols), slice(0, 1))]
    edge = sum(column_as_row(end, None, i * levels) for i, end in enumerate(ends))
    place = lax.broadcasted_iota(jnp.int32, (1, cap), 1)
    edge = edge + jnp.where(place == 6 * levels, off[:, cols - 1 :], 0.0)
    edge = edge + jnp.where(place == 6 * levels + 1, off[:, :1], 0.0)
    edge = jnp.broadcast_to(edge, (EXTRA, cap))
    both = jnp.concatenate(halves(jnp.concatenate([obs, base], axis=0)), axis=0)
    tgts = [tgt_ref[0, pl.ds(peer, 1), :] for peer in peers]
    src = jnp.concatenate([src_ref[0, pl.ds(peer, 1), :] for peer in peers], axis=0).astype(F32)
    index = jnp.concatenate(tgts, axis=0).astype(F32) * float(band) + src
    factor = jnp.concatenate([factor_of(counts_ref, weight_ref, peer) for peer in peers], axis=0)
    for r, out_ref in enumerate(out_refs):
        picked = product(both, one_hot(tgts[r], cols))
        out_ref[: 2 * levels, :] = picked[: 2 * levels] + picked[2 * levels :]
        out_ref[rows.factor : rows.factor + n, :] = factor
        out_ref[rows.index : rows.index + n, :] = index
        out_ref[rows.edge :, :] = edge


def blocks_kernel(groups, levels, relayed, *refs):
    sums, refs = refs[:groups], refs[groups:]
    count = (len(refs) - 1 - relayed) // 2
    rests, relays, total_ref, out_refs = refs[:count], refs[count : count + relayed], refs[count + relayed], refs[-count:]
    total = sum(ref[...] for ref in sums)
    cap = total_ref.shape[1]
    total = jnp.concatenate([total[:, at : at + cap] for at in range(0, total.shape[1], cap)], axis=0)
    total_ref[...] = total
    for i, (rest_ref, out_ref) in enumerate(zip(rests, out_refs)):
        parts = [total, rest_ref[...]]
        if i == count - 1:
            parts += [ref[: 2 * levels, :] for ref in relays]
        out_ref[...] = jnp.concatenate(parts, axis=0)


def relay_kernel(levels, stacked, got_ref, *out_refs):
    head = got_ref.shape[0] - len(out_refs) * 2 * levels
    for i, out_ref in enumerate(out_refs):
        at = head + 2 * levels * i
        out_ref[...] = jnp.concatenate(
            [got_ref[:stacked, :], got_ref[at : at + 2 * levels, :], got_ref[stacked + 2 * levels : head, :]], axis=0
        )


class Block:
    def __init__(self, refs, n, levels, band):
        cap = refs[0].shape[1]
        self.levels, self.parts, self.cap = levels, band // cap, cap
        self.sums_ref, self.rest_ref = refs[0], refs[-1]
        self.head = 0 if len(refs) == 2 else self.parts * levels
        self.rows = Rows(levels, n)
        words = self.rest(self.rows.index, n)
        self.tgt = jnp.floor((words + 0.5) * (1.0 / band))
        self.src = words - self.tgt * float(band)
        self.factor = self.rest(self.rows.factor, n)

    def rest(self, at, size):
        return self.rest_ref[self.head + at : self.head + at + size, :]

    def sums(self):
        parts = [self.sums_ref[i * self.levels : (i + 1) * self.levels, :] for i in range(self.parts)]
        return jnp.concatenate(halves(jnp.concatenate(parts, axis=1)), axis=0)


def line(table, i):
    return table[i : i + 1]


def pick_source(block, r):
    band = block.parts * block.cap
    column = lax.broadcasted_iota(jnp.int32, (band, block.cap), 0).astype(F32)
    return jnp.where(column == line(block.src, r), 1.0, 0.0).astype(BF16)


def fill_slots(bands, blocks, n, slots_ref):
    for i, s in enumerate(bands):
        block = blocks[s]
        both = block.sums()
        for d in range(n):
            picked = product(both, pick_source(block, s ^ d))
            values = (picked[: block.levels] + picked[block.levels :]) * line(block.factor, s ^ d)
            slots_ref[d, :, i * block.cap : (i + 1) * block.cap] = jnp.concatenate(halves(values), axis=0)


def met_at(d, block, bands, slots_ref):
    own = jnp.broadcast_to(line(block.tgt, d), (block.cap, block.cap)).T
    same = [jnp.where(own == line(block.tgt, s ^ d), 1.0, 0.0).astype(BF16) for s in bands]
    met = product(slots_ref[d], jnp.concatenate(same, axis=1), ((1,), (1,)))
    return met[: block.levels] + met[block.levels :]


def land(table, bands, slots_ref, cols):
    cap = table.shape[1]
    row = lax.broadcasted_iota(jnp.int32, (cols, cap), 0).astype(F32)
    total = 0.0
    for i, s in enumerate(bands):
        landing = jnp.where(row == line(table, s), 1.0, 0.0).astype(BF16)
        total = total + product(slots_ref[0, :, i * cap : (i + 1) * cap], landing, ((1,), (1,)))
    levels = total.shape[0] // 2
    return total[:levels] + total[levels:]


def open_blocks(labels, refs, n, levels, band):
    blocks = {0: Block(refs[:2], n, levels, band)}
    refs = refs[2:]
    for i, r in enumerate(labels[1:]):
        blocks[r] = Block(refs[i : i + 1], n, levels, band)
    return blocks, refs[len(labels) - 1 :]


def stage_kernel(n, levels, band, cols, stages, *refs):
    known = sum(stages[:-1], [])
    blocks, refs = open_blocks(known + stages[-1], refs, n, levels, band)
    old, refs = refs[: len(stages) - 1], refs[len(stages) - 1 :]
    if known:
        met_old, remap_old, slots_ref, met_ref, remap_ref = refs
    else:
        slots_ref, met_ref, remap_ref, pick_ref = refs
        for d in range(n):
            pick_ref[d] = pick_source(blocks[0], d)
    fill_slots(stages[-1], blocks, n, slots_ref)
    for i, (d, block) in enumerate(blocks.items()):
        met = met_at(d, block, stages[-1], slots_ref)
        if d in known:
            met = met + met_old[i]
        else:
            for bands, ref in zip(stages, old):
                met = met + met_at(d, block, bands, ref)
        met_ref[i] = met
    landed = land(blocks[0].tgt, stages[-1], slots_ref, cols)
    remap_ref[...] = landed + remap_old[...] if known else landed


def shared_kernel(n, levels, band, cols, stages, pos_ref, lev_ref, mix_ref, *refs):
    known = sum(stages[:-1], [])
    blocks, refs = open_blocks(known + stages[-1], refs, n, levels, band)
    old, refs = refs[: len(stages) - 1], refs[len(stages) - 1 :]
    met_old, pick_ref, out_ref, slots_ref, tables_ref = refs
    me = pos_ref[0]
    for r, block in blocks.items():
        there = me ^ relabel(r, n, lev_ref[0])
        tables_ref[there, :n, :] = block.tgt
        tables_ref[there, n:, :] = block.rest(block.rows.edge, EXTRA)
    fill_slots(stages[-1], blocks, n, slots_ref)
    last = cols - 1.0
    total = jnp.zeros((levels, band), F32)
    for i, (d, block) in enumerate(blocks.items()):
        value = met_at(d, block, stages[-1], slots_ref) + block.rest(levels, levels)
        if d in known:
            value = value + met_old[i]
        else:
            for bands, ref in zip(stages, old):
                value = value + met_at(d, block, bands, ref)
        edge = block.rest(block.rows.edge, 1)
        own = line(block.tgt, d)
        there = me ^ relabel(d, n, lev_ref[0])
        before = tables_ref[jnp.maximum(there - 1, 0), n : n + 1, :]
        near = jnp.where((own == 0.0) & (there > 0), edge[:, 6 * levels + 1 : 6 * levels + 2], 0.0)
        value = value + row_as_column(before, levels, 0) * near
        after = tables_ref[jnp.minimum(there + 1, n - 1), n : n + 1, :]
        near = jnp.where((own == last) & (there < n - 1), edge[:, 6 * levels : 6 * levels + 1], 0.0)
        value = value + row_as_column(after, levels, levels) * near
        given = block.rest(0, levels) * value * line(blocks[0].factor, d)
        total = total + select(given, pick_ref[d], ((1,), (1,)))
    out_ref[...] = band_rows(total, mix_ref[...])


def outputs_kernel(stages, pos_ref, lev_ref, *refs):
    slots_refs, refs = refs[: len(stages)], refs[len(stages) :]
    remap_ref, tables_ref, static_ref, diag_ref, off_ref, obs_ref, innov_ref, increment_ref, grad_ref = refs
    levels, cols = static_ref.shape
    n = tables_ref.shape[0]
    cap = tables_ref.shape[2]
    me = pos_ref[0]
    given = [
        (s, ref, slice(i * cap, (i + 1) * cap)) for bands, ref in zip(stages, slots_refs) for i, s in enumerate(bands)
    ]
    remapped = remap_ref[...] + land(tables_ref[me, :n, :], stages[-1], slots_refs[-1], cols)
    static, off = static_ref[...], off_ref[...]
    lane = lax.broadcasted_iota(jnp.int32, (levels, cols), 1)

    def beside(there, exists, column, own_end, side):
        edge = tables_ref[there, n : n + 1, :]
        static_end, coupling, base = (row_as_column(edge, levels, (2 * i + side) * levels) for i in range(3))
        far = relabel(me ^ there, n, lev_ref[0])
        landed = []
        for s, ref, place in given:
            values = ref[far, :levels, place].astype(F32) + ref[far, levels:, place].astype(F32)
            landed.append(jnp.where(tables_ref[there, pl.ds(s ^ far, 1), :] == column, values, 0.0))
        remap_end = jnp.sum(sum(landed), axis=1, keepdims=True)
        off_end = edge[:, 6 * levels + side : 6 * levels + side + 1]
        coupled = coupling * (remap_end + base + off_end * own_end)
        return jnp.where(exists, static_end, 0.0), jnp.where(exists, coupled, 0.0)

    before, coupled_before = beside(jnp.maximum(me - 1, 0), me > 0, cols - 1.0, static[:, :1], 0)
    after, coupled_after = beside(jnp.minimum(me + 1, n - 1), me < n - 1, 0.0, static[:, cols - 1 :], 1)
    left = jnp.where(lane == 0, before, pltpu.roll(static, 1, 1))
    right = jnp.where(lane == cols - 1, after, pltpu.roll(static, cols - 1, 1))
    increment = remapped + diag_ref[...] * static + off * (left + right)
    increment_ref[...] = increment
    misfit = obs_ref[...] * (increment - innov_ref[...])
    coupled = off * misfit
    left = jnp.where(lane == 0, coupled_before, pltpu.roll(coupled, 1, 1))
    right = jnp.where(lane == cols - 1, coupled_after, pltpu.roll(coupled, cols - 1, 1))
    grad_ref[...] = static + diag_ref[...] * misfit + left + right


def call(kernel, out_shape, spaces, scratch=(), out=VMEM, cost=None):
    return pl.pallas_call(
        kernel,
        out_shape=out_shape,
        in_specs=spaces,
        out_specs=jax.tree.map(lambda _: out, out_shape),
        scratch_shapes=scratch,
        cost_estimate=cost,
        compiler_params=pltpu.CompilerParams(vmem_limit_bytes=40 * MIB),
    )


def body(
    perturb,
    control,
    level_loc,
    static_control,
    filter_diag,
    filter_off,
    send_src,
    send_wt,
    counts,
    recv_tgt,
    obs_weight,
    innovation,
):
    levels, members, band_cols = control.shape
    tile_cols = static_control.shape[1]
    n = lax.axis_size("tile")
    groups = lax.axis_size("grp")
    cap = send_src.shape[2]
    shape = jax.ShapeDtypeStruct
    swap = [(0, 1), (1, 0)]
    lev = lax.axis_index("lev").astype(jnp.int32).reshape(1)
    pos = lax.axis_index("tile").astype(jnp.int32).reshape(1)
    other_control = lax.ppermute(control, "lev", swap)
    width = levels * SUB
    level_mix, own_mix, given_mix = call(
        mix_kernel,
        (shape((2, width, 2 * width), BF16), shape((2, width, width), BF16), shape((levels, width), F32)),
        [SMEM, VMEM],
        cost=pl.CostEstimate(flops=10**9, bytes_accessed=0, transcendentals=0),
    )(lev, level_loc)
    own_sum = call(sum_kernel, shape((levels, band_cols), F32), [VMEM] * 4)(perturb, control, other_control, level_mix)
    flat = shape((levels, tile_cols), F32)
    mine_shape = shape((band_cols // width * levels + levels, width), F32)
    diag, off = filter_diag.reshape(1, -1), filter_off.reshape(1, -1)
    if n * cap <= tile_cols and n >= 4 and lax.axis_size("lev") == 2 and n & (n - 1) == 0 and band_cols * tile_cols <= 2**20:
        rows = Rows(levels, n)
        stacked = band_cols // cap * levels
        rests = call(functools.partial(static_kernel, band_cols), [shape((rows.total, cap), F32)] * n, [SMEM] * 3 + [VMEM] * 8)(
            pos, lev, counts, static_control, diag, off, obs_weight, innovation, send_src, send_wt, recv_tgt
        )
        sums = [own_sum]
        sums[0], other_perturb = lax.optimization_barrier((sums[0], lax.ppermute(perturb, "lev", swap)))
        for k in range(1, groups):
            sums.append(lax.ppermute(sums[0], "grp", [(g, (g + k) % groups) for g in range(groups)]))
        high = n // 2
        near = list(range(1, high))
        stages = [[0, *near], [high, *(r + high for r in reversed(near[1:]))], [high + 1]]
        block = stacked + rows.total
        total, *blocks = call(
            functools.partial(blocks_kernel, groups, levels, high - 1),
            [shape((stacked, cap), F32)]
            + [shape((block, cap), F32)] * (high - 1)
            + [shape((block + 2 * levels * (high - 1), cap), F32)],
            [VMEM] * (groups + n - 1),
        )(*sums, *rests[1:])

        def to(r, block):
            pairs = [(i * 2 + v, (i ^ relabel(r, n, v)) * 2 + v) for i in range(n) for v in range(2)]
            return [lax.ppermute(block, ("tile", "lev"), pairs)]

        arrived = {0: [total, rests[0]]} | {r: to(r, blocks[r - 1]) for r in (high, *near)}
        passed = call(
            functools.partial(relay_kernel, levels, stacked), [shape((block, cap), F32)] * (high - 1), [VMEM]
        )(*arrived[high])
        for r in reversed(near):
            arrived[r + high] = to(r, passed[r - 1])
        slots, carried, picks = [], [], []
        for count in range(1, len(stages)):
            labels = sum(stages[:count], [])
            refs = [ref for r in labels for ref in arrived[r]]
            outs = [
                shape((n, 2 * levels, len(stages[count - 1]) * cap), BF16),
                shape((len(labels), levels, cap), F32),
                flat,
            ] + [shape((n, band_cols, cap), BF16)] * (count == 1)
            new, *carried = call(
                functools.partial(stage_kernel, n, levels, band_cols, tile_cols, stages[:count]),
                outs,
                [VMEM] * (len(refs) + len(slots) + len(carried)),
                cost=pl.CostEstimate(flops=(10**9, 10**6)[count - 1], bytes_accessed=0, transcendentals=0),
            )(*refs, *slots, *carried)
            slots.append(new)
            picks += carried[2:]
            carried = carried[:2]
        met, remap = carried
        refs = [ref for r in sum(stages, []) for ref in arrived[r]] + slots + [met] + picks
        mine, new, tables = call(
            functools.partial(shared_kernel, n, levels, band_cols, tile_cols, stages),
            (mine_shape, shape((n, 2 * levels, len(stages[-1]) * cap), BF16), shape((n, n + EXTRA, cap), F32)),
            [SMEM] * 2 + [VMEM] * (1 + len(refs)),
            cost=pl.CostEstimate(flops=10**9, bytes_accessed=0, transcendentals=0),
        )(pos, lev, given_mix, *refs)
        slots.append(new)
        increment, grad_static = call(
            functools.partial(outputs_kernel, stages), (flat, flat), [SMEM] * 2 + [VMEM] * (len(slots) + 7)
        )(pos, lev, *slots, remap, tables, static_control, diag, off, obs_weight, innovation)
    else:
        other_perturb = lax.ppermute(perturb, "lev", swap)
        payload = call(
            band_kernel,
            shape((groups, n, levels + EXTRA, cap), F32),
            [SMEM] + [VMEM] * 4,
            [pltpu.VMEM((2 * levels, band_cols), BF16)],
        )(counts, own_sum, static_control, send_src, send_wt)
        arrived = lax.all_to_all(
            payload.reshape(groups * n, levels + EXTRA, cap), ("grp", "tile"), split_axis=0, concat_axis=0, tiled=True
        ).reshape(groups, n, levels + EXTRA, cap)
        increment, partial, giving = call(
            tile_kernel, (flat, flat, shape((n, levels + EXTRA, cap), F32)), [SMEM] + [VMEM] * 7
        )(pos, arrived, recv_tgt, static_control, diag, off, obs_weight, innovation)
        returned = lax.all_to_all(giving, "tile", split_axis=0, concat_axis=0, tiled=True)
        grad_static, mine = call(
            functools.partial(adjoint_kernel, band_cols), (flat, mine_shape), [SMEM, SMEM] + [VMEM] * 5
        )(pos, counts, returned, send_src, send_wt, partial, given_mix)
    theirs = lax.ppermute(mine, "lev", swap)
    own = call(ens_own_kernel, shape(control.shape, F32), [VMEM] * 4)(perturb, mine, own_mix, control)
    grad_ens, increment, grad_static = call(
        ens_kernel,
        (shape(control.shape, F32), flat, flat),
        [VMEM] * 5,
        [pltpu.VMEM(control.shape, F32), pltpu.SemaphoreType.DMA((2 + members // SUB,))],
        out=HBM,
    )(other_perturb, theirs, own, increment, grad_static)
    return (increment, grad_static, grad_ens)


def solution(mesh):
    return jax.shard_map(
        body,
        mesh=mesh,
        in_specs=(
            P("lev", "grp", "tile"),
            P("lev", "grp", "tile"),
            P("lev", None),
            P("lev", "tile"),
            P("tile"),
            P("tile"),
            P("tile", None, None),
            P("tile", None, None),
            P("tile", None),
            P("tile", None, None),
            P("lev", "tile"),
            P("lev", "tile"),
        ),
        out_specs=(P("lev", "tile"), P("lev", "tile"), P("lev", "grp", "tile")),
        check_vma=False,
    )
```

```python
import functools

import jax
import jax.numpy as jnp
from jax import lax
from jax.experimental import pallas as pl
from jax.experimental.pallas import tpu as pltpu
from jax.sharding import PartitionSpec as P

F32 = jnp.float32
BF16 = jnp.bfloat16
SUB = 8
EXTRA = 8
VMEM = pl.BlockSpec(memory_space=pltpu.VMEM)
HBM = pl.BlockSpec(memory_space=pltpu.HBM)
SMEM = pl.BlockSpec(memory_space=pltpu.SMEM)
MIB = 1024 * 1024


def halves(values):
    high = values.astype(BF16)
    low = (values - high.astype(F32)).astype(BF16)
    return high, low


def product(a, b, dims=((1,), (0,))):
    return lax.dot_general(a, b, (dims, ((), ())), preferred_element_type=F32)


def select(values, chosen, dims=((1,), (0,))):
    rows = values.shape[0]
    both = product(jnp.concatenate(halves(values), axis=0), chosen, dims)
    return both[:rows] + both[rows:]


def iota(shape, axis):
    return lax.broadcasted_iota(jnp.int32, shape, axis)


def wide_rows(matrix, start, count):
    cols = matrix.shape[1]
    shape = (cols, count * SUB)
    place = (iota(shape, 1) // SUB + start) % cols
    pick = (place == iota(shape, 0)).astype(BF16)
    high, low = halves(matrix)
    return product(high, pick) + product(low, pick)


def spread(wide):
    rows, cols = wide.shape
    tall = jnp.broadcast_to(wide[:, None, :], (rows, SUB, cols)).reshape(rows * SUB, cols)
    return jnp.where(iota(tall.shape, 0) % SUB == iota(tall.shape, 1) % SUB, tall, 0.0)


def mix(weights, values):
    high, low = halves(values)
    rows = weights[0].shape[0]
    both = product(jnp.concatenate(weights, axis=0), high)
    return both[:rows] + (product(weights[0], low) + both[rows:])


def one_hot(index, size):
    rows = lax.broadcasted_iota(jnp.int32, (size, index.shape[1]), 0)
    return jnp.where(rows == index, 1.0, 0.0).astype(BF16)


def column_as_row(column, lane, offset):
    n = column.shape[0]
    place = lax.broadcasted_iota(jnp.int32, (n, 128), 1) == lax.broadcasted_iota(jnp.int32, (n, 128), 0) + offset
    return jnp.sum(jnp.where(place, column, 0.0), axis=0, keepdims=True)


def row_as_column(row, n, offset):
    place = lax.broadcasted_iota(jnp.int32, (n, 128), 1) == lax.broadcasted_iota(jnp.int32, (n, 128), 0) + offset
    return jnp.sum(jnp.where(place, row, 0.0), axis=1, keepdims=True)


def edge_rows(values):
    n = values.shape[0]
    row = column_as_row(values[:, -1:], None, 0) + column_as_row(values[:, :1], None, n)
    return jnp.broadcast_to(row, (EXTRA, 128))


def factor_of(counts_ref, weight_ref, d):
    slot = lax.broadcasted_iota(jnp.int32, (1, weight_ref.shape[2]), 1)
    return jnp.where(slot < counts_ref[0, d], weight_ref[0, pl.ds(d, 1), :], 0.0)


def loop(n, step, init):
    return lax.fori_loop(0, n, step, init, unroll=n if n <= 8 else 1)


def mix_kernel(lev_ref, loc_ref, mix_ref, own_ref, given_ref):
    levels = loc_ref.shape[0]
    start = lev_ref[0] * levels
    loc = loc_ref[...]
    mix_ref[0], mix_ref[1] = halves(spread(wide_rows(loc, start, 2 * levels)))
    own_ref[0], own_ref[1] = halves(spread(wide_rows(loc, start, levels)).T)
    given_ref[...] = wide_rows(loc, levels - start, levels)


def sum_kernel(perturb_ref, control_ref, other_ref, mix_ref, out_ref):
    levels, members, cols = perturb_ref.shape
    perturb = perturb_ref[...].astype(F32)
    total = jnp.zeros((levels, SUB, cols), F32)
    for m in range(0, members, SUB):
        tile = jnp.concatenate([control_ref[:, m : m + SUB, :], other_ref[:, m : m + SUB, :]], axis=0)
        mixed = mix((mix_ref[0], mix_ref[1]), tile.reshape(2 * levels * SUB, cols))
        total = total + perturb[:, m : m + SUB, :] * mixed.reshape(levels, SUB, cols)
    out_ref[...] = jnp.sum(total, axis=1)


def band_kernel(counts_ref, sum_ref, static_ref, src_ref, weight_ref, out_ref, acc_ref):
    levels, cols = sum_ref.shape
    acc_ref[...] = jnp.concatenate(halves(sum_ref[...]), axis=0)
    n = src_ref.shape[1]
    edges = edge_rows(static_ref[...])

    def step(d, carry):
        chosen = one_hot(src_ref[0, pl.ds(d, 1), :], cols)
        both = product(acc_ref[...], chosen)
        payload = (both[:levels] + both[levels:]) * factor_of(counts_ref, weight_ref, d)
        for g in range(out_ref.shape[0]):
            out_ref[g, d, :levels, :] = payload
            out_ref[g, d, levels:, :] = edges
        return carry

    loop(n, step, 0)


def tile_kernel(pos_ref, arrived_ref, tgt_ref, static_ref, diag_ref, off_ref, obs_ref, innov_ref,
                increment_ref, partial_ref, out_ref):
    levels, cols = static_ref.shape
    groups, n = arrived_ref.shape[:2]
    me = pos_ref[0]

    def step(s, total):
        values = sum(arrived_ref[g, s, :levels, :] for g in range(groups))
        chosen = one_hot(tgt_ref[0, pl.ds(s, 1), :], cols)
        return total + select(values, chosen, ((1,), (1,)))

    remapped = loop(n, step, jnp.zeros((levels, cols), F32))
    before = arrived_ref[0, jnp.maximum(me - 1, 0), levels : levels + 1, :]
    after = arrived_ref[0, jnp.minimum(me + 1, n - 1), levels : levels + 1, :]
    before = jnp.where(me > 0, row_as_column(before, levels, 0), 0.0)
    after = jnp.where(me < n - 1, row_as_column(after, levels, levels), 0.0)
    static = static_ref[...]
    lane = lax.broadcasted_iota(jnp.int32, (levels, cols), 1)
    left = jnp.where(lane == 0, before, pltpu.roll(static, 1, 1))
    right = jnp.where(lane == cols - 1, after, pltpu.roll(static, cols - 1, 1))
    increment = remapped + diag_ref[...] * static + off_ref[...] * (left + right)
    increment_ref[...] = increment
    misfit = obs_ref[...] * (increment - innov_ref[...])
    coupled = off_ref[...] * misfit
    left = jnp.where(lane == 0, 0.0, pltpu.roll(coupled, 1, 1))
    right = jnp.where(lane == cols - 1, 0.0, pltpu.roll(coupled, cols - 1, 1))
    partial_ref[...] = static + diag_ref[...] * misfit + left + right
    edges = edge_rows(coupled)
    both = jnp.concatenate(halves(misfit), axis=0)

    def give(s, carry):
        chosen = one_hot(tgt_ref[0, pl.ds(s, 1), :], cols)
        picked = product(both, chosen)
        out_ref[s, :levels, :] = picked[:levels] + picked[levels:]
        out_ref[s, levels:, :] = edges
        return carry

    loop(n, give, 0)


def adjoint_kernel(band, pos_ref, counts_ref, returned_ref, src_ref, weight_ref, partial_ref, mix_ref, grad_ref, out_ref):
    levels, cols = partial_ref.shape
    n = returned_ref.shape[0]
    me = pos_ref[0]

    def step(d, total):
        values = returned_ref[d, :levels, :] * factor_of(counts_ref, weight_ref, d)
        return total + select(values, one_hot(src_ref[0, pl.ds(d, 1), :], band), ((1,), (1,)))

    out_ref[...] = band_rows(loop(n, step, jnp.zeros((levels, band), F32)), mix_ref[...])
    before = returned_ref[jnp.maximum(me - 1, 0), levels : levels + 1, :]
    after = returned_ref[jnp.minimum(me + 1, n - 1), levels : levels + 1, :]
    before = jnp.where(me > 0, row_as_column(before, levels, 0), 0.0)
    after = jnp.where(me < n - 1, row_as_column(after, levels, levels), 0.0)
    lane = lax.broadcasted_iota(jnp.int32, (levels, cols), 1)
    grad_ref[...] = partial_ref[...] + (jnp.where(lane == 0, before, 0.0) + jnp.where(lane == cols - 1, after, 0.0))


def band_rows(band, weights):
    width = weights.shape[1]
    return jnp.concatenate([band[:, at : at + width] for at in range(0, band.shape[1], width)] + [weights], axis=0)


def ens_tiles(perturb_ref, rows_ref, weights, before_ref):
    levels, members, cols = perturb_ref.shape
    width = rows_ref.shape[1]
    parts = [rows_ref[i * levels : (i + 1) * levels, :] for i in range(cols // width)]
    grad = jnp.concatenate(parts, axis=1)[:, None, :]
    perturb = perturb_ref[...].astype(F32)
    for m in range(0, members, SUB):
        place = (slice(None), slice(m, m + SUB), slice(None))
        tile = (perturb[place] * grad).reshape(levels * SUB, cols)
        yield place, before_ref[place] + mix(weights, tile).reshape(levels, SUB, cols)


def ens_own_kernel(perturb_ref, mine_ref, weights_ref, control_ref, out_ref):
    for place, values in ens_tiles(perturb_ref, mine_ref, (weights_ref[0], weights_ref[1]), control_ref):
        out_ref[place] = values


def ens_kernel(perturb_ref, theirs_ref, own_ref, *refs):
    count = (len(refs) - 3) // 2
    flats, (out_hbm, *flat_hbms), (out_ref, sems) = refs[:count], refs[count : 2 * count + 1], refs[2 * count + 1 :]
    copies = [pltpu.make_async_copy(a, b, sems.at[i]) for i, (a, b) in enumerate(zip(flats, flat_hbms))]
    for copy in copies:
        copy.start()
    levels = perturb_ref.shape[0]
    weights = halves(spread(theirs_ref[theirs_ref.shape[0] - levels :, :]).T)
    for place, values in ens_tiles(perturb_ref, theirs_ref, weights, own_ref):
        out_ref[place] = values
        copies.append(pltpu.make_async_copy(out_ref.at[place], out_hbm.at[place], sems.at[len(copies)]))
        copies[-1].start()
    for copy in copies:
        copy.wait()


class Rows:
    def __init__(self, levels, n):
        self.weight = slice(0, levels)
        self.base = slice(levels, 2 * levels)
        at = 2 * levels
        self.factor, self.index, self.edge = at, at + n, at + 2 * n
        self.total = at + 2 * n + EXTRA


def static_kernel(band, pos_ref, counts_ref, static_ref, diag_ref, off_ref, obs_ref, innov_ref, src_ref, weight_ref, tgt_ref,
                  *out_refs):
    levels, cols = static_ref.shape
    n = len(out_refs)
    cap = src_ref.shape[2]
    rows = Rows(levels, n)
    peers = [pos_ref[0] ^ r for r in range(n)]
    static, off, obs = static_ref[...], off_ref[...], obs_ref[...]
    lane = lax.broadcasted_iota(jnp.int32, (levels, cols), 1)
    left = jnp.where(lane == 0, 0.0, pltpu.roll(static, 1, 1))
    right = jnp.where(lane == cols - 1, 0.0, pltpu.roll(static, cols - 1, 1))
    base = diag_ref[...] * static + off * (left + right) - innov_ref[...]
    coupled = off * obs
    ends = [v[:, i] for v in (static, coupled, base) for i in (slice(cols - 1, cols), slice(0, 1))]
    edge = sum(column_as_row(end, None, i * levels) for i, end in enumerate(ends))
    place = lax.broadcasted_iota(jnp.int32, (1, cap), 1)
    edge = edge + jnp.where(place == 6 * levels, off[:, cols - 1 :], 0.0)
    edge = edge + jnp.where(place == 6 * levels + 1, off[:, :1], 0.0)
    edge = jnp.broadcast_to(edge, (EXTRA, cap))
    both = jnp.concatenate(halves(jnp.concatenate([obs, base], axis=0)), axis=0)
    tgts = [tgt_ref[0, pl.ds(peer, 1), :] for peer in peers]
    src = jnp.concatenate([src_ref[0, pl.ds(peer, 1), :] for peer in peers], axis=0).astype(F32)
    index = jnp.concatenate(tgts, axis=0).astype(F32) * float(band) + src
    factor = jnp.concatenate([factor_of(counts_ref, weight_ref, peer) for peer in peers], axis=0)
    for r, out_ref in enumerate(out_refs):
        picked = product(both, one_hot(tgts[r], cols))
        out_ref[: 2 * levels, :] = picked[: 2 * levels] + picked[2 * levels :]
        out_ref[rows.factor : rows.factor + n, :] = factor
        out_ref[rows.index : rows.index + n, :] = index
        out_ref[rows.edge :, :] = edge


def blocks_kernel(groups, levels, relayed, *refs):
    sums, refs = refs[:groups], refs[groups:]
    count = (len(refs) - 1 - relayed) // 2
    rests, relays, total_ref, out_refs = refs[:count], refs[count : count + relayed], refs[count + relayed], refs[-count:]
    total = sum(ref[...] for ref in sums)
    cap = total_ref.shape[1]
    total = jnp.concatenate([total[:, at : at + cap] for at in range(0, total.shape[1], cap)], axis=0)
    total_ref[...] = total
    for i, (rest_ref, out_ref) in enumerate(zip(rests, out_refs)):
        parts = [total, rest_ref[...]]
        if i == count - 1:
            parts += [ref[: 2 * levels, :] for ref in relays]
        out_ref[...] = jnp.concatenate(parts, axis=0)


def relay_kernel(levels, stacked, count, got_ref, *refs):
    total = got_ref.shape[0]
    own_refs, out_refs = refs[:count], refs[count:]
    head = total - len(out_refs) * 2 * levels
    alone = len(out_refs) - len(own_refs)
    for i, out_ref in enumerate(out_refs):
        at = head + 2 * levels * i
        parts = [got_ref[:stacked, :], got_ref[at : at + 2 * levels, :], got_ref[stacked + 2 * levels : head, :]]
        if i >= alone:
            parts = [own_refs[i - alone][...], *parts]
        out_ref[...] = jnp.concatenate(parts, axis=0)


class Block:
    def __init__(self, refs, n, levels, band, base=0):
        cap = refs[0].shape[1]
        self.levels, self.parts, self.cap = levels, band // cap, cap
        self.sums_ref, self.rest_ref = refs[0], refs[-1]
        self.base = base
        self.head = 0 if len(refs) == 2 else base + self.parts * levels
        self.rows = Rows(levels, n)
        words = self.rest(self.rows.index, n)
        self.tgt = jnp.floor((words + 0.5) * (1.0 / band))
        self.src = words - self.tgt * float(band)
        self.factor = self.rest(self.rows.factor, n)

    def rest(self, at, size):
        return self.rest_ref[self.head + at : self.head + at + size, :]

    def sums(self):
        base = self.base
        parts = [self.sums_ref[base + i * self.levels : base + (i + 1) * self.levels, :] for i in range(self.parts)]
        return jnp.concatenate(halves(jnp.concatenate(parts, axis=1)), axis=0)


def line(table, i):
    return table[i : i + 1]


def pick_source(block, r):
    band = block.parts * block.cap
    column = lax.broadcasted_iota(jnp.int32, (band, block.cap), 0).astype(F32)
    return jnp.where(column == line(block.src, r), 1.0, 0.0).astype(BF16)


def fill_slots(bands, blocks, n, slots_ref):
    for i, s in enumerate(bands):
        block = blocks[s]
        both = block.sums()
        for d in range(n):
            picked = product(both, pick_source(block, s ^ d))
            values = (picked[: block.levels] + picked[block.levels :]) * line(block.factor, s ^ d)
            slots_ref[d, :, i * block.cap : (i + 1) * block.cap] = jnp.concatenate(halves(values), axis=0)


def met_at(d, block, bands, slots_ref):
    own = jnp.broadcast_to(line(block.tgt, d), (block.cap, block.cap)).T
    same = [jnp.where(own == line(block.tgt, s ^ d), 1.0, 0.0).astype(BF16) for s in bands]
    met = product(slots_ref[d], jnp.concatenate(same, axis=1), ((1,), (1,)))
    return met[: block.levels] + met[block.levels :]


def land(table, bands, slots_ref, cols):
    cap = table.shape[1]
    row = lax.broadcasted_iota(jnp.int32, (cols, cap), 0).astype(F32)
    total = 0.0
    for i, s in enumerate(bands):
        landing = jnp.where(row == line(table, s), 1.0, 0.0).astype(BF16)
        total = total + product(slots_ref[0, :, i * cap : (i + 1) * cap], landing, ((1,), (1,)))
    levels = total.shape[0] // 2
    return total[:levels] + total[levels:]


def open_blocks(labels, refs, n, levels, band):
    blocks = {0: Block(refs[:2], n, levels, band)}
    refs = refs[2:]
    for i, r in enumerate(labels[1:]):
        base = refs[i].shape[0] // 2 if r >= n // 2 + n // 4 else 0
        blocks[r] = Block(refs[i : i + 1], n, levels, band, base)
    return blocks, refs[len(labels) - 1 :]


def stage_kernel(n, levels, band, cols, stages, *refs):
    known = sum(stages[:-1], [])
    blocks, refs = open_blocks(known + stages[-1], refs, n, levels, band)
    old, refs = refs[: len(stages) - 1], refs[len(stages) - 1 :]
    if known:
        met_old, remap_old, slots_ref, met_ref, remap_ref = refs
    else:
        slots_ref, met_ref, remap_ref, pick_ref = refs
        for d in range(n):
            pick_ref[d] = pick_source(blocks[0], d)
    fill_slots(stages[-1], blocks, n, slots_ref)
    for i, (d, block) in enumerate(blocks.items()):
        met = met_at(d, block, stages[-1], slots_ref)
        if d in known:
            met = met + met_old[i]
        else:
            for bands, ref in zip(stages, old):
                met = met + met_at(d, block, bands, ref)
        met_ref[i] = met
    landed = land(blocks[0].tgt, stages[-1], slots_ref, cols)
    remap_ref[...] = landed + remap_old[...] if known else landed


def shared_kernel(n, levels, band, cols, stages, pos_ref, mix_ref, *refs):
    known = sum(stages[:-1], [])
    blocks, refs = open_blocks(known + stages[-1], refs, n, levels, band)
    old, refs = refs[: len(stages) - 1], refs[len(stages) - 1 :]
    met_old, pick_ref, out_ref, slots_ref, tables_ref = refs
    me = pos_ref[0]
    for r, block in blocks.items():
        there = me ^ r
        tables_ref[there, :n, :] = block.tgt
        tables_ref[there, n:, :] = block.rest(block.rows.edge, EXTRA)
    fill_slots(stages[-1], blocks, n, slots_ref)
    last = cols - 1.0
    total = jnp.zeros((levels, band), F32)
    for i, (d, block) in enumerate(blocks.items()):
        value = met_at(d, block, stages[-1], slots_ref) + block.rest(levels, levels)
        if d in known:
            value = value + met_old[i]
        else:
            for bands, ref in zip(stages, old):
                value = value + met_at(d, block, bands, ref)
        edge = block.rest(block.rows.edge, 1)
        own = line(block.tgt, d)
        there = me ^ d
        before = tables_ref[jnp.maximum(there - 1, 0), n : n + 1, :]
        near = jnp.where((own == 0.0) & (there > 0), edge[:, 6 * levels + 1 : 6 * levels + 2], 0.0)
        value = value + row_as_column(before, levels, 0) * near
        after = tables_ref[jnp.minimum(there + 1, n - 1), n : n + 1, :]
        near = jnp.where((own == last) & (there < n - 1), edge[:, 6 * levels : 6 * levels + 1], 0.0)
        value = value + row_as_column(after, levels, levels) * near
        given = block.rest(0, levels) * value * line(blocks[0].factor, d)
        total = total + select(given, pick_ref[d], ((1,), (1,)))
    out_ref[...] = band_rows(total, mix_ref[...])


def outputs_kernel(stages, pos_ref, *refs):
    slots_refs, refs = refs[: len(stages)], refs[len(stages) :]
    remap_ref, tables_ref, static_ref, diag_ref, off_ref, obs_ref, innov_ref, increment_ref, grad_ref = refs
    levels, cols = static_ref.shape
    n = tables_ref.shape[0]
    cap = tables_ref.shape[2]
    me = pos_ref[0]
    given = [
        (s, ref, slice(i * cap, (i + 1) * cap)) for bands, ref in zip(stages, slots_refs) for i, s in enumerate(bands)
    ]
    remapped = remap_ref[...] + land(tables_ref[me, :n, :], stages[-1], slots_refs[-1], cols)
    static, off = static_ref[...], off_ref[...]
    lane = lax.broadcasted_iota(jnp.int32, (levels, cols), 1)

    def beside(there, exists, column, own_end, side):
        edge = tables_ref[there, n : n + 1, :]
        static_end, coupling, base = (row_as_column(edge, levels, (2 * i + side) * levels) for i in range(3))
        far = me ^ there
        landed = []
        for s, ref, place in given:
            values = ref[far, :levels, place].astype(F32) + ref[far, levels:, place].astype(F32)
            landed.append(jnp.where(tables_ref[there, pl.ds(s ^ far, 1), :] == column, values, 0.0))
        remap_end = jnp.sum(sum(landed), axis=1, keepdims=True)
        off_end = edge[:, 6 * levels + side : 6 * levels + side + 1]
        coupled = coupling * (remap_end + base + off_end * own_end)
        return jnp.where(exists, static_end, 0.0), jnp.where(exists, coupled, 0.0)

    before, coupled_before = beside(jnp.maximum(me - 1, 0), me > 0, cols - 1.0, static[:, :1], 0)
    after, coupled_after = beside(jnp.minimum(me + 1, n - 1), me < n - 1, 0.0, static[:, cols - 1 :], 1)
    left = jnp.where(lane == 0, before, pltpu.roll(static, 1, 1))
    right = jnp.where(lane == cols - 1, after, pltpu.roll(static, cols - 1, 1))
    increment = remapped + diag_ref[...] * static + off * (left + right)
    increment_ref[...] = increment
    misfit = obs_ref[...] * (increment - innov_ref[...])
    coupled = off * misfit
    left = jnp.where(lane == 0, coupled_before, pltpu.roll(coupled, 1, 1))
    right = jnp.where(lane == cols - 1, coupled_after, pltpu.roll(coupled, cols - 1, 1))
    grad_ref[...] = static + diag_ref[...] * misfit + left + right


def call(kernel, out_shape, spaces, scratch=(), out=VMEM, cost=None):
    return pl.pallas_call(
        kernel,
        out_shape=out_shape,
        in_specs=spaces,
        out_specs=jax.tree.map(lambda _: out, out_shape),
        scratch_shapes=scratch,
        cost_estimate=cost,
        compiler_params=pltpu.CompilerParams(vmem_limit_bytes=40 * MIB),
    )


def body(
    perturb,
    control,
    level_loc,
    static_control,
    filter_diag,
    filter_off,
    send_src,
    send_wt,
    counts,
    recv_tgt,
    obs_weight,
    innovation,
):
    levels, members, band_cols = control.shape
    tile_cols = static_control.shape[1]
    n = lax.axis_size("tile")
    groups = lax.axis_size("grp")
    cap = send_src.shape[2]
    shape = jax.ShapeDtypeStruct
    swap = [(0, 1), (1, 0)]
    lev = lax.axis_index("lev").astype(jnp.int32).reshape(1)
    pos = lax.axis_index("tile").astype(jnp.int32).reshape(1)
    other_control = lax.ppermute(control, "lev", swap)
    width = levels * SUB
    level_mix, own_mix, given_mix = call(
        mix_kernel,
        (shape((2, width, 2 * width), BF16), shape((2, width, width), BF16), shape((levels, width), F32)),
        [SMEM, VMEM],
        cost=pl.CostEstimate(flops=10**9, bytes_accessed=0, transcendentals=0),
    )(lev, level_loc)
    own_sum = call(sum_kernel, shape((levels, band_cols), F32), [VMEM] * 4)(perturb, control, other_control, level_mix)
    flat = shape((levels, tile_cols), F32)
    mine_shape = shape((band_cols // width * levels + levels, width), F32)
    diag, off = filter_diag.reshape(1, -1), filter_off.reshape(1, -1)
    if n * cap <= tile_cols and n >= 4 and lax.axis_size("lev") == 2 and n & (n - 1) == 0 and band_cols * tile_cols <= 2**20:
        rows = Rows(levels, n)
        stacked = band_cols // cap * levels
        rests = call(functools.partial(static_kernel, band_cols), [shape((rows.total, cap), F32)] * n, [SMEM] * 2 + [VMEM] * 8)(
            pos, counts, static_control, diag, off, obs_weight, innovation, send_src, send_wt, recv_tgt
        )
        sums = [own_sum]
        sums[0], other_perturb = lax.optimization_barrier((sums[0], lax.ppermute(perturb, "lev", swap)))
        for k in range(1, groups):
            sums.append(lax.ppermute(sums[0], "grp", [(g, (g + k) % groups) for g in range(groups)]))
        low, high = n // 4, n // 2
        pairs_of = [r for k in reversed(range(low + 1, high)) for r in (k, k + high)]
        stages = [[0, *range(1, low), high], [r + high for r in range(1, low)] + pairs_of, [low, low + high]]
        block = stacked + rows.total
        total, *blocks = call(
            functools.partial(blocks_kernel, groups, levels, high - 1),
            [shape((stacked, cap), F32)]
            + [shape((block, cap), F32)] * (high - 1)
            + [shape((block + 2 * levels * (high - 1), cap), F32)],
            [VMEM] * (groups + n - 1),
        )(*sums, *rests[1:])

        def to(r, block):
            return [lax.ppermute(block, "tile", [(i, i ^ r) for i in range(n)])]

        arrived = {0: [total, rests[0]]} | {r: to(r, blocks[r - 1]) for r in (high, *range(1, low))}
        passed = call(
            functools.partial(relay_kernel, levels, stacked, high - low),
            [shape((block * (1 + (r >= low)), cap), F32) for r in range(1, high)],
            [VMEM] * (1 + high - low),
        )(*arrived[high], *blocks[low - 1 : high - 1])
        for r in reversed(range(1, high)):
            arrived[r + high] = to(r, passed[r - 1])
            if r >= low:
                arrived[r] = arrived[r + high]
        slots, carried, picks = [], [], []
        for count in range(1, len(stages)):
            labels = sum(stages[:count], [])
            refs = [ref for r in labels for ref in arrived[r]]
            outs = [
                shape((n, 2 * levels, len(stages[count - 1]) * cap), BF16),
                shape((len(labels), levels, cap), F32),
                flat,
            ] + [shape((n, band_cols, cap), BF16)] * (count == 1)
            new, *carried = call(
                functools.partial(stage_kernel, n, levels, band_cols, tile_cols, stages[:count]),
                outs,
                [VMEM] * (len(refs) + len(slots) + len(carried)),
                cost=pl.CostEstimate(flops=10**9 if count == 1 else 10**6, bytes_accessed=0, transcendentals=0),
            )(*refs, *slots, *carried)
            slots.append(new)
            picks += carried[2:]
            carried = carried[:2]
        met, remap = carried
        refs = [ref for r in sum(stages, []) for ref in arrived[r]] + slots + [met] + picks
        mine, new, tables = call(
            functools.partial(shared_kernel, n, levels, band_cols, tile_cols, stages),
            (mine_shape, shape((n, 2 * levels, len(stages[-1]) * cap), BF16), shape((n, n + EXTRA, cap), F32)),
            [SMEM] + [VMEM] * (1 + len(refs)),
            cost=pl.CostEstimate(flops=10**9, bytes_accessed=0, transcendentals=0),
        )(pos, given_mix, *refs)
        slots.append(new)
        increment, grad_static = call(
            functools.partial(outputs_kernel, stages), (flat, flat), [SMEM] + [VMEM] * (len(slots) + 7)
        )(pos, *slots, remap, tables, static_control, diag, off, obs_weight, innovation)
    else:
        other_perturb = lax.ppermute(perturb, "lev", swap)
        payload = call(
            band_kernel,
            shape((groups, n, levels + EXTRA, cap), F32),
            [SMEM] + [VMEM] * 4,
            [pltpu.VMEM((2 * levels, band_cols), BF16)],
        )(counts, own_sum, static_control, send_src, send_wt)
        arrived = lax.all_to_all(
            payload.reshape(groups * n, levels + EXTRA, cap), ("grp", "tile"), split_axis=0, concat_axis=0, tiled=True
        ).reshape(groups, n, levels + EXTRA, cap)
        increment, partial, giving = call(
            tile_kernel, (flat, flat, shape((n, levels + EXTRA, cap), F32)), [SMEM] + [VMEM] * 7
        )(pos, arrived, recv_tgt, static_control, diag, off, obs_weight, innovation)
        returned = lax.all_to_all(giving, "tile", split_axis=0, concat_axis=0, tiled=True)
        grad_static, mine = call(
            functools.partial(adjoint_kernel, band_cols), (flat, mine_shape), [SMEM, SMEM] + [VMEM] * 5
        )(pos, counts, returned, send_src, send_wt, partial, given_mix)
    theirs = lax.ppermute(mine, "lev", swap)
    own = call(ens_own_kernel, shape(control.shape, F32), [VMEM] * 4)(perturb, mine, own_mix, control)
    grad_ens, increment, grad_static = call(
        ens_kernel,
        (shape(control.shape, F32), flat, flat),
        [VMEM] * 5,
        [pltpu.VMEM(control.shape, F32), pltpu.SemaphoreType.DMA((2 + members // SUB,))],
        out=HBM,
    )(other_perturb, theirs, own, increment, grad_static)
    return (increment, grad_static, grad_ens)


def solution(mesh):
    return jax.shard_map(
        body,
        mesh=mesh,
        in_specs=(
            P("lev", "grp", "tile"),
            P("lev", "grp", "tile"),
            P("lev", None),
            P("lev", "tile"),
            P("tile"),
            P("tile"),
            P("tile", None, None),
            P("tile", None, None),
            P("tile", None),
            P("tile", None, None),
            P("lev", "tile"),
            P("lev", "tile"),
        ),
        out_specs=(P("lev", "tile"), P("lev", "tile"), P("lev", "grp", "tile")),
        check_vma=False,
    )
```

```python
import functools

import jax
import jax.numpy as jnp
from jax import lax
from jax.experimental import pallas as pl
from jax.experimental.pallas import tpu as pltpu
from jax.sharding import PartitionSpec as P

F32 = jnp.float32
BF16 = jnp.bfloat16
SUB = 8
EXTRA = 8
VMEM = pl.BlockSpec(memory_space=pltpu.VMEM)
HBM = pl.BlockSpec(memory_space=pltpu.HBM)
SMEM = pl.BlockSpec(memory_space=pltpu.SMEM)
MIB = 1024 * 1024


def halves(values):
    high = values.astype(BF16)
    low = (values - high.astype(F32)).astype(BF16)
    return high, low


def product(a, b, dims=((1,), (0,))):
    return lax.dot_general(a, b, (dims, ((), ())), preferred_element_type=F32)


def select(values, chosen, dims=((1,), (0,))):
    rows = values.shape[0]
    both = product(jnp.concatenate(halves(values), axis=0), chosen, dims)
    return both[:rows] + both[rows:]


def iota(shape, axis):
    return lax.broadcasted_iota(jnp.int32, shape, axis)


def wide_rows(matrix, start, count):
    cols = matrix.shape[1]
    shape = (cols, count * SUB)
    place = (iota(shape, 1) // SUB + start) % cols
    pick = (place == iota(shape, 0)).astype(BF16)
    high, low = halves(matrix)
    return product(high, pick) + product(low, pick)


def spread(wide):
    rows, cols = wide.shape
    tall = jnp.broadcast_to(wide[:, None, :], (rows, SUB, cols)).reshape(rows * SUB, cols)
    return jnp.where(iota(tall.shape, 0) % SUB == iota(tall.shape, 1) % SUB, tall, 0.0)


def mix(weights, values):
    high, low = halves(values)
    rows = weights[0].shape[0]
    both = product(jnp.concatenate(weights, axis=0), high)
    return both[:rows] + (product(weights[0], low) + both[rows:])


def one_hot(index, size):
    rows = lax.broadcasted_iota(jnp.int32, (size, index.shape[1]), 0)
    return jnp.where(rows == index, 1.0, 0.0).astype(BF16)


def column_as_row(column, lane, offset):
    n = column.shape[0]
    place = lax.broadcasted_iota(jnp.int32, (n, 128), 1) == lax.broadcasted_iota(jnp.int32, (n, 128), 0) + offset
    return jnp.sum(jnp.where(place, column, 0.0), axis=0, keepdims=True)


def row_as_column(row, n, offset):
    place = lax.broadcasted_iota(jnp.int32, (n, 128), 1) == lax.broadcasted_iota(jnp.int32, (n, 128), 0) + offset
    return jnp.sum(jnp.where(place, row, 0.0), axis=1, keepdims=True)


def edge_rows(values):
    n = values.shape[0]
    row = column_as_row(values[:, -1:], None, 0) + column_as_row(values[:, :1], None, n)
    return jnp.broadcast_to(row, (EXTRA, 128))


def factor_of(counts_ref, weight_ref, d):
    slot = lax.broadcasted_iota(jnp.int32, (1, weight_ref.shape[2]), 1)
    return jnp.where(slot < counts_ref[0, d], weight_ref[0, pl.ds(d, 1), :], 0.0)


def loop(n, step, init):
    return lax.fori_loop(0, n, step, init, unroll=n if n <= 8 else 1)


def mix_kernel(lev_ref, loc_ref, mix_ref, own_ref, given_ref):
    levels = loc_ref.shape[0]
    start = lev_ref[0] * levels
    loc = loc_ref[...]
    mix_ref[0], mix_ref[1] = halves(spread(wide_rows(loc, start, 2 * levels)))
    own_ref[0], own_ref[1] = halves(spread(wide_rows(loc, start, levels)).T)
    given_ref[...] = wide_rows(loc, levels - start, levels)


def sum_kernel(perturb_ref, control_ref, other_ref, mix_ref, out_ref):
    levels, members, cols = perturb_ref.shape
    perturb = perturb_ref[...].astype(F32)
    total = jnp.zeros((levels, SUB, cols), F32)
    for m in range(0, members, SUB):
        tile = jnp.concatenate([control_ref[:, m : m + SUB, :], other_ref[:, m : m + SUB, :]], axis=0)
        mixed = mix((mix_ref[0], mix_ref[1]), tile.reshape(2 * levels * SUB, cols))
        total = total + perturb[:, m : m + SUB, :] * mixed.reshape(levels, SUB, cols)
    out_ref[...] = jnp.sum(total, axis=1)


def band_kernel(counts_ref, sum_ref, static_ref, src_ref, weight_ref, out_ref, acc_ref):
    levels, cols = sum_ref.shape
    acc_ref[...] = jnp.concatenate(halves(sum_ref[...]), axis=0)
    n = src_ref.shape[1]
    edges = edge_rows(static_ref[...])

    def step(d, carry):
        chosen = one_hot(src_ref[0, pl.ds(d, 1), :], cols)
        both = product(acc_ref[...], chosen)
        payload = (both[:levels] + both[levels:]) * factor_of(counts_ref, weight_ref, d)
        for g in range(out_ref.shape[0]):
            out_ref[g, d, :levels, :] = payload
            out_ref[g, d, levels:, :] = edges
        return carry

    loop(n, step, 0)


def tile_kernel(pos_ref, arrived_ref, tgt_ref, static_ref, diag_ref, off_ref, obs_ref, innov_ref,
                increment_ref, partial_ref, out_ref):
    levels, cols = static_ref.shape
    groups, n = arrived_ref.shape[:2]
    me = pos_ref[0]

    def step(s, total):
        values = sum(arrived_ref[g, s, :levels, :] for g in range(groups))
        chosen = one_hot(tgt_ref[0, pl.ds(s, 1), :], cols)
        return total + select(values, chosen, ((1,), (1,)))

    remapped = loop(n, step, jnp.zeros((levels, cols), F32))
    before = arrived_ref[0, jnp.maximum(me - 1, 0), levels : levels + 1, :]
    after = arrived_ref[0, jnp.minimum(me + 1, n - 1), levels : levels + 1, :]
    before = jnp.where(me > 0, row_as_column(before, levels, 0), 0.0)
    after = jnp.where(me < n - 1, row_as_column(after, levels, levels), 0.0)
    static = static_ref[...]
    lane = lax.broadcasted_iota(jnp.int32, (levels, cols), 1)
    left = jnp.where(lane == 0, before, pltpu.roll(static, 1, 1))
    right = jnp.where(lane == cols - 1, after, pltpu.roll(static, cols - 1, 1))
    increment = remapped + diag_ref[...] * static + off_ref[...] * (left + right)
    increment_ref[...] = increment
    misfit = obs_ref[...] * (increment - innov_ref[...])
    coupled = off_ref[...] * misfit
    left = jnp.where(lane == 0, 0.0, pltpu.roll(coupled, 1, 1))
    right = jnp.where(lane == cols - 1, 0.0, pltpu.roll(coupled, cols - 1, 1))
    partial_ref[...] = static + diag_ref[...] * misfit + left + right
    edges = edge_rows(coupled)
    both = jnp.concatenate(halves(misfit), axis=0)

    def give(s, carry):
        chosen = one_hot(tgt_ref[0, pl.ds(s, 1), :], cols)
        picked = product(both, chosen)
        out_ref[s, :levels, :] = picked[:levels] + picked[levels:]
        out_ref[s, levels:, :] = edges
        return carry

    loop(n, give, 0)


def adjoint_kernel(band, pos_ref, counts_ref, returned_ref, src_ref, weight_ref, partial_ref, mix_ref, grad_ref, out_ref):
    levels, cols = partial_ref.shape
    n = returned_ref.shape[0]
    me = pos_ref[0]

    def step(d, total):
        values = returned_ref[d, :levels, :] * factor_of(counts_ref, weight_ref, d)
        return total + select(values, one_hot(src_ref[0, pl.ds(d, 1), :], band), ((1,), (1,)))

    out_ref[...] = band_rows(loop(n, step, jnp.zeros((levels, band), F32)), mix_ref[...])
    before = returned_ref[jnp.maximum(me - 1, 0), levels : levels + 1, :]
    after = returned_ref[jnp.minimum(me + 1, n - 1), levels : levels + 1, :]
    before = jnp.where(me > 0, row_as_column(before, levels, 0), 0.0)
    after = jnp.where(me < n - 1, row_as_column(after, levels, levels), 0.0)
    lane = lax.broadcasted_iota(jnp.int32, (levels, cols), 1)
    grad_ref[...] = partial_ref[...] + (jnp.where(lane == 0, before, 0.0) + jnp.where(lane == cols - 1, after, 0.0))


def band_rows(band, weights):
    width = weights.shape[1]
    return jnp.concatenate([band[:, at : at + width] for at in range(0, band.shape[1], width)] + [weights], axis=0)


def ens_tiles(perturb_ref, rows_ref, weights, before_ref):
    levels, members, cols = perturb_ref.shape
    width = rows_ref.shape[1]
    parts = [rows_ref[i * levels : (i + 1) * levels, :] for i in range(cols // width)]
    grad = jnp.concatenate(parts, axis=1)[:, None, :]
    perturb = perturb_ref[...].astype(F32)
    for m in range(0, members, SUB):
        place = (slice(None), slice(m, m + SUB), slice(None))
        tile = (perturb[place] * grad).reshape(levels * SUB, cols)
        yield place, before_ref[place] + mix(weights, tile).reshape(levels, SUB, cols)


def ens_own_kernel(perturb_ref, mine_ref, weights_ref, control_ref, out_ref):
    for place, values in ens_tiles(perturb_ref, mine_ref, (weights_ref[0], weights_ref[1]), control_ref):
        out_ref[place] = values


def ens_kernel(perturb_ref, theirs_ref, own_ref, *refs):
    count = (len(refs) - 3) // 2
    flats, (out_hbm, *flat_hbms), (out_ref, sems) = refs[:count], refs[count : 2 * count + 1], refs[2 * count + 1 :]
    copies = [pltpu.make_async_copy(a, b, sems.at[i]) for i, (a, b) in enumerate(zip(flats, flat_hbms))]
    for copy in copies:
        copy.start()
    levels = perturb_ref.shape[0]
    weights = halves(spread(theirs_ref[theirs_ref.shape[0] - levels :, :]).T)
    for place, values in ens_tiles(perturb_ref, theirs_ref, weights, own_ref):
        out_ref[place] = values
        copies.append(pltpu.make_async_copy(out_ref.at[place], out_hbm.at[place], sems.at[len(copies)]))
        copies[-1].start()
    for copy in copies:
        copy.wait()


class Rows:
    def __init__(self, levels, n):
        self.weight = slice(0, levels)
        self.base = slice(levels, 2 * levels)
        at = 2 * levels
        self.factor, self.index, self.edge = at, at + n, at + 2 * n
        self.total = at + 2 * n + EXTRA


def static_kernel(band, pos_ref, counts_ref, static_ref, diag_ref, off_ref, obs_ref, innov_ref, src_ref, weight_ref, tgt_ref,
                  *out_refs):
    levels, cols = static_ref.shape
    n = len(out_refs)
    cap = src_ref.shape[2]
    rows = Rows(levels, n)
    peers = [pos_ref[0] ^ r for r in range(n)]
    static, off, obs = static_ref[...], off_ref[...], obs_ref[...]
    lane = lax.broadcasted_iota(jnp.int32, (levels, cols), 1)
    left = jnp.where(lane == 0, 0.0, pltpu.roll(static, 1, 1))
    right = jnp.where(lane == cols - 1, 0.0, pltpu.roll(static, cols - 1, 1))
    base = diag_ref[...] * static + off * (left + right) - innov_ref[...]
    coupled = off * obs
    ends = [v[:, i] for v in (static, coupled, base) for i in (slice(cols - 1, cols), slice(0, 1))]
    edge = sum(column_as_row(end, None, i * levels) for i, end in enumerate(ends))
    place = lax.broadcasted_iota(jnp.int32, (1, cap), 1)
    edge = edge + jnp.where(place == 6 * levels, off[:, cols - 1 :], 0.0)
    edge = edge + jnp.where(place == 6 * levels + 1, off[:, :1], 0.0)
    edge = jnp.broadcast_to(edge, (EXTRA, cap))
    both = jnp.concatenate(halves(jnp.concatenate([obs, base], axis=0)), axis=0)
    tgts = [tgt_ref[0, pl.ds(peer, 1), :] for peer in peers]
    src = jnp.concatenate([src_ref[0, pl.ds(peer, 1), :] for peer in peers], axis=0).astype(F32)
    index = jnp.concatenate(tgts, axis=0).astype(F32) * float(band) + src
    factor = jnp.concatenate([factor_of(counts_ref, weight_ref, peer) for peer in peers], axis=0)
    for r, out_ref in enumerate(out_refs):
        picked = product(both, one_hot(tgts[r], cols))
        out_ref[: 2 * levels, :] = picked[: 2 * levels] + picked[2 * levels :]
        out_ref[rows.factor : rows.factor + n, :] = factor
        out_ref[rows.index : rows.index + n, :] = index
        out_ref[rows.edge :, :] = edge


def blocks_kernel(groups, levels, relayed, *refs):
    sums, refs = refs[:groups], refs[groups:]
    count = (len(refs) - 1 - relayed) // 2
    rests, relays, total_ref, out_refs = refs[:count], refs[count : count + relayed], refs[count + relayed], refs[-count:]
    total = sum(ref[...] for ref in sums)
    cap = total_ref.shape[1]
    total = jnp.concatenate([total[:, at : at + cap] for at in range(0, total.shape[1], cap)], axis=0)
    total_ref[...] = total
    for i, (rest_ref, out_ref) in enumerate(zip(rests, out_refs)):
        parts = [total, rest_ref[...]]
        if i == count - 1:
            parts += [ref[: 2 * levels, :] for ref in relays]
        out_ref[...] = jnp.concatenate(parts, axis=0)


def relay_kernel(levels, stacked, got_ref, *out_refs):
    head = got_ref.shape[0] - len(out_refs) * 2 * levels
    for i, out_ref in enumerate(out_refs):
        at = head + 2 * levels * i
        out_ref[...] = jnp.concatenate(
            [got_ref[:stacked, :], got_ref[at : at + 2 * levels, :], got_ref[stacked + 2 * levels : head, :]], axis=0
        )


class Block:
    def __init__(self, refs, n, levels, band):
        cap = refs[0].shape[1]
        self.levels, self.parts, self.cap = levels, band // cap, cap
        self.sums_ref, self.rest_ref = refs[0], refs[-1]
        self.head = 0 if len(refs) == 2 else self.parts * levels
        self.rows = Rows(levels, n)
        words = self.rest(self.rows.index, n)
        self.tgt = jnp.floor((words + 0.5) * (1.0 / band))
        self.src = words - self.tgt * float(band)
        self.factor = self.rest(self.rows.factor, n)

    def rest(self, at, size):
        return self.rest_ref[self.head + at : self.head + at + size, :]

    def sums(self):
        parts = [self.sums_ref[i * self.levels : (i + 1) * self.levels, :] for i in range(self.parts)]
        return jnp.concatenate(halves(jnp.concatenate(parts, axis=1)), axis=0)


def line(table, i):
    return table[i : i + 1]


def pick_source(block, r):
    band = block.parts * block.cap
    column = lax.broadcasted_iota(jnp.int32, (band, block.cap), 0).astype(F32)
    return jnp.where(column == line(block.src, r), 1.0, 0.0).astype(BF16)


def fill_slots(bands, blocks, n, slots_ref):
    for i, s in enumerate(bands):
        block = blocks[s]
        both = block.sums()
        for d in range(n):
            picked = product(both, pick_source(block, s ^ d))
            values = (picked[: block.levels] + picked[block.levels :]) * line(block.factor, s ^ d)
            slots_ref[d, :, i * block.cap : (i + 1) * block.cap] = jnp.concatenate(halves(values), axis=0)


def met_at(d, block, bands, slots_ref):
    own = jnp.broadcast_to(line(block.tgt, d), (block.cap, block.cap)).T
    same = [jnp.where(own == line(block.tgt, s ^ d), 1.0, 0.0).astype(BF16) for s in bands]
    met = product(slots_ref[d], jnp.concatenate(same, axis=1), ((1,), (1,)))
    return met[: block.levels] + met[block.levels :]


def land(table, bands, slots_ref, cols):
    cap = table.shape[1]
    row = lax.broadcasted_iota(jnp.int32, (cols, cap), 0).astype(F32)
    total = 0.0
    for i, s in enumerate(bands):
        landing = jnp.where(row == line(table, s), 1.0, 0.0).astype(BF16)
        total = total + product(slots_ref[0, :, i * cap : (i + 1) * cap], landing, ((1,), (1,)))
    levels = total.shape[0] // 2
    return total[:levels] + total[levels:]


def open_blocks(labels, refs, n, levels, band):
    blocks = {0: Block(refs[:2], n, levels, band)}
    refs = refs[2:]
    for i, r in enumerate(labels[1:]):
        blocks[r] = Block(refs[i : i + 1], n, levels, band)
    return blocks, refs[len(labels) - 1 :]


def stage_kernel(n, levels, band, cols, stages, *refs):
    known = sum(stages[:-1], [])
    blocks, refs = open_blocks(known + stages[-1], refs, n, levels, band)
    old, refs = refs[: len(stages) - 1], refs[len(stages) - 1 :]
    if known:
        met_old, remap_old, slots_ref, met_ref, remap_ref = refs
    else:
        slots_ref, met_ref, remap_ref, pick_ref = refs
        for d in range(n):
            pick_ref[d] = pick_source(blocks[0], d)
    fill_slots(stages[-1], blocks, n, slots_ref)
    for i, (d, block) in enumerate(blocks.items()):
        met = met_at(d, block, stages[-1], slots_ref)
        if d in known:
            met = met + met_old[i]
        else:
            for bands, ref in zip(stages, old):
                met = met + met_at(d, block, bands, ref)
        met_ref[i] = met
    landed = land(blocks[0].tgt, stages[-1], slots_ref, cols)
    remap_ref[...] = landed + remap_old[...] if known else landed


def shared_kernel(n, levels, band, cols, stages, pos_ref, mix_ref, *refs):
    known = sum(stages[:-1], [])
    blocks, refs = open_blocks(known + stages[-1], refs, n, levels, band)
    old, refs = refs[: len(stages) - 1], refs[len(stages) - 1 :]
    met_old, pick_ref, out_ref, slots_ref, tables_ref = refs
    me = pos_ref[0]
    for r, block in blocks.items():
        there = me ^ r
        tables_ref[there, :n, :] = block.tgt
        tables_ref[there, n:, :] = block.rest(block.rows.edge, EXTRA)
    fill_slots(stages[-1], blocks, n, slots_ref)
    last = cols - 1.0
    total = jnp.zeros((levels, band), F32)
    for i, (d, block) in enumerate(blocks.items()):
        value = met_at(d, block, stages[-1], slots_ref) + block.rest(levels, levels)
        if d in known:
            value = value + met_old[i]
        else:
            for bands, ref in zip(stages, old):
                value = value + met_at(d, block, bands, ref)
        edge = block.rest(block.rows.edge, 1)
        own = line(block.tgt, d)
        there = me ^ d
        before = tables_ref[jnp.maximum(there - 1, 0), n : n + 1, :]
        near = jnp.where((own == 0.0) & (there > 0), edge[:, 6 * levels + 1 : 6 * levels + 2], 0.0)
        value = value + row_as_column(before, levels, 0) * near
        after = tables_ref[jnp.minimum(there + 1, n - 1), n : n + 1, :]
        near = jnp.where((own == last) & (there < n - 1), edge[:, 6 * levels : 6 * levels + 1], 0.0)
        value = value + row_as_column(after, levels, levels) * near
        given = block.rest(0, levels) * value * line(blocks[0].factor, d)
        total = total + select(given, pick_ref[d], ((1,), (1,)))
    out_ref[...] = band_rows(total, mix_ref[...])


def outputs_kernel(stages, pos_ref, *refs):
    slots_refs, refs = refs[: len(stages)], refs[len(stages) :]
    remap_ref, tables_ref, static_ref, diag_ref, off_ref, obs_ref, innov_ref, increment_ref, grad_ref = refs
    levels, cols = static_ref.shape
    n = tables_ref.shape[0]
    cap = tables_ref.shape[2]
    me = pos_ref[0]
    given = [
        (s, ref, slice(i * cap, (i + 1) * cap)) for bands, ref in zip(stages, slots_refs) for i, s in enumerate(bands)
    ]
    remapped = remap_ref[...] + land(tables_ref[me, :n, :], stages[-1], slots_refs[-1], cols)
    static, off = static_ref[...], off_ref[...]
    lane = lax.broadcasted_iota(jnp.int32, (levels, cols), 1)

    def beside(there, exists, column, own_end, side):
        edge = tables_ref[there, n : n + 1, :]
        static_end, coupling, base = (row_as_column(edge, levels, (2 * i + side) * levels) for i in range(3))
        far = me ^ there
        landed = []
        for s, ref, place in given:
            values = ref[far, :levels, place].astype(F32) + ref[far, levels:, place].astype(F32)
            landed.append(jnp.where(tables_ref[there, pl.ds(s ^ far, 1), :] == column, values, 0.0))
        remap_end = jnp.sum(sum(landed), axis=1, keepdims=True)
        off_end = edge[:, 6 * levels + side : 6 * levels + side + 1]
        coupled = coupling * (remap_end + base + off_end * own_end)
        return jnp.where(exists, static_end, 0.0), jnp.where(exists, coupled, 0.0)

    before, coupled_before = beside(jnp.maximum(me - 1, 0), me > 0, cols - 1.0, static[:, :1], 0)
    after, coupled_after = beside(jnp.minimum(me + 1, n - 1), me < n - 1, 0.0, static[:, cols - 1 :], 1)
    left = jnp.where(lane == 0, before, pltpu.roll(static, 1, 1))
    right = jnp.where(lane == cols - 1, after, pltpu.roll(static, cols - 1, 1))
    increment = remapped + diag_ref[...] * static + off * (left + right)
    increment_ref[...] = increment
    misfit = obs_ref[...] * (increment - innov_ref[...])
    coupled = off * misfit
    left = jnp.where(lane == 0, coupled_before, pltpu.roll(coupled, 1, 1))
    right = jnp.where(lane == cols - 1, coupled_after, pltpu.roll(coupled, cols - 1, 1))
    grad_ref[...] = static + diag_ref[...] * misfit + left + right


def call(kernel, out_shape, spaces, scratch=(), out=VMEM, cost=None):
    return pl.pallas_call(
        kernel,
        out_shape=out_shape,
        in_specs=spaces,
        out_specs=jax.tree.map(lambda _: out, out_shape),
        scratch_shapes=scratch,
        cost_estimate=cost,
        compiler_params=pltpu.CompilerParams(vmem_limit_bytes=40 * MIB),
    )


def body(
    perturb,
    control,
    level_loc,
    static_control,
    filter_diag,
    filter_off,
    send_src,
    send_wt,
    counts,
    recv_tgt,
    obs_weight,
    innovation,
):
    levels, members, band_cols = control.shape
    tile_cols = static_control.shape[1]
    n = lax.axis_size("tile")
    groups = lax.axis_size("grp")
    cap = send_src.shape[2]
    shape = jax.ShapeDtypeStruct
    swap = [(0, 1), (1, 0)]
    lev = lax.axis_index("lev").astype(jnp.int32).reshape(1)
    pos = lax.axis_index("tile").astype(jnp.int32).reshape(1)
    other_control = lax.ppermute(control, "lev", swap)
    width = levels * SUB
    level_mix, own_mix, given_mix = call(
        mix_kernel,
        (shape((2, width, 2 * width), BF16), shape((2, width, width), BF16), shape((levels, width), F32)),
        [SMEM, VMEM],
        cost=pl.CostEstimate(flops=10**9, bytes_accessed=0, transcendentals=0),
    )(lev, level_loc)
    own_sum = call(sum_kernel, shape((levels, band_cols), F32), [VMEM] * 4)(perturb, control, other_control, level_mix)
    flat = shape((levels, tile_cols), F32)
    mine_shape = shape((band_cols // width * levels + levels, width), F32)
    diag, off = filter_diag.reshape(1, -1), filter_off.reshape(1, -1)
    if n * cap <= tile_cols and n >= 4 and lax.axis_size("lev") == 2 and n & (n - 1) == 0 and band_cols * tile_cols <= 2**20:
        rows = Rows(levels, n)
        stacked = band_cols // cap * levels
        rests = call(functools.partial(static_kernel, band_cols), [shape((rows.total, cap), F32)] * n, [SMEM] * 2 + [VMEM] * 8)(
            pos, counts, static_control, diag, off, obs_weight, innovation, send_src, send_wt, recv_tgt
        )
        sums = [own_sum]
        sums[0], other_perturb = lax.optimization_barrier((sums[0], lax.ppermute(perturb, "lev", swap)))
        for k in range(1, groups):
            sums.append(lax.ppermute(sums[0], "grp", [(g, (g + k) % groups) for g in range(groups)]))
        high = n // 2
        near = list(range(1, high))
        after = [near[0], *reversed(near[1:])]
        stages = [[0, *near], [high, *(r + high for r in after[:-1])], [after[-1] + high]]
        block = stacked + rows.total
        total, *blocks = call(
            functools.partial(blocks_kernel, groups, levels, high - 1),
            [shape((stacked, cap), F32)]
            + [shape((block, cap), F32)] * (high - 1)
            + [shape((block + 2 * levels * (high - 1), cap), F32)],
            [VMEM] * (groups + n - 1),
        )(*sums, *rests[1:])

        def to(r, block):
            return [lax.ppermute(block, "tile", [(i, i ^ r) for i in range(n)])]

        arrived = {0: [total, rests[0]]} | {r: to(r, blocks[r - 1]) for r in (high, *near)}
        passed = call(
            functools.partial(relay_kernel, levels, stacked), [shape((block, cap), F32)] * (high - 1), [VMEM]
        )(*arrived[high])
        for r in after:
            arrived[r + high] = to(r, passed[r - 1])
        slots, carried, picks = [], [], []
        for count in range(1, len(stages)):
            labels = sum(stages[:count], [])
            refs = [ref for r in labels for ref in arrived[r]]
            outs = [
                shape((n, 2 * levels, len(stages[count - 1]) * cap), BF16),
                shape((len(labels), levels, cap), F32),
                flat,
            ] + [shape((n, band_cols, cap), BF16)] * (count == 1)
            new, *carried = call(
                functools.partial(stage_kernel, n, levels, band_cols, tile_cols, stages[:count]),
                outs,
                [VMEM] * (len(refs) + len(slots) + len(carried)),
                cost=pl.CostEstimate(flops=(10**9, 10**6)[count - 1], bytes_accessed=0, transcendentals=0),
            )(*refs, *slots, *carried)
            slots.append(new)
            picks += carried[2:]
            carried = carried[:2]
        met, remap = carried
        refs = [ref for r in sum(stages, []) for ref in arrived[r]] + slots + [met] + picks
        mine, new, tables = call(
            functools.partial(shared_kernel, n, levels, band_cols, tile_cols, stages),
            (mine_shape, shape((n, 2 * levels, len(stages[-1]) * cap), BF16), shape((n, n + EXTRA, cap), F32)),
            [SMEM] + [VMEM] * (1 + len(refs)),
            cost=pl.CostEstimate(flops=10**9, bytes_accessed=0, transcendentals=0),
        )(pos, given_mix, *refs)
        slots.append(new)
        increment, grad_static = call(
            functools.partial(outputs_kernel, stages), (flat, flat), [SMEM] + [VMEM] * (len(slots) + 7)
        )(pos, *slots, remap, tables, static_control, diag, off, obs_weight, innovation)
    else:
        other_perturb = lax.ppermute(perturb, "lev", swap)
        payload = call(
            band_kernel,
            shape((groups, n, levels + EXTRA, cap), F32),
            [SMEM] + [VMEM] * 4,
            [pltpu.VMEM((2 * levels, band_cols), BF16)],
        )(counts, own_sum, static_control, send_src, send_wt)
        arrived = lax.all_to_all(
            payload.reshape(groups * n, levels + EXTRA, cap), ("grp", "tile"), split_axis=0, concat_axis=0, tiled=True
        ).reshape(groups, n, levels + EXTRA, cap)
        increment, partial, giving = call(
            tile_kernel, (flat, flat, shape((n, levels + EXTRA, cap), F32)), [SMEM] + [VMEM] * 7
        )(pos, arrived, recv_tgt, static_control, diag, off, obs_weight, innovation)
        returned = lax.all_to_all(giving, "tile", split_axis=0, concat_axis=0, tiled=True)
        grad_static, mine = call(
            functools.partial(adjoint_kernel, band_cols), (flat, mine_shape), [SMEM, SMEM] + [VMEM] * 5
        )(pos, counts, returned, send_src, send_wt, partial, given_mix)
    theirs = lax.ppermute(mine, "lev", swap)
    own = call(ens_own_kernel, shape(control.shape, F32), [VMEM] * 4)(perturb, mine, own_mix, control)
    grad_ens, increment, grad_static = call(
        ens_kernel,
        (shape(control.shape, F32), flat, flat),
        [VMEM] * 5,
        [pltpu.VMEM(control.shape, F32), pltpu.SemaphoreType.DMA((2 + members // SUB,))],
        out=HBM,
    )(other_perturb, theirs, own, increment, grad_static)
    return (increment, grad_static, grad_ens)


def solution(mesh):
    return jax.shard_map(
        body,
        mesh=mesh,
        in_specs=(
            P("lev", "grp", "tile"),
            P("lev", "grp", "tile"),
            P("lev", None),
            P("lev", "tile"),
            P("tile"),
            P("tile"),
            P("tile", None, None),
            P("tile", None, None),
            P("tile", None),
            P("tile", None, None),
            P("lev", "tile"),
            P("lev", "tile"),
        ),
        out_specs=(P("lev", "tile"), P("lev", "tile"), P("lev", "grp", "tile")),
        check_vma=False,
    )
```

```python
import functools

import jax
import jax.numpy as jnp
from jax import lax
from jax.experimental import pallas as pl
from jax.experimental.pallas import tpu as pltpu
from jax.sharding import PartitionSpec as P

F32 = jnp.float32
BF16 = jnp.bfloat16
SUB = 8
EXTRA = 8
VMEM = pl.BlockSpec(memory_space=pltpu.VMEM)
HBM = pl.BlockSpec(memory_space=pltpu.HBM)
SMEM = pl.BlockSpec(memory_space=pltpu.SMEM)
MIB = 1024 * 1024


def halves(values):
    high = values.astype(BF16)
    low = (values - high.astype(F32)).astype(BF16)
    return high, low


def product(a, b, dims=((1,), (0,))):
    return lax.dot_general(a, b, (dims, ((), ())), preferred_element_type=F32)


def select(values, chosen, dims=((1,), (0,))):
    rows = values.shape[0]
    both = product(jnp.concatenate(halves(values), axis=0), chosen, dims)
    return both[:rows] + both[rows:]


def iota(shape, axis):
    return lax.broadcasted_iota(jnp.int32, shape, axis)


def wide_rows(matrix, start, count):
    cols = matrix.shape[1]
    shape = (cols, count * SUB)
    place = (iota(shape, 1) // SUB + start) % cols
    pick = (place == iota(shape, 0)).astype(BF16)
    high, low = halves(matrix)
    return product(high, pick) + product(low, pick)


def spread(wide):
    rows, cols = wide.shape
    tall = jnp.broadcast_to(wide[:, None, :], (rows, SUB, cols)).reshape(rows * SUB, cols)
    return jnp.where(iota(tall.shape, 0) % SUB == iota(tall.shape, 1) % SUB, tall, 0.0)


def mix(weights, values):
    high, low = halves(values)
    rows = weights[0].shape[0]
    both = product(jnp.concatenate(weights, axis=0), high)
    return both[:rows] + (product(weights[0], low) + both[rows:])


def one_hot(index, size):
    rows = lax.broadcasted_iota(jnp.int32, (size, index.shape[1]), 0)
    return jnp.where(rows == index, 1.0, 0.0).astype(BF16)


def column_as_row(column, lane, offset):
    n = column.shape[0]
    place = lax.broadcasted_iota(jnp.int32, (n, 128), 1) == lax.broadcasted_iota(jnp.int32, (n, 128), 0) + offset
    return jnp.sum(jnp.where(place, column, 0.0), axis=0, keepdims=True)


def row_as_column(row, n, offset):
    place = lax.broadcasted_iota(jnp.int32, (n, 128), 1) == lax.broadcasted_iota(jnp.int32, (n, 128), 0) + offset
    return jnp.sum(jnp.where(place, row, 0.0), axis=1, keepdims=True)


def edge_rows(values):
    n = values.shape[0]
    row = column_as_row(values[:, -1:], None, 0) + column_as_row(values[:, :1], None, n)
    return jnp.broadcast_to(row, (EXTRA, 128))


def factor_of(counts_ref, weight_ref, d):
    slot = lax.broadcasted_iota(jnp.int32, (1, weight_ref.shape[2]), 1)
    return jnp.where(slot < counts_ref[0, d], weight_ref[0, pl.ds(d, 1), :], 0.0)


def loop(n, step, init):
    return lax.fori_loop(0, n, step, init, unroll=n if n <= 8 else 1)


def mix_kernel(lev_ref, loc_ref, mix_ref, own_ref, given_ref):
    levels = loc_ref.shape[0]
    start = lev_ref[0] * levels
    loc = loc_ref[...]
    mix_ref[0], mix_ref[1] = halves(spread(wide_rows(loc, start, 2 * levels)))
    own_ref[0], own_ref[1] = halves(spread(wide_rows(loc, start, levels)).T)
    given_ref[...] = wide_rows(loc, levels - start, levels)


def sum_kernel(perturb_ref, control_ref, other_ref, mix_ref, out_ref):
    levels, members, cols = perturb_ref.shape
    perturb = perturb_ref[...].astype(F32)
    total = jnp.zeros((levels, SUB, cols), F32)
    for m in range(0, members, SUB):
        tile = jnp.concatenate([control_ref[:, m : m + SUB, :], other_ref[:, m : m + SUB, :]], axis=0)
        mixed = mix((mix_ref[0], mix_ref[1]), tile.reshape(2 * levels * SUB, cols))
        total = total + perturb[:, m : m + SUB, :] * mixed.reshape(levels, SUB, cols)
    out_ref[...] = jnp.sum(total, axis=1)


def band_kernel(counts_ref, sum_ref, static_ref, src_ref, weight_ref, out_ref, acc_ref):
    levels, cols = sum_ref.shape
    acc_ref[...] = jnp.concatenate(halves(sum_ref[...]), axis=0)
    n = src_ref.shape[1]
    edges = edge_rows(static_ref[...])

    def step(d, carry):
        chosen = one_hot(src_ref[0, pl.ds(d, 1), :], cols)
        both = product(acc_ref[...], chosen)
        payload = (both[:levels] + both[levels:]) * factor_of(counts_ref, weight_ref, d)
        for g in range(out_ref.shape[0]):
            out_ref[g, d, :levels, :] = payload
            out_ref[g, d, levels:, :] = edges
        return carry

    loop(n, step, 0)


def tile_kernel(pos_ref, arrived_ref, tgt_ref, static_ref, diag_ref, off_ref, obs_ref, innov_ref,
                increment_ref, partial_ref, out_ref):
    levels, cols = static_ref.shape
    groups, n = arrived_ref.shape[:2]
    me = pos_ref[0]

    def step(s, total):
        values = sum(arrived_ref[g, s, :levels, :] for g in range(groups))
        chosen = one_hot(tgt_ref[0, pl.ds(s, 1), :], cols)
        return total + select(values, chosen, ((1,), (1,)))

    remapped = loop(n, step, jnp.zeros((levels, cols), F32))
    before = arrived_ref[0, jnp.maximum(me - 1, 0), levels : levels + 1, :]
    after = arrived_ref[0, jnp.minimum(me + 1, n - 1), levels : levels + 1, :]
    before = jnp.where(me > 0, row_as_column(before, levels, 0), 0.0)
    after = jnp.where(me < n - 1, row_as_column(after, levels, levels), 0.0)
    static = static_ref[...]
    lane = lax.broadcasted_iota(jnp.int32, (levels, cols), 1)
    left = jnp.where(lane == 0, before, pltpu.roll(static, 1, 1))
    right = jnp.where(lane == cols - 1, after, pltpu.roll(static, cols - 1, 1))
    increment = remapped + diag_ref[...] * static + off_ref[...] * (left + right)
    increment_ref[...] = increment
    misfit = obs_ref[...] * (increment - innov_ref[...])
    coupled = off_ref[...] * misfit
    left = jnp.where(lane == 0, 0.0, pltpu.roll(coupled, 1, 1))
    right = jnp.where(lane == cols - 1, 0.0, pltpu.roll(coupled, cols - 1, 1))
    partial_ref[...] = static + diag_ref[...] * misfit + left + right
    edges = edge_rows(coupled)
    both = jnp.concatenate(halves(misfit), axis=0)

    def give(s, carry):
        chosen = one_hot(tgt_ref[0, pl.ds(s, 1), :], cols)
        picked = product(both, chosen)
        out_ref[s, :levels, :] = picked[:levels] + picked[levels:]
        out_ref[s, levels:, :] = edges
        return carry

    loop(n, give, 0)


def adjoint_kernel(band, pos_ref, counts_ref, returned_ref, src_ref, weight_ref, partial_ref, mix_ref, grad_ref, out_ref):
    levels, cols = partial_ref.shape
    n = returned_ref.shape[0]
    me = pos_ref[0]

    def step(d, total):
        values = returned_ref[d, :levels, :] * factor_of(counts_ref, weight_ref, d)
        return total + select(values, one_hot(src_ref[0, pl.ds(d, 1), :], band), ((1,), (1,)))

    out_ref[...] = band_rows(loop(n, step, jnp.zeros((levels, band), F32)), mix_ref[...])
    before = returned_ref[jnp.maximum(me - 1, 0), levels : levels + 1, :]
    after = returned_ref[jnp.minimum(me + 1, n - 1), levels : levels + 1, :]
    before = jnp.where(me > 0, row_as_column(before, levels, 0), 0.0)
    after = jnp.where(me < n - 1, row_as_column(after, levels, levels), 0.0)
    lane = lax.broadcasted_iota(jnp.int32, (levels, cols), 1)
    grad_ref[...] = partial_ref[...] + (jnp.where(lane == 0, before, 0.0) + jnp.where(lane == cols - 1, after, 0.0))


def band_rows(band, weights):
    width = weights.shape[1]
    return jnp.concatenate([band[:, at : at + width] for at in range(0, band.shape[1], width)] + [weights], axis=0)


def ens_tiles(perturb_ref, rows_ref, weights, before_ref):
    levels, members, cols = perturb_ref.shape
    width = rows_ref.shape[1]
    parts = [rows_ref[i * levels : (i + 1) * levels, :] for i in range(cols // width)]
    grad = jnp.concatenate(parts, axis=1)[:, None, :]
    perturb = perturb_ref[...].astype(F32)
    for m in range(0, members, SUB):
        place = (slice(None), slice(m, m + SUB), slice(None))
        tile = (perturb[place] * grad).reshape(levels * SUB, cols)
        yield place, before_ref[place] + mix(weights, tile).reshape(levels, SUB, cols)


def ens_own_kernel(perturb_ref, mine_ref, weights_ref, control_ref, out_ref):
    for place, values in ens_tiles(perturb_ref, mine_ref, (weights_ref[0], weights_ref[1]), control_ref):
        out_ref[place] = values


def ens_kernel(perturb_ref, theirs_ref, own_ref, *refs):
    count = (len(refs) - 3) // 2
    flats, (out_hbm, *flat_hbms), (out_ref, sems) = refs[:count], refs[count : 2 * count + 1], refs[2 * count + 1 :]
    copies = [pltpu.make_async_copy(a, b, sems.at[i]) for i, (a, b) in enumerate(zip(flats, flat_hbms))]
    for copy in copies:
        copy.start()
    levels = perturb_ref.shape[0]
    weights = halves(spread(theirs_ref[theirs_ref.shape[0] - levels :, :]).T)
    for place, values in ens_tiles(perturb_ref, theirs_ref, weights, own_ref):
        out_ref[place] = values
        half = out_ref.shape[0] // 2
        for part in (slice(0, half), slice(half, 2 * half)):
            piece = (part, *place[1:])
            copies.append(pltpu.make_async_copy(out_ref.at[piece], out_hbm.at[piece], sems.at[len(copies)]))
            copies[-1].start()
    for copy in copies:
        copy.wait()


class Rows:
    def __init__(self, levels, n):
        self.weight = slice(0, levels)
        self.base = slice(levels, 2 * levels)
        at = 2 * levels
        self.factor, self.index, self.edge = at, at + n, at + 2 * n
        self.total = at + 2 * n + EXTRA


def static_kernel(band, pos_ref, counts_ref, static_ref, diag_ref, off_ref, obs_ref, innov_ref, src_ref, weight_ref, tgt_ref,
                  *out_refs):
    levels, cols = static_ref.shape
    n = len(out_refs)
    cap = src_ref.shape[2]
    rows = Rows(levels, n)
    peers = [pos_ref[0] ^ r for r in range(n)]
    static, off, obs = static_ref[...], off_ref[...], obs_ref[...]
    lane = lax.broadcasted_iota(jnp.int32, (levels, cols), 1)
    left = jnp.where(lane == 0, 0.0, pltpu.roll(static, 1, 1))
    right = jnp.where(lane == cols - 1, 0.0, pltpu.roll(static, cols - 1, 1))
    base = diag_ref[...] * static + off * (left + right) - innov_ref[...]
    coupled = off * obs
    ends = [v[:, i] for v in (static, coupled, base) for i in (slice(cols - 1, cols), slice(0, 1))]
    edge = sum(column_as_row(end, None, i * levels) for i, end in enumerate(ends))
    place = lax.broadcasted_iota(jnp.int32, (1, cap), 1)
    edge = edge + jnp.where(place == 6 * levels, off[:, cols - 1 :], 0.0)
    edge = edge + jnp.where(place == 6 * levels + 1, off[:, :1], 0.0)
    edge = jnp.broadcast_to(edge, (EXTRA, cap))
    both = jnp.concatenate(halves(jnp.concatenate([obs, base], axis=0)), axis=0)
    tgts = [tgt_ref[0, pl.ds(peer, 1), :] for peer in peers]
    src = jnp.concatenate([src_ref[0, pl.ds(peer, 1), :] for peer in peers], axis=0).astype(F32)
    index = jnp.concatenate(tgts, axis=0).astype(F32) * float(band) + src
    factor = jnp.concatenate([factor_of(counts_ref, weight_ref, peer) for peer in peers], axis=0)
    for r, out_ref in enumerate(out_refs):
        picked = product(both, one_hot(tgts[r], cols))
        out_ref[: 2 * levels, :] = picked[: 2 * levels] + picked[2 * levels :]
        out_ref[rows.factor : rows.factor + n, :] = factor
        out_ref[rows.index : rows.index + n, :] = index
        out_ref[rows.edge :, :] = edge


def blocks_kernel(groups, levels, relayed, *refs):
    sums, refs = refs[:groups], refs[groups:]
    count = (len(refs) - 1 - relayed) // 2
    rests, relays, total_ref, out_refs = refs[:count], refs[count : count + relayed], refs[count + relayed], refs[-count:]
    total = sum(ref[...] for ref in sums)
    cap = total_ref.shape[1]
    total = jnp.concatenate([total[:, at : at + cap] for at in range(0, total.shape[1], cap)], axis=0)
    total_ref[...] = total
    for i, (rest_ref, out_ref) in enumerate(zip(rests, out_refs)):
        parts = [total, rest_ref[...]]
        if i == count - 1:
            parts += [ref[: 2 * levels, :] for ref in relays]
        out_ref[...] = jnp.concatenate(parts, axis=0)


def relay_kernel(levels, stacked, got_ref, *refs):
    count = len(refs) // 2
    head = refs[0].shape[0]
    for i, (block_ref, out_ref) in enumerate(zip(refs[:count], refs[count:])):
        at = head + 2 * levels * i
        out_ref[...] = jnp.concatenate(
            [block_ref[...], got_ref[:stacked, :], got_ref[at : at + 2 * levels, :], got_ref[stacked + 2 * levels : head, :]],
            axis=0,
        )


class Block:
    def __init__(self, refs, n, levels, band, base=0):
        cap = refs[0].shape[1]
        self.levels, self.parts, self.cap = levels, band // cap, cap
        self.sums_ref, self.rest_ref = refs[0], refs[-1]
        self.base = base
        self.head = 0 if len(refs) == 2 else base + self.parts * levels
        self.rows = Rows(levels, n)
        words = self.rest(self.rows.index, n)
        self.tgt = jnp.floor((words + 0.5) * (1.0 / band))
        self.src = words - self.tgt * float(band)
        self.factor = self.rest(self.rows.factor, n)

    def rest(self, at, size):
        return self.rest_ref[self.head + at : self.head + at + size, :]

    def sums(self):
        parts = [self.sums_ref[self.base + i * self.levels : self.base + (i + 1) * self.levels, :] for i in range(self.parts)]
        return jnp.concatenate(halves(jnp.concatenate(parts, axis=1)), axis=0)


def line(table, i):
    return table[i : i + 1]


def pick_source(block, r):
    band = block.parts * block.cap
    column = lax.broadcasted_iota(jnp.int32, (band, block.cap), 0).astype(F32)
    return jnp.where(column == line(block.src, r), 1.0, 0.0).astype(BF16)


def fill_slots(bands, blocks, n, slots_ref):
    for i, s in enumerate(bands):
        block = blocks[s]
        both = block.sums()
        for d in range(n):
            picked = product(both, pick_source(block, s ^ d))
            values = (picked[: block.levels] + picked[block.levels :]) * line(block.factor, s ^ d)
            slots_ref[d, :, i * block.cap : (i + 1) * block.cap] = jnp.concatenate(halves(values), axis=0)


def met_at(d, block, bands, slots_ref):
    own = jnp.broadcast_to(line(block.tgt, d), (block.cap, block.cap)).T
    same = [jnp.where(own == line(block.tgt, s ^ d), 1.0, 0.0).astype(BF16) for s in bands]
    met = product(slots_ref[d], jnp.concatenate(same, axis=1), ((1,), (1,)))
    return met[: block.levels] + met[block.levels :]


def land(table, bands, slots_ref, cols):
    cap = table.shape[1]
    row = lax.broadcasted_iota(jnp.int32, (cols, cap), 0).astype(F32)
    total = 0.0
    for i, s in enumerate(bands):
        landing = jnp.where(row == line(table, s), 1.0, 0.0).astype(BF16)
        total = total + product(slots_ref[0, :, i * cap : (i + 1) * cap], landing, ((1,), (1,)))
    levels = total.shape[0] // 2
    return total[:levels] + total[levels:]


def open_blocks(labels, refs, n, levels, band):
    blocks = {0: Block(refs[:2], n, levels, band)}
    refs = refs[2:]
    for i, r in enumerate(labels[1:]):
        base = refs[i].shape[0] // 2 if r >= n // 2 + n // 4 else 0
        blocks[r] = Block(refs[i : i + 1], n, levels, band, base)
    return blocks, refs[len(labels) - 1 :]


def stage_kernel(n, levels, band, cols, stages, *refs):
    known = sum(stages[:-1], [])
    blocks, refs = open_blocks(known + stages[-1], refs, n, levels, band)
    old, refs = refs[: len(stages) - 1], refs[len(stages) - 1 :]
    if known:
        met_old, remap_old, slots_ref, met_ref, remap_ref = refs
    else:
        slots_ref, met_ref, remap_ref, pick_ref = refs
        for d in range(n):
            pick_ref[d] = pick_source(blocks[0], d)
    fill_slots(stages[-1], blocks, n, slots_ref)
    for i, (d, block) in enumerate(blocks.items()):
        met = met_at(d, block, stages[-1], slots_ref)
        if d in known:
            met = met + met_old[i]
        else:
            for bands, ref in zip(stages, old):
                met = met + met_at(d, block, bands, ref)
        met_ref[i] = met
    landed = land(blocks[0].tgt, stages[-1], slots_ref, cols)
    remap_ref[...] = landed + remap_old[...] if known else landed


def shared_kernel(n, levels, band, cols, stages, pos_ref, mix_ref, *refs):
    known = sum(stages[:-1], [])
    blocks, refs = open_blocks(known + stages[-1], refs, n, levels, band)
    old, refs = refs[: len(stages) - 1], refs[len(stages) - 1 :]
    met_old, pick_ref, out_ref, slots_ref, tables_ref = refs
    me = pos_ref[0]
    for r, block in blocks.items():
        there = me ^ r
        tables_ref[there, :n, :] = block.tgt
        tables_ref[there, n:, :] = block.rest(block.rows.edge, EXTRA)
    fill_slots(stages[-1], blocks, n, slots_ref)
    last = cols - 1.0
    total = jnp.zeros((levels, band), F32)
    for i, (d, block) in enumerate(blocks.items()):
        value = met_at(d, block, stages[-1], slots_ref) + block.rest(levels, levels)
        if d in known:
            value = value + met_old[i]
        else:
            for bands, ref in zip(stages, old):
                value = value + met_at(d, block, bands, ref)
        edge = block.rest(block.rows.edge, 1)
        own = line(block.tgt, d)
        there = me ^ d
        before = tables_ref[jnp.maximum(there - 1, 0), n : n + 1, :]
        near = jnp.where((own == 0.0) & (there > 0), edge[:, 6 * levels + 1 : 6 * levels + 2], 0.0)
        value = value + row_as_column(before, levels, 0) * near
        after = tables_ref[jnp.minimum(there + 1, n - 1), n : n + 1, :]
        near = jnp.where((own == last) & (there < n - 1), edge[:, 6 * levels : 6 * levels + 1], 0.0)
        value = value + row_as_column(after, levels, levels) * near
        given = block.rest(0, levels) * value * line(blocks[0].factor, d)
        total = total + select(given, pick_ref[d], ((1,), (1,)))
    out_ref[...] = band_rows(total, mix_ref[...])


def outputs_kernel(stages, pos_ref, *refs):
    slots_refs, refs = refs[: len(stages)], refs[len(stages) :]
    remap_ref, tables_ref, static_ref, diag_ref, off_ref, obs_ref, innov_ref, increment_ref, grad_ref = refs
    levels, cols = static_ref.shape
    n = tables_ref.shape[0]
    cap = tables_ref.shape[2]
    me = pos_ref[0]
    given = [
        (s, ref, slice(i * cap, (i + 1) * cap)) for bands, ref in zip(stages, slots_refs) for i, s in enumerate(bands)
    ]
    remapped = remap_ref[...] + land(tables_ref[me, :n, :], stages[-1], slots_refs[-1], cols)
    static, off = static_ref[...], off_ref[...]
    lane = lax.broadcasted_iota(jnp.int32, (levels, cols), 1)

    def beside(there, exists, column, own_end, side):
        edge = tables_ref[there, n : n + 1, :]
        static_end, coupling, base = (row_as_column(edge, levels, (2 * i + side) * levels) for i in range(3))
        far = me ^ there
        landed = []
        for s, ref, place in given:
            values = ref[far, :levels, place].astype(F32) + ref[far, levels:, place].astype(F32)
            landed.append(jnp.where(tables_ref[there, pl.ds(s ^ far, 1), :] == column, values, 0.0))
        remap_end = jnp.sum(sum(landed), axis=1, keepdims=True)
        off_end = edge[:, 6 * levels + side : 6 * levels + side + 1]
        coupled = coupling * (remap_end + base + off_end * own_end)
        return jnp.where(exists, static_end, 0.0), jnp.where(exists, coupled, 0.0)

    before, coupled_before = beside(jnp.maximum(me - 1, 0), me > 0, cols - 1.0, static[:, :1], 0)
    after, coupled_after = beside(jnp.minimum(me + 1, n - 1), me < n - 1, 0.0, static[:, cols - 1 :], 1)
    left = jnp.where(lane == 0, before, pltpu.roll(static, 1, 1))
    right = jnp.where(lane == cols - 1, after, pltpu.roll(static, cols - 1, 1))
    increment = remapped + diag_ref[...] * static + off * (left + right)
    increment_ref[...] = increment
    misfit = obs_ref[...] * (increment - innov_ref[...])
    coupled = off * misfit
    left = jnp.where(lane == 0, coupled_before, pltpu.roll(coupled, 1, 1))
    right = jnp.where(lane == cols - 1, coupled_after, pltpu.roll(coupled, cols - 1, 1))
    grad_ref[...] = static + diag_ref[...] * misfit + left + right


def call(kernel, out_shape, spaces, scratch=(), out=VMEM, cost=None):
    return pl.pallas_call(
        kernel,
        out_shape=out_shape,
        in_specs=spaces,
        out_specs=jax.tree.map(lambda _: out, out_shape),
        scratch_shapes=scratch,
        cost_estimate=cost,
        compiler_params=pltpu.CompilerParams(vmem_limit_bytes=40 * MIB),
    )


def body(
    perturb,
    control,
    level_loc,
    static_control,
    filter_diag,
    filter_off,
    send_src,
    send_wt,
    counts,
    recv_tgt,
    obs_weight,
    innovation,
):
    levels, members, band_cols = control.shape
    tile_cols = static_control.shape[1]
    n = lax.axis_size("tile")
    groups = lax.axis_size("grp")
    cap = send_src.shape[2]
    shape = jax.ShapeDtypeStruct
    swap = [(0, 1), (1, 0)]
    lev = lax.axis_index("lev").astype(jnp.int32).reshape(1)
    pos = lax.axis_index("tile").astype(jnp.int32).reshape(1)
    other_control = lax.ppermute(control, "lev", swap)
    width = levels * SUB
    level_mix, own_mix, given_mix = call(
        mix_kernel,
        (shape((2, width, 2 * width), BF16), shape((2, width, width), BF16), shape((levels, width), F32)),
        [SMEM, VMEM],
        cost=pl.CostEstimate(flops=10**9, bytes_accessed=0, transcendentals=0),
    )(lev, level_loc)
    own_sum = call(sum_kernel, shape((levels, band_cols), F32), [VMEM] * 4)(perturb, control, other_control, level_mix)
    flat = shape((levels, tile_cols), F32)
    mine_shape = shape((band_cols // width * levels + levels, width), F32)
    diag, off = filter_diag.reshape(1, -1), filter_off.reshape(1, -1)
    if n * cap <= tile_cols and n >= 8 and lax.axis_size("lev") == 2 and n & (n - 1) == 0 and band_cols * tile_cols <= 2**20:
        rows = Rows(levels, n)
        stacked = band_cols // cap * levels
        rests = call(functools.partial(static_kernel, band_cols), [shape((rows.total, cap), F32)] * n, [SMEM] * 2 + [VMEM] * 8)(
            pos, counts, static_control, diag, off, obs_weight, innovation, send_src, send_wt, recv_tgt
        )
        sums = [own_sum]
        sums[0], other_perturb = lax.optimization_barrier((sums[0], lax.ppermute(perturb, "lev", swap)))
        for k in range(1, groups):
            sums.append(lax.ppermute(sums[0], "grp", [(g, (g + k) % groups) for g in range(groups)]))
        low, high = n // 4, n // 2
        order = [high, *range(1, low), *range(high + 1, high + low), *reversed(range(low, high))]
        stages = [[0] + order[: -low], *([r, r + high] for r in order[-low:])]
        direct = order[::-1]
        total, *blocks = call(
            functools.partial(blocks_kernel, groups, levels, low),
            [shape((stacked, cap), F32)]
            + [shape((stacked + rows.total + (r == high) * 2 * levels * low, cap), F32) for r in direct],
            [VMEM] * (groups + len(direct) + low),
        )(*sums, *[rests[r] for r in direct], *rests[high + low :])
        blocks = dict(zip(direct, blocks))

        def to(r):
            return lax.ppermute(blocks[r], "tile", [(i, i ^ r) for i in range(n)])

        arrived = {0: [total, rests[0]]} | {r: [to(r)] for r in order[:-low]}
        carriers = list(range(low, high))
        joined = call(
            functools.partial(relay_kernel, levels, stacked),
            [shape((2 * (stacked + rows.total), cap), F32)] * low,
            [VMEM] * (1 + low),
        )(arrived[high][0], *[blocks[r] for r in carriers])
        blocks |= dict(zip(carriers, joined))
        for r in order[-low:]:
            arrived[r] = arrived[r + high] = [to(r)]
        slots, carried, picks = [], [], []
        for count in range(1, len(stages)):
            labels = sum(stages[:count], [])
            refs = [ref for r in labels for ref in arrived[r]]
            outs = [
                shape((n, 2 * levels, len(stages[count - 1]) * cap), BF16),
                shape((len(labels), levels, cap), F32),
                flat,
            ] + [shape((n, band_cols, cap), BF16)] * (count == 1)
            new, *carried = call(
                functools.partial(stage_kernel, n, levels, band_cols, tile_cols, stages[:count]),
                outs,
                [VMEM] * (len(refs) + len(slots) + len(carried)),
                cost=pl.CostEstimate(flops=10**9, bytes_accessed=0, transcendentals=0),
            )(*refs, *slots, *carried)
            slots.append(new)
            picks += carried[2:]
            carried = carried[:2]
        met, remap = carried
        refs = [ref for r in sum(stages, []) for ref in arrived[r]] + slots + [met] + picks
        mine, new, tables = call(
            functools.partial(shared_kernel, n, levels, band_cols, tile_cols, stages),
            (mine_shape, shape((n, 2 * levels, len(stages[-1]) * cap), BF16), shape((n, n + EXTRA, cap), F32)),
            [SMEM] + [VMEM] * (1 + len(refs)),
            cost=pl.CostEstimate(flops=10**9, bytes_accessed=0, transcendentals=0),
        )(pos, given_mix, *refs)
        slots.append(new)
        increment, grad_static = call(
            functools.partial(outputs_kernel, stages), (flat, flat), [SMEM] + [VMEM] * (len(slots) + 7)
        )(pos, *slots, remap, tables, static_control, diag, off, obs_weight, innovation)
    else:
        other_perturb = lax.ppermute(perturb, "lev", swap)
        payload = call(
            band_kernel,
            shape((groups, n, levels + EXTRA, cap), F32),
            [SMEM] + [VMEM] * 4,
            [pltpu.VMEM((2 * levels, band_cols), BF16)],
        )(counts, own_sum, static_control, send_src, send_wt)
        arrived = lax.all_to_all(
            payload.reshape(groups * n, levels + EXTRA, cap), ("grp", "tile"), split_axis=0, concat_axis=0, tiled=True
        ).reshape(groups, n, levels + EXTRA, cap)
        increment, partial, giving = call(
            tile_kernel, (flat, flat, shape((n, levels + EXTRA, cap), F32)), [SMEM] + [VMEM] * 7
        )(pos, arrived, recv_tgt, static_control, diag, off, obs_weight, innovation)
        returned = lax.all_to_all(giving, "tile", split_axis=0, concat_axis=0, tiled=True)
        grad_static, mine = call(
            functools.partial(adjoint_kernel, band_cols), (flat, mine_shape), [SMEM, SMEM] + [VMEM] * 5
        )(pos, counts, returned, send_src, send_wt, partial, given_mix)
    theirs = lax.ppermute(mine, "lev", swap)
    own = call(ens_own_kernel, shape(control.shape, F32), [VMEM] * 4)(perturb, mine, own_mix, control)
    grad_ens, increment, grad_static = call(
        ens_kernel,
        (shape(control.shape, F32), flat, flat),
        [VMEM] * 5,
        [pltpu.VMEM(control.shape, F32), pltpu.SemaphoreType.DMA((2 + 2 * (members // SUB),))],
        out=HBM,
    )(other_perturb, theirs, own, increment, grad_static)
    return (increment, grad_static, grad_ens)


def solution(mesh):
    return jax.shard_map(
        body,
        mesh=mesh,
        in_specs=(
            P("lev", "grp", "tile"),
            P("lev", "grp", "tile"),
            P("lev", None),
            P("lev", "tile"),
            P("tile"),
            P("tile"),
            P("tile", None, None),
            P("tile", None, None),
            P("tile", None),
            P("tile", None, None),
            P("lev", "tile"),
            P("lev", "tile"),
        ),
        out_specs=(P("lev", "tile"), P("lev", "tile"), P("lev", "grp", "tile")),
        check_vma=False,
    )
```
